32 devices in a mesh: dp: 32 (over z, y, x, core).
Axes of the slice: x: 2, y: 2, z: 4, core: 2. Of those that a mesh axis runs over, the one named last changes fastest.
Arguments:
- frames: bfloat16 [160, 1536, 120], P('dp'), may hold values from -6 to 6
- lengths: int32 [160], P('dp'), may hold values from 384 to 1536, as said below
- cotangent: bfloat16 [160, 1536, 120], P('dp'), may hold values from -6 to 6
- master: float32 [339968], P('dp')
- moment_one: float32 [339968], P('dp')
- moment_two: float32 [339968], P('dp'), as said below
- average: float32 [339968], P('dp')
Outputs:
- output: bfloat16 [160, 1536, 120], P('dp')
- input_grad: float32 [160, 1536, 120], P('dp')
- weight_grad: float32 [339968], P('dp')
- new_master: float32 [339968], P('dp')
- new_moment_one: float32 [339968], P('dp')
- new_moment_two: float32 [339968], P('dp')
- new_average: float32 [339968], P('dp')
The draws below stay inside these ranges and needn't reach their ends.
Inputs may be any that keep to these rules, and one draw needn't show every extreme that they name: `lengths`: each length is a multiple of 3, and some utterance has all 1536 frames. `moment_two`: second moments are positive.
All inputs are finite; a program needn't handle non-finite values.
Results may differ from the reference program's by a relative error of at most 0.012.
The reference program's roundings to bfloat16 on the way count: a program that leaves them out, or rounds other values in their place, can miss the bound.
Values may be sent and summed in bfloat16 or wider, within the bound.
No kernel may reach another device: no remote copies, remote signals or barrier semaphores. Data moves between devices by JAX's collectives and lax.ppermute only.
A program may use at most 320 MiB of HBM per device.

```python
import math
import jax
import jax.numpy as jnp
import numpy as np
from jax import lax

D = 120
HEADS = 4
FF = 480
KERNEL = 15
GROUP = 3
REL = 127
STEP = 5
MAXLEN = 1536
LG = 512
HEAD = 90
UTT = 160
TOTAL_FRAMES = 245760
PARAMS = 337500
PFLAT = 339968


def ffn_entries_drawn(prefix):
    return [(prefix + '_gain', (D,), 'gain', 1.0), (prefix + '_bias', (D,), 'bias', 1.0), (prefix + '_up', (D, FF), 'matrix', float(D)), (prefix + '_up_bias', (FF,), 'bias', 1.0), (prefix + '_down', (FF, D), 'matrix', float(FF)), (prefix + '_down_bias', (D,), 'bias', 1.0)]


def layout_drawn():
    attention_part = [('attn_gain', (D,), 'gain', 1.0), ('attn_bias', (D,), 'bias', 1.0), ('query', (D, D), 'matrix', float(D)), ('query_bias', (D,), 'bias', 1.0), ('key', (D, D), 'matrix', float(D)), ('value', (D, D), 'matrix', float(D)), ('value_bias', (D,), 'bias', 1.0), ('output', (D, D), 'matrix', 6.0 * D / MAXLEN), ('output_bias', (D,), 'bias', 1.0), ('relative', (HEADS, 2 * REL + 1), 'table', 1.0)]
    conv_part = [('conv_gain', (D,), 'gain', 1.0), ('conv_bias', (D,), 'bias', 1.0), ('pointwise', (D, 2 * D), 'matrix', float(D)), ('pointwise_bias', (2 * D,), 'bias', 1.0), ('depthwise', (KERNEL, D), 'matrix', float(KERNEL)), ('depthwise_bias', (D,), 'bias', 1.0), ('batch_gain', (D,), 'gain', 1.0), ('batch_bias', (D,), 'bias', 1.0), ('project', (D, D), 'matrix', float(D)), ('project_bias', (D,), 'bias', 1.0)]
    final_part = [('final_gain', (D,), 'gain', 1.0), ('final_bias', (D,), 'bias', 1.0)]
    return ffn_entries_drawn('ffn_one') + attention_part + conv_part + ffn_entries_drawn('ffn_two') + final_part


def normal_piece(key, entries):
    return jax.random.truncated_normal(key, -3.0, 3.0, (entries,), jnp.float32)


def weight_draw(key):
    pieces = []
    for index, entry in enumerate(layout_drawn()):
        seg_name, seg_shape, family, fan_in = entry
        entries = int(math.prod(seg_shape))
        noise = normal_piece(jax.random.fold_in(key, index), entries)
        if family == 'gain':
            pieces.append(1.0 + 0.1 * noise)
        elif family == 'bias':
            pieces.append(0.2 * noise)
        elif family == 'matrix':
            pieces.append(noise * fan_in ** (-0.5))
        else:
            pieces.append(noise)
    pieces.append(0.2 * normal_piece(jax.random.fold_in(key, 1000), PFLAT - PARAMS))
    return jnp.concatenate(pieces)


def grad_scale(family):
    base_size = math.sqrt(TOTAL_FRAMES / 2.0)
    if family == 'gain' or family == 'bias':
        return base_size
    return 0.3 * base_size


def draw_lengths(key, part):
    lowest = max(1, LG // 4)
    span = LG - lowest
    order = jnp.arange(UTT, dtype=jnp.int32)
    centre = lowest + span * order // max(1, UTT - 1)
    reach = max(1, span // 8)
    jitter = jax.random.randint(key, (UTT,), -reach, reach + 1)
    groups = jnp.clip(centre + jitter, lowest, LG)
    groups = groups.at[UTT - 1].set(LG)
    return (groups * GROUP).astype(jnp.int32)


def draw_master(key, part):
    return weight_draw(jax.random.fold_in(key, 11))


def draw_average(key, part):
    return weight_draw(jax.random.fold_in(key, 99))


def draw_moment_one(key, part):
    pieces = []
    for index, entry in enumerate(layout_drawn()):
        seg_name, seg_shape, family, fan_in = entry
        entries = int(math.prod(seg_shape))
        noise = normal_piece(jax.random.fold_in(key, index + 200), entries)
        pieces.append(noise * grad_scale(family))
    pieces.append(normal_piece(jax.random.fold_in(key, 2000), PFLAT - PARAMS))
    return jnp.concatenate(pieces)


def draw_moment_two(key, part):
    pieces = []
    for index, entry in enumerate(layout_drawn()):
        seg_name, seg_shape, family, fan_in = entry
        entries = int(math.prod(seg_shape))
        factor = jnp.exp(jax.random.uniform(jax.random.fold_in(key, index + 400), (entries,), jnp.float32, 0.0, math.log(4.0)))
        pieces.append(factor * grad_scale(family) ** 2)
    pieces.append(jnp.exp(jax.random.uniform(jax.random.fold_in(key, 4000), (PFLAT - PARAMS,), jnp.float32, 0.0, math.log(4.0))))
    return jnp.concatenate(pieces)


def level_of(own_key, extent, split, least, high):
    loudness = 1.0
    for axis_at, parts in split:
        heights = jax.random.uniform(jax.random.fold_in(jax.random.fold_in(own_key, 6), axis_at), (parts,), jnp.float32, least / len(split), high / len(split))
        loudness = loudness * jnp.repeat(jnp.exp(heights), extent[axis_at] // parts).reshape((-1,) + (1,) * (len(extent) - 1 - axis_at))
    return loudness


def gaussian(own_key, shape, scale, limit, cuts=(), held_as=jnp.bfloat16):
    array = scale * jax.random.normal(own_key, shape, jnp.float32)
    if cuts:
        array = array * level_of(own_key, shape, cuts, -0.22, 0.18)
    return jnp.clip(array, -limit, limit).astype(held_as)


def setup_inputs(seed: int = 0) -> dict:
    streams_of = jax.random.split(jax.random.key(seed), 8)
    return {
        "frames": gaussian(streams_of[0], (UTT, MAXLEN, D), 1.0, 6.0, ((0, 32),)),
        "lengths": draw_lengths(jax.random.fold_in(streams_of[7], 71), 0),
        "cotangent": gaussian(streams_of[2], (UTT, MAXLEN, D), 1.0, 6.0, ((0, 32),)),
        "master": draw_master(jax.random.fold_in(streams_of[7], 71), 0),
        "moment_one": draw_moment_one(jax.random.fold_in(streams_of[7], 71), 0),
        "moment_two": draw_moment_two(jax.random.fold_in(streams_of[7], 71), 0),
        "average": draw_average(jax.random.fold_in(streams_of[7], 71), 0),
    }


EPS_NORM = 1e-05
EPS_ADAM = 1e-08
NEG_FILL = -1000000000.0
HIGHEST = lax.Precision.HIGHEST

@jax.custom_vjp
def low(v):
    return lax.optimization_barrier(v.astype(jnp.bfloat16)).astype(jnp.float32)

@jax.custom_vjp
def low_back(v):
    return v

def low_keep(v):
    return (low(v), None)

def low_pass(kept, grad):
    return (grad,)

def back_keep(v):
    return (v, None)

def back_low(kept, grad):
    return (low(grad),)
low.defvjp(low_keep, low_pass)
low_back.defvjp(back_keep, back_low)

def ffn_entries(prefix):
    return [(prefix + '_gain', (D,), 'gain', 1.0), (prefix + '_bias', (D,), 'bias', 1.0), (prefix + '_up', (D, FF), 'matrix', float(D)), (prefix + '_up_bias', (FF,), 'bias', 1.0), (prefix + '_down', (FF, D), 'matrix', float(FF)), (prefix + '_down_bias', (D,), 'bias', 1.0)]

def layout():
    attention_part = [('attn_gain', (D,), 'gain', 1.0), ('attn_bias', (D,), 'bias', 1.0), ('query', (D, D), 'matrix', float(D)), ('query_bias', (D,), 'bias', 1.0), ('key', (D, D), 'matrix', float(D)), ('value', (D, D), 'matrix', float(D)), ('value_bias', (D,), 'bias', 1.0), ('output', (D, D), 'matrix', 6.0 * D / MAXLEN), ('output_bias', (D,), 'bias', 1.0), ('relative', (HEADS, 2 * REL + 1), 'table', 1.0)]
    conv_part = [('conv_gain', (D,), 'gain', 1.0), ('conv_bias', (D,), 'bias', 1.0), ('pointwise', (D, 2 * D), 'matrix', float(D)), ('pointwise_bias', (2 * D,), 'bias', 1.0), ('depthwise', (KERNEL, D), 'matrix', float(KERNEL)), ('depthwise_bias', (D,), 'bias', 1.0), ('batch_gain', (D,), 'gain', 1.0), ('batch_bias', (D,), 'bias', 1.0), ('project', (D, D), 'matrix', float(D)), ('project_bias', (D,), 'bias', 1.0)]
    final_part = [('final_gain', (D,), 'gain', 1.0), ('final_bias', (D,), 'bias', 1.0)]
    return ffn_entries('ffn_one') + attention_part + conv_part + ffn_entries('ffn_two') + final_part

def unpack(flat_vec):
    params = {}
    offset = 0
    for seg_name, seg_shape, family, fan_in in layout():
        entries = int(np.prod(seg_shape))
        params[seg_name] = flat_vec[offset:offset + entries].reshape(seg_shape)
        offset += entries
    return params

def update_tables(total_len):
    rates = np.zeros(total_len, np.float32)
    decays = np.zeros(total_len, np.float32)
    offset = 0
    for seg_name, seg_shape, family, fan_in in layout():
        entries = int(np.prod(seg_shape))
        if family == 'gain':
            rate_value, decay_value = (0.3, 0.0)
        elif family == 'bias':
            rate_value, decay_value = (0.1, 0.0)
        elif family == 'matrix':
            rate_value, decay_value = (fan_in ** (-0.5), 0.01)
        else:
            rate_value, decay_value = (0.5, 0.0)
        rates[offset:offset + entries] = rate_value
        decays[offset:offset + entries] = decay_value
        offset += entries
    return (rates, decays)

def layer_norm(values, gain_vec, shift_vec):
    centre = values - lax.optimization_barrier(jnp.mean(values, axis=-1, keepdims=True))
    spread = lax.optimization_barrier(jnp.mean(centre * centre, axis=-1, keepdims=True))
    return centre * lax.rsqrt(spread + EPS_NORM) * gain_vec + shift_vec

def highest(left, right):
    return jnp.dot(left, right, precision=HIGHEST, preferred_element_type=jnp.float32)

def gate_unit(pre_in, frame_mask):
    return pre_in[..., :D] * jax.nn.sigmoid(pre_in[..., D:]) * frame_mask

def depthwise(gated_in, kernel, shift_vec):
    half_kernel = KERNEL // 2
    time_axis = gated_in.ndim - 2
    widths = [(0, 0)] * time_axis + [(half_kernel, half_kernel), (0, 0)]
    padded = jnp.pad(gated_in, widths)
    result = shift_vec
    for position in range(KERNEL):
        result = result + kernel[position] * lax.slice_in_dim(padded, position, position + MAXLEN, axis=time_axis)
    return result

def feed_forward(values, params, prefix):
    normed = layer_norm(values, params[prefix + '_gain'], params[prefix + '_bias'])
    pre_act = low_back(highest(low(normed), params[prefix + '_up']) + params[prefix + '_up_bias'])
    hidden = jax.nn.silu(pre_act)
    branch = low_back(highest(low(hidden), params[prefix + '_down']) + params[prefix + '_down_bias'])
    return values + 0.5 * branch

def grouped(values):
    return low(values).reshape(LG, HEADS, HEAD).transpose(1, 0, 2)

def attention(values, length, params, rel_bias):
    normed = layer_norm(values, params['attn_gain'], params['attn_bias'])
    normed_low = low(normed)
    query_proj = low_back(highest(normed_low, params['query']) + params['query_bias'])
    key_proj = low_back(highest(normed_low, params['key']))
    value_proj = low_back(highest(normed_low, params['value']) + params['value_bias'])
    scores = jnp.einsum('hid,hjd->hij', grouped(query_proj), grouped(key_proj), precision=HIGHEST) * HEAD ** (-0.5) + rel_bias
    key_valid = jnp.arange(LG) * GROUP < length
    scores = low_back(jnp.where(key_valid[None, None, :], scores, NEG_FILL))
    row_peak = lax.optimization_barrier(jnp.max(scores, axis=-1, keepdims=True))
    exponent = jnp.exp(scores - row_peak)
    soft_weights = exponent / lax.optimization_barrier(jnp.sum(exponent, axis=-1, keepdims=True))
    mixed_heads = jnp.einsum('hij,hjd->hid', low(soft_weights), grouped(value_proj), precision=HIGHEST)
    attended = low_back(mixed_heads.transpose(1, 0, 2).reshape(MAXLEN, D))
    return values + low_back(highest(low(attended), params['output']) + params['output_bias'])

def section_one(values, length, params, rel_bias):
    frame_mask = (jnp.arange(MAXLEN) < length).astype(jnp.float32)[:, None]
    after_one = feed_forward(values, params, 'ffn_one')
    after_attn = attention(after_one, length, params, rel_bias)
    normed = layer_norm(after_attn, params['conv_gain'], params['conv_bias'])
    pre_conv = low_back(highest(low(normed), params['pointwise']) + params['pointwise_bias'])
    gated_out = gate_unit(pre_conv, frame_mask)
    depth_out = depthwise(gated_out, params['depthwise'], params['depthwise_bias'])
    return (after_attn, depth_out)

def section_two(after_attn, depth_out, length, params, centre_vec, scale_vec):
    frame_mask = (jnp.arange(MAXLEN) < length).astype(jnp.float32)[:, None]
    normal = (depth_out - centre_vec) * scale_vec
    activated = jax.nn.silu(normal * params['batch_gain'] + params['batch_bias'])
    after_conv = after_attn + low_back(highest(low(activated), params['project']) + params['project_bias'])
    after_two = feed_forward(after_conv, params, 'ffn_two')
    return layer_norm(after_two, params['final_gain'], params['final_bias']) * frame_mask

def reference(frames, lengths, cotangent, master, moment_one, moment_two, average):
    inputs = frames.astype(jnp.float32)
    upstream = cotangent.astype(jnp.float32)

    def forward(input_vals, flat_master):
        params = unpack(low(flat_master))
        index_grid = jnp.clip(jnp.arange(LG)[None, :] - jnp.arange(LG)[:, None], -REL, REL) + REL
        rel_bias = params['relative'][:, index_grid]
        first_section = jax.checkpoint(lambda element: section_one(element[0], element[1], params, rel_bias))
        after_attn, depth_out = lax.map(first_section, (input_vals, lengths))
        mask_grid = (jnp.arange(MAXLEN)[None, :] < lengths[:, None]).astype(jnp.float32)[:, :, None]
        frame_total = jnp.sum(lengths).astype(jnp.float32)
        centre_vec = lax.optimization_barrier(jnp.sum(depth_out * mask_grid, axis=(0, 1))) / frame_total
        deviation = depth_out - centre_vec
        variance = lax.optimization_barrier(jnp.sum(mask_grid * deviation * deviation, axis=(0, 1))) / frame_total
        scale_vec = lax.rsqrt(variance + EPS_NORM)
        second_section = jax.checkpoint(lambda element: section_two(element[0], element[1], element[2], params, centre_vec, scale_vec))
        return lax.map(second_section, (after_attn, depth_out, lengths))
    result, pullback = jax.vjp(forward, inputs, master)
    input_grad, weight_grad = pullback(upstream)
    rates_np, decays_np = update_tables(PFLAT)
    rates = jnp.asarray(rates_np)
    decays = jnp.asarray(decays_np)
    correction = 1.0 - 0.5 ** STEP
    new_one = 0.5 * moment_one + 0.5 * weight_grad
    new_two = 0.5 * moment_two + 0.5 * weight_grad * weight_grad
    direction = new_one / correction / (jnp.sqrt(new_two / correction) + EPS_ADAM)
    new_master = master - rates * (direction + decays * master)
    new_average = 0.75 * average + 0.25 * new_master
    return (result.astype(jnp.bfloat16), input_grad, weight_grad, new_master, new_one, new_two, new_average)
```

```python
import math

import jax
import jax.numpy as jnp
import numpy as np
from jax import lax
from jax.experimental import pallas as pl
from jax.experimental.pallas import tpu as pltpu
from jax.sharding import PartitionSpec as P

D = 120
HEADS = 4
FF = 480
KERNEL = 15
GROUP = 3
REL = 127
STEP = 5
MAXLEN = 1536
LG = 512
HEAD = 90
HP = 96
GP = HEADS * HP
HALF = KERNEL // 2

EPS_NORM = 1e-05
EPS_ADAM = 1e-08
NEG_FILL = -1000000000.0
LOG2E = math.log2(math.e)
SCALE = HEAD ** (-0.5)

f32 = jnp.float32
bf16 = jnp.bfloat16
VMEM_BYTES = 58 * 2**20

REL_AT = 174240
TAIL_AT = 175260
TAIL = 1456
ROWS_HEAD = 1452
ROWS_TAIL = 1352
TABLE = 2824
F1 = 0
AT = 967
CV = TAIL
F2 = TAIL + 383
FN = TAIL + 1350
LIVE = 337500

C_F1, C_AT, C_CV, C_BN, C_F2, C_FN, C_DWB, C_DW = 0, 2, 4, 6, 8, 10, 12, 13


def dot(a, b):
    return lax.dot_general(a, b, (((1,), (0,)), ((), ())), preferred_element_type=f32)


def dot_nt(a, b):
    return lax.dot_general(a, b, (((1,), (1,)), ((), ())), preferred_element_type=f32)


def dot_tn(a, b):
    return lax.dot_general(a, b, (((0,), (0,)), ((), ())), preferred_element_type=f32)


def lane_iota(shape):
    return lax.broadcasted_iota(jnp.int32, shape, len(shape) - 1)


def row_iota(shape):
    return lax.broadcasted_iota(jnp.int32, shape, 0)


def segments():
    found = []
    for h in range(HEADS):
        for r in range(GROUP):
            lo, hi = max(HEAD * h, D * r), min(HEAD * h + HEAD, D * r + D)
            if lo < hi:
                found.append((HP * h + lo - HEAD * h, r, lo - D * r, hi - lo))
    return found


def pad8(values):
    return jnp.concatenate([values, jnp.zeros((8, values.shape[1]), f32)], axis=0)


def ext(values):
    width = values.shape[1]
    ones = jnp.where(row_iota((8, width)) == 0, 1.0, 0.0).astype(f32)
    return jnp.concatenate([values, ones], axis=0).astype(bf16)


def norm(values):
    mean = jnp.sum(values, axis=0, keepdims=True) * (1.0 / D)
    centre = values - mean
    var = jnp.sum(centre * centre, axis=0, keepdims=True) * (1.0 / D)
    rstd = lax.rsqrt(var + EPS_NORM)
    return centre * rstd, rstd


def norm_back(upstream, xhat, rstd, gain):
    scaled = upstream * gain
    mean_one = jnp.sum(scaled, axis=0, keepdims=True) * (1.0 / D)
    mean_two = jnp.sum(scaled * xhat, axis=0, keepdims=True) * (1.0 / D)
    return rstd * (scaled - mean_one - xhat * mean_two)


def fold(values):
    total = values[:, 0:128]
    for at in range(128, values.shape[1], 128):
        total = total + values[:, at : at + 128]
    return total


def permute_in(values, pm):
    low = pad8(values).astype(bf16)
    stack = jnp.concatenate([low[:, 384 * b : 384 * b + 384] for b in range(4)], axis=0)
    out = dot(stack, pm)
    tiles = [out[128 * b : 128 * b + D, 128 * r : 128 * r + 128] for r in range(3) for b in range(4)]
    return jnp.concatenate(tiles, axis=1)


def stack_out(values):
    low = pad8(values).astype(bf16)
    blocks = []
    for b in range(4):
        blocks.append(
            jnp.concatenate([low[:, 512 * r + 128 * b : 512 * r + 128 * b + 128] for r in range(3)], axis=1)
        )
    return jnp.concatenate(blocks, axis=0)


def unstack_out(out):
    return jnp.concatenate([out[128 * b : 128 * b + D, :] for b in range(4)], axis=1)


def permute_out(values, pm):
    return unstack_out(dot_nt(stack_out(values), pm))


def permute_out_wide(values, pm):
    high = values.astype(bf16).astype(f32)
    rest = values - high
    mid = rest.astype(bf16).astype(f32)
    return unstack_out(dot_nt(stack_out(high), pm) + dot_nt(stack_out(mid), pm))


def plane_mask(r, length):
    return jnp.where(lane_iota((1, LG)) * GROUP + r < length, 1.0, 0.0).astype(f32)


def sigmoid(values):
    return 0.5 + 0.5 * jnp.tanh(0.5 * values)


def plane(r):
    return pl.ds(pl.multiple_of(r * LG, LG), LG)


def plane_rows(r):
    return pl.ds(pl.multiple_of(r * 128, 128), 128)


def planes(body):
    def step(r, carry):
        body(r)
        return carry

    lax.fori_loop(0, GROUP, step, 0)


def shifted_planes(tiles):
    zero = jnp.zeros((8, 128), f32)
    padded = [jnp.concatenate([tile, zero], axis=1) for tile in tiles]
    made = {}

    def get(m):
        r, s = m % GROUP, m // GROUP
        if s == 0:
            return tiles[r]
        if m not in made:
            made[m] = pltpu.roll(padded[r], (-s) % (LG + 128), 1)[:, :LG]
        return made[m]

    return get


def prepare_body(
    g_ref, up1_ref, upp1_ref, dn1_ref, dnp1_ref, up2_ref, upp2_ref, dn2_ref, dnp2_ref, pw_ref, pwp_ref, pr_ref, prp_ref,
    wqkv_ref, wqkvt_ref, wo_ref, wob_ref, cols_ref, tab_ref, pm_ref, flat, tb, wt, big, rows,
):
    parts, part_rows = g_ref.shape[0], g_ref.shape[1]
    for d in range(parts):
        flat[part_rows * d : part_rows * (d + 1), :] = g_ref[d].astype(f32)
    tb[...] = jnp.zeros_like(tb)
    for start, count, base in ((0, ROWS_HEAD, 0), (TAIL_AT, ROWS_TAIL, TAIL)):
        for r in range(16):
            at = start + D * r
            first, col = at // 128, at % 128
            many = (count - r + 15) // 16
            here = flat[pl.ds(first, many, stride=15), :]
            then = flat[pl.ds(first + 1, many, stride=15), :]
            lanes = lane_iota((many, 128))
            got = jnp.where(lanes >= col, here, then)
            if col:
                got = pltpu.roll(got, 128 - col, 1)
            tb[pl.ds(base + r, many, stride=16), :] = jnp.where(lanes < D, got, 0.0)

    def with_row(block, row):
        tail = jnp.where(row_iota((8, 128)) == 0, row, 0.0)
        return jnp.concatenate([block, tail], axis=0)

    for base, up_ref, upp_ref, dn_ref, dnp_ref in (
        (F1, up1_ref, upp1_ref, dn1_ref, dnp1_ref),
        (F2, up2_ref, upp2_ref, dn2_ref, dnp2_ref),
    ):
        parts_t = []
        for q in range(4):
            block = tb[pl.ds(base + 2 + q, D, stride=4), :]
            parts_t.append(with_row(block, tb[base + 482 + q : base + 483 + q, :]).T[:D, :])
        up_t = jnp.concatenate(parts_t, axis=0)
        up_ref[...] = up_t.astype(bf16)
        full = jnp.concatenate([up_t, jnp.zeros((32, 128), f32)], axis=0)
        upp_ref[...] = full.T[:, :FF].astype(bf16)
        down = tb[base + 486 : base + 966, :]
        dnp_ref[...] = down.astype(bf16)
        bias = jnp.where(row_iota((32, 128)) == 0, tb[base + 966 : base + 967, :], 0.0)
        dn_ref[...] = jnp.concatenate([down, bias], axis=0).T.astype(bf16)

    parts_t = []
    for q in range(2):
        block = tb[pl.ds(CV + 2 + q, D, stride=2), :]
        parts_t.append(with_row(block, tb[CV + 242 + q : CV + 243 + q, :]).T[:D, :])
    pw_t = jnp.concatenate(parts_t, axis=0)
    pw_ref[...] = pw_t.astype(bf16)
    pwp_ref[...] = jnp.concatenate([pw_t, jnp.zeros((16, 128), f32)], axis=0).T[:, :240].astype(bf16)
    block = with_row(tb[CV + 262 : CV + 382, :], tb[CV + 382 : CV + 383, :])
    prp_ref[...] = block.astype(bf16)
    pr_ref[...] = block.T.astype(bf16)

    none = jnp.zeros((1, 128), f32)
    for w, at, bias_at in ((0, AT + 2, AT + 122), (1, AT + 123, None), (2, AT + 243, AT + 363)):
        bias = none if bias_at is None else tb[bias_at : bias_at + 1, :]
        wt[...] = with_row(tb[at : at + D, :], bias).T
        big[...] = jnp.zeros_like(big)
        for to, r, src, many in segments():
            big[to : to + many, 128 * r : 128 * r + 128] = wt[src : src + many, :]
        made = big[...]
        wqkv_ref[GP * w : GP * w + GP, :] = made.astype(bf16)
        wqkvt_ref[:, GP * w : GP * w + GP] = made.T.astype(bf16)
    wt[...] = with_row(tb[AT + 364 : AT + 484, :], none)
    big[...] = jnp.zeros_like(big)
    for to, r, src, many in segments():
        big[to : to + many, 128 * r : 128 * r + 128] = wt[src : src + many, :]
    wob_ref[...] = big[...].astype(bf16)
    for r in range(GROUP):
        big[HEAD : HEAD + 1, 128 * r : 128 * r + 128] = tb[AT + 484 : AT + 485, :]
    wo_ref[...] = big[...].T.astype(bf16)

    rows[...] = jnp.zeros_like(rows)
    listed = []
    for base in (F1, AT, CV, CV + 260, F2, FN):
        listed += [base, base + 1]
    listed += [CV + 259] + [CV + 244 + k for k in range(KERNEL)]
    for to, src in enumerate(listed):
        rows[to : to + 1, :] = tb[src : src + 1, :]
    cols_ref[...] = rows[...].T

    rel_rows = []
    lanes = lane_iota((1, 128))
    for h in range(HEADS):
        at = REL_AT + (2 * REL + 1) * h
        first, col = at // 128, at % 128
        pieces = []
        for k in range(2):
            got = jnp.where(lanes >= col, flat[first + k : first + k + 1, :], flat[first + k + 1 : first + k + 2, :])
            pieces.append(pltpu.roll(got, (128 - col) % 128, 1) if col else got)
        rel_rows.append(jnp.concatenate(pieces, axis=1))
    rel = jnp.concatenate(rel_rows + [jnp.zeros((4, 256), f32)], axis=0)
    rel = jnp.where(lane_iota((8, 256)) < 2 * REL + 1, rel, 0.0)
    base = dot(rel.astype(bf16), distance_select()) * LOG2E
    for h in range(HEADS):
        spread = jnp.broadcast_to(base[h : h + 1, :], (LG, 2 * LG))
        tab_ref[h] = pltpu.roll(spread, 0, 1, stride=1, stride_axis=0)[:, :LG]
    t = row_iota((384, 384))
    c = lane_iota((384, 384))
    pm_ref[...] = jnp.where(t == GROUP * (c % 128) + c // 128, 1.0, 0.0).astype(bf16)


def distance_select():
    l = lane_iota((256, 2 * LG))
    gap = jnp.where(l < LG, -l, 2 * LG - l)
    index = jnp.clip(gap, -REL, REL) + REL
    return jnp.where(row_iota((256, 2 * LG)) == index, 1.0, 0.0).astype(bf16)


def diagonal_sum(values):
    wide = jnp.concatenate([values, jnp.zeros((LG, LG), f32)], axis=1)
    half = LG // 2
    while half:
        upper, lower = wide[:half], wide[half : 2 * half]
        if half % 128 == 0:
            lower = jnp.concatenate([lower[:, half:], lower[:, :half]], axis=1)
        else:
            lower = pltpu.roll(lower, 2 * LG - half, 1)
        wide = upper + lower
        half //= 2
    return wide


def prepare(gathered):
    total = gathered.shape[0] * gathered.shape[1]

    def o(shape, kind=bf16):
        return jax.ShapeDtypeStruct(shape, kind)

    ffn = [o((FF, 128)), o((128, FF)), o((128, 512)), o((FF, 128))]
    return pl.pallas_call(
        prepare_body,
        out_shape=ffn
        + ffn
        + [o((240, 128)), o((128, 240)), o((128, 128)), o((128, 128))]
        + [o((3 * GP, GP)), o((GP, 3 * GP)), o((GP, GP)), o((GP, GP))]
        + [o((128, 128), f32), o((HEADS, LG, LG), f32), o((384, 384))],
        scratch_shapes=[
            pltpu.VMEM((total, 128), f32),
            pltpu.VMEM((TABLE, 128), f32),
            pltpu.VMEM((128, 128), f32),
            pltpu.VMEM((GP, GP), f32),
            pltpu.VMEM((128, 128), f32),
        ],
        compiler_params=pltpu.CompilerParams(vmem_limit_bytes=VMEM_BYTES),
        name="prepare",
    )(gathered)


def column(cols, k):
    return cols[:D, k : k + 1]


def valid_keys(length):
    return row_iota((LG, 1)) * GROUP < length


def set_tail(hid):
    hid[FF:, :] = jnp.where(row_iota((512 - FF, hid.shape[1])) == 0, 1.0, 0.0).astype(bf16)


def first_body(
    len_ref, x_ref, cols_ref, up_ref, dn_ref, wqkv_ref, wo_ref, pw_ref, tab_ref, pm_ref,
    xp_ref, one_ref, qkv_ref, att_ref, lse_ref, aa_ref, dep_ref, st_ref,
    hid, nrm, gat, run,
):
    u = pl.program_id(0)
    length = len_ref[u]

    @pl.when(u == 0)
    def _():
        set_tail(hid)
        run[...] = jnp.zeros_like(run)

    xp_ref[0] = permute_in(x_ref[0].astype(f32), pm_ref[...]).astype(bf16)
    cols = cols_ref

    def ffn(r):
        at = plane(r)
        x = xp_ref[0, :, at].astype(f32)
        xhat, _ = norm(x)
        low = ext(xhat * column(cols, C_F1) + column(cols, C_F1 + 1))
        half = 0.5 * dot(up_ref[...], low)
        hid[:FF, :] = (half + half * jnp.tanh(half)).astype(bf16)
        one = x + 0.5 * dot(dn_ref[...], hid[...])[:D]
        one_ref[0, :, at] = one
        xhat, _ = norm(one)
        nrm[plane_rows(r), :] = ext(xhat * column(cols, C_AT) + column(cols, C_AT + 1))

    planes(ffn)
    qkv_ref[0] = dot(wqkv_ref[...], nrm[...]).astype(bf16)
    keys = valid_keys(length)

    def head(h, carry):
        def rows(w):
            return pl.ds(pl.multiple_of(GP * w + HP * h, 32), HP)

        key = qkv_ref[0, rows(1), :]
        value = qkv_ref[0, rows(2), :]
        for part in range(2):
            at = slice(256 * part, 256 * part + 256)
            query = qkv_ref[0, rows(0), at]
            scores = dot_tn(key, query) * (SCALE * LOG2E) + tab_ref[h, :, at]
            scores = jnp.where(keys, scores, NEG_FILL * LOG2E)
            peak = jnp.max(scores, axis=0, keepdims=True)
            power = jnp.exp2(scores - peak)
            total = jnp.sum(power, axis=0, keepdims=True)
            probs = (power * (1.0 / total)).astype(bf16)
            mixed = dot(value, probs)
            mark = (row_iota((HP, 256)) == HEAD) & (h == 0)
            att_ref[0, rows(0), at] = jnp.where(mark, 1.0, mixed).astype(bf16)
            lse_ref[0, pl.ds(h, 1), at] = peak + jnp.log2(total)
        return carry

    lax.fori_loop(0, HEADS, head, 0)
    mixed = dot(wo_ref[...], att_ref[0])
    for r in range(GROUP):
        at = slice(LG * r, LG * r + LG)
        aa_ref[0, :, at] = one_ref[0, :, at] + mixed[128 * r : 128 * r + D]

    def gate(r):
        at = plane(r)
        xhat, _ = norm(aa_ref[0, :, at])
        pre = dot(pw_ref[...], ext(xhat * column(cols, C_CV) + column(cols, C_CV + 1)))
        gat[:, at] = pre[:D] * sigmoid(pre[D:]) * plane_mask(r, length)

    planes(gate)

    def conv(f, carry):
        rows = pl.ds(pl.multiple_of(8 * f, 8), 8)
        get = shifted_planes([gat[rows, LG * r : LG * r + LG] for r in range(GROUP)])
        here = cols[rows, :]
        for r in range(GROUP):
            total = jnp.broadcast_to(here[:, C_DWB : C_DWB + 1], (8, LG))
            for k in range(KERNEL):
                total = total + here[:, C_DW + k : C_DW + k + 1] * get(r + k - HALF)
            dep_ref[0, rows, LG * r : LG * r + LG] = total
        return carry

    lax.fori_loop(0, D // 8, conv, 0)

    count = length.astype(f32)
    mask = jnp.concatenate([plane_mask(r, length) for r in range(GROUP)], axis=1)
    dep = dep_ref[0]
    mean = jnp.sum(dep * mask, axis=1, keepdims=True) / count
    gap = (dep - mean) * mask
    spread = jnp.sum(gap * gap, axis=1, keepdims=True)
    old_mean, old_spread, old_count = run[0], run[1], run[2]
    new_count = old_count + count
    step = mean - old_mean
    new_mean = old_mean + step * (count / new_count)
    new_spread = old_spread + spread + step * step * (old_count * count / new_count)
    run[0] = new_mean
    run[1] = new_spread
    run[2] = new_count
    lanes = lane_iota((D, 128))
    picked = jnp.where(lanes == 0, new_mean, jnp.where(lanes == 1, new_spread, jnp.where(lanes == 2, new_count, 0.0)))
    st_ref[...] = pad8(picked).T[0:8]


def whole(shape):
    zeros = (0,) * len(shape)
    return pl.BlockSpec(shape, lambda u: zeros)


def per_utt(shape):
    zeros = (0,) * len(shape)
    return pl.BlockSpec((1,) + shape, lambda u: (u,) + zeros)


SMEM = pl.BlockSpec(memory_space=pltpu.SMEM)


def first(lengths, x, weights):
    cols, up, dn, wqkv, wo, pw, tab, pm = weights
    utts = x.shape[0]
    per = [
        ((D, MAXLEN), bf16),
        ((D, MAXLEN), f32),
        ((3 * GP, LG), bf16),
        ((GP, LG), bf16),
        ((8, LG), f32),
        ((D, MAXLEN), f32),
        ((D, MAXLEN), f32),
    ]
    return pl.pallas_call(
        first_body,
        grid=(utts,),
        in_specs=[SMEM, per_utt((D, MAXLEN))] + [whole(w.shape) for w in weights],
        out_specs=[per_utt(s) for s, k in per] + [whole((8, 128))],
        out_shape=[jax.ShapeDtypeStruct((utts,) + s, k) for s, k in per] + [jax.ShapeDtypeStruct((8, 128), f32)],
        scratch_shapes=[
            pltpu.VMEM((512, LG), bf16),
            pltpu.VMEM((GP, LG), bf16),
            pltpu.VMEM((D, MAXLEN), f32),
            pltpu.VMEM((3, D, 128), f32),
        ],
        compiler_params=pltpu.CompilerParams(vmem_limit_bytes=VMEM_BYTES),
        name="first",
    )(lengths, x, *weights)


def second_body(
    len_ref, stats_ref, cot_ref, aa_ref, dep_ref, cols_ref, up_ref, upp_ref, dn_ref, dnp_ref, pr_ref, prp_ref, pm_ref,
    out_ref, bgd_ref, gc_ref, sums_ref, stc_ref, gdn_ref, gup_ref, gpr_ref, vec_ref,
    hid, cotp, outp, acc,
):
    u = pl.program_id(0)
    length = len_ref[u]
    cols = cols_ref

    @pl.when(u == 0)
    def _():
        set_tail(hid)
        parts = stats_ref.shape[0]
        count = jnp.zeros((1, 128), f32)
        total = jnp.zeros((1, 128), f32)
        for d in range(parts):
            many = stats_ref[d, 2:3, :]
            count = count + many
            total = total + many * stats_ref[d, 0:1, :]
        here = lane_iota((1, 128)) < D
        count = jnp.where(here, count, 1.0)
        mean = total / count
        spread = jnp.zeros((1, 128), f32)
        for d in range(parts):
            gap = stats_ref[d, 0:1, :] - mean
            spread = spread + stats_ref[d, 1:2, :] + stats_ref[d, 2:3, :] * gap * gap
        scale = lax.rsqrt(spread / count + EPS_NORM)
        at = row_iota((128, 128))
        table = jnp.where(at == 0, mean, jnp.where(at == 1, scale, jnp.where(at == 2, 1.0 / count, 0.0)))
        stc_ref[...] = table.T
        gdn_ref[...] = jnp.zeros_like(gdn_ref)
        gup_ref[...] = jnp.zeros_like(gup_ref)
        gpr_ref[...] = jnp.zeros_like(gpr_ref)
        vec_ref[...] = jnp.zeros_like(vec_ref)
        acc[...] = jnp.zeros_like(acc)

    cotp[...] = permute_in(cot_ref[0].astype(f32), pm_ref[...])

    def tile(r):
        at = plane(r)
        mask = plane_mask(r, length)
        normal = (dep_ref[0, :, at] - stc_ref[:D, 0:1]) * stc_ref[:D, 1:2]
        z = normal * column(cols, C_BN) + column(cols, C_BN + 1)
        z_sig = sigmoid(z)
        act = z * z_sig
        act_low = ext(act)
        after_conv = aa_ref[0, :, at] + dot(pr_ref[...], act_low)[:D]
        xhat, rstd = norm(after_conv)
        low = ext(xhat * column(cols, C_F2) + column(cols, C_F2 + 1))
        pre = dot(up_ref[...], low)
        sig = sigmoid(pre)
        hidden = pre * sig
        hid[:FF, :] = hidden.astype(bf16)
        slope = sig + hidden * (1.0 - sig)
        after_two = after_conv + 0.5 * dot(dn_ref[...], hid[...])[:D]
        xhat_f, rstd_f = norm(after_two)
        outp[:, at] = (xhat_f * column(cols, C_FN) + column(cols, C_FN + 1)) * mask
        up_grad = cotp[:, at] * mask
        vec_ref[2] += fold(up_grad * xhat_f)
        vec_ref[3] += fold(up_grad)
        grad_two = norm_back(up_grad, xhat_f, rstd_f, column(cols, C_FN))
        branch = pad8(0.5 * grad_two).astype(bf16)
        gdn_ref[...] += dot_nt(hid[...], branch)
        pre_low = (slope * dot(dnp_ref[...], branch)).astype(bf16)
        gup_ref[...] += dot_nt(pre_low, low)
        back = dot(upp_ref[...], pre_low)[:D]
        vec_ref[0] += fold(back * xhat)
        vec_ref[1] += fold(back)
        grad_conv = grad_two + norm_back(back, xhat, rstd, column(cols, C_F2))
        gc_ref[0, :, at] = grad_conv
        project = pad8(grad_conv).astype(bf16)
        gpr_ref[...] += dot_nt(act_low, project)
        batch = (z_sig + act * (1.0 - z_sig)) * dot(prp_ref[...], project)[:D]
        bgd_ref[0, :, at] = batch
        acc[0] += fold(batch * normal)
        acc[1] += fold(batch)

    planes(tile)
    out_ref[0] = permute_out(outp[...], pm_ref[...]).astype(bf16)
    lanes = lane_iota((D, 128))
    gain = jnp.sum(acc[0], axis=1, keepdims=True)
    shift = jnp.sum(acc[1], axis=1, keepdims=True)
    sums_ref[...] = pad8(jnp.where(lanes == 0, gain, jnp.where(lanes == 1, shift, 0.0))).T[0:8]


def second(lengths, stats, cot, aa, dep, weights):
    utts = cot.shape[0]
    big = (D, MAXLEN)
    outs = [
        (per_utt(big), (utts,) + big, bf16),
        (per_utt(big), (utts,) + big, f32),
        (per_utt(big), (utts,) + big, f32),
    ]
    for s in ((8, 128), (128, 128), (512, 128), (FF, 128), (128, 128), (4, D, 128)):
        outs.append((whole(s), s, f32))
    return pl.pallas_call(
        second_body,
        grid=(utts,),
        in_specs=[SMEM, whole(stats.shape)] + [per_utt(big)] * 3 + [whole(w.shape) for w in weights],
        out_specs=[o[0] for o in outs],
        out_shape=[jax.ShapeDtypeStruct(o[1], o[2]) for o in outs],
        scratch_shapes=[
            pltpu.VMEM((512, LG), bf16),
            pltpu.VMEM(big, f32),
            pltpu.VMEM(big, f32),
            pltpu.VMEM((2, D, 128), f32),
        ],
        compiler_params=pltpu.CompilerParams(vmem_limit_bytes=VMEM_BYTES),
        name="second",
    )(lengths, stats, cot, aa, dep, *weights)


def third_body(
    len_ref, sums_ref, stc_ref, bgd_ref, gc_ref, xp_ref, one_ref, qkv_ref, att_ref, lse_ref, aa_ref, dep_ref,
    cols_ref, up_ref, upp_ref, dnp_ref, wqkv_t_ref, wob_ref, pw_ref, pwp_ref, tab_ref, pm_ref,
    gin_ref, gdn_ref, gup_ref, gpw_ref, gqkv_ref, go_ref, rel_ref, vec_ref,
    hid, nrm, cn, gat, sig_s, dgs, olg, agr, back_s, ng, relacc, tot,
):
    u = pl.program_id(0)
    length = len_ref[u]
    cols = cols_ref

    @pl.when(u == 0)
    def _():
        set_tail(hid)
        parts = sums_ref.shape[0]
        total = sums_ref[0]
        for d in range(1, parts):
            total = total + sums_ref[d]
        tot[...] = jnp.concatenate([total, jnp.zeros((120, 128), f32)], axis=0).T
        for ref in (gdn_ref, gup_ref, gpw_ref, gqkv_ref, go_ref, vec_ref, relacc):
            ref[...] = jnp.zeros_like(ref)

    def conv_in(r):
        at = plane(r)
        mask = plane_mask(r, length)
        gain = column(cols, C_BN)
        scale = stc_ref[:D, 1:2]
        per = stc_ref[:D, 2:3]
        normal = (dep_ref[0, :, at] - stc_ref[:D, 0:1]) * scale
        shift_part = gain * tot[:D, 1:2] * per * scale
        gain_part = gain * tot[:D, 0:1] * per * scale
        dgs[:, at] = bgd_ref[0, :, at] * (gain * scale) - mask * (shift_part + normal * gain_part)
        xhat, _ = norm(aa_ref[0, :, at])
        low = ext(xhat * column(cols, C_CV) + column(cols, C_CV + 1))
        cn[:, at] = low
        pre = dot(pw_ref[...], low)
        sig = sigmoid(pre[D:])
        sig_s[:, at] = sig
        gat[:, at] = pre[:D] * sig * mask

    planes(conv_in)

    def conv(f, carry):
        rows = pl.ds(pl.multiple_of(8 * f, 8), 8)
        get = shifted_planes([dgs[rows, LG * r : LG * r + LG] for r in range(GROUP)])
        here = cols[rows, :]
        taps = [None] * KERNEL
        bias = None
        made = []
        for r in range(GROUP):
            gated = gat[rows, LG * r : LG * r + LG]
            total = None
            for k in range(KERNEL):
                moved = get(r - k + HALF)
                term = here[:, C_DW + k : C_DW + k + 1] * moved
                total = term if total is None else total + term
                tap = fold(gated * moved)
                taps[k] = tap if taps[k] is None else taps[k] + tap
            part = fold(get(r))
            bias = part if bias is None else bias + part
            made.append(total)
        for r in range(GROUP):
            ng[rows, LG * r : LG * r + LG] = made[r]
        vec_ref[6, rows, :] += bias
        for k in range(KERNEL):
            vec_ref[7 + k, rows, :] += taps[k]
        return carry

    lax.fori_loop(0, D // 8, conv, 0)

    def conv_out(r):
        at = plane(r)
        grad = ng[:, at]
        sig = sig_s[:, at]
        left = grad * plane_mask(r, length) * sig
        right = grad * gat[:, at] * (1.0 - sig)
        pre_low = jnp.concatenate([left, right], axis=0).astype(bf16)
        gpw_ref[...] += dot_nt(pre_low, cn[:, at])
        back = dot(pwp_ref[...], pre_low)[:D]
        xhat, rstd = norm(aa_ref[0, :, at])
        vec_ref[0] += fold(back * xhat)
        vec_ref[1] += fold(back)
        grad_attn = gc_ref[0, :, at] + norm_back(back, xhat, rstd, column(cols, C_CV))
        dgs[:, at] = grad_attn
        olg[plane_rows(r), :] = pad8(grad_attn).astype(bf16)
        xhat, _ = norm(one_ref[0, :, at])
        nrm[plane_rows(r), :] = ext(xhat * column(cols, C_AT) + column(cols, C_AT + 1))

    planes(conv_out)
    go_ref[...] += dot_nt(att_ref[0], olg[...])
    agr[...] = dot(wob_ref[...], olg[...]).astype(bf16)
    keys = valid_keys(length)

    def head(h, carry):
        def rows(w):
            return pl.ds(pl.multiple_of(GP * w + HP * h, 32), HP)

        key = qkv_ref[0, rows(1), :]
        value = qkv_ref[0, rows(2), :]
        key_grad = jnp.zeros((HP, LG), f32)
        value_grad = jnp.zeros((HP, LG), f32)
        for part in range(2):
            at = slice(256 * part, 256 * part + 256)
            query = qkv_ref[0, rows(0), at]
            grad = agr[rows(0), at]
            scores = dot_tn(key, query) * (SCALE * LOG2E) + tab_ref[h, :, at]
            scores = jnp.where(keys, scores, NEG_FILL * LOG2E)
            probs = jnp.exp2(scores - lse_ref[0, pl.ds(h, 1), at])
            prob_grad = dot_tn(value, grad)
            inner = jnp.sum(probs * prob_grad, axis=0, keepdims=True)
            score_low = (probs * (prob_grad - inner)).astype(bf16)
            relacc[h, :, at] += score_low.astype(f32)
            back_s[rows(0), at] = (dot(key, score_low) * SCALE).astype(bf16)
            key_grad = key_grad + dot_nt(query, score_low)
            value_grad = value_grad + dot_nt(grad, probs.astype(bf16))
        back_s[rows(1), :] = (key_grad * SCALE).astype(bf16)
        back_s[rows(2), :] = value_grad.astype(bf16)
        return carry

    lax.fori_loop(0, HEADS, head, 0)
    gqkv_ref[...] += dot_nt(back_s[...], nrm[...])
    normed_grad = dot(wqkv_t_ref[...], back_s[...])
    for r in range(GROUP):
        ng[:, LG * r : LG * r + LG] = normed_grad[128 * r : 128 * r + D]

    def ffn(r):
        at = plane(r)
        back = ng[:, at]
        xhat, rstd = norm(one_ref[0, :, at])
        vec_ref[2] += fold(back * xhat)
        vec_ref[3] += fold(back)
        grad_one = dgs[:, at] + norm_back(back, xhat, rstd, column(cols, C_AT))
        xhat, rstd = norm(xp_ref[0, :, at].astype(f32))
        low = ext(xhat * column(cols, C_F1) + column(cols, C_F1 + 1))
        pre = dot(up_ref[...], low)
        sig = sigmoid(pre)
        hidden = pre * sig
        hid[:FF, :] = hidden.astype(bf16)
        slope = sig + hidden * (1.0 - sig)
        branch = pad8(0.5 * grad_one).astype(bf16)
        gdn_ref[...] += dot_nt(hid[...], branch)
        pre_low = (slope * dot(dnp_ref[...], branch)).astype(bf16)
        gup_ref[...] += dot_nt(pre_low, low)
        back = dot(upp_ref[...], pre_low)[:D]
        vec_ref[4] += fold(back * xhat)
        vec_ref[5] += fold(back)
        sig_s[:, at] = grad_one + norm_back(back, xhat, rstd, column(cols, C_F1))

    planes(ffn)
    gin_ref[0] = permute_out_wide(sig_s[...], pm_ref[...])

    @pl.when(u == pl.num_programs(0) - 1)
    def _():
        found = []
        for h in range(HEADS):
            found.append(diagonal_sum(relacc[h]))
        stacked = jnp.concatenate(found + [jnp.zeros((4, 2 * LG), f32)], axis=0)
        high = stacked.astype(bf16)
        rest = stacked - high.astype(f32)
        mid = rest.astype(bf16)
        rest = rest - mid.astype(f32)
        select = distance_select()
        rel_ref[...] = dot_nt(high, select) + dot_nt(mid, select) + dot_nt(rest.astype(bf16), select)


def third(lengths, sums, stc, bgd, gc, saved, weights):
    utts = bgd.shape[0]
    big = (D, MAXLEN)
    outs = [(per_utt(big), (utts,) + big)]
    for s in ((512, 128), (FF, 128), (240, 128), (3 * GP, GP), (GP, GP), (8, 256), (22, D, 128)):
        outs.append((whole(s), s))
    return pl.pallas_call(
        third_body,
        grid=(utts,),
        in_specs=[SMEM, whole(sums.shape), whole(stc.shape), per_utt(big), per_utt(big)]
        + [per_utt(s.shape[1:]) for s in saved]
        + [whole(w.shape) for w in weights],
        out_specs=[o[0] for o in outs],
        out_shape=[jax.ShapeDtypeStruct(o[1], f32) for o in outs],
        scratch_shapes=[
            pltpu.VMEM((512, LG), bf16),
            pltpu.VMEM((GP, LG), bf16),
            pltpu.VMEM((128, MAXLEN), bf16),
            pltpu.VMEM(big, f32),
            pltpu.VMEM(big, f32),
            pltpu.VMEM(big, f32),
            pltpu.VMEM((GP, LG), bf16),
            pltpu.VMEM((GP, LG), bf16),
            pltpu.VMEM((3 * GP, LG), bf16),
            pltpu.VMEM(big, f32),
            pltpu.VMEM((HEADS, LG, LG), f32),
            pltpu.VMEM((128, 128), f32),
        ],
        compiler_params=pltpu.CompilerParams(vmem_limit_bytes=VMEM_BYTES),
        name="third",
    )(lengths, sums, stc, bgd, gc, *saved, *weights)


def pack_body(
    dn1_ref, up1_ref, dn2_ref, up2_ref, pr_ref, pw_ref, qkv_ref, o_ref, rel_ref, vecs2_ref, vecs3_ref, sums_ref,
    out_ref, tb, flat, wt,
):
    tb[...] = jnp.zeros_like(tb)
    flat[...] = jnp.zeros_like(flat)
    lanes = lane_iota((D, 128))
    table = jnp.zeros((D, 128), f32)
    listed = []
    for ref, at in (
        (vecs2_ref, (F2, F2 + 1, FN, FN + 1)),
        (vecs3_ref, (CV, CV + 1, AT, AT + 1, F1, F1 + 1, CV + 259) + tuple(CV + 244 + k for k in range(KERNEL))),
    ):
        for k, to in enumerate(at):
            table = jnp.where(lanes == len(listed), jnp.sum(ref[k], axis=1, keepdims=True), table)
            listed.append(to)
    wt[...] = pad8(table).T
    keep = lane_iota((1, 128)) < D
    for k, to in enumerate(listed):
        tb[to : to + 1, :] = wt[k : k + 1, :]
    tb[CV + 260 : CV + 262, :] = sums_ref[0:2, :]

    def clean(block):
        return jnp.where(lane_iota(block.shape) < D, block, 0.0)

    for base, dn_ref, up_ref in ((F1, dn1_ref, up1_ref), (F2, dn2_ref, up2_ref)):
        tb[base + 486 : base + 967, :] = clean(dn_ref[0 : FF + 1, :])
        for q in range(4):
            block = pad8(up_ref[D * q : D * q + D, :]).T
            tb[pl.ds(base + 2 + q, D, stride=4), :] = block[:D]
            tb[base + 482 + q : base + 483 + q, :] = block[D : D + 1]
    for q in range(2):
        block = pad8(pw_ref[D * q : D * q + D, :]).T
        tb[pl.ds(CV + 2 + q, D, stride=2), :] = block[:D]
        tb[CV + 242 + q : CV + 243 + q, :] = block[D : D + 1]
    tb[CV + 262 : CV + 383, :] = clean(pr_ref[0 : D + 1, :])

    def gathered(ref, base):
        wt[...] = jnp.zeros_like(wt)
        for to, r, src, many in segments():
            wt[src : src + many, :] += ref[base + to : base + to + many, 128 * r : 128 * r + 128]
        return wt[...]

    for w, at, bias_at in ((0, AT + 2, AT + 122), (1, AT + 123, None), (2, AT + 243, AT + 363)):
        block = gathered(qkv_ref, GP * w).T
        tb[at : at + D, :] = block[:D]
        if bias_at is not None:
            tb[bias_at : bias_at + 1, :] = block[D : D + 1]
    tb[AT + 364 : AT + 484, :] = clean(gathered(o_ref, 0)[:D])
    bias = o_ref[HEAD : HEAD + 1, 0:128] + o_ref[HEAD : HEAD + 1, 128:256] + o_ref[HEAD : HEAD + 1, 256:384]
    tb[AT + 484 : AT + 485, :] = jnp.where(keep, bias, 0.0)

    last = (LIVE - 1) // 128
    for y_first, y_count, offset, base in (
        (0, REL_AT // 128 + 1, 0, 0),
        (TAIL_AT // 128, last - TAIL_AT // 128 + 1, 128 * (TAIL_AT // 128) - TAIL_AT + D, TAIL - 1),
    ):
        for k in range(15):
            at = 128 * k + offset
            first_row, col = at // D, at % D
            many = (y_count - k + 14) // 15
            here = lane_iota((many, 128))
            got = tb[pl.ds(base + first_row, many, stride=16), :]
            if col:
                got = pltpu.roll(got, 128 - col, 1)
            then = pltpu.roll(tb[pl.ds(base + first_row + 1, many, stride=16), :], D - col, 1)
            got = jnp.where(here < D - col, got, then)
            if 2 * D - col < 128:
                then = pltpu.roll(tb[pl.ds(base + first_row + 2, many, stride=16), :], 2 * D - col, 1)
                got = jnp.where(here < 2 * D - col, got, then)
            flat[pl.ds(y_first + k, many, stride=15), :] = got
    here = lane_iota((1, 128))
    width = 2 * REL + 1
    for h in range(HEADS):
        at = REL_AT + width * h
        for y in range(at // 128, (at + width - 1) // 128 + 1):
            lo, hi = max(at - 128 * y, 0), min(at + width - 128 * y, 128)
            shift = (at - 128 * y) % 256
            turned = rel_ref[h : h + 1, :]
            if shift:
                turned = pltpu.roll(turned, shift, 1)
            flat[y : y + 1, :] += jnp.where((here >= lo) & (here < hi), turned[:, :128], 0.0)
    rows = out_ref.shape[1]
    for d in range(out_ref.shape[0]):
        out_ref[d] = flat[rows * d : rows * (d + 1), :]


def pack(parts, rows, grads):
    return pl.pallas_call(
        pack_body,
        out_shape=jax.ShapeDtypeStruct((parts, rows, 128), f32),
        scratch_shapes=[
            pltpu.VMEM((TABLE, 128), f32),
            pltpu.VMEM((parts * rows, 128), f32),
            pltpu.VMEM((128, 128), f32),
        ],
        compiler_params=pltpu.CompilerParams(vmem_limit_bytes=VMEM_BYTES),
        name="pack",
    )(*grads)


def update_tables(total_len):
    rates = np.zeros(total_len, np.float32)
    decays = np.zeros(total_len, np.float32)
    vector, gain, ffn = (D, 0.1, 0.0), (D, 0.3, 0.0), lambda n, fan: (n, fan**-0.5, 0.01)
    block = [gain, vector, ffn(D * FF, D), (FF, 0.1, 0.0), ffn(FF * D, FF), vector]
    square = ffn(D * D, D)
    pieces = block + [gain, vector, square, vector, square, square, vector, ffn(D * D, 6.0 * D / MAXLEN), vector]
    pieces += [(HEADS * (2 * REL + 1), 0.5, 0.0)]
    pieces += [gain, vector, ffn(2 * D * D, D), (2 * D, 0.1, 0.0), ffn(KERNEL * D, KERNEL), vector, gain, vector]
    pieces += [square, vector] + block + [gain, vector]
    offset = 0
    for entries, rate, decay in pieces:
        rates[offset : offset + entries] = rate
        decays[offset : offset + entries] = decay
        offset += entries
    return rates, decays


def everyone(values, devices):
    return lax.all_to_all(jnp.broadcast_to(values[None], (devices,) + values.shape), "dp", 0, 0)


def local(frames, lengths, cotangent, master, moment_one, moment_two, average):
    shard_len = master.shape[0]
    devices = lax.axis_size("dp")
    rows = shard_len // 128
    gathered = everyone(master.astype(bf16).reshape(rows, 128), devices)
    (
        up1, upp1, dn1, dnp1, up2, upp2, dn2, dnp2, pw, pwp, pr, prp, wqkv, wqkvt, wo, wob, cols, tab, pm,
    ) = prepare(gathered)
    x = jnp.transpose(frames, (0, 2, 1))
    cot = jnp.transpose(cotangent, (0, 2, 1))
    xp, one, qkv, att, lse, aa, dep, st = first(lengths, x, (cols, up1, dn1, wqkv, wo, pw, tab, pm))
    stats = everyone(st, devices)
    out, bgd, gc, sums, stc, gdn2, gup2, gpr, vec2 = second(
        lengths, stats, cot, aa, dep, (cols, up2, upp2, dn2, dnp2, pr, prp, pm)
    )
    all_sums = everyone(sums, devices)
    gin, gdn1, gup1, gpw, gqkv, go, rel, vec3 = third(
        lengths, all_sums, stc, bgd, gc, (xp, one, qkv, att, lse, aa, dep),
        (cols, up1, upp1, dnp1, wqkvt, wob, pw, pwp, tab, pm),
    )
    flat = pack(devices, rows, (gdn1, gup1, gdn2, gup2, gpr, gpw, gqkv, go, rel, vec2, vec3, sums))
    reduced = jnp.sum(lax.all_to_all(flat, "dp", 0, 0), axis=0).reshape(shard_len)
    rates_np, decays_np = update_tables(shard_len * devices)
    start_at = lax.axis_index("dp") * shard_len
    rates = lax.dynamic_slice_in_dim(jnp.asarray(rates_np), start_at, shard_len)
    decays = lax.dynamic_slice_in_dim(jnp.asarray(decays_np), start_at, shard_len)
    correction = 1.0 - 0.5**STEP
    new_one = 0.5 * moment_one + 0.5 * reduced
    new_two = 0.5 * moment_two + 0.5 * reduced * reduced
    direction = new_one / correction / (jnp.sqrt(new_two / correction) + EPS_ADAM)
    new_master = master - rates * (direction + decays * master)
    new_average = 0.75 * average + 0.25 * new_master
    return (
        jnp.transpose(out, (0, 2, 1)),
        jnp.transpose(gin, (0, 2, 1)),
        reduced,
        new_master,
        new_one,
        new_two,
        new_average,
    )


def solution(mesh):
    three = P("dp", None, None)
    one = P("dp")
    in_specs = (three, one, three, one, one, one, one)
    out_specs = (three, three, one, one, one, one, one)
    return jax.shard_map(local, mesh=mesh, in_specs=in_specs, out_specs=out_specs, check_vma=False)
```

```python
import math

import jax
import jax.numpy as jnp
import numpy as np
from jax import lax
from jax.experimental import pallas as pl
from jax.experimental.pallas import tpu as pltpu
from jax.sharding import PartitionSpec as P

D = 120
HEADS = 4
FF = 480
KERNEL = 15
GROUP = 3
REL = 127
STEP = 5
MAXLEN = 1536
LG = 512
HEAD = 90
HP = 96
GP = HEADS * HP
HALF = KERNEL // 2
WIN = (0, 112, 240)
WROWS = 144
MARKS = tuple(HP * r + HEAD - WIN[r] for r in range(GROUP))

EPS_NORM = 1e-05
EPS_ADAM = 1e-08
NEG_FILL = -1000000000.0
LOG2E = math.log2(math.e)
SCALE = HEAD ** (-0.5)

f32 = jnp.float32
bf16 = jnp.bfloat16
VMEM_BYTES = 58 * 2**20

REL_AT = 174240
TAIL_AT = 175260
TAIL = 1456
ROWS_HEAD = 1452
ROWS_TAIL = 1352
TABLE = 2824
F1 = 0
AT = 967
CV = TAIL
F2 = TAIL + 383
FN = TAIL + 1350
LIVE = 337500

C_F1, C_AT, C_CV, C_BN, C_F2, C_FN, C_DWB, C_DW = 0, 2, 4, 6, 8, 10, 12, 13


def dot(a, b):
    return lax.dot_general(a, b, (((1,), (0,)), ((), ())), preferred_element_type=f32)


def dot_nt(a, b):
    return lax.dot_general(a, b, (((1,), (1,)), ((), ())), preferred_element_type=f32)


def dot_tn(a, b):
    return lax.dot_general(a, b, (((0,), (0,)), ((), ())), preferred_element_type=f32)


def lane_iota(shape):
    return lax.broadcasted_iota(jnp.int32, shape, len(shape) - 1)


def row_iota(shape):
    return lax.broadcasted_iota(jnp.int32, shape, 0)


def segments():
    found = []
    for h in range(HEADS):
        for r in range(GROUP):
            lo, hi = max(HEAD * h, D * r), min(HEAD * h + HEAD, D * r + D)
            if lo < hi:
                found.append((HP * h + lo - HEAD * h, r, lo - D * r, hi - lo))
    return found


def pad8(values):
    return jnp.concatenate([values, jnp.zeros((8, values.shape[1]), f32)], axis=0)


def ext(values):
    width = values.shape[1]
    ones = jnp.where(row_iota((8, width)) == 0, 1.0, 0.0).astype(f32)
    return jnp.concatenate([values, ones], axis=0).astype(bf16)


def norm(values):
    mean = jnp.sum(values, axis=0, keepdims=True) * (1.0 / D)
    centre = values - mean
    var = jnp.sum(centre * centre, axis=0, keepdims=True) * (1.0 / D)
    rstd = lax.rsqrt(var + EPS_NORM)
    return centre * rstd, rstd


def norm_back(upstream, xhat, rstd, gain):
    scaled = upstream * gain
    mean_one = jnp.sum(scaled, axis=0, keepdims=True) * (1.0 / D)
    mean_two = jnp.sum(scaled * xhat, axis=0, keepdims=True) * (1.0 / D)
    return rstd * (scaled - mean_one - xhat * mean_two)


def fold(values):
    total = values[:, 0:128]
    for at in range(128, values.shape[1], 128):
        total = total + values[:, at : at + 128]
    return total


def permute_in(values, pm):
    low = pad8(values).astype(bf16)
    stack = jnp.concatenate([low[:, 384 * b : 384 * b + 384] for b in range(4)], axis=0)
    out = dot(stack, pm)
    tiles = [out[128 * b : 128 * b + D, 128 * r : 128 * r + 128] for r in range(3) for b in range(4)]
    return jnp.concatenate(tiles, axis=1)


def stack_out(values):
    low = pad8(values).astype(bf16)
    blocks = []
    for b in range(4):
        blocks.append(
            jnp.concatenate([low[:, 512 * r + 128 * b : 512 * r + 128 * b + 128] for r in range(3)], axis=1)
        )
    return jnp.concatenate(blocks, axis=0)


def unstack_out(out):
    return jnp.concatenate([out[128 * b : 128 * b + D, :] for b in range(4)], axis=1)


def permute_out(values, pm):
    return unstack_out(dot_nt(stack_out(values), pm))


def permute_out_wide(values, pm):
    high = values.astype(bf16).astype(f32)
    rest = values - high
    mid = rest.astype(bf16).astype(f32)
    return unstack_out(dot_nt(stack_out(high), pm) + dot_nt(stack_out(mid), pm))


def plane_mask(r, length):
    return jnp.where(lane_iota((1, LG)) * GROUP + r < length, 1.0, 0.0).astype(f32)


def span(r):
    return slice(LG * r, LG * r + LG)


def skewed(count, stages):
    held = [None] * count
    for step in range(count + len(stages) - 1):
        for k, stage in enumerate(stages):
            n = step - k
            if 0 <= n < count:
                held[n] = stage(n, held[n])


def window(ref, r, base=0):
    return ref[base + WIN[r] : base + WIN[r] + WROWS, :]


def join_windows(parts):
    a, b, c = parts
    return jnp.concatenate([a[:112], a[112:128] + b[:16], b[16:128], b[128:144] + c[:16], c[16:]], axis=0)


def shifted_planes(tiles):
    lanes = lane_iota((8, 128))
    zero = jnp.zeros((8, 128), f32)
    made = {}
    for m in range(-HALF, HALF + GROUP):
        r, s = m % GROUP, m // GROUP
        if s == 0:
            made[m] = tiles[r]
            continue
        turned = [pltpu.roll(tiles[r][:, 128 * k : 128 * k + 128], (-s) % 128, 1) for k in range(4)]
        if s > 0:
            pairs = zip(turned, turned[1:] + [zero])
            parts = [jnp.where(lanes < 128 - s, a, b) for a, b in pairs]
        else:
            pairs = zip([zero] + turned[:-1], turned)
            parts = [jnp.where(lanes < -s, a, b) for a, b in pairs]
        made[m] = jnp.concatenate(parts, axis=1)
    return made


def prepare_body(
    me_ref, g_ref, up1_ref, upp1_ref, dn1_ref, dnp1_ref, up2_ref, upp2_ref, dn2_ref, dnp2_ref, pw_ref, pwp_ref, pr_ref, prp_ref,
    wqkv_ref, wqkvt_ref, wo_ref, wob_ref, cols_ref, tab_ref, pm_ref, flat, tb, wt, wins, rows,
):
    parts, part_rows = g_ref.shape[0], g_ref.shape[1]
    for d in range(parts):
        flat[part_rows * d : part_rows * (d + 1), :] = g_ref[place(me_ref[0] ^ d, parts)].astype(f32)
    tb[...] = jnp.zeros_like(tb)
    for start, count, base in ((0, ROWS_HEAD, 0), (TAIL_AT, ROWS_TAIL, TAIL)):
        for r in range(16):
            at = start + D * r
            first, col = at // 128, at % 128
            many = (count - r + 15) // 16
            here = flat[pl.ds(first, many, stride=15), :]
            then = flat[pl.ds(first + 1, many, stride=15), :]
            lanes = lane_iota((many, 128))
            got = jnp.where(lanes >= col, here, then)
            if col:
                got = pltpu.roll(got, 128 - col, 1)
            tb[pl.ds(base + r, many, stride=16), :] = jnp.where(lanes < D, got, 0.0)

    def with_row(block, row):
        tail = jnp.where(row_iota((8, 128)) == 0, row, 0.0)
        return jnp.concatenate([block, tail], axis=0)

    for base, up_ref, upp_ref, dn_ref, dnp_ref in (
        (F1, up1_ref, upp1_ref, dn1_ref, dnp1_ref),
        (F2, up2_ref, upp2_ref, dn2_ref, dnp2_ref),
    ):
        parts_t = []
        for q in range(4):
            block = tb[pl.ds(base + 2 + q, D, stride=4), :]
            parts_t.append(with_row(block, tb[base + 482 + q : base + 483 + q, :]).T[:D, :])
        up_t = jnp.concatenate(parts_t, axis=0)
        up_ref[...] = (0.5 * up_t).astype(bf16)
        full = jnp.concatenate([up_t, jnp.zeros((32, 128), f32)], axis=0)
        upp_ref[...] = full.T[:, :FF].astype(bf16)
        down = tb[base + 486 : base + 966, :]
        dnp_ref[...] = (0.25 * down).astype(bf16)
        bias = jnp.where(row_iota((32, 128)) == 0, tb[base + 966 : base + 967, :], 0.0)
        dn_ref[...] = (0.5 * jnp.concatenate([down, bias], axis=0)).T.astype(bf16)

    parts_t = []
    for q in range(2):
        block = tb[pl.ds(CV + 2 + q, D, stride=2), :]
        parts_t.append(with_row(block, tb[CV + 242 + q : CV + 243 + q, :]).T[:D, :])
    pw_t = jnp.concatenate(parts_t, axis=0)
    pw_ref[...] = (0.5 * pw_t).astype(bf16)
    pwp_ref[...] = jnp.concatenate([pw_t, jnp.zeros((16, 128), f32)], axis=0).T[:, :240].astype(bf16)
    block = with_row(tb[CV + 262 : CV + 382, :], tb[CV + 382 : CV + 383, :])
    prp_ref[...] = (0.5 * block).astype(bf16)
    pr_ref[...] = block.T.astype(bf16)

    none = jnp.zeros((1, 128), f32)
    wins[...] = jnp.zeros_like(wins)
    for w, at, bias_at in ((0, AT + 2, AT + 122), (1, AT + 123, None), (2, AT + 243, AT + 363)):
        bias = none if bias_at is None else tb[bias_at : bias_at + 1, :]
        wt[...] = with_row(tb[at : at + D, :], bias).T
        for to, r, src, many in segments():
            start = WROWS * w + to - WIN[r]
            wins[r, start : start + many, :] = wt[src : src + many, :]
    for r in range(GROUP):
        made = wins[r]
        wqkv_ref[r] = made[: 3 * WROWS].astype(bf16)
        wqkvt_ref[r] = made.T[:, : 3 * WROWS].astype(bf16)
    wt[...] = with_row(tb[AT + 364 : AT + 484, :], none)
    wins[:, 0:256, :] = jnp.zeros((GROUP, 256, 128), f32)
    for to, r, src, many in segments():
        start = to - WIN[r]
        wins[r, start : start + many, :] = wt[src : src + many, :]
    for r in range(GROUP):
        wob_ref[r] = wins[r, 0:WROWS, :].astype(bf16)
        wins[r, MARKS[r] : MARKS[r] + 1, :] = tb[AT + 484 : AT + 485, :]
        wo_ref[r] = wins[r, 0:256, :].T[:, :WROWS].astype(bf16)

    rows[...] = jnp.zeros_like(rows)
    listed = []
    for base in (F1, AT, CV, CV + 260, F2, FN):
        listed += [base, base + 1]
    listed += [CV + 259] + [CV + 244 + k for k in range(KERNEL)]
    for to, src in enumerate(listed):
        rows[to : to + 1, :] = tb[src : src + 1, :]
    cols_ref[...] = rows[...].T

    rel_rows = []
    lanes = lane_iota((1, 128))
    for h in range(HEADS):
        at = REL_AT + (2 * REL + 1) * h
        first, col = at // 128, at % 128
        pieces = []
        for k in range(2):
            got = jnp.where(lanes >= col, flat[first + k : first + k + 1, :], flat[first + k + 1 : first + k + 2, :])
            pieces.append(pltpu.roll(got, (128 - col) % 128, 1) if col else got)
        rel_rows.append(jnp.concatenate(pieces, axis=1))
    rel = jnp.concatenate(rel_rows + [jnp.zeros((4, 256), f32)], axis=0)
    rel = jnp.where(lane_iota((8, 256)) < 2 * REL + 1, rel, 0.0)
    base = dot(rel.astype(bf16), distance_select()) * LOG2E
    for h in range(HEADS):
        spread = jnp.broadcast_to(base[h : h + 1, :], (LG, 2 * LG))
        tab_ref[h] = pltpu.roll(spread, 0, 1, stride=1, stride_axis=0)[:, :LG]
    t = row_iota((384, 384))
    c = lane_iota((384, 384))
    pm_ref[...] = jnp.where(t == GROUP * (c % 128) + c // 128, 1.0, 0.0).astype(bf16)


def distance_select():
    l = lane_iota((256, 2 * LG))
    gap = jnp.where(l < LG, -l, 2 * LG - l)
    index = jnp.clip(gap, -REL, REL) + REL
    return jnp.where(row_iota((256, 2 * LG)) == index, 1.0, 0.0).astype(bf16)


def diagonal_sum(values):
    wide = jnp.concatenate([values, jnp.zeros((LG, LG), f32)], axis=1)
    half = LG // 2
    while half:
        upper, lower = wide[:half], wide[half : 2 * half]
        if half % 128 == 0:
            lower = jnp.concatenate([lower[:, half:], lower[:, :half]], axis=1)
        else:
            lower = pltpu.roll(lower, 2 * LG - half, 1)
        wide = upper + lower
        half //= 2
    return wide


SMEM = pl.BlockSpec(memory_space=pltpu.SMEM)


def prepare(me, gathered):
    total = gathered.shape[0] * gathered.shape[1]

    def o(shape, kind=bf16):
        return jax.ShapeDtypeStruct(shape, kind)

    ffn = [o((FF, 128)), o((128, FF)), o((128, 512)), o((FF, 128))]
    return pl.pallas_call(
        prepare_body,
        in_specs=[SMEM, pl.BlockSpec(memory_space=pltpu.VMEM)],
        out_shape=ffn
        + ffn
        + [o((240, 128)), o((128, 240)), o((128, 128)), o((128, 128))]
        + [o((GROUP, 3 * WROWS, 128)), o((GROUP, 128, 3 * WROWS)), o((GROUP, 128, WROWS)), o((GROUP, WROWS, 128))]
        + [o((128, 128), f32), o((HEADS, LG, LG), f32), o((384, 384))],
        scratch_shapes=[
            pltpu.VMEM((total, 128), f32),
            pltpu.VMEM((TABLE, 128), f32),
            pltpu.VMEM((128, 128), f32),
            pltpu.VMEM((GROUP, 512, 128), f32),
            pltpu.VMEM((128, 128), f32),
        ],
        compiler_params=pltpu.CompilerParams(vmem_limit_bytes=VMEM_BYTES),
        name="prepare",
    )(me, gathered)


def column(cols, k):
    return cols[:D, k : k + 1]


def valid_keys(length):
    return row_iota((LG, 1)) * GROUP < length


def set_tail(hid):
    hid[FF:, :] = jnp.where(row_iota((512 - FF, hid.shape[1])) == 0, 1.0, 0.0).astype(bf16)


def conv_columns(cols, cb):
    for k in range(KERNEL + 1):
        cb[k] = jnp.broadcast_to(cols[:D, C_DWB + k : C_DWB + k + 1], (D, 128))


def wide(tile, copies=4):
    return jnp.concatenate([tile] * copies, axis=1)


def first_body(
    len_ref, x_ref, cols_ref, up_ref, dn_ref, wqkv_ref, wo_ref, pw_ref, tab_ref, pm_ref,
    xf_ref, lf_ref, xa_ref, nrm_ref, qkv_ref, prob_ref, att_ref, aa_ref, xc_ref, cn_ref, gat_ref, sig_ref, rgt_ref,
    rs_ref, dep_ref, st_ref,
    hid, xp, one, cb, run,
):
    u = pl.program_id(0)
    length = len_ref[u]

    @pl.when(u == 0)
    def _():
        set_tail(hid)
        run[...] = jnp.zeros_like(run)
        conv_columns(cols_ref, cb)

    xp[...] = permute_in(x_ref[0].astype(f32), pm_ref[...])
    cols = cols_ref

    def ffn_up(r, held):
        xhat, rstd = norm(xp[:, span(r)])
        xf_ref[0, :, span(r)] = xhat
        rs_ref[0, 0:1, span(r)] = rstd
        low = ext(xhat * column(cols, C_F1) + column(cols, C_F1 + 1))
        lf_ref[0, :, span(r)] = low
        return dot(up_ref[...], low)

    def ffn_down(r, half):
        hid[:FF, span(r)] = (half + half * jnp.tanh(half)).astype(bf16)
        return dot(dn_ref[...], hid[:, span(r)])[:D]

    def ffn_norm(r, branch):
        after = xp[:, span(r)] + branch
        one[:, span(r)] = after
        xhat, rstd = norm(after)
        xa_ref[0, :, span(r)] = xhat
        rs_ref[0, 1:2, span(r)] = rstd
        low = ext(xhat * column(cols, C_AT) + column(cols, C_AT + 1))
        nrm_ref[0, 128 * r : 128 * r + 128, :] = low
        return dot(wqkv_ref[r], low)

    made = [None] * GROUP

    def ffn_keep(r, found):
        made[r] = found

    skewed(GROUP, (ffn_up, ffn_down, ffn_norm, ffn_keep))
    for w in range(3):
        joined = join_windows([made[r][WROWS * w : WROWS * w + WROWS] for r in range(GROUP)])
        qkv_ref[0, GP * w : GP * w + GP, :] = joined.astype(bf16)
    keys = valid_keys(length)

    def rows(w, h):
        return slice(GP * w + HP * h, GP * w + HP * h + HP)

    def score(h, held):
        return dot_tn(qkv_ref[0, rows(1, h), :], qkv_ref[0, rows(0, h), :])

    def soften(h, raw):
        scores = raw * (SCALE * LOG2E) + tab_ref[h]
        scores = jnp.where(keys, scores, NEG_FILL * LOG2E)
        peak = jnp.max(scores, axis=0, keepdims=True)
        power = jnp.exp2(scores - peak)
        total = jnp.sum(power, axis=0, keepdims=True)
        prob_ref[0, h] = (power * (1.0 / total)).astype(bf16)
        mixed = dot(qkv_ref[0, rows(2, h), :], prob_ref[0, h])
        if h < GROUP:
            mixed = jnp.where(row_iota((HP, LG)) == HEAD, 1.0, mixed)
        att_ref[0, rows(0, h), :] = mixed.astype(bf16)

    skewed(HEADS, (score, soften))

    def project(r, held):
        return dot(wo_ref[r], window(att_ref.at[0], r))[:D]

    def gate_in(r, mixed):
        after = one[:, span(r)] + mixed
        aa_ref[0, :, span(r)] = after
        xhat, rstd = norm(after)
        xc_ref[0, :, span(r)] = xhat
        rs_ref[0, 2:3, span(r)] = rstd
        low = ext(xhat * column(cols, C_CV) + column(cols, C_CV + 1))
        cn_ref[0, :, span(r)] = low
        return dot(pw_ref[...], low)

    def gate_out(r, pre):
        mask = plane_mask(r, length)
        sig = (0.5 + 0.5 * jnp.tanh(pre[D:])) * mask
        gated = (pre[:D] + pre[:D]) * sig
        gat_ref[0, :, span(r)] = gated
        sig_ref[0, :, span(r)] = sig
        rgt_ref[0, :, span(r)] = gated * (1.0 - sig)

    skewed(GROUP, (project, gate_in, gate_out))

    def shift(f, held):
        return shifted_planes([gat_ref[0, 8 * f : 8 * f + 8, span(r)] for r in range(GROUP)])

    def taps(f, moved):
        at = slice(8 * f, 8 * f + 8)
        for r in range(GROUP):
            total = wide(cb[0, at, :])
            for k in range(KERNEL):
                total = total + wide(cb[1 + k, at, :]) * moved[r + k - HALF]
            dep_ref[0, at, span(r)] = total

    skewed(D // 8, (shift, taps))

    count = length.astype(f32)
    mask = jnp.concatenate([plane_mask(r, length) for r in range(GROUP)], axis=1)
    dep = dep_ref[0]
    mean = jnp.sum(dep * mask, axis=1, keepdims=True) / count
    gap = (dep - mean) * mask
    spread = jnp.sum(gap * gap, axis=1, keepdims=True)
    old_mean, old_spread, old_count = run[0], run[1], run[2]
    new_count = old_count + count
    step = mean - old_mean
    new_mean = old_mean + step * (count / new_count)
    new_spread = old_spread + spread + step * step * (old_count * count / new_count)
    run[0] = new_mean
    run[1] = new_spread
    run[2] = new_count

    @pl.when(u == pl.num_programs(0) - 1)
    def _():
        lanes = lane_iota((D, 128))
        picked = jnp.where(lanes == 0, run[0], jnp.where(lanes == 1, run[1], jnp.where(lanes == 2, run[2], 0.0)))
        line = pad8(picked).T[0:8]
        for d in range(st_ref.shape[0]):
            st_ref[d] = line


def whole(shape):
    zeros = (0,) * len(shape)
    return pl.BlockSpec(shape, lambda u: zeros)


def per_utt(shape):
    zeros = (0,) * len(shape)
    return pl.BlockSpec((1,) + shape, lambda u: (u,) + zeros)


def first(devices, lengths, x, weights):
    utts = x.shape[0]
    big = (D, MAXLEN)
    low = (128, MAXLEN)
    per = [
        (big, f32),
        (low, bf16),
        (big, f32),
        ((GP, LG), bf16),
        ((3 * GP, LG), bf16),
        ((HEADS, LG, LG), bf16),
        ((GP, LG), bf16),
        (big, f32),
        (big, f32),
        (low, bf16),
        (big, f32),
        (big, f32),
        (big, f32),
        ((8, MAXLEN), f32),
        (big, f32),
    ]
    line = (devices, 8, 128)
    return pl.pallas_call(
        first_body,
        grid=(utts,),
        in_specs=[SMEM, per_utt(big)] + [whole(w.shape) for w in weights],
        out_specs=[per_utt(s) for s, k in per] + [whole(line)],
        out_shape=[jax.ShapeDtypeStruct((utts,) + s, k) for s, k in per] + [jax.ShapeDtypeStruct(line, f32)],
        scratch_shapes=[
            pltpu.VMEM((512, MAXLEN), bf16),
            pltpu.VMEM(big, f32),
            pltpu.VMEM(big, f32),
            pltpu.VMEM((KERNEL + 1, D, 128), f32),
            pltpu.VMEM((3, D, 128), f32),
        ],
        compiler_params=pltpu.CompilerParams(vmem_limit_bytes=VMEM_BYTES),
        name="first",
    )(lengths, x, *weights)


def second_body(
    len_ref, stats_ref, cot_ref, aa_ref, dep_ref, cols_ref, up_ref, upp_ref, dn_ref, dnp_ref, pr_ref, prp_ref, pm_ref,
    out_ref, bgd_ref, gc_ref, sums_ref, stc_ref, gdn_ref, gup_ref, gpr_ref, vec_ref,
    hid, cotp, outp, acc,
):
    u = pl.program_id(0)
    length = len_ref[u]
    cols = cols_ref

    @pl.when(u == 0)
    def _():
        set_tail(hid)
        parts = stats_ref.shape[0]
        count = jnp.zeros((1, 128), f32)
        total = jnp.zeros((1, 128), f32)
        for d in range(parts):
            many = stats_ref[d, 2:3, :]
            count = count + many
            total = total + many * stats_ref[d, 0:1, :]
        here = lane_iota((1, 128)) < D
        count = jnp.where(here, count, 1.0)
        mean = total / count
        spread = jnp.zeros((1, 128), f32)
        for d in range(parts):
            gap = stats_ref[d, 0:1, :] - mean
            spread = spread + stats_ref[d, 1:2, :] + stats_ref[d, 2:3, :] * gap * gap
        scale = lax.rsqrt(spread / count + EPS_NORM)
        at = row_iota((128, 128))
        table = jnp.where(at == 0, mean, jnp.where(at == 1, scale, jnp.where(at == 2, 1.0 / count, 0.0)))
        stc_ref[...] = table.T
        gdn_ref[...] = jnp.zeros_like(gdn_ref)
        gup_ref[...] = jnp.zeros_like(gup_ref)
        gpr_ref[...] = jnp.zeros_like(gpr_ref)
        vec_ref[...] = jnp.zeros_like(vec_ref)
        acc[...] = jnp.zeros_like(acc)

    cotp[...] = permute_in(cot_ref[0].astype(f32), pm_ref[...])
    half_gain = 0.5 * column(cols, C_BN)
    half_bias = 0.5 * column(cols, C_BN + 1)

    def enter(r, held):
        normal = (dep_ref[0, :, span(r)] - stc_ref[:D, 0:1]) * stc_ref[:D, 1:2]
        z = normal * half_gain + half_bias
        t = jnp.tanh(z)
        act = z + z * t
        act_low = ext(act)
        slope = (1.0 + t) * (1.0 + z * (1.0 - t))
        return act_low, normal, slope, dot(pr_ref[...], act_low)[:D]

    def ffn_up(r, held):
        act_low, normal, slope, moved = held
        after_conv = aa_ref[0, :, span(r)] + moved
        xhat, rstd = norm(after_conv)
        low = ext(xhat * column(cols, C_F2) + column(cols, C_F2 + 1))
        return act_low, normal, slope, after_conv, xhat, rstd, low, dot(up_ref[...], low)

    def ffn_down(r, held):
        act_low, normal, slope, after_conv, xhat, rstd, low, half = held
        t = jnp.tanh(half)
        hid[:FF, span(r)] = (half + half * t).astype(bf16)
        bend = (1.0 + t) * (1.0 + half * (1.0 - t))
        return act_low, normal, slope, after_conv, xhat, rstd, low, bend, dot(dn_ref[...], hid[:, span(r)])[:D]

    def finish(r, held):
        act_low, normal, slope, after_conv, xhat, rstd, low, bend, branch = held
        mask = plane_mask(r, length)
        xhat_f, rstd_f = norm(after_conv + branch)
        outp[:, span(r)] = (xhat_f * column(cols, C_FN) + column(cols, C_FN + 1)) * mask
        up_grad = cotp[:, span(r)] * mask
        vec_ref[2] += fold(up_grad * xhat_f)
        vec_ref[3] += fold(up_grad)
        grad_two = norm_back(up_grad, xhat_f, rstd_f, column(cols, C_FN))
        branch = pad8(grad_two).astype(bf16)
        gdn_ref[...] += dot_nt(hid[:, span(r)], branch)
        return act_low, normal, slope, xhat, rstd, low, bend, grad_two, dot(dnp_ref[...], branch)

    def ffn_back(r, held):
        act_low, normal, slope, xhat, rstd, low, bend, grad_two, back = held
        pre_low = (bend * back).astype(bf16)
        gup_ref[...] += dot_nt(pre_low, low)
        return act_low, normal, slope, xhat, rstd, grad_two, dot(upp_ref[...], pre_low)[:D]

    def leave(r, held):
        act_low, normal, slope, xhat, rstd, grad_two, back = held
        vec_ref[0] += fold(back * xhat)
        vec_ref[1] += fold(back)
        grad_conv = grad_two + norm_back(back, xhat, rstd, column(cols, C_F2))
        gc_ref[0, :, span(r)] = grad_conv
        project = pad8(grad_conv).astype(bf16)
        gpr_ref[...] += dot_nt(act_low, project)
        return normal, slope, dot(prp_ref[...], project)[:D]

    def last(r, held):
        normal, slope, back = held
        batch = slope * back
        bgd_ref[0, :, span(r)] = batch
        acc[0] += fold(batch * normal)
        acc[1] += fold(batch)

    skewed(GROUP, (enter, ffn_up, ffn_down, finish, ffn_back, leave, last))
    out_ref[0] = permute_out(outp[...], pm_ref[...]).astype(bf16)

    @pl.when(u == pl.num_programs(0) - 1)
    def _():
        lanes = lane_iota((D, 128))
        gain = jnp.sum(acc[0], axis=1, keepdims=True)
        shift = jnp.sum(acc[1], axis=1, keepdims=True)
        line = pad8(jnp.where(lanes == 0, gain, jnp.where(lanes == 1, shift, 0.0))).T[0:8]
        for d in range(sums_ref.shape[0]):
            sums_ref[d] = line


def second(lengths, stats, cot, aa, dep, weights):
    utts = cot.shape[0]
    big = (D, MAXLEN)
    outs = [
        (per_utt(big), (utts,) + big, bf16),
        (per_utt(big), (utts,) + big, f32),
        (per_utt(big), (utts,) + big, f32),
    ]
    for s in (stats.shape, (128, 128), (512, 128), (FF, 128), (128, 128), (4, D, 128)):
        outs.append((whole(s), s, f32))
    return pl.pallas_call(
        second_body,
        grid=(utts,),
        in_specs=[SMEM, whole(stats.shape)] + [per_utt(big)] * 3 + [whole(w.shape) for w in weights],
        out_specs=[o[0] for o in outs],
        out_shape=[jax.ShapeDtypeStruct(o[1], o[2]) for o in outs],
        scratch_shapes=[
            pltpu.VMEM((512, MAXLEN), bf16),
            pltpu.VMEM(big, f32),
            pltpu.VMEM(big, f32),
            pltpu.VMEM((2, D, 128), f32),
        ],
        compiler_params=pltpu.CompilerParams(vmem_limit_bytes=VMEM_BYTES),
        name="second",
    )(lengths, stats, cot, aa, dep, *weights)


def third_body(
    len_ref, sums_ref, stc_ref, bgd_ref, gc_ref, dep_ref, xf_ref, lf_ref, xa_ref, nrm_ref, qkv_ref, prob_ref, att_ref, xc_ref,
    cn_ref, gat_ref, sig_ref, rgt_ref, rs_ref,
    cols_ref, up_ref, upp_ref, dnp_ref, wqkv_t_ref, wob_ref, pwp_ref, pm_ref,
    gin_ref, gdn_ref, gup_ref, gpw_ref, gqkv_ref, go_ref, rel_ref, vec_ref,
    hid, dgs, olg, agr, back_s, gg, relacc, cb, tot,
):
    u = pl.program_id(0)
    length = len_ref[u]
    cols = cols_ref

    @pl.when(u == 0)
    def _():
        set_tail(hid)
        conv_columns(cols_ref, cb)
        parts = sums_ref.shape[0]
        total = sums_ref[0]
        for d in range(1, parts):
            total = total + sums_ref[d]
        tot[...] = jnp.concatenate([total, jnp.zeros((120, 128), f32)], axis=0).T
        for ref in (gdn_ref, gup_ref, gpw_ref, gqkv_ref, go_ref, vec_ref, relacc):
            ref[...] = jnp.zeros_like(ref)

    scale = stc_ref[:D, 1:2]
    lead = column(cols, C_BN) * scale
    share = lead * stc_ref[:D, 2:3]
    shift_part = share * tot[:D, 1:2]
    gain_part = share * tot[:D, 0:1] * scale
    for r in range(GROUP):
        normal = dep_ref[0, :, span(r)] - stc_ref[:D, 0:1]
        mask = plane_mask(r, length)
        dgs[:, span(r)] = bgd_ref[0, :, span(r)] * lead - mask * (shift_part + normal * gain_part)

    def shift(f, held):
        return shifted_planes([dgs[8 * f : 8 * f + 8, span(r)] for r in range(GROUP)])

    def taps(f, moved):
        at = slice(8 * f, 8 * f + 8)
        gated = [gat_ref[0, at, span(r)] for r in range(GROUP)]
        totals = [None] * GROUP
        for k in range(KERNEL):
            weight = wide(cb[1 + k, at, :])
            tap = None
            for r in range(GROUP):
                here = moved[r - k + HALF]
                term = weight * here
                totals[r] = term if totals[r] is None else totals[r] + term
                part = gated[r] * here
                tap = part if tap is None else tap + part
            vec_ref[7 + k, at, :] += fold(tap)
        vec_ref[6, at, :] += fold(moved[0] + moved[1] + moved[2])
        for r in range(GROUP):
            gg[at, span(r)] = totals[r]

    skewed(D // 8, (shift, taps))

    def gate(r, held):
        grad = gg[:, span(r)]
        left = grad * sig_ref[0, :, span(r)]
        right = grad * rgt_ref[0, :, span(r)]
        pre_low = jnp.concatenate([left, right], axis=0).astype(bf16)
        gpw_ref[...] += dot_nt(pre_low, cn_ref[0, :, span(r)])
        return dot(pwp_ref[...], pre_low)[:D]

    def residual(r, back):
        xhat = xc_ref[0, :, span(r)]
        vec_ref[0] += fold(back * xhat)
        vec_ref[1] += fold(back)
        grad = gc_ref[0, :, span(r)] + norm_back(back, xhat, rs_ref[0, 2:3, span(r)], column(cols, C_CV))
        dgs[:, span(r)] = grad
        low = pad8(grad).astype(bf16)
        olg[128 * r : 128 * r + 128, :] = low
        return dot(wob_ref[r], low)

    made = [None] * GROUP

    def keep(r, found):
        go_ref[r] += dot_nt(window(att_ref.at[0], r), olg[128 * r : 128 * r + 128, :])
        made[r] = found

    skewed(GROUP, (gate, residual, keep))
    agr[...] = join_windows(made).astype(bf16)

    def rows(w, h):
        return slice(GP * w + HP * h, GP * w + HP * h + HP)

    def enter(h, held):
        grad = agr[rows(0, h), :]
        back_s[rows(2, h), :] = dot_nt(grad, prob_ref[0, h]).astype(bf16)
        return dot_tn(qkv_ref[0, rows(2, h), :], grad)

    def soften(h, prob_grad):
        probs = prob_ref[0, h].astype(f32)
        inner = jnp.sum(probs * prob_grad, axis=0, keepdims=True)
        score = probs * (prob_grad - inner)
        relacc[h] += score
        low = score.astype(bf16)
        back_s[rows(0, h), :] = (dot(qkv_ref[0, rows(1, h), :], low) * SCALE).astype(bf16)
        back_s[rows(1, h), :] = (dot_nt(qkv_ref[0, rows(0, h), :], low) * SCALE).astype(bf16)

    skewed(HEADS, (enter, soften))

    def project(r, held):
        stack = jnp.concatenate([window(back_s, r, GP * w) for w in range(3)], axis=0)
        gqkv_ref[r] += dot_nt(stack, nrm_ref[0, 128 * r : 128 * r + 128, :])
        return dot(wqkv_t_ref[r], stack)[:D], dot(up_ref[...], lf_ref[0, :, span(r)])

    def ffn_in(r, held):
        back, half = held
        xhat = xa_ref[0, :, span(r)]
        vec_ref[2] += fold(back * xhat)
        vec_ref[3] += fold(back)
        grad = dgs[:, span(r)] + norm_back(back, xhat, rs_ref[0, 1:2, span(r)], column(cols, C_AT))
        low = pad8(grad).astype(bf16)
        return grad, low, half, dot(dnp_ref[...], low)

    def ffn_mid(r, held):
        grad, branch, half, back = held
        t = jnp.tanh(half)
        hid[:FF, span(r)] = (half + half * t).astype(bf16)
        pre_low = ((1.0 + t) * (1.0 + half * (1.0 - t)) * back).astype(bf16)
        gdn_ref[...] += dot_nt(hid[:, span(r)], branch)
        gup_ref[...] += dot_nt(pre_low, lf_ref[0, :, span(r)])
        return grad, dot(upp_ref[...], pre_low)[:D]

    def ffn_out(r, held):
        grad, back = held
        xhat = xf_ref[0, :, span(r)]
        vec_ref[4] += fold(back * xhat)
        vec_ref[5] += fold(back)
        gg[:, span(r)] = grad + norm_back(back, xhat, rs_ref[0, 0:1, span(r)], column(cols, C_F1))

    skewed(GROUP, (project, ffn_in, ffn_mid, ffn_out))
    gin_ref[0] = permute_out_wide(gg[...], pm_ref[...])

    @pl.when(u == pl.num_programs(0) - 1)
    def _():
        found = []
        for h in range(HEADS):
            found.append(diagonal_sum(relacc[h]))
        stacked = jnp.concatenate(found + [jnp.zeros((4, 2 * LG), f32)], axis=0)
        high = stacked.astype(bf16)
        rest = stacked - high.astype(f32)
        mid = rest.astype(bf16)
        rest = rest - mid.astype(f32)
        select = distance_select()
        rel_ref[...] = dot_nt(high, select) + dot_nt(mid, select) + dot_nt(rest.astype(bf16), select)


def third(lengths, sums, stc, saved, weights):
    utts = saved[0].shape[0]
    big = (D, MAXLEN)
    outs = [(per_utt(big), (utts,) + big)]
    for s in ((512, 128), (FF, 128), (240, 128), (GROUP, 3 * WROWS, 128), (GROUP, WROWS, 128), (8, 256), (22, D, 128)):
        outs.append((whole(s), s))
    return pl.pallas_call(
        third_body,
        grid=(utts,),
        in_specs=[SMEM, whole(sums.shape), whole(stc.shape)]
        + [per_utt(s.shape[1:]) for s in saved]
        + [whole(w.shape) for w in weights],
        out_specs=[o[0] for o in outs],
        out_shape=[jax.ShapeDtypeStruct(o[1], f32) for o in outs],
        scratch_shapes=[
            pltpu.VMEM((512, MAXLEN), bf16),
            pltpu.VMEM(big, f32),
            pltpu.VMEM((GP, LG), bf16),
            pltpu.VMEM((GP, LG), bf16),
            pltpu.VMEM((3 * GP, LG), bf16),
            pltpu.VMEM(big, f32),
            pltpu.VMEM((HEADS, LG, LG), f32),
            pltpu.VMEM((KERNEL + 1, D, 128), f32),
            pltpu.VMEM((128, 128), f32),
        ],
        compiler_params=pltpu.CompilerParams(vmem_limit_bytes=VMEM_BYTES),
        name="third",
    )(lengths, sums, stc, *saved, *weights)


def pack_body(
    me_ref, dn1_ref, up1_ref, dn2_ref, up2_ref, pr_ref, pw_ref, qkv_ref, o_ref, rel_ref, vecs2_ref, vecs3_ref, sums_ref,
    keep_ref, send_ref, tb, flat, stage, wt,
):
    tb[...] = jnp.zeros_like(tb)
    flat[...] = jnp.zeros_like(flat)
    lanes = lane_iota((D, 128))
    table = jnp.zeros((D, 128), f32)
    listed = []
    for ref, at in (
        (vecs2_ref, (F2, F2 + 1, FN, FN + 1)),
        (vecs3_ref, (CV, CV + 1, AT, AT + 1, F1, F1 + 1, CV + 259) + tuple(CV + 244 + k for k in range(KERNEL))),
    ):
        for k, to in enumerate(at):
            table = jnp.where(lanes == len(listed), jnp.sum(ref[k], axis=1, keepdims=True), table)
            listed.append(to)
    wt[...] = pad8(table).T
    keep = lane_iota((1, 128)) < D
    for k, to in enumerate(listed):
        tb[to : to + 1, :] = wt[k : k + 1, :]
    tb[CV + 260 : CV + 262, :] = sums_ref[0, 0:2, :]

    def clean(block):
        return jnp.where(lane_iota(block.shape) < D, block, 0.0)

    for base, dn_ref, up_ref in ((F1, dn1_ref, up1_ref), (F2, dn2_ref, up2_ref)):
        tb[base + 486 : base + 967, :] = 0.5 * clean(dn_ref[0 : FF + 1, :])
        for q in range(4):
            block = pad8(up_ref[D * q : D * q + D, :]).T
            tb[pl.ds(base + 2 + q, D, stride=4), :] = block[:D]
            tb[base + 482 + q : base + 483 + q, :] = block[D : D + 1]
    for q in range(2):
        block = pad8(pw_ref[D * q : D * q + D, :]).T
        tb[pl.ds(CV + 2 + q, D, stride=2), :] = block[:D]
        tb[CV + 242 + q : CV + 243 + q, :] = block[D : D + 1]
    tb[CV + 262 : CV + 383, :] = clean(pr_ref[0 : D + 1, :])

    def gathered(ref, base):
        wt[...] = jnp.zeros_like(wt)
        for to, r, src, many in segments():
            start = base + to - WIN[r]
            wt[src : src + many, :] += ref[r, start : start + many, :]
        return wt[...]

    for w, at, bias_at in ((0, AT + 2, AT + 122), (1, AT + 123, None), (2, AT + 243, AT + 363)):
        block = gathered(qkv_ref, WROWS * w).T
        tb[at : at + D, :] = block[:D]
        if bias_at is not None:
            tb[bias_at : bias_at + 1, :] = block[D : D + 1]
    tb[AT + 364 : AT + 484, :] = clean(gathered(o_ref, 0)[:D])
    bias = sum(o_ref[r, MARKS[r] : MARKS[r] + 1, :] for r in range(GROUP))
    tb[AT + 484 : AT + 485, :] = jnp.where(keep, bias, 0.0)

    last = (LIVE - 1) // 128
    for y_first, y_count, offset, base in (
        (0, REL_AT // 128 + 1, 0, 0),
        (TAIL_AT // 128, last - TAIL_AT // 128 + 1, 128 * (TAIL_AT // 128) - TAIL_AT + D, TAIL - 1),
    ):
        for k in range(15):
            at = 128 * k + offset
            first_row, col = at // D, at % D
            many = (y_count - k + 14) // 15
            here = lane_iota((many, 128))
            got = tb[pl.ds(base + first_row, many, stride=16), :]
            if col:
                got = pltpu.roll(got, 128 - col, 1)
            then = pltpu.roll(tb[pl.ds(base + first_row + 1, many, stride=16), :], D - col, 1)
            got = jnp.where(here < D - col, got, then)
            if 2 * D - col < 128:
                then = pltpu.roll(tb[pl.ds(base + first_row + 2, many, stride=16), :], 2 * D - col, 1)
                got = jnp.where(here < 2 * D - col, got, then)
            flat[pl.ds(y_first + k, many, stride=15), :] = got
    here = lane_iota((1, 128))
    width = 2 * REL + 1
    for h in range(HEADS):
        at = REL_AT + width * h
        for y in range(at // 128, (at + width - 1) // 128 + 1):
            lo, hi = max(at - 128 * y, 0), min(at + width - 128 * y, 128)
            shift = (at - 128 * y) % 256
            turned = rel_ref[h : h + 1, :]
            if shift:
                turned = pltpu.roll(turned, shift, 1)
            flat[y : y + 1, :] += jnp.where((here >= lo) & (here < hi), turned[:, :128], 0.0)
    parts, rows = 2 * keep_ref.shape[0], keep_ref.shape[1]
    for d in range(parts):
        stage[d] = flat[rows * d : rows * (d + 1), :]
    for offset in range(0, parts, 2):
        keep_ref[place(offset, parts)] = stage[me_ref[0] ^ offset]
        send_ref[place(offset, parts)] = stage[me_ref[0] ^ (offset + 1)]


def pack(parts, rows, me, grads):
    half = jax.ShapeDtypeStruct((parts // 2, rows, 128), f32)
    return pl.pallas_call(
        pack_body,
        in_specs=[SMEM] + [pl.BlockSpec(memory_space=pltpu.VMEM)] * len(grads),
        out_shape=[half, half],
        scratch_shapes=[
            pltpu.VMEM((TABLE, 128), f32),
            pltpu.VMEM((parts * rows, 128), f32),
            pltpu.VMEM((parts, rows, 128), f32),
            pltpu.VMEM((128, 128), f32),
        ],
        compiler_params=pltpu.CompilerParams(vmem_limit_bytes=VMEM_BYTES),
        name="pack",
    )(me, *grads)


def update_tables(total_len):
    rates = np.zeros(total_len, np.float32)
    decays = np.zeros(total_len, np.float32)
    vector, gain, ffn = (D, 0.1, 0.0), (D, 0.3, 0.0), lambda n, fan: (n, fan**-0.5, 0.01)
    block = [gain, vector, ffn(D * FF, D), (FF, 0.1, 0.0), ffn(FF * D, FF), vector]
    square = ffn(D * D, D)
    pieces = block + [gain, vector, square, vector, square, square, vector, ffn(D * D, 6.0 * D / MAXLEN), vector]
    pieces += [(HEADS * (2 * REL + 1), 0.5, 0.0)]
    pieces += [gain, vector, ffn(2 * D * D, D), (2 * D, 0.1, 0.0), ffn(KERNEL * D, KERNEL), vector, gain, vector]
    pieces += [square, vector] + block + [gain, vector]
    offset = 0
    for entries, rate, decay in pieces:
        rates[offset : offset + entries] = rate
        decays[offset : offset + entries] = decay
        offset += entries
    return rates, decays


def digits(devices):
    found, stride = [], 1
    while stride < devices:
        size = min(2 if stride == 1 else 4, devices // stride)
        found.append((stride, size))
        stride *= size
    return found


def place(offset, devices):
    at, weight = 0, devices
    for stride, size in digits(devices):
        weight //= size
        at = at + ((offset // stride) % size) * weight
    return at


def partner(values, offset, devices):
    return lax.ppermute(values, "dp", [(i, i ^ offset) for i in range(devices)])


def gather(values, devices):
    held = values[None]
    for stride, size in reversed(digits(devices)):
        held = jnp.concatenate([held] + [partner(held, stride * j, devices) for j in range(1, size)], axis=0)
    return held


def scatter_sum(keep, send, devices):
    total = keep + partner(send, 1, devices)
    for stride, size in digits(devices)[1:]:
        parts = total.reshape((size, total.shape[0] // size) + total.shape[1:])
        total = parts[0]
        for j in range(1, size):
            total = total + partner(parts[j], stride * j, devices)
    return total


def local(frames, lengths, cotangent, master, moment_one, moment_two, average):
    shard_len = master.shape[0]
    devices = lax.axis_size("dp")
    rows = shard_len // 128
    me = lax.axis_index("dp").astype(jnp.int32).reshape(1)
    gathered = gather(master.astype(bf16).reshape(rows, 128), devices)
    (
        up1, upp1, dn1, dnp1, up2, upp2, dn2, dnp2, pw, pwp, pr, prp, wqkv, wqkvt, wo, wob, cols, tab, pm,
    ) = prepare(me, gathered)
    x = jnp.transpose(frames, (0, 2, 1))
    cot = jnp.transpose(cotangent, (0, 2, 1))
    xf, lf, xa, nrm, qkv, prob, att, aa, xc, cn, gat, sig, rgt, rs, dep, st = first(
        devices, lengths, x, (cols, up1, dn1, wqkv, wo, pw, tab, pm)
    )
    stats = lax.all_to_all(st, "dp", 0, 0)
    out, bgd, gc, sums, stc, gdn2, gup2, gpr, vec2 = second(
        lengths, stats, cot, aa, dep, (cols, up2, upp2, dn2, dnp2, pr, prp, pm)
    )
    all_sums = lax.all_to_all(sums, "dp", 0, 0)
    gin, gdn1, gup1, gpw, gqkv, go, rel, vec3 = third(
        lengths, all_sums, stc,
        (bgd, gc, dep, xf, lf, xa, nrm, qkv, prob, att, xc, cn, gat, sig, rgt, rs),
        (cols, up1, upp1, dnp1, wqkvt, wob, pwp, pm),
    )
    keep, send = pack(devices, rows, me, (gdn1, gup1, gdn2, gup2, gpr, gpw, gqkv, go, rel, vec2, vec3, sums))
    reduced = scatter_sum(keep, send, devices).reshape(shard_len)
    rates_np, decays_np = update_tables(shard_len * devices)
    start_at = lax.axis_index("dp") * shard_len
    rates = lax.dynamic_slice_in_dim(jnp.asarray(rates_np), start_at, shard_len)
    decays = lax.dynamic_slice_in_dim(jnp.asarray(decays_np), start_at, shard_len)
    correction = 1.0 - 0.5**STEP
    new_one = 0.5 * moment_one + 0.5 * reduced
    new_two = 0.5 * moment_two + 0.5 * reduced * reduced
    direction = new_one / correction / (jnp.sqrt(new_two / correction) + EPS_ADAM)
    new_master = master - rates * (direction + decays * master)
    new_average = 0.75 * average + 0.25 * new_master
    return (
        jnp.transpose(out, (0, 2, 1)),
        jnp.transpose(gin, (0, 2, 1)),
        reduced,
        new_master,
        new_one,
        new_two,
        new_average,
    )


def solution(mesh):
    three = P("dp", None, None)
    one = P("dp")
    in_specs = (three, one, three, one, one, one, one)
    out_specs = (three, three, one, one, one, one, one)
    return jax.shard_map(local, mesh=mesh, in_specs=in_specs, out_specs=out_specs, check_vma=False)
```

```python
import math

import jax
import jax.numpy as jnp
import numpy as np
from jax import lax
from jax.experimental import pallas as pl
from jax.experimental.pallas import tpu as pltpu
from jax.sharding import PartitionSpec as P

D = 120
HEADS = 4
FF = 480
KERNEL = 15
GROUP = 3
REL = 127
STEP = 5
MAXLEN = 1536
LG = 512
HEAD = 90
HP = 96
GP = HEADS * HP
HALF = KERNEL // 2
WIN = (0, 112, 240)
WROWS = 144
MARKS = tuple(HP * r + HEAD - WIN[r] for r in range(GROUP))

EPS_NORM = 1e-05
EPS_ADAM = 1e-08
NEG_FILL = -1000000000.0
LOG2E = math.log2(math.e)
SCALE = HEAD ** (-0.5)

f32 = jnp.float32
bf16 = jnp.bfloat16
VMEM_BYTES = 58 * 2**20

REL_AT = 174240
TAIL_AT = 175260
TAIL = 1456
ROWS_HEAD = 1452
ROWS_TAIL = 1352
TABLE = 2824
F1 = 0
AT = 967
CV = TAIL
F2 = TAIL + 383
FN = TAIL + 1350
LIVE = 337500

C_F1, C_AT, C_CV, C_BN, C_F2, C_FN, C_DWB, C_DW = 0, 2, 4, 6, 8, 10, 12, 13


def dot(a, b):
    return lax.dot_general(a, b, (((1,), (0,)), ((), ())), preferred_element_type=f32)


def dot_nt(a, b):
    return lax.dot_general(a, b, (((1,), (1,)), ((), ())), preferred_element_type=f32)


def dot_tn(a, b):
    return lax.dot_general(a, b, (((0,), (0,)), ((), ())), preferred_element_type=f32)


def lane_iota(shape):
    return lax.broadcasted_iota(jnp.int32, shape, len(shape) - 1)


def row_iota(shape):
    return lax.broadcasted_iota(jnp.int32, shape, 0)


def segments():
    found = []
    for h in range(HEADS):
        for r in range(GROUP):
            lo, hi = max(HEAD * h, D * r), min(HEAD * h + HEAD, D * r + D)
            if lo < hi:
                found.append((HP * h + lo - HEAD * h, r, lo - D * r, hi - lo))
    return found


def pad8(values):
    return jnp.concatenate([values, jnp.zeros((8, values.shape[1]), f32)], axis=0)


def ext(values):
    width = values.shape[1]
    ones = jnp.where(row_iota((8, width)) == 0, 1.0, 0.0).astype(f32)
    return jnp.concatenate([values, ones], axis=0).astype(bf16)


def norm(values):
    mean = jnp.sum(values, axis=0, keepdims=True) * (1.0 / D)
    centre = values - mean
    var = jnp.sum(centre * centre, axis=0, keepdims=True) * (1.0 / D)
    rstd = lax.rsqrt(var + EPS_NORM)
    return centre * rstd, rstd


def norm_back(upstream, xhat, rstd, gain):
    scaled = upstream * gain
    mean_one = jnp.sum(scaled, axis=0, keepdims=True) * (1.0 / D)
    mean_two = jnp.sum(scaled * xhat, axis=0, keepdims=True) * (1.0 / D)
    return rstd * (scaled - mean_one - xhat * mean_two)


def fold(values):
    total = values[:, 0:128]
    for at in range(128, values.shape[1], 128):
        total = total + values[:, at : at + 128]
    return total


def permute_in(values, pm):
    low = pad8(values).astype(bf16)
    stack = jnp.concatenate([low[:, 384 * b : 384 * b + 384] for b in range(4)], axis=0)
    out = dot(stack, pm)
    tiles = [out[128 * b : 128 * b + D, 128 * r : 128 * r + 128] for r in range(3) for b in range(4)]
    return jnp.concatenate(tiles, axis=1)


def stack_out(values):
    low = pad8(values).astype(bf16)
    blocks = []
    for b in range(4):
        blocks.append(
            jnp.concatenate([low[:, 512 * r + 128 * b : 512 * r + 128 * b + 128] for r in range(3)], axis=1)
        )
    return jnp.concatenate(blocks, axis=0)


def unstack_out(out):
    return jnp.concatenate([out[128 * b : 128 * b + D, :] for b in range(4)], axis=1)


def permute_out(values, pm):
    return unstack_out(dot_nt(stack_out(values), pm))


def permute_out_wide(values, pm):
    high = values.astype(bf16).astype(f32)
    rest = values - high
    mid = rest.astype(bf16).astype(f32)
    return unstack_out(dot_nt(stack_out(high), pm) + dot_nt(stack_out(mid), pm))


def plane_mask(r, length):
    return jnp.where(lane_iota((1, LG)) * GROUP + r < length, 1.0, 0.0).astype(f32)


def span(r):
    return slice(LG * r, LG * r + LG)


def skewed(count, stages):
    held = [None] * count
    for step in range(count + len(stages) - 1):
        for k, stage in enumerate(stages):
            n = step - k
            if 0 <= n < count:
                held[n] = stage(n, held[n])


def window(ref, r, base=0):
    return ref[base + WIN[r] : base + WIN[r] + WROWS, :]


def join_windows(parts):
    a, b, c = parts
    return jnp.concatenate([a[:112], a[112:128] + b[:16], b[16:128], b[128:144] + c[:16], c[16:]], axis=0)


def shifted_planes(tiles):
    lanes = lane_iota((8, 128))
    zero = jnp.zeros((8, 128), f32)
    made = {}
    for m in range(-HALF, HALF + GROUP):
        r, s = m % GROUP, m // GROUP
        if s == 0:
            made[m] = tiles[r]
            continue
        turned = [pltpu.roll(tiles[r][:, 128 * k : 128 * k + 128], (-s) % 128, 1) for k in range(4)]
        if s > 0:
            pairs = zip(turned, turned[1:] + [zero])
            parts = [jnp.where(lanes < 128 - s, a, b) for a, b in pairs]
        else:
            pairs = zip([zero] + turned[:-1], turned)
            parts = [jnp.where(lanes < -s, a, b) for a, b in pairs]
        made[m] = jnp.concatenate(parts, axis=1)
    return made


def shifted(tiles, m):
    r, s = m % GROUP, m // GROUP
    if s == 0:
        return tiles[r]
    lanes = lane_iota((8, 128))
    zero = jnp.zeros((8, 128), f32)
    turned = [pltpu.roll(tiles[r][:, 128 * k : 128 * k + 128], (-s) % 128, 1) for k in range(4)]
    if s > 0:
        pairs = zip(turned, turned[1:] + [zero])
        parts = [jnp.where(lanes < 128 - s, a, b) for a, b in pairs]
    else:
        pairs = zip([zero] + turned[:-1], turned)
        parts = [jnp.where(lanes < -s, a, b) for a, b in pairs]
    return jnp.concatenate(parts, axis=1)


SMEM = pl.BlockSpec(memory_space=pltpu.SMEM)
VMEM = pl.BlockSpec(memory_space=pltpu.VMEM)
BIG = (D, MAXLEN)
LOW = (128, MAXLEN)


def whole(shape):
    zeros = (0,) * len(shape)
    return pl.BlockSpec(shape, lambda u: zeros)


def per_utt(shape):
    zeros = (0,) * len(shape)
    return pl.BlockSpec((1,) + shape, lambda u: (u,) + zeros)


def o(shape, kind=bf16):
    return jax.ShapeDtypeStruct(shape, kind)


def params(flops=0, moved=0):
    cost = pl.CostEstimate(flops=flops, bytes_accessed=moved, transcendentals=0)
    return dict(compiler_params=pltpu.CompilerParams(vmem_limit_bytes=VMEM_BYTES), cost_estimate=cost)


def permutation():
    t = row_iota((384, 384))
    c = lane_iota((384, 384))
    return jnp.where(t == GROUP * (c % 128) + c // 128, 1.0, 0.0).astype(bf16)


def enter_body(x_ref, cot_ref, xp_ref, cp_ref, xf_ref, rs_ref, pm_ref):
    @pl.when(pl.program_id(0) == 0)
    def _():
        pm_ref[...] = permutation()

    x = permute_in(x_ref[0].astype(f32), pm_ref[...])
    xp_ref[0] = x.astype(bf16)
    xhat, rstd = norm(x)
    xf_ref[0] = xhat
    rs_ref[0] = jnp.broadcast_to(rstd, (8, MAXLEN))
    cp_ref[0] = permute_in(cot_ref[0].astype(f32), pm_ref[...]).astype(bf16)


def enter(x, cot):
    utts = x.shape[0]
    return pl.pallas_call(
        enter_body,
        grid=(utts,),
        in_specs=[per_utt(BIG)] * 2,
        out_specs=[per_utt(BIG)] * 3 + [per_utt((8, MAXLEN)), whole((384, 384))],
        out_shape=[o((utts,) + BIG), o((utts,) + BIG), o((utts,) + BIG, f32), o((utts, 8, MAXLEN), f32), o((384, 384))],
        name="enter",
        **params(2 * 10**9, 16 * 10**6),
    )(x, cot)


def leave_body(out_ref, grad_ref, back_ref, xf_ref, rs_ref, cols_ref, pm_ref, done_ref, gin_ref):
    done_ref[0] = permute_out(out_ref[0].astype(f32), pm_ref[...]).astype(bf16)
    back = norm_back(back_ref[0], xf_ref[0], rs_ref[0, 0:1, :], column(cols_ref, C_F1))
    gin_ref[0] = permute_out_wide(grad_ref[0] + back, pm_ref[...])


def leave(out, grad, back, xf, rs, cols, pm):
    utts = out.shape[0]
    return pl.pallas_call(
        leave_body,
        grid=(utts,),
        in_specs=[per_utt(BIG)] * 4 + [per_utt((8, MAXLEN)), whole(cols.shape), whole(pm.shape)],
        out_specs=[per_utt(BIG)] * 2,
        out_shape=[o((utts,) + BIG), o((utts,) + BIG, f32)],
        name="leave",
        **params(3 * 10**9, 20 * 10**6),
    )(out, grad, back, xf, rs, cols, pm)


def unpack(me_ref, g_ref, flat, tb):
    parts, part_rows = g_ref.shape[0], g_ref.shape[1]
    for d in range(parts):
        flat[part_rows * d : part_rows * (d + 1), :] = g_ref[place(me_ref[0] ^ d, parts)].astype(f32)
    tb[ROWS_HEAD:TAIL, :] = jnp.zeros((TAIL - ROWS_HEAD, 128), f32)
    for start, count, base in ((0, ROWS_HEAD, 0), (TAIL_AT, ROWS_TAIL, TAIL)):
        for r in range(16):
            at = start + D * r
            first_row, col = at // 128, at % 128
            many = (count - r + 15) // 16
            here = flat[pl.ds(first_row, many, stride=15), :]
            then = flat[pl.ds(first_row + 1, many, stride=15), :]
            lanes = lane_iota((many, 128))
            got = jnp.where(lanes >= col, here, then)
            if col:
                got = pltpu.roll(got, 128 - col, 1)
            tb[pl.ds(base + r, many, stride=16), :] = jnp.where(lanes < D, got, 0.0)


def with_row(block, row):
    tail = jnp.where(row_iota((8, 128)) == 0, row, 0.0)
    return jnp.concatenate([block, tail], axis=0)


def up_rows(tb, base):
    parts_t = []
    for q in range(4):
        block = tb[pl.ds(base + 2 + q, D, stride=4), :]
        parts_t.append(with_row(block, tb[base + 482 + q : base + 483 + q, :]).T[:D, :])
    return jnp.concatenate(parts_t, axis=0)


def up_across(up_t):
    return jnp.concatenate([up_t, jnp.zeros((32, 128), f32)], axis=0).T[:, :FF].astype(bf16)


def down_across(tb, base):
    bias = jnp.where(row_iota((32, 128)) == 0, tb[base + 966 : base + 967, :], 0.0)
    down = jnp.concatenate([tb[base + 486 : base + 966, :], bias], axis=0)
    return (0.5 * down).T.astype(bf16)


def point_rows(tb):
    parts_t = []
    for q in range(2):
        block = tb[pl.ds(CV + 2 + q, D, stride=2), :]
        parts_t.append(with_row(block, tb[CV + 242 + q : CV + 243 + q, :]).T[:D, :])
    return jnp.concatenate(parts_t, axis=0)


def fill_windows(tb, wt, wins):
    none = jnp.zeros((1, 128), f32)
    wins[...] = jnp.zeros_like(wins)
    for w, at, bias_at in ((0, AT + 2, AT + 122), (1, AT + 123, None), (2, AT + 243, AT + 363)):
        bias = none if bias_at is None else tb[bias_at : bias_at + 1, :]
        wt[...] = with_row(tb[at : at + D, :], bias).T
        for to, r, src, many in segments():
            start = WROWS * w + to - WIN[r]
            wins[r, start : start + many, :] = wt[src : src + many, :]


def fill_output(tb, wins):
    wins[:, 0:256, :] = jnp.zeros((GROUP, 256, 128), f32)
    for to, r, src, many in segments():
        start = to - WIN[r]
        wins[r, start : start + many, :] = tb[AT + 364 + src : AT + 364 + src + many, :]


def early_body(me_ref, g_ref, up_ref, dn_ref, wqkv_ref, wo_ref, pw_ref, cols_ref, base_ref, flat, tb, wt, wins, rows):
    unpack(me_ref, g_ref, flat, tb)
    up_ref[...] = (0.5 * up_rows(tb, F1)).astype(bf16)
    dn_ref[...] = down_across(tb, F1)
    pw_ref[...] = (0.5 * point_rows(tb)).astype(bf16)
    fill_windows(tb, wt, wins)
    for r in range(GROUP):
        wqkv_ref[r] = wins[r, : 3 * WROWS].astype(bf16)
    fill_output(tb, wins)
    for r in range(GROUP):
        wins[r, MARKS[r] : MARKS[r] + 1, :] = tb[AT + 484 : AT + 485, :]
        wo_ref[r] = wins[r, 0:256, :].T[:, :WROWS].astype(bf16)

    rows[...] = jnp.zeros_like(rows)
    listed = []
    for base in (F1, AT, CV, CV + 260, F2, FN):
        listed += [base, base + 1]
    listed += [CV + 259] + [CV + 244 + k for k in range(KERNEL)]
    for to, src in enumerate(listed):
        rows[to : to + 1, :] = tb[src : src + 1, :]
    cols_ref[...] = rows[...].T

    rel_rows = []
    lanes = lane_iota((1, 128))
    for h in range(HEADS):
        at = REL_AT + (2 * REL + 1) * h
        first_row, col = at // 128, at % 128
        pieces = []
        for k in range(2):
            here = flat[first_row + k : first_row + k + 1, :]
            got = jnp.where(lanes >= col, here, flat[first_row + k + 1 : first_row + k + 2, :])
            pieces.append(pltpu.roll(got, (128 - col) % 128, 1) if col else got)
        rel_rows.append(jnp.concatenate(pieces, axis=1))
    rel = jnp.concatenate(rel_rows + [jnp.zeros((4, 256), f32)], axis=0)
    rel = jnp.where(lane_iota((8, 256)) < 2 * REL + 1, rel, 0.0)
    base_ref[...] = dot(rel.astype(bf16), distance_select()) * LOG2E


def late_body(
    me_ref, g_ref, upp1_ref, dnp1_ref, up2_ref, upp2_ref, dn2_ref, dnp2_ref, pwp_ref, pr_ref, prp_ref, wqkvt_ref, wob_ref,
    flat, tb, wt, wins,
):
    unpack(me_ref, g_ref, flat, tb)
    upp1_ref[...] = up_across(up_rows(tb, F1))
    dnp1_ref[...] = (0.25 * tb[F1 + 486 : F1 + 966, :]).astype(bf16)
    up_t = up_rows(tb, F2)
    up2_ref[...] = (0.5 * up_t).astype(bf16)
    upp2_ref[...] = up_across(up_t)
    dn2_ref[...] = down_across(tb, F2)
    dnp2_ref[...] = (0.25 * tb[F2 + 486 : F2 + 966, :]).astype(bf16)
    pwp_ref[...] = jnp.concatenate([point_rows(tb), jnp.zeros((16, 128), f32)], axis=0).T[:, :240].astype(bf16)
    block = with_row(tb[CV + 262 : CV + 382, :], tb[CV + 382 : CV + 383, :])
    prp_ref[...] = (0.5 * block).astype(bf16)
    pr_ref[...] = block.T.astype(bf16)
    fill_windows(tb, wt, wins)
    for r in range(GROUP):
        wqkvt_ref[r] = wins[r].T[:, : 3 * WROWS].astype(bf16)
    fill_output(tb, wins)
    for r in range(GROUP):
        wob_ref[r] = wins[r, 0:WROWS, :].astype(bf16)


def distance_select():
    l = lane_iota((256, 2 * LG))
    gap = jnp.where(l < LG, -l, 2 * LG - l)
    index = jnp.clip(gap, -REL, REL) + REL
    return jnp.where(row_iota((256, 2 * LG)) == index, 1.0, 0.0).astype(bf16)


def diagonal_sum(values):
    wide = jnp.concatenate([values, jnp.zeros((LG, LG), f32)], axis=1)
    half = LG // 2
    while half:
        upper, lower = wide[:half], wide[half : 2 * half]
        if half % 128 == 0:
            lower = jnp.concatenate([lower[:, half:], lower[:, :half]], axis=1)
        else:
            lower = pltpu.roll(lower, 2 * LG - half, 1)
        wide = upper + lower
        half //= 2
    return wide


def prepare(me, gathered):
    total = gathered.shape[0] * gathered.shape[1]
    room = [
        pltpu.VMEM((total, 128), f32),
        pltpu.VMEM((TABLE, 128), f32),
        pltpu.VMEM((128, 128), f32),
        pltpu.VMEM((GROUP, 512, 128), f32),
    ]
    early = pl.pallas_call(
        early_body,
        in_specs=[SMEM, VMEM],
        out_shape=[o((FF, 128)), o((128, 512)), o((GROUP, 3 * WROWS, 128)), o((GROUP, 128, WROWS)), o((240, 128))]
        + [o((128, 128), f32), o((8, 2 * LG), f32)],
        scratch_shapes=room + [pltpu.VMEM((128, 128), f32)],
        name="prepare",
        **params(10**9, 2 * 10**6),
    )(me, gathered)
    late = pl.pallas_call(
        late_body,
        in_specs=[SMEM, VMEM],
        out_shape=[o((128, FF)), o((FF, 128)), o((FF, 128)), o((128, FF)), o((128, 512)), o((FF, 128))]
        + [o((128, 240)), o((128, 128)), o((128, 128)), o((GROUP, 128, 3 * WROWS)), o((GROUP, WROWS, 128))],
        scratch_shapes=room,
        name="late",
        **params(3 * 10**9, 10 * 10**6),
    )(me, gathered)
    return early, late


def column(cols, k):
    return cols[:D, k : k + 1]


def valid_keys(length):
    return row_iota((LG, 1)) * GROUP < length


def set_tail(hid):
    hid[FF:, :] = jnp.where(row_iota((512 - FF, hid.shape[1])) == 0, 1.0, 0.0).astype(bf16)


def conv_columns(cols, cb):
    for k in range(KERNEL + 1):
        cb[k] = jnp.broadcast_to(cols[:D, C_DWB + k : C_DWB + k + 1], (D, 128))


def wide(tile, copies=4):
    return jnp.concatenate([tile] * copies, axis=1)


def first_body(
    len_ref, xp_ref, xf_ref, cols_ref, up_ref, dn_ref, wqkv_ref, wo_ref, pw_ref, base_ref,
    lf_ref, xa_ref, nrm_ref, qkv_ref, prob_ref, att_ref, aa_ref, xc_ref, cn_ref, gat_ref, sig_ref, rgt_ref,
    rs_ref, dep_ref, st_ref,
    hid, one, cb, tab, run,
):
    u = pl.program_id(0)
    length = len_ref[u]

    @pl.when(u == 0)
    def _():
        set_tail(hid)
        run[...] = jnp.zeros_like(run)
        conv_columns(cols_ref, cb)
        for h in range(HEADS):
            spread = jnp.broadcast_to(base_ref[h : h + 1, :], (LG, 2 * LG))
            tab[h] = pltpu.roll(spread, 0, 1, stride=1, stride_axis=0)[:, :LG]

    cols = cols_ref

    def ffn_up(r, held):
        low = ext(xf_ref[0, :, span(r)] * column(cols, C_F1) + column(cols, C_F1 + 1))
        lf_ref[0, :, span(r)] = low
        return dot(up_ref[...], low)

    def ffn_down(r, half):
        hid[:FF, span(r)] = (half + half * jnp.tanh(half)).astype(bf16)
        return dot(dn_ref[...], hid[:, span(r)])[:D]

    def ffn_norm(r, branch):
        after = xp_ref[0, :, span(r)].astype(f32) + branch
        one[:, span(r)] = after
        xhat, rstd = norm(after)
        xa_ref[0, :, span(r)] = xhat
        rs_ref[0, 1:2, span(r)] = rstd
        low = ext(xhat * column(cols, C_AT) + column(cols, C_AT + 1))
        nrm_ref[0, 128 * r : 128 * r + 128, :] = low
        return dot(wqkv_ref[r], low)

    made = [None] * GROUP

    def ffn_keep(r, found):
        made[r] = found

    skewed(GROUP, (ffn_up, ffn_down, ffn_norm, ffn_keep))
    for w in range(3):
        joined = join_windows([made[r][WROWS * w : WROWS * w + WROWS] for r in range(GROUP)])
        qkv_ref[0, GP * w : GP * w + GP, :] = joined.astype(bf16)
    keys = valid_keys(length)

    def rows(w, h):
        return slice(GP * w + HP * h, GP * w + HP * h + HP)

    def score(h, held):
        return dot_tn(qkv_ref[0, rows(1, h), :], qkv_ref[0, rows(0, h), :])

    def soften(h, raw):
        scores = raw * (SCALE * LOG2E) + tab[h]
        scores = jnp.where(keys, scores, NEG_FILL * LOG2E)
        peak = jnp.max(scores, axis=0, keepdims=True)
        power = jnp.exp2(scores - peak)
        total = jnp.sum(power, axis=0, keepdims=True)
        prob_ref[0, h] = (power * (1.0 / total)).astype(bf16)

    def mix(h, held):
        mixed = dot(qkv_ref[0, rows(2, h), :], prob_ref[0, h])
        if h < GROUP:
            mixed = jnp.where(row_iota((HP, LG)) == HEAD, 1.0, mixed)
        att_ref[0, rows(0, h), :] = mixed.astype(bf16)

    skewed(HEADS, (score, soften, mix))

    def project(r, held):
        return dot(wo_ref[r], window(att_ref.at[0], r))[:D]

    def gate_in(r, mixed):
        after = one[:, span(r)] + mixed
        aa_ref[0, :, span(r)] = after
        xhat, rstd = norm(after)
        xc_ref[0, :, span(r)] = xhat
        rs_ref[0, 2:3, span(r)] = rstd
        low = ext(xhat * column(cols, C_CV) + column(cols, C_CV + 1))
        cn_ref[0, :, span(r)] = low
        return dot(pw_ref[...], low)

    def gate_out(r, pre):
        mask = plane_mask(r, length)
        sig = (0.5 + 0.5 * jnp.tanh(pre[D:])) * mask
        gated = (pre[:D] + pre[:D]) * sig
        gat_ref[0, :, span(r)] = gated
        sig_ref[0, :, span(r)] = sig
        rgt_ref[0, :, span(r)] = gated * (1.0 - sig)

    skewed(GROUP, (project, gate_in, gate_out))

    def conv(f, carry):
        at = slice(8 * f, 8 * f + 8)
        tiles = [gat_ref[0, at, span(r)] for r in range(GROUP)]
        totals = [wide(cb[0, at, :])] * GROUP
        for m in range(-HALF, HALF + GROUP):
            here = shifted(tiles, m)
            for r in range(GROUP):
                k = m + HALF - r
                if 0 <= k < KERNEL:
                    totals[r] = totals[r] + wide(cb[1 + k, at, :]) * here
        for r in range(GROUP):
            dep_ref[0, at, span(r)] = totals[r]
        return carry

    for f in range(D // 8):
        conv(f, 0)

    count = length.astype(f32)
    mask = jnp.concatenate([plane_mask(r, length) for r in range(GROUP)], axis=1)
    dep = dep_ref[0]
    mean = jnp.sum(dep * mask, axis=1, keepdims=True) / count
    gap = (dep - mean) * mask
    spread = jnp.sum(gap * gap, axis=1, keepdims=True)
    old_mean, old_spread, old_count = run[0], run[1], run[2]
    new_count = old_count + count
    step = mean - old_mean
    new_mean = old_mean + step * (count / new_count)
    new_spread = old_spread + spread + step * step * (old_count * count / new_count)
    run[0] = new_mean
    run[1] = new_spread
    run[2] = new_count

    @pl.when(u == pl.num_programs(0) - 1)
    def _():
        lanes = lane_iota((D, 128))
        picked = jnp.where(lanes == 0, run[0], jnp.where(lanes == 1, run[1], jnp.where(lanes == 2, run[2], 0.0)))
        line = pad8(picked).T[0:8]
        for d in range(st_ref.shape[0]):
            st_ref[d] = line


def first(devices, lengths, xp, xf, weights):
    utts = xp.shape[0]
    per = [
        (LOW, bf16),
        (BIG, f32),
        ((GP, LG), bf16),
        ((3 * GP, LG), bf16),
        ((HEADS, LG, LG), bf16),
        ((GP, LG), bf16),
        (BIG, f32),
        (BIG, f32),
        (LOW, bf16),
        (BIG, f32),
        (BIG, f32),
        (BIG, f32),
        ((8, MAXLEN), f32),
        (BIG, f32),
    ]
    line = (devices, 8, 128)
    return pl.pallas_call(
        first_body,
        grid=(utts,),
        in_specs=[SMEM, per_utt(BIG), per_utt(BIG)] + [whole(w.shape) for w in weights],
        out_specs=[per_utt(s) for s, k in per] + [whole(line)],
        out_shape=[o((utts,) + s, k) for s, k in per] + [o(line, f32)],
        scratch_shapes=[
            pltpu.VMEM((512, MAXLEN), bf16),
            pltpu.VMEM(BIG, f32),
            pltpu.VMEM((KERNEL + 1, D, 128), f32),
            pltpu.VMEM((HEADS, LG, LG), f32),
            pltpu.VMEM((3, D, 128), f32),
        ],
        name="first",
        **params(10 * 10**9, 60 * 10**6),
    )(lengths, xp, xf, *weights)


def second_body(
    len_ref, stats_ref, cot_ref, aa_ref, dep_ref, cols_ref, up_ref, upp_ref, dn_ref, dnp_ref, pr_ref, prp_ref,
    out_ref, bgd_ref, gc_ref, sums_ref, stc_ref, gdn_ref, gup_ref, gpr_ref, vec_ref,
    hid, acc,
):
    u = pl.program_id(0)
    length = len_ref[u]
    cols = cols_ref

    @pl.when(u == 0)
    def _():
        set_tail(hid)
        parts = stats_ref.shape[0]
        count = jnp.zeros((1, 128), f32)
        total = jnp.zeros((1, 128), f32)
        for d in range(parts):
            many = stats_ref[d, 2:3, :]
            count = count + many
            total = total + many * stats_ref[d, 0:1, :]
        here = lane_iota((1, 128)) < D
        count = jnp.where(here, count, 1.0)
        mean = total / count
        spread = jnp.zeros((1, 128), f32)
        for d in range(parts):
            gap = stats_ref[d, 0:1, :] - mean
            spread = spread + stats_ref[d, 1:2, :] + stats_ref[d, 2:3, :] * gap * gap
        scale = lax.rsqrt(spread / count + EPS_NORM)
        at = row_iota((128, 128))
        table = jnp.where(at == 0, mean, jnp.where(at == 1, scale, jnp.where(at == 2, 1.0 / count, 0.0)))
        stc_ref[...] = table.T
        gdn_ref[...] = jnp.zeros_like(gdn_ref)
        gup_ref[...] = jnp.zeros_like(gup_ref)
        gpr_ref[...] = jnp.zeros_like(gpr_ref)
        vec_ref[...] = jnp.zeros_like(vec_ref)
        acc[...] = jnp.zeros_like(acc)

    half_gain = 0.5 * column(cols, C_BN)
    half_bias = 0.5 * column(cols, C_BN + 1)

    def enter(r, held):
        normal = (dep_ref[0, :, span(r)] - stc_ref[:D, 0:1]) * stc_ref[:D, 1:2]
        z = normal * half_gain + half_bias
        t = jnp.tanh(z)
        act = z + z * t
        act_low = ext(act)
        slope = (1.0 + t) * (1.0 + z * (1.0 - t))
        return act_low, normal, slope, dot(pr_ref[...], act_low)[:D]

    def ffn_up(r, held):
        act_low, normal, slope, moved = held
        after_conv = aa_ref[0, :, span(r)] + moved
        xhat, rstd = norm(after_conv)
        low = ext(xhat * column(cols, C_F2) + column(cols, C_F2 + 1))
        return act_low, normal, slope, after_conv, xhat, rstd, low, dot(up_ref[...], low)

    def ffn_down(r, held):
        act_low, normal, slope, after_conv, xhat, rstd, low, half = held
        t = jnp.tanh(half)
        hid[:FF, span(r)] = (half + half * t).astype(bf16)
        bend = (1.0 + t) * (1.0 + half * (1.0 - t))
        return act_low, normal, slope, after_conv, xhat, rstd, low, bend, dot(dn_ref[...], hid[:, span(r)])[:D]

    def finish(r, held):
        act_low, normal, slope, after_conv, xhat, rstd, low, bend, branch = held
        mask = plane_mask(r, length)
        xhat_f, rstd_f = norm(after_conv + branch)
        made = (xhat_f * column(cols, C_FN) + column(cols, C_FN + 1)) * mask
        out_ref[0, :, span(r)] = made.astype(bf16)
        up_grad = cot_ref[0, :, span(r)].astype(f32) * mask
        vec_ref[2] += fold(up_grad * xhat_f)
        vec_ref[3] += fold(up_grad)
        grad_two = norm_back(up_grad, xhat_f, rstd_f, column(cols, C_FN))
        branch = pad8(grad_two).astype(bf16)
        gdn_ref[...] += dot_nt(hid[:, span(r)], branch)
        return act_low, normal, slope, xhat, rstd, low, bend, grad_two, dot(dnp_ref[...], branch)

    def ffn_back(r, held):
        act_low, normal, slope, xhat, rstd, low, bend, grad_two, back = held
        pre_low = (bend * back).astype(bf16)
        gup_ref[...] += dot_nt(pre_low, low)
        return act_low, normal, slope, xhat, rstd, grad_two, dot(upp_ref[...], pre_low)[:D]

    def leave(r, held):
        act_low, normal, slope, xhat, rstd, grad_two, back = held
        vec_ref[0] += fold(back * xhat)
        vec_ref[1] += fold(back)
        grad_conv = grad_two + norm_back(back, xhat, rstd, column(cols, C_F2))
        gc_ref[0, :, span(r)] = grad_conv
        project = pad8(grad_conv).astype(bf16)
        gpr_ref[...] += dot_nt(act_low, project)
        return normal, slope, dot(prp_ref[...], project)[:D]

    def last(r, held):
        normal, slope, back = held
        batch = slope * back
        bgd_ref[0, :, span(r)] = batch
        acc[0] += fold(batch * normal)
        acc[1] += fold(batch)

    skewed(GROUP, (enter, ffn_up, ffn_down, finish, ffn_back, leave, last))

    @pl.when(u == pl.num_programs(0) - 1)
    def _():
        lanes = lane_iota((D, 128))
        gain = jnp.sum(acc[0], axis=1, keepdims=True)
        shift = jnp.sum(acc[1], axis=1, keepdims=True)
        line = pad8(jnp.where(lanes == 0, gain, jnp.where(lanes == 1, shift, 0.0))).T[0:8]
        for d in range(sums_ref.shape[0]):
            sums_ref[d] = line


def second(lengths, stats, cot, aa, dep, weights):
    utts = cot.shape[0]
    big = (D, MAXLEN)
    outs = [
        (per_utt(big), (utts,) + big, bf16),
        (per_utt(big), (utts,) + big, f32),
        (per_utt(big), (utts,) + big, f32),
    ]
    for s in (stats.shape, (128, 128), (512, 128), (FF, 128), (128, 128), (4, D, 128)):
        outs.append((whole(s), s, f32))
    return pl.pallas_call(
        second_body,
        grid=(utts,),
        in_specs=[SMEM, whole(stats.shape)] + [per_utt(big)] * 3 + [whole(w.shape) for w in weights],
        out_specs=[o[0] for o in outs],
        out_shape=[jax.ShapeDtypeStruct(o[1], o[2]) for o in outs],
        scratch_shapes=[
            pltpu.VMEM((512, MAXLEN), bf16),
            pltpu.VMEM((2, D, 128), f32),
        ],
        name="second",
        **params(15000000000, 30000000),
    )(lengths, stats, cot, aa, dep, *weights)


def third_body(
    len_ref, sums_ref, stc_ref, bgd_ref, gc_ref, dep_ref, xf_ref, lf_ref, xa_ref, nrm_ref, qkv_ref, prob_ref, att_ref, xc_ref,
    cn_ref, gat_ref, sig_ref, rgt_ref, rs_ref,
    cols_ref, up_ref, upp_ref, dnp_ref, wqkv_t_ref, wob_ref, pwp_ref,
    grad_ref, back_ref, gdn_ref, gup_ref, gpw_ref, gqkv_ref, go_ref, rel_ref, vec_ref,
    hid, dgs, olg, agr, back_s, gg, relacc, cb, tot,
):
    u = pl.program_id(0)
    length = len_ref[u]
    cols = cols_ref

    @pl.when(u == 0)
    def _():
        set_tail(hid)
        conv_columns(cols_ref, cb)
        parts = sums_ref.shape[0]
        total = sums_ref[0]
        for d in range(1, parts):
            total = total + sums_ref[d]
        tot[...] = jnp.concatenate([total, jnp.zeros((120, 128), f32)], axis=0).T
        for ref in (gdn_ref, gup_ref, gpw_ref, gqkv_ref, go_ref, vec_ref, relacc):
            ref[...] = jnp.zeros_like(ref)

    scale = stc_ref[:D, 1:2]
    lead = column(cols, C_BN) * scale
    share = lead * stc_ref[:D, 2:3]
    shift_part = share * tot[:D, 1:2]
    gain_part = share * tot[:D, 0:1] * scale
    for r in range(GROUP):
        normal = dep_ref[0, :, span(r)] - stc_ref[:D, 0:1]
        mask = plane_mask(r, length)
        dgs[:, span(r)] = bgd_ref[0, :, span(r)] * lead - mask * (shift_part + normal * gain_part)

    def conv(f, carry):
        at = slice(8 * f, 8 * f + 8)
        tiles = [dgs[at, span(r)] for r in range(GROUP)]
        gated = [gat_ref[0, at, span(r)] for r in range(GROUP)]
        totals = [None] * GROUP
        taps = [None] * KERNEL
        for m in range(-HALF, HALF + GROUP):
            here = shifted(tiles, m)
            for r in range(GROUP):
                k = r + HALF - m
                if 0 <= k < KERNEL:
                    term = wide(cb[1 + k, at, :]) * here
                    totals[r] = term if totals[r] is None else totals[r] + term
                    part = fold(gated[r] * here)
                    taps[k] = part if taps[k] is None else taps[k] + part
        vec_ref[6, at, :] += fold(tiles[0] + tiles[1] + tiles[2])
        for k in range(KERNEL):
            vec_ref[7 + k, at, :] += taps[k]
        for r in range(GROUP):
            gg[at, span(r)] = totals[r]
        return carry

    for f in range(D // 8):
        conv(f, 0)

    def gate(r, held):
        grad = gg[:, span(r)]
        left = grad * sig_ref[0, :, span(r)]
        right = grad * rgt_ref[0, :, span(r)]
        pre_low = jnp.concatenate([left, right], axis=0).astype(bf16)
        gpw_ref[...] += dot_nt(pre_low, cn_ref[0, :, span(r)])
        return dot(pwp_ref[...], pre_low)[:D]

    def residual(r, back):
        xhat = xc_ref[0, :, span(r)]
        vec_ref[0] += fold(back * xhat)
        vec_ref[1] += fold(back)
        grad = gc_ref[0, :, span(r)] + norm_back(back, xhat, rs_ref[0, 2:3, span(r)], column(cols, C_CV))
        dgs[:, span(r)] = grad
        low = pad8(grad).astype(bf16)
        olg[128 * r : 128 * r + 128, :] = low
        return dot(wob_ref[r], low)

    made = [None] * GROUP

    def keep(r, found):
        go_ref[r] += dot_nt(window(att_ref.at[0], r), olg[128 * r : 128 * r + 128, :])
        made[r] = found

    skewed(GROUP, (gate, residual, keep))
    agr[...] = join_windows(made).astype(bf16)

    def rows(w, h):
        return slice(GP * w + HP * h, GP * w + HP * h + HP)

    def enter(h, held):
        grad = agr[rows(0, h), :]
        back_s[rows(2, h), :] = dot_nt(grad, prob_ref[0, h]).astype(bf16)
        return dot_tn(qkv_ref[0, rows(2, h), :], grad)

    def soften(h, prob_grad):
        probs = prob_ref[0, h].astype(f32)
        inner = jnp.sum(probs * prob_grad, axis=0, keepdims=True)
        score = probs * (prob_grad - inner)
        relacc[h] += score
        return score.astype(bf16)

    def turn(h, low):
        back_s[rows(0, h), :] = (dot(qkv_ref[0, rows(1, h), :], low) * SCALE).astype(bf16)
        back_s[rows(1, h), :] = (dot_nt(qkv_ref[0, rows(0, h), :], low) * SCALE).astype(bf16)

    skewed(HEADS, (enter, soften, turn))

    def project(r, held):
        stack = jnp.concatenate([window(back_s, r, GP * w) for w in range(3)], axis=0)
        gqkv_ref[r] += dot_nt(stack, nrm_ref[0, 128 * r : 128 * r + 128, :])
        return dot(wqkv_t_ref[r], stack)[:D], dot(up_ref[...], lf_ref[0, :, span(r)])

    def ffn_in(r, held):
        back, half = held
        xhat = xa_ref[0, :, span(r)]
        vec_ref[2] += fold(back * xhat)
        vec_ref[3] += fold(back)
        grad = dgs[:, span(r)] + norm_back(back, xhat, rs_ref[0, 1:2, span(r)], column(cols, C_AT))
        grad_ref[0, :, span(r)] = grad
        low = pad8(grad).astype(bf16)
        return low, half, dot(dnp_ref[...], low)

    def ffn_mid(r, held):
        branch, half, back = held
        t = jnp.tanh(half)
        hid[:FF, span(r)] = (half + half * t).astype(bf16)
        pre_low = ((1.0 + t) * (1.0 + half * (1.0 - t)) * back).astype(bf16)
        gdn_ref[...] += dot_nt(hid[:, span(r)], branch)
        gup_ref[...] += dot_nt(pre_low, lf_ref[0, :, span(r)])
        return dot(upp_ref[...], pre_low)[:D]

    def ffn_out(r, back):
        back_ref[0, :, span(r)] = back
        vec_ref[4] += fold(back * xf_ref[0, :, span(r)])
        vec_ref[5] += fold(back)

    skewed(GROUP, (project, ffn_in, ffn_mid, ffn_out))

    @pl.when(u == pl.num_programs(0) - 1)
    def _():
        found = []
        for h in range(HEADS):
            found.append(diagonal_sum(relacc[h]))
        stacked = jnp.concatenate(found + [jnp.zeros((4, 2 * LG), f32)], axis=0)
        high = stacked.astype(bf16)
        rest = stacked - high.astype(f32)
        mid = rest.astype(bf16)
        rest = rest - mid.astype(f32)
        select = distance_select()
        rel_ref[...] = dot_nt(high, select) + dot_nt(mid, select) + dot_nt(rest.astype(bf16), select)


def third(lengths, sums, stc, saved, weights):
    utts = saved[0].shape[0]
    big = (D, MAXLEN)
    outs = [(per_utt(big), (utts,) + big)] * 2
    for s in ((512, 128), (FF, 128), (240, 128), (GROUP, 3 * WROWS, 128), (GROUP, WROWS, 128), (8, 256), (22, D, 128)):
        outs.append((whole(s), s))
    return pl.pallas_call(
        third_body,
        grid=(utts,),
        in_specs=[SMEM, whole(sums.shape), whole(stc.shape)]
        + [per_utt(s.shape[1:]) for s in saved]
        + [whole(w.shape) for w in weights],
        out_specs=[o[0] for o in outs],
        out_shape=[jax.ShapeDtypeStruct(o[1], f32) for o in outs],
        scratch_shapes=[
            pltpu.VMEM((512, MAXLEN), bf16),
            pltpu.VMEM(big, f32),
            pltpu.VMEM((GP, LG), bf16),
            pltpu.VMEM((GP, LG), bf16),
            pltpu.VMEM((3 * GP, LG), bf16),
            pltpu.VMEM(big, f32),
            pltpu.VMEM((HEADS, LG, LG), f32),
            pltpu.VMEM((KERNEL + 1, D, 128), f32),
            pltpu.VMEM((128, 128), f32),
        ],
        name="third",
        **params(20000000000, 80000000),
    )(lengths, sums, stc, *saved, *weights)


def clean(block):
    return jnp.where(lane_iota(block.shape) < D, block, 0.0)


def set_rows(tb, wt, ref, at):
    lanes = lane_iota((D, 128))
    table = jnp.zeros((D, 128), f32)
    for k in range(len(at)):
        table = jnp.where(lanes == k, jnp.sum(ref[k], axis=1, keepdims=True), table)
    wt[...] = pad8(table).T
    for k, to in enumerate(at):
        tb[to : to + 1, :] = wt[k : k + 1, :]


def set_ffn(tb, base, dn_ref, up_ref):
    tb[base + 486 : base + 967, :] = 0.5 * clean(dn_ref[0 : FF + 1, :])
    for q in range(4):
        block = pad8(up_ref[D * q : D * q + D, :]).T
        tb[pl.ds(base + 2 + q, D, stride=4), :] = block[:D]
        tb[base + 482 + q : base + 483 + q, :] = block[D : D + 1]


def flatten(tb, base, flat, at_row, y_count, offset):
    for k in range(15):
        at = 128 * k + offset
        first_row, col = at // D, at % D
        many = (y_count - k + 14) // 15
        here = lane_iota((many, 128))
        got = tb[pl.ds(base + first_row, many, stride=16), :]
        if col:
            got = pltpu.roll(got, 128 - col, 1)
        then = pltpu.roll(tb[pl.ds(base + first_row + 1, many, stride=16), :], D - col, 1)
        got = jnp.where(here < D - col, got, then)
        if 2 * D - col < 128:
            then = pltpu.roll(tb[pl.ds(base + first_row + 2, many, stride=16), :], 2 * D - col, 1)
            got = jnp.where(here < 2 * D - col, got, then)
        flat[pl.ds(at_row + k, many, stride=15), :] = got


SPLIT = F2 - TAIL
ROWS_LAST = ROWS_TAIL - SPLIT
LAST_AT = TAIL_AT + D * SPLIT
LAST_Y = LAST_AT // 128
LAST_COUNT = (LIVE - 1) // 128 - LAST_Y + 1


def ahead_body(dn_ref, up_ref, vec_ref, out_ref, tb, wt):
    tb[0:8, :] = jnp.zeros((8, 128), f32)
    tb[8 + ROWS_LAST :, :] = jnp.zeros((tb.shape[0] - 8 - ROWS_LAST, 128), f32)
    set_rows(tb, wt, vec_ref, (8, 9, 8 + FN - F2, 9 + FN - F2))
    set_ffn(tb, 8, dn_ref, up_ref)
    flatten(tb, 7, out_ref, 0, LAST_COUNT, D + 128 * LAST_Y - LAST_AT)


def pack_ahead(dn, up, vec):
    return pl.pallas_call(
        ahead_body,
        out_shape=o((LAST_COUNT, 128), f32),
        scratch_shapes=[pltpu.VMEM((ROWS_LAST + 24, 128), f32), pltpu.VMEM((128, 128), f32)],
        name="ahead",
        **params(2 * 10**9, 8 * 10**6),
    )(dn, up, vec)


def pack_body(
    me_ref, last_ref, dn1_ref, up1_ref, pr_ref, pw_ref, qkv_ref, o_ref, rel_ref, vec_ref, sums_ref,
    keep_ref, send_ref, tb, flat, stage, wt,
):
    tb[ROWS_HEAD:TAIL, :] = jnp.zeros((TAIL - ROWS_HEAD, 128), f32)
    tb[F2:, :] = jnp.zeros((tb.shape[0] - F2, 128), f32)
    set_rows(
        tb, wt, vec_ref, (CV, CV + 1, AT, AT + 1, F1, F1 + 1, CV + 259) + tuple(CV + 244 + k for k in range(KERNEL))
    )
    tb[CV + 260 : CV + 262, :] = sums_ref[0, 0:2, :]
    set_ffn(tb, F1, dn1_ref, up1_ref)
    for q in range(2):
        block = pad8(pw_ref[D * q : D * q + D, :]).T
        tb[pl.ds(CV + 2 + q, D, stride=2), :] = block[:D]
        tb[CV + 242 + q : CV + 243 + q, :] = block[D : D + 1]
    tb[CV + 262 : CV + 383, :] = clean(pr_ref[0 : D + 1, :])

    def gathered(ref, base):
        wt[...] = jnp.zeros_like(wt)
        for to, r, src, many in segments():
            start = base + to - WIN[r]
            wt[src : src + many, :] += ref[r, start : start + many, :]
        return wt[...]

    for w, at, bias_at in ((0, AT + 2, AT + 122), (1, AT + 123, None), (2, AT + 243, AT + 363)):
        block = gathered(qkv_ref, WROWS * w).T
        tb[at : at + D, :] = block[:D]
        if bias_at is not None:
            tb[bias_at : bias_at + 1, :] = block[D : D + 1]
    tb[AT + 364 : AT + 484, :] = clean(gathered(o_ref, 0)[:D])
    bias = sum(o_ref[r, MARKS[r] : MARKS[r] + 1, :] for r in range(GROUP))
    tb[AT + 484 : AT + 485, :] = clean(bias)

    tail_y = TAIL_AT // 128
    flat[LAST_Y + LAST_COUNT :, :] = jnp.zeros((flat.shape[0] - LAST_Y - LAST_COUNT, 128), f32)
    flat[REL_AT // 128 + 1 : tail_y, :] = jnp.zeros((tail_y - REL_AT // 128 - 1, 128), f32)
    flatten(tb, 0, flat, 0, REL_AT // 128 + 1, 0)
    flatten(tb, TAIL - 1, flat, tail_y, LAST_Y - tail_y + 1, 128 * tail_y - TAIL_AT + D)
    flat[LAST_Y : LAST_Y + 1, :] += last_ref[0:1, :]
    flat[LAST_Y + 1 : LAST_Y + LAST_COUNT, :] = last_ref[1:, :]
    here = lane_iota((1, 128))
    width = 2 * REL + 1
    for h in range(HEADS):
        at = REL_AT + width * h
        for y in range(at // 128, (at + width - 1) // 128 + 1):
            lo, hi = max(at - 128 * y, 0), min(at + width - 128 * y, 128)
            shift = (at - 128 * y) % 256
            turned = rel_ref[h : h + 1, :]
            if shift:
                turned = pltpu.roll(turned, shift, 1)
            flat[y : y + 1, :] += jnp.where((here >= lo) & (here < hi), turned[:, :128], 0.0)
    parts, rows = 2 * keep_ref.shape[0], keep_ref.shape[1]
    for d in range(parts):
        stage[d] = flat[rows * d : rows * (d + 1), :]
    for offset in range(0, parts, 2):
        keep_ref[place(offset, parts)] = stage[me_ref[0] ^ offset]
        send_ref[place(offset, parts)] = stage[me_ref[0] ^ (offset + 1)]


def pack(parts, rows, me, grads):
    half = o((parts // 2, rows, 128), f32)
    return pl.pallas_call(
        pack_body,
        in_specs=[SMEM] + [VMEM] * len(grads),
        out_shape=[half, half],
        scratch_shapes=[
            pltpu.VMEM((F2 + 24, 128), f32),
            pltpu.VMEM((parts * rows, 128), f32),
            pltpu.VMEM((parts, rows, 128), f32),
            pltpu.VMEM((128, 128), f32),
        ],
        name="pack",
        **params(10**9, 5 * 10**6),
    )(me, *grads)


def update_tables(total_len):
    rates = np.zeros(total_len, np.float32)
    decays = np.zeros(total_len, np.float32)
    vector, gain, ffn = (D, 0.1, 0.0), (D, 0.3, 0.0), lambda n, fan: (n, fan**-0.5, 0.01)
    block = [gain, vector, ffn(D * FF, D), (FF, 0.1, 0.0), ffn(FF * D, FF), vector]
    square = ffn(D * D, D)
    pieces = block + [gain, vector, square, vector, square, square, vector, ffn(D * D, 6.0 * D / MAXLEN), vector]
    pieces += [(HEADS * (2 * REL + 1), 0.5, 0.0)]
    pieces += [gain, vector, ffn(2 * D * D, D), (2 * D, 0.1, 0.0), ffn(KERNEL * D, KERNEL), vector, gain, vector]
    pieces += [square, vector] + block + [gain, vector]
    offset = 0
    for entries, rate, decay in pieces:
        rates[offset : offset + entries] = rate
        decays[offset : offset + entries] = decay
        offset += entries
    return rates, decays


def digits(devices):
    found, stride = [], 1
    while stride < devices:
        size = min(2 if stride == 1 else 4, devices // stride)
        found.append((stride, size))
        stride *= size
    return found


def place(offset, devices):
    at, weight = 0, devices
    for stride, size in digits(devices):
        weight //= size
        at = at + ((offset // stride) % size) * weight
    return at


def partner(values, offset, devices):
    return lax.ppermute(values, "dp", [(i, i ^ offset) for i in range(devices)])


def gather(values, devices, beside):
    held = values[None]
    for stride, size in reversed(digits(devices)):
        parts = [held] + [partner(held, stride * j, devices) for j in range(1, size)]
        if beside is not None:
            parts, made = lax.optimization_barrier((parts, beside))
            beside = None
        held = jnp.concatenate(parts, axis=0)
    return held, made


def scatter_sum(keep, send, devices):
    total = keep + partner(send, 1, devices)
    for stride, size in digits(devices)[1:]:
        parts = total.reshape((size, total.shape[0] // size) + total.shape[1:])
        total = parts[0]
        for j in range(1, size):
            total = total + partner(parts[j], stride * j, devices)
    return total


def local(frames, lengths, cotangent, master, moment_one, moment_two, average):
    shard_len = master.shape[0]
    devices = lax.axis_size("dp")
    rows = shard_len // 128
    me = lax.axis_index("dp").astype(jnp.int32).reshape(1)
    entered = enter(jnp.transpose(frames, (0, 2, 1)), jnp.transpose(cotangent, (0, 2, 1)))
    gathered, (xp, cp, xf, rs_in, pm) = gather(master.astype(bf16).reshape(rows, 128), devices, entered)
    early, late = prepare(me, gathered)
    up1, dn1, wqkv, wo, pw, cols, base = early
    upp1, dnp1, up2, upp2, dn2, dnp2, pwp, pr, prp, wqkvt, wob = late
    lf, xa, nrm, qkv, prob, att, aa, xc, cn, gat, sig, rgt, rs, dep, st = first(
        devices, lengths, xp, xf, (cols, up1, dn1, wqkv, wo, pw, base)
    )
    stats = lax.all_to_all(st, "dp", 0, 0)
    out, bgd, gc, sums, stc, gdn2, gup2, gpr, vec2 = second(
        lengths, stats, cp, aa, dep, (cols, up2, upp2, dn2, dnp2, pr, prp)
    )
    all_sums = lax.all_to_all(sums, "dp", 0, 0)
    last = pack_ahead(gdn2, gup2, vec2)
    grad, back, gdn1, gup1, gpw, gqkv, go, rel, vec3 = third(
        lengths, all_sums, stc,
        (bgd, gc, dep, xf, lf, xa, nrm, qkv, prob, att, xc, cn, gat, sig, rgt, rs),
        (cols, up1, upp1, dnp1, wqkvt, wob, pwp),
    )
    keep, send = pack(devices, rows, me, (last, gdn1, gup1, gpr, gpw, gqkv, go, rel, vec3, sums))
    out, gin = leave(out, grad, back, xf, rs_in, cols, pm)
    reduced = scatter_sum(keep, send, devices).reshape(shard_len)
    rates_np, decays_np = update_tables(shard_len * devices)
    start_at = lax.axis_index("dp") * shard_len
    rates = lax.dynamic_slice_in_dim(jnp.asarray(rates_np), start_at, shard_len)
    decays = lax.dynamic_slice_in_dim(jnp.asarray(decays_np), start_at, shard_len)
    correction = 1.0 - 0.5**STEP
    new_one = 0.5 * moment_one + 0.5 * reduced
    new_two = 0.5 * moment_two + 0.5 * reduced * reduced
    direction = new_one / correction / (jnp.sqrt(new_two / correction) + EPS_ADAM)
    new_master = master - rates * (direction + decays * master)
    new_average = 0.75 * average + 0.25 * new_master
    return (
        jnp.transpose(out, (0, 2, 1)),
        jnp.transpose(gin, (0, 2, 1)),
        reduced,
        new_master,
        new_one,
        new_two,
        new_average,
    )


def solution(mesh):
    three = P("dp", None, None)
    one = P("dp")
    in_specs = (three, one, three, one, one, one, one)
    out_specs = (three, three, one, one, one, one, one)
    return jax.shard_map(local, mesh=mesh, in_specs=in_specs, out_specs=out_specs, check_vma=False)
```

```python
import math

import jax
import jax.numpy as jnp
import numpy as np
from jax import lax
from jax.experimental import pallas as pl
from jax.experimental.pallas import tpu as pltpu
from jax.sharding import PartitionSpec as P

D = 120
HEADS = 4
FF = 480
KERNEL = 15
GROUP = 3
REL = 127
STEP = 5
MAXLEN = 1536
LG = 512
HEAD = 90
HP = 96
GP = HEADS * HP
HALF = KERNEL // 2
WIN = (0, 112, 240)
WROWS = 144
MARKS = tuple(HP * r + HEAD - WIN[r] for r in range(GROUP))

EPS_NORM = 1e-05
EPS_ADAM = 1e-08
NEG_FILL = -1000000000.0
LOG2E = math.log2(math.e)
SCALE = HEAD ** (-0.5)

f32 = jnp.float32
bf16 = jnp.bfloat16
VMEM_BYTES = 58 * 2**20

REL_AT = 174240
TAIL_AT = 175260
TAIL = 1456
ROWS_HEAD = 1452
ROWS_TAIL = 1352
TABLE = 2824
F1 = 0
AT = 967
CV = TAIL
F2 = TAIL + 383
FN = TAIL + 1350
LIVE = 337500

C_F1, C_AT, C_CV, C_BN, C_F2, C_FN, C_DWB, C_DW = 0, 2, 4, 6, 8, 10, 12, 13


def dot(a, b):
    return lax.dot_general(a, b, (((1,), (0,)), ((), ())), preferred_element_type=f32)


def dot_nt(a, b):
    return lax.dot_general(a, b, (((1,), (1,)), ((), ())), preferred_element_type=f32)


def dot_tn(a, b):
    return lax.dot_general(a, b, (((0,), (0,)), ((), ())), preferred_element_type=f32)


def lane_iota(shape):
    return lax.broadcasted_iota(jnp.int32, shape, len(shape) - 1)


def row_iota(shape):
    return lax.broadcasted_iota(jnp.int32, shape, 0)


def segments():
    found = []
    for h in range(HEADS):
        for r in range(GROUP):
            lo, hi = max(HEAD * h, D * r), min(HEAD * h + HEAD, D * r + D)
            if lo < hi:
                found.append((HP * h + lo - HEAD * h, r, lo - D * r, hi - lo))
    return found


def pad8(values):
    return jnp.concatenate([values, jnp.zeros((8, values.shape[1]), f32)], axis=0)


def ext(values):
    width = values.shape[1]
    ones = jnp.where(row_iota((8, width)) == 0, 1.0, 0.0).astype(f32)
    return jnp.concatenate([values, ones], axis=0).astype(bf16)


def norm(values):
    mean = jnp.sum(values, axis=0, keepdims=True) * (1.0 / D)
    centre = values - mean
    var = jnp.sum(centre * centre, axis=0, keepdims=True) * (1.0 / D)
    rstd = lax.rsqrt(var + EPS_NORM)
    return centre * rstd, rstd


def norm_back(upstream, xhat, rstd, gain):
    scaled = upstream * gain
    mean_one = jnp.sum(scaled, axis=0, keepdims=True) * (1.0 / D)
    mean_two = jnp.sum(scaled * xhat, axis=0, keepdims=True) * (1.0 / D)
    return rstd * (scaled - mean_one - xhat * mean_two)


def fold(values):
    total = values[:, 0:128]
    for at in range(128, values.shape[1], 128):
        total = total + values[:, at : at + 128]
    return total


def permute_in(values, pm):
    low = pad8(values).astype(bf16)
    stack = jnp.concatenate([low[:, 384 * b : 384 * b + 384] for b in range(4)], axis=0)
    out = dot(stack, pm)
    tiles = [out[128 * b : 128 * b + D, 128 * r : 128 * r + 128] for r in range(3) for b in range(4)]
    return jnp.concatenate(tiles, axis=1)


def stack_out(values):
    low = pad8(values).astype(bf16)
    blocks = []
    for b in range(4):
        blocks.append(
            jnp.concatenate([low[:, 512 * r + 128 * b : 512 * r + 128 * b + 128] for r in range(3)], axis=1)
        )
    return jnp.concatenate(blocks, axis=0)


def unstack_out(out):
    return jnp.concatenate([out[128 * b : 128 * b + D, :] for b in range(4)], axis=1)


def permute_out(values, pm):
    return unstack_out(dot_nt(stack_out(values), pm))


def permute_out_wide(values, pm):
    high = values.astype(bf16).astype(f32)
    rest = values - high
    mid = rest.astype(bf16).astype(f32)
    return unstack_out(dot_nt(stack_out(high), pm) + dot_nt(stack_out(mid), pm))


def plane_mask(r, length):
    return jnp.where(lane_iota((1, LG)) * GROUP + r < length, 1.0, 0.0).astype(f32)


def span(r):
    return slice(LG * r, LG * r + LG)


def skewed(count, stages):
    held = [None] * count
    for step in range(count + len(stages) - 1):
        for k, stage in enumerate(stages):
            n = step - k
            if 0 <= n < count:
                held[n] = stage(n, held[n])


def window(ref, r, base=0):
    return ref[base + WIN[r] : base + WIN[r] + WROWS, :]


def join_windows(parts):
    a, b, c = parts
    return jnp.concatenate([a[:112], a[112:128] + b[:16], b[16:128], b[128:144] + c[:16], c[16:]], axis=0)


def shifted_planes(tiles):
    lanes = lane_iota((8, 128))
    zero = jnp.zeros((8, 128), f32)
    made = {}
    for m in range(-HALF, HALF + GROUP):
        r, s = m % GROUP, m // GROUP
        if s == 0:
            made[m] = tiles[r]
            continue
        turned = [pltpu.roll(tiles[r][:, 128 * k : 128 * k + 128], (-s) % 128, 1) for k in range(4)]
        if s > 0:
            pairs = zip(turned, turned[1:] + [zero])
            parts = [jnp.where(lanes < 128 - s, a, b) for a, b in pairs]
        else:
            pairs = zip([zero] + turned[:-1], turned)
            parts = [jnp.where(lanes < -s, a, b) for a, b in pairs]
        made[m] = jnp.concatenate(parts, axis=1)
    return made


def shifted(tiles, m):
    r, s = m % GROUP, m // GROUP
    if s == 0:
        return tiles[r]
    lanes = lane_iota((8, 128))
    zero = jnp.zeros((8, 128), f32)
    turned = [pltpu.roll(tiles[r][:, 128 * k : 128 * k + 128], (-s) % 128, 1) for k in range(4)]
    if s > 0:
        pairs = zip(turned, turned[1:] + [zero])
        parts = [jnp.where(lanes < 128 - s, a, b) for a, b in pairs]
    else:
        pairs = zip([zero] + turned[:-1], turned)
        parts = [jnp.where(lanes < -s, a, b) for a, b in pairs]
    return jnp.concatenate(parts, axis=1)


SMEM = pl.BlockSpec(memory_space=pltpu.SMEM)
VMEM = pl.BlockSpec(memory_space=pltpu.VMEM)
BIG = (D, MAXLEN)
LOW = (128, MAXLEN)


def whole(shape):
    zeros = (0,) * len(shape)
    return pl.BlockSpec(shape, lambda u: zeros)


def per_utt(shape):
    zeros = (0,) * len(shape)
    return pl.BlockSpec((1,) + shape, lambda u: (u,) + zeros)


def o(shape, kind=bf16):
    return jax.ShapeDtypeStruct(shape, kind)


def params(flops=0, moved=0):
    cost = pl.CostEstimate(flops=flops, bytes_accessed=moved, transcendentals=0)
    return dict(compiler_params=pltpu.CompilerParams(vmem_limit_bytes=VMEM_BYTES), cost_estimate=cost)


def permutation():
    t = row_iota((384, 384))
    c = lane_iota((384, 384))
    return jnp.where(t == GROUP * (c % 128) + c // 128, 1.0, 0.0).astype(bf16)


def enter_body(x_ref, xp_ref, xf_ref, rs_ref, pm_ref):
    @pl.when(pl.program_id(0) == 0)
    def _():
        pm_ref[...] = permutation()

    x = permute_in(x_ref[0].astype(f32), pm_ref[...])
    xp_ref[0] = x.astype(bf16)
    xhat, rstd = norm(x)
    xf_ref[0] = xhat
    rs_ref[0] = jnp.broadcast_to(rstd, (8, MAXLEN))


def enter(x):
    utts = x.shape[0]
    return pl.pallas_call(
        enter_body,
        grid=(utts,),
        in_specs=[per_utt(BIG)],
        out_specs=[per_utt(BIG)] * 2 + [per_utt((8, MAXLEN)), whole((384, 384))],
        out_shape=[o((utts,) + BIG), o((utts,) + BIG, f32), o((utts, 8, MAXLEN), f32), o((384, 384))],
        name="enter",
        **params(2 * 10**9, 8 * 10**6),
    )(x)


def inward_body(cot_ref, pm_ref, cp_ref):
    cp_ref[0] = permute_in(cot_ref[0].astype(f32), pm_ref[...]).astype(bf16)


def outward_body(out_ref, pm_ref, done_ref):
    done_ref[0] = permute_out(out_ref[0].astype(f32), pm_ref[...]).astype(bf16)


def leave_body(grad_ref, pm_ref, gin_ref):
    gin_ref[0] = permute_out_wide(grad_ref[0], pm_ref[...])


def reorder(body, values, pm, name):
    utts = values.shape[0]
    return pl.pallas_call(
        body,
        grid=(utts,),
        in_specs=[per_utt(BIG), whole(pm.shape)],
        out_specs=per_utt(BIG),
        out_shape=o((utts,) + BIG, values.dtype),
        name=name,
        **params(2 * 10**9, 8 * 10**6),
    )(values, pm)


def unpack(me_ref, g_ref, flat, tb):
    parts, part_rows = g_ref.shape[0], g_ref.shape[1]
    for d in range(parts):
        flat[part_rows * d : part_rows * (d + 1), :] = g_ref[place(me_ref[0] ^ d, parts)].astype(f32)
    tb[ROWS_HEAD:TAIL, :] = jnp.zeros((TAIL - ROWS_HEAD, 128), f32)
    for start, count, base in ((0, ROWS_HEAD, 0), (TAIL_AT, ROWS_TAIL, TAIL)):
        for r in range(16):
            at = start + D * r
            first_row, col = at // 128, at % 128
            many = (count - r + 15) // 16
            here = flat[pl.ds(first_row, many, stride=15), :]
            then = flat[pl.ds(first_row + 1, many, stride=15), :]
            lanes = lane_iota((many, 128))
            got = jnp.where(lanes >= col, here, then)
            if col:
                got = pltpu.roll(got, 128 - col, 1)
            tb[pl.ds(base + r, many, stride=16), :] = jnp.where(lanes < D, got, 0.0)


def with_row(block, row):
    tail = jnp.where(row_iota((8, 128)) == 0, row, 0.0)
    return jnp.concatenate([block, tail], axis=0)


def up_rows(tb, base):
    parts_t = []
    for q in range(4):
        block = tb[pl.ds(base + 2 + q, D, stride=4), :]
        parts_t.append(with_row(block, tb[base + 482 + q : base + 483 + q, :]).T[:D, :])
    return jnp.concatenate(parts_t, axis=0)


def up_across(up_t):
    return jnp.concatenate([up_t, jnp.zeros((32, 128), f32)], axis=0).T[:, :FF].astype(bf16)


def down_across(tb, base):
    bias = jnp.where(row_iota((32, 128)) == 0, tb[base + 966 : base + 967, :], 0.0)
    down = jnp.concatenate([tb[base + 486 : base + 966, :], bias], axis=0)
    return (0.5 * down).T.astype(bf16)


def point_rows(tb):
    parts_t = []
    for q in range(2):
        block = tb[pl.ds(CV + 2 + q, D, stride=2), :]
        parts_t.append(with_row(block, tb[CV + 242 + q : CV + 243 + q, :]).T[:D, :])
    return jnp.concatenate(parts_t, axis=0)


def fill_windows(tb, wt, wins):
    none = jnp.zeros((1, 128), f32)
    wins[...] = jnp.zeros_like(wins)
    for w, at, bias_at in ((0, AT + 2, AT + 122), (1, AT + 123, None), (2, AT + 243, AT + 363)):
        bias = none if bias_at is None else tb[bias_at : bias_at + 1, :]
        wt[...] = with_row(tb[at : at + D, :], bias).T
        for to, r, src, many in segments():
            start = WROWS * w + to - WIN[r]
            wins[r, start : start + many, :] = wt[src : src + many, :]


def fill_output(tb, wins):
    wins[:, 0:256, :] = jnp.zeros((GROUP, 256, 128), f32)
    for to, r, src, many in segments():
        start = to - WIN[r]
        wins[r, start : start + many, :] = tb[AT + 364 + src : AT + 364 + src + many, :]


def early_body(me_ref, g_ref, up_ref, dn_ref, wqkv_ref, wo_ref, pw_ref, cols_ref, base_ref, flat, tb, wt, wins, rows):
    unpack(me_ref, g_ref, flat, tb)
    up_ref[...] = (0.5 * up_rows(tb, F1)).astype(bf16)
    dn_ref[...] = down_across(tb, F1)
    pw_ref[...] = (0.5 * point_rows(tb)).astype(bf16)
    fill_windows(tb, wt, wins)
    for r in range(GROUP):
        wqkv_ref[r] = wins[r, : 3 * WROWS].astype(bf16)
    fill_output(tb, wins)
    for r in range(GROUP):
        wins[r, MARKS[r] : MARKS[r] + 1, :] = tb[AT + 484 : AT + 485, :]
        wo_ref[r] = wins[r, 0:256, :].T[:, :WROWS].astype(bf16)

    rows[...] = jnp.zeros_like(rows)
    listed = []
    for base in (F1, AT, CV, CV + 260, F2, FN):
        listed += [base, base + 1]
    listed += [CV + 259] + [CV + 244 + k for k in range(KERNEL)]
    for to, src in enumerate(listed):
        rows[to : to + 1, :] = tb[src : src + 1, :]
    cols_ref[...] = rows[...].T

    rel_rows = []
    lanes = lane_iota((1, 128))
    for h in range(HEADS):
        at = REL_AT + (2 * REL + 1) * h
        first_row, col = at // 128, at % 128
        pieces = []
        for k in range(2):
            here = flat[first_row + k : first_row + k + 1, :]
            got = jnp.where(lanes >= col, here, flat[first_row + k + 1 : first_row + k + 2, :])
            pieces.append(pltpu.roll(got, (128 - col) % 128, 1) if col else got)
        rel_rows.append(jnp.concatenate(pieces, axis=1))
    rel = jnp.concatenate(rel_rows + [jnp.zeros((4, 256), f32)], axis=0)
    rel = jnp.where(lane_iota((8, 256)) < 2 * REL + 1, rel, 0.0)
    base_ref[...] = dot(rel.astype(bf16), distance_select()) * LOG2E


def late_body(
    me_ref, g_ref, upp1_ref, dnp1_ref, up2_ref, upp2_ref, dn2_ref, dnp2_ref, pwp_ref, pr_ref, prp_ref, wqkvt_ref, wob_ref,
    flat, tb, wt, wins,
):
    unpack(me_ref, g_ref, flat, tb)
    upp1_ref[...] = up_across(up_rows(tb, F1))
    dnp1_ref[...] = (0.25 * tb[F1 + 486 : F1 + 966, :]).astype(bf16)
    up_t = up_rows(tb, F2)
    up2_ref[...] = (0.5 * up_t).astype(bf16)
    upp2_ref[...] = up_across(up_t)
    dn2_ref[...] = down_across(tb, F2)
    dnp2_ref[...] = (0.25 * tb[F2 + 486 : F2 + 966, :]).astype(bf16)
    pwp_ref[...] = jnp.concatenate([point_rows(tb), jnp.zeros((16, 128), f32)], axis=0).T[:, :240].astype(bf16)
    block = with_row(tb[CV + 262 : CV + 382, :], tb[CV + 382 : CV + 383, :])
    prp_ref[...] = (0.5 * block).astype(bf16)
    pr_ref[...] = block.T.astype(bf16)
    fill_windows(tb, wt, wins)
    for r in range(GROUP):
        wqkvt_ref[r] = wins[r].T[:, : 3 * WROWS].astype(bf16)
    fill_output(tb, wins)
    for r in range(GROUP):
        wob_ref[r] = wins[r, 0:WROWS, :].astype(bf16)


def distance_select():
    l = lane_iota((256, 2 * LG))
    gap = jnp.where(l < LG, -l, 2 * LG - l)
    index = jnp.clip(gap, -REL, REL) + REL
    return jnp.where(row_iota((256, 2 * LG)) == index, 1.0, 0.0).astype(bf16)


def diagonal_sum(values):
    wide = jnp.concatenate([values, jnp.zeros((LG, LG), f32)], axis=1)
    half = LG // 2
    while half:
        upper, lower = wide[:half], wide[half : 2 * half]
        if half % 128 == 0:
            lower = jnp.concatenate([lower[:, half:], lower[:, :half]], axis=1)
        else:
            lower = pltpu.roll(lower, 2 * LG - half, 1)
        wide = upper + lower
        half //= 2
    return wide


def prepare(me, gathered):
    total = gathered.shape[0] * gathered.shape[1]
    room = [
        pltpu.VMEM((total, 128), f32),
        pltpu.VMEM((TABLE, 128), f32),
        pltpu.VMEM((128, 128), f32),
        pltpu.VMEM((GROUP, 512, 128), f32),
    ]
    early = pl.pallas_call(
        early_body,
        in_specs=[SMEM, VMEM],
        out_shape=[o((FF, 128)), o((128, 512)), o((GROUP, 3 * WROWS, 128)), o((GROUP, 128, WROWS)), o((240, 128))]
        + [o((128, 128), f32), o((8, 2 * LG), f32)],
        scratch_shapes=room + [pltpu.VMEM((128, 128), f32)],
        name="prepare",
        **params(10**9, 2 * 10**6),
    )(me, gathered)
    late = pl.pallas_call(
        late_body,
        in_specs=[SMEM, VMEM],
        out_shape=[o((128, FF)), o((FF, 128)), o((FF, 128)), o((128, FF)), o((128, 512)), o((FF, 128))]
        + [o((128, 240)), o((128, 128)), o((128, 128)), o((GROUP, 128, 3 * WROWS)), o((GROUP, WROWS, 128))],
        scratch_shapes=room,
        name="late",
        **params(3 * 10**9, 10 * 10**6),
    )(me, gathered)
    return early, late


def column(cols, k):
    return cols[:D, k : k + 1]


def valid_keys(length):
    return row_iota((LG, 1)) * GROUP < length


def set_tail(hid):
    hid[FF:, :] = jnp.where(row_iota((512 - FF, hid.shape[1])) == 0, 1.0, 0.0).astype(bf16)


def conv_columns(cols, cb):
    for k in range(KERNEL + 1):
        cb[k] = jnp.broadcast_to(cols[:D, C_DWB + k : C_DWB + k + 1], (D, 128))


def wide(tile, copies=4):
    return jnp.concatenate([tile] * copies, axis=1)


def first_body(
    len_ref, xp_ref, xf_ref, cols_ref, up_ref, dn_ref, wqkv_ref, wo_ref, pw_ref, base_ref,
    lf_ref, xa_ref, nrm_ref, qkv_ref, prob_ref, att_ref, aa_ref, xc_ref, cn_ref, gat_ref, sig_ref, rgt_ref,
    rs_ref, dep_ref, st_ref,
    hid, one, cb, tab, run,
):
    u = pl.program_id(0)
    length = len_ref[u]

    @pl.when(u == 0)
    def _():
        set_tail(hid)
        run[...] = jnp.zeros_like(run)
        conv_columns(cols_ref, cb)
        for h in range(HEADS):
            spread = jnp.broadcast_to(base_ref[h : h + 1, :], (LG, 2 * LG))
            tab[h] = pltpu.roll(spread, 0, 1, stride=1, stride_axis=0)[:, :LG]

    cols = cols_ref

    def ffn_up(r, held):
        low = ext(xf_ref[0, :, span(r)] * column(cols, C_F1) + column(cols, C_F1 + 1))
        lf_ref[0, :, span(r)] = low
        return dot(up_ref[...], low)

    def ffn_down(r, half):
        hid[:FF, span(r)] = (half + half * jnp.tanh(half)).astype(bf16)
        return dot(dn_ref[...], hid[:, span(r)])[:D]

    def ffn_norm(r, branch):
        after = xp_ref[0, :, span(r)].astype(f32) + branch
        one[:, span(r)] = after
        xhat, rstd = norm(after)
        xa_ref[0, :, span(r)] = xhat
        rs_ref[0, 1:2, span(r)] = rstd
        low = ext(xhat * column(cols, C_AT) + column(cols, C_AT + 1))
        nrm_ref[0, 128 * r : 128 * r + 128, :] = low
        return dot(wqkv_ref[r], low)

    made = [None] * GROUP

    def ffn_keep(r, found):
        made[r] = found

    skewed(GROUP, (ffn_up, ffn_down, ffn_norm, ffn_keep))
    for w in range(3):
        joined = join_windows([made[r][WROWS * w : WROWS * w + WROWS] for r in range(GROUP)])
        qkv_ref[0, GP * w : GP * w + GP, :] = joined.astype(bf16)
    keys = valid_keys(length)

    def rows(w, h):
        return slice(GP * w + HP * h, GP * w + HP * h + HP)

    def score(h, held):
        return dot_tn(qkv_ref[0, rows(1, h), :], qkv_ref[0, rows(0, h), :])

    def soften(h, raw):
        scores = raw * (SCALE * LOG2E) + tab[h]
        scores = jnp.where(keys, scores, NEG_FILL * LOG2E)
        peak = jnp.max(scores, axis=0, keepdims=True)
        power = jnp.exp2(scores - peak)
        total = jnp.sum(power, axis=0, keepdims=True)
        prob_ref[0, h] = (power * (1.0 / total)).astype(bf16)

    def mix(h, held):
        mixed = dot(qkv_ref[0, rows(2, h), :], prob_ref[0, h])
        if h < GROUP:
            mixed = jnp.where(row_iota((HP, LG)) == HEAD, 1.0, mixed)
        att_ref[0, rows(0, h), :] = mixed.astype(bf16)

    skewed(HEADS, (score, soften, mix))

    def project(r, held):
        return dot(wo_ref[r], window(att_ref.at[0], r))[:D]

    def gate_in(r, mixed):
        after = one[:, span(r)] + mixed
        aa_ref[0, :, span(r)] = after
        xhat, rstd = norm(after)
        xc_ref[0, :, span(r)] = xhat
        rs_ref[0, 2:3, span(r)] = rstd
        low = ext(xhat * column(cols, C_CV) + column(cols, C_CV + 1))
        cn_ref[0, :, span(r)] = low
        return dot(pw_ref[...], low)

    def gate_out(r, pre):
        mask = plane_mask(r, length)
        sig = (0.5 + 0.5 * jnp.tanh(pre[D:])) * mask
        gated = (pre[:D] + pre[:D]) * sig
        gat_ref[0, :, span(r)] = gated
        sig_ref[0, :, span(r)] = sig
        rgt_ref[0, :, span(r)] = gated * (1.0 - sig)

    skewed(GROUP, (project, gate_in, gate_out))

    def conv(f, carry):
        at = slice(8 * f, 8 * f + 8)
        tiles = [gat_ref[0, at, span(r)] for r in range(GROUP)]
        totals = [wide(cb[0, at, :])] * GROUP
        for m in range(-HALF, HALF + GROUP):
            here = shifted(tiles, m)
            for r in range(GROUP):
                k = m + HALF - r
                if 0 <= k < KERNEL:
                    totals[r] = totals[r] + wide(cb[1 + k, at, :]) * here
        for r in range(GROUP):
            dep_ref[0, at, span(r)] = totals[r]
        return carry

    for f in range(D // 8):
        conv(f, 0)

    count = length.astype(f32)
    mask = jnp.concatenate([plane_mask(r, length) for r in range(GROUP)], axis=1)
    dep = dep_ref[0]
    mean = jnp.sum(dep * mask, axis=1, keepdims=True) / count
    gap = (dep - mean) * mask
    spread = jnp.sum(gap * gap, axis=1, keepdims=True)
    old_mean, old_spread, old_count = run[0], run[1], run[2]
    new_count = old_count + count
    step = mean - old_mean
    new_mean = old_mean + step * (count / new_count)
    new_spread = old_spread + spread + step * step * (old_count * count / new_count)
    run[0] = new_mean
    run[1] = new_spread
    run[2] = new_count

    @pl.when(u == pl.num_programs(0) - 1)
    def _():
        lanes = lane_iota((D, 128))
        picked = jnp.where(lanes == 0, run[0], jnp.where(lanes == 1, run[1], jnp.where(lanes == 2, run[2], 0.0)))
        line = pad8(picked).T[0:8]
        for d in range(st_ref.shape[0]):
            st_ref[d] = line


def first(devices, lengths, xp, xf, weights):
    utts = xp.shape[0]
    per = [
        (LOW, bf16),
        (BIG, f32),
        ((GP, LG), bf16),
        ((3 * GP, LG), bf16),
        ((HEADS, LG, LG), bf16),
        ((GP, LG), bf16),
        (BIG, f32),
        (BIG, f32),
        (LOW, bf16),
        (BIG, f32),
        (BIG, f32),
        (BIG, f32),
        ((8, MAXLEN), f32),
        (BIG, f32),
    ]
    line = (devices, 8, 128)
    return pl.pallas_call(
        first_body,
        grid=(utts,),
        in_specs=[SMEM, per_utt(BIG), per_utt(BIG)] + [whole(w.shape) for w in weights],
        out_specs=[per_utt(s) for s, k in per] + [whole(line)],
        out_shape=[o((utts,) + s, k) for s, k in per] + [o(line, f32)],
        scratch_shapes=[
            pltpu.VMEM((512, MAXLEN), bf16),
            pltpu.VMEM(BIG, f32),
            pltpu.VMEM((KERNEL + 1, D, 128), f32),
            pltpu.VMEM((HEADS, LG, LG), f32),
            pltpu.VMEM((3, D, 128), f32),
        ],
        name="first",
        **params(10 * 10**9, 60 * 10**6),
    )(lengths, xp, xf, *weights)


def second_body(
    len_ref, stats_ref, cot_ref, aa_ref, dep_ref, cols_ref, up_ref, upp_ref, dn_ref, dnp_ref, pr_ref, prp_ref,
    out_ref, bgd_ref, gc_ref, sums_ref, stc_ref, gdn_ref, gup_ref, gpr_ref, vec_ref,
    hid, acc,
):
    u = pl.program_id(0)
    length = len_ref[u]
    cols = cols_ref

    @pl.when(u == 0)
    def _():
        set_tail(hid)
        parts = stats_ref.shape[0]
        count = jnp.zeros((1, 128), f32)
        total = jnp.zeros((1, 128), f32)
        for d in range(parts):
            many = stats_ref[d, 2:3, :]
            count = count + many
            total = total + many * stats_ref[d, 0:1, :]
        here = lane_iota((1, 128)) < D
        count = jnp.where(here, count, 1.0)
        mean = total / count
        spread = jnp.zeros((1, 128), f32)
        for d in range(parts):
            gap = stats_ref[d, 0:1, :] - mean
            spread = spread + stats_ref[d, 1:2, :] + stats_ref[d, 2:3, :] * gap * gap
        scale = lax.rsqrt(spread / count + EPS_NORM)
        at = row_iota((128, 128))
        table = jnp.where(at == 0, mean, jnp.where(at == 1, scale, jnp.where(at == 2, 1.0 / count, 0.0)))
        stc_ref[...] = table.T
        gdn_ref[...] = jnp.zeros_like(gdn_ref)
        gup_ref[...] = jnp.zeros_like(gup_ref)
        gpr_ref[...] = jnp.zeros_like(gpr_ref)
        vec_ref[...] = jnp.zeros_like(vec_ref)
        acc[...] = jnp.zeros_like(acc)

    half_gain = 0.5 * column(cols, C_BN)
    half_bias = 0.5 * column(cols, C_BN + 1)

    def enter(r, held):
        normal = (dep_ref[0, :, span(r)] - stc_ref[:D, 0:1]) * stc_ref[:D, 1:2]
        z = normal * half_gain + half_bias
        t = jnp.tanh(z)
        act = z + z * t
        act_low = ext(act)
        slope = (1.0 + t) * (1.0 + z * (1.0 - t))
        return act_low, normal, slope, dot(pr_ref[...], act_low)[:D]

    def ffn_up(r, held):
        act_low, normal, slope, moved = held
        after_conv = aa_ref[0, :, span(r)] + moved
        xhat, rstd = norm(after_conv)
        low = ext(xhat * column(cols, C_F2) + column(cols, C_F2 + 1))
        return act_low, normal, slope, after_conv, xhat, rstd, low, dot(up_ref[...], low)

    def ffn_down(r, held):
        act_low, normal, slope, after_conv, xhat, rstd, low, half = held
        t = jnp.tanh(half)
        hid[:FF, span(r)] = (half + half * t).astype(bf16)
        bend = (1.0 + t) * (1.0 + half * (1.0 - t))
        return act_low, normal, slope, after_conv, xhat, rstd, low, bend, dot(dn_ref[...], hid[:, span(r)])[:D]

    def finish(r, held):
        act_low, normal, slope, after_conv, xhat, rstd, low, bend, branch = held
        mask = plane_mask(r, length)
        xhat_f, rstd_f = norm(after_conv + branch)
        made = (xhat_f * column(cols, C_FN) + column(cols, C_FN + 1)) * mask
        out_ref[0, :, span(r)] = made.astype(bf16)
        up_grad = cot_ref[0, :, span(r)].astype(f32) * mask
        vec_ref[2] += fold(up_grad * xhat_f)
        vec_ref[3] += fold(up_grad)
        grad_two = norm_back(up_grad, xhat_f, rstd_f, column(cols, C_FN))
        branch = pad8(grad_two).astype(bf16)
        gdn_ref[...] += dot_nt(hid[:, span(r)], branch)
        return act_low, normal, slope, xhat, rstd, low, bend, grad_two, dot(dnp_ref[...], branch)

    def ffn_back(r, held):
        act_low, normal, slope, xhat, rstd, low, bend, grad_two, back = held
        pre_low = (bend * back).astype(bf16)
        gup_ref[...] += dot_nt(pre_low, low)
        return act_low, normal, slope, xhat, rstd, grad_two, dot(upp_ref[...], pre_low)[:D]

    def leave(r, held):
        act_low, normal, slope, xhat, rstd, grad_two, back = held
        vec_ref[0] += fold(back * xhat)
        vec_ref[1] += fold(back)
        grad_conv = grad_two + norm_back(back, xhat, rstd, column(cols, C_F2))
        gc_ref[0, :, span(r)] = grad_conv
        project = pad8(grad_conv).astype(bf16)
        gpr_ref[...] += dot_nt(act_low, project)
        return normal, slope, dot(prp_ref[...], project)[:D]

    def last(r, held):
        normal, slope, back = held
        batch = slope * back
        bgd_ref[0, :, span(r)] = batch
        acc[0] += fold(batch * normal)
        acc[1] += fold(batch)

    skewed(GROUP, (enter, ffn_up, ffn_down, finish, ffn_back, leave, last))

    @pl.when(u == pl.num_programs(0) - 1)
    def _():
        lanes = lane_iota((D, 128))
        gain = jnp.sum(acc[0], axis=1, keepdims=True)
        shift = jnp.sum(acc[1], axis=1, keepdims=True)
        line = pad8(jnp.where(lanes == 0, gain, jnp.where(lanes == 1, shift, 0.0))).T[0:8]
        for d in range(sums_ref.shape[0]):
            sums_ref[d] = line


def second(lengths, stats, cot, aa, dep, weights):
    utts = cot.shape[0]
    big = (D, MAXLEN)
    outs = [
        (per_utt(big), (utts,) + big, bf16),
        (per_utt(big), (utts,) + big, f32),
        (per_utt(big), (utts,) + big, f32),
    ]
    for s in (stats.shape, (128, 128), (512, 128), (FF, 128), (128, 128), (4, D, 128)):
        outs.append((whole(s), s, f32))
    return pl.pallas_call(
        second_body,
        grid=(utts,),
        in_specs=[SMEM, whole(stats.shape)] + [per_utt(big)] * 3 + [whole(w.shape) for w in weights],
        out_specs=[o[0] for o in outs],
        out_shape=[jax.ShapeDtypeStruct(o[1], o[2]) for o in outs],
        scratch_shapes=[
            pltpu.VMEM((512, MAXLEN), bf16),
            pltpu.VMEM((2, D, 128), f32),
        ],
        name="second",
        **params(15000000000, 30000000),
    )(lengths, stats, cot, aa, dep, *weights)


def third_body(
    len_ref, sums_ref, stc_ref, bgd_ref, gc_ref, dep_ref, xf_ref, lf_ref, xa_ref, nrm_ref, qkv_ref, prob_ref, att_ref, xc_ref,
    cn_ref, gat_ref, sig_ref, rgt_ref, ri_ref, rs_ref,
    cols_ref, up_ref, upp_ref, dnp_ref, wqkv_t_ref, wob_ref, pwp_ref,
    grad_ref, gdn_ref, gup_ref, gpw_ref, gqkv_ref, go_ref, rel_ref, vec_ref,
    hid, dgs, olg, agr, back_s, gg, relacc, cb, tot,
):
    u = pl.program_id(0)
    length = len_ref[u]
    cols = cols_ref

    @pl.when(u == 0)
    def _():
        set_tail(hid)
        conv_columns(cols_ref, cb)
        parts = sums_ref.shape[0]
        total = sums_ref[0]
        for d in range(1, parts):
            total = total + sums_ref[d]
        tot[...] = jnp.concatenate([total, jnp.zeros((120, 128), f32)], axis=0).T
        for ref in (gdn_ref, gup_ref, gpw_ref, gqkv_ref, go_ref, vec_ref, relacc):
            ref[...] = jnp.zeros_like(ref)

    scale = stc_ref[:D, 1:2]
    lead = column(cols, C_BN) * scale
    share = lead * stc_ref[:D, 2:3]
    shift_part = share * tot[:D, 1:2]
    gain_part = share * tot[:D, 0:1] * scale
    for r in range(GROUP):
        normal = dep_ref[0, :, span(r)] - stc_ref[:D, 0:1]
        mask = plane_mask(r, length)
        dgs[:, span(r)] = bgd_ref[0, :, span(r)] * lead - mask * (shift_part + normal * gain_part)

    def conv(f, carry):
        at = slice(8 * f, 8 * f + 8)
        tiles = [dgs[at, span(r)] for r in range(GROUP)]
        gated = [gat_ref[0, at, span(r)] for r in range(GROUP)]
        totals = [None] * GROUP
        taps = [None] * KERNEL
        for m in range(-HALF, HALF + GROUP):
            here = shifted(tiles, m)
            for r in range(GROUP):
                k = r + HALF - m
                if 0 <= k < KERNEL:
                    term = wide(cb[1 + k, at, :]) * here
                    totals[r] = term if totals[r] is None else totals[r] + term
                    part = fold(gated[r] * here)
                    taps[k] = part if taps[k] is None else taps[k] + part
        vec_ref[6, at, :] += fold(tiles[0] + tiles[1] + tiles[2])
        for k in range(KERNEL):
            vec_ref[7 + k, at, :] += taps[k]
        for r in range(GROUP):
            gg[at, span(r)] = totals[r]
        return carry

    for f in range(D // 8):
        conv(f, 0)

    def gate(r, held):
        grad = gg[:, span(r)]
        left = grad * sig_ref[0, :, span(r)]
        right = grad * rgt_ref[0, :, span(r)]
        pre_low = jnp.concatenate([left, right], axis=0).astype(bf16)
        gpw_ref[...] += dot_nt(pre_low, cn_ref[0, :, span(r)])
        return dot(pwp_ref[...], pre_low)[:D]

    def residual(r, back):
        xhat = xc_ref[0, :, span(r)]
        vec_ref[0] += fold(back * xhat)
        vec_ref[1] += fold(back)
        grad = gc_ref[0, :, span(r)] + norm_back(back, xhat, rs_ref[0, 2:3, span(r)], column(cols, C_CV))
        dgs[:, span(r)] = grad
        low = pad8(grad).astype(bf16)
        olg[128 * r : 128 * r + 128, :] = low
        return dot(wob_ref[r], low)

    made = [None] * GROUP

    def keep(r, found):
        go_ref[r] += dot_nt(window(att_ref.at[0], r), olg[128 * r : 128 * r + 128, :])
        made[r] = found

    skewed(GROUP, (gate, residual, keep))
    agr[...] = join_windows(made).astype(bf16)

    def rows(w, h):
        return slice(GP * w + HP * h, GP * w + HP * h + HP)

    def enter(h, held):
        grad = agr[rows(0, h), :]
        back_s[rows(2, h), :] = dot_nt(grad, prob_ref[0, h]).astype(bf16)
        return dot_tn(qkv_ref[0, rows(2, h), :], grad)

    def soften(h, prob_grad):
        probs = prob_ref[0, h].astype(f32)
        inner = jnp.sum(probs * prob_grad, axis=0, keepdims=True)
        score = probs * (prob_grad - inner)
        relacc[h] += score
        return score.astype(bf16)

    def turn(h, low):
        back_s[rows(0, h), :] = (dot(qkv_ref[0, rows(1, h), :], low) * SCALE).astype(bf16)
        back_s[rows(1, h), :] = (dot_nt(qkv_ref[0, rows(0, h), :], low) * SCALE).astype(bf16)

    skewed(HEADS, (enter, soften, turn))

    def project(r, held):
        stack = jnp.concatenate([window(back_s, r, GP * w) for w in range(3)], axis=0)
        gqkv_ref[r] += dot_nt(stack, nrm_ref[0, 128 * r : 128 * r + 128, :])
        return dot(wqkv_t_ref[r], stack)[:D], dot(up_ref[...], lf_ref[0, :, span(r)])

    def ffn_in(r, held):
        back, half = held
        xhat = xa_ref[0, :, span(r)]
        vec_ref[2] += fold(back * xhat)
        vec_ref[3] += fold(back)
        grad = dgs[:, span(r)] + norm_back(back, xhat, rs_ref[0, 1:2, span(r)], column(cols, C_AT))
        low = pad8(grad).astype(bf16)
        return grad, low, half, dot(dnp_ref[...], low)

    def ffn_mid(r, held):
        grad, branch, half, back = held
        t = jnp.tanh(half)
        hid[:FF, span(r)] = (half + half * t).astype(bf16)
        pre_low = ((1.0 + t) * (1.0 + half * (1.0 - t)) * back).astype(bf16)
        gdn_ref[...] += dot_nt(hid[:, span(r)], branch)
        gup_ref[...] += dot_nt(pre_low, lf_ref[0, :, span(r)])
        return grad, dot(upp_ref[...], pre_low)[:D]

    def ffn_out(r, held):
        grad, back = held
        xhat = xf_ref[0, :, span(r)]
        vec_ref[4] += fold(back * xhat)
        vec_ref[5] += fold(back)
        grad_ref[0, :, span(r)] = grad + norm_back(back, xhat, ri_ref[0, 0:1, span(r)], column(cols, C_F1))

    skewed(GROUP, (project, ffn_in, ffn_mid, ffn_out))

    @pl.when(u == pl.num_programs(0) - 1)
    def _():
        found = []
        for h in range(HEADS):
            found.append(diagonal_sum(relacc[h]))
        stacked = jnp.concatenate(found + [jnp.zeros((4, 2 * LG), f32)], axis=0)
        high = stacked.astype(bf16)
        rest = stacked - high.astype(f32)
        mid = rest.astype(bf16)
        rest = rest - mid.astype(f32)
        select = distance_select()
        rel_ref[...] = dot_nt(high, select) + dot_nt(mid, select) + dot_nt(rest.astype(bf16), select)


def third(lengths, sums, stc, saved, weights):
    utts = saved[0].shape[0]
    big = (D, MAXLEN)
    outs = [(per_utt(big), (utts,) + big)]
    for s in ((512, 128), (FF, 128), (240, 128), (GROUP, 3 * WROWS, 128), (GROUP, WROWS, 128), (8, 256), (22, D, 128)):
        outs.append((whole(s), s))
    return pl.pallas_call(
        third_body,
        grid=(utts,),
        in_specs=[SMEM, whole(sums.shape), whole(stc.shape)]
        + [per_utt(s.shape[1:]) for s in saved]
        + [whole(w.shape) for w in weights],
        out_specs=[o[0] for o in outs],
        out_shape=[jax.ShapeDtypeStruct(o[1], f32) for o in outs],
        scratch_shapes=[
            pltpu.VMEM((512, MAXLEN), bf16),
            pltpu.VMEM(big, f32),
            pltpu.VMEM((GP, LG), bf16),
            pltpu.VMEM((GP, LG), bf16),
            pltpu.VMEM((3 * GP, LG), bf16),
            pltpu.VMEM(big, f32),
            pltpu.VMEM((HEADS, LG, LG), f32),
            pltpu.VMEM((KERNEL + 1, D, 128), f32),
            pltpu.VMEM((128, 128), f32),
        ],
        name="third",
        **params(20000000000, 80000000),
    )(lengths, sums, stc, *saved, *weights)


def clean(block):
    return jnp.where(lane_iota(block.shape) < D, block, 0.0)


def set_rows(tb, wt, ref, at):
    lanes = lane_iota((D, 128))
    table = jnp.zeros((D, 128), f32)
    for k in range(len(at)):
        table = jnp.where(lanes == k, jnp.sum(ref[k], axis=1, keepdims=True), table)
    wt[...] = pad8(table).T
    for k, to in enumerate(at):
        tb[to : to + 1, :] = wt[k : k + 1, :]


def set_ffn(tb, base, dn_ref, up_ref):
    tb[base + 486 : base + 967, :] = 0.5 * clean(dn_ref[0 : FF + 1, :])
    for q in range(4):
        block = pad8(up_ref[D * q : D * q + D, :]).T
        tb[pl.ds(base + 2 + q, D, stride=4), :] = block[:D]
        tb[base + 482 + q : base + 483 + q, :] = block[D : D + 1]


def flatten(tb, base, flat, at_row, y_count, offset):
    for k in range(15):
        at = 128 * k + offset
        first_row, col = at // D, at % D
        many = (y_count - k + 14) // 15
        here = lane_iota((many, 128))
        got = tb[pl.ds(base + first_row, many, stride=16), :]
        if col:
            got = pltpu.roll(got, 128 - col, 1)
        then = pltpu.roll(tb[pl.ds(base + first_row + 1, many, stride=16), :], D - col, 1)
        got = jnp.where(here < D - col, got, then)
        if 2 * D - col < 128:
            then = pltpu.roll(tb[pl.ds(base + first_row + 2, many, stride=16), :], 2 * D - col, 1)
            got = jnp.where(here < 2 * D - col, got, then)
        flat[pl.ds(at_row + k, many, stride=15), :] = got


SPLIT = F2 - TAIL
ROWS_LAST = ROWS_TAIL - SPLIT
LAST_AT = TAIL_AT + D * SPLIT
LAST_Y = LAST_AT // 128
LAST_COUNT = (LIVE - 1) // 128 - LAST_Y + 1


def ahead_body(dn_ref, up_ref, vec_ref, out_ref, tb, wt):
    tb[0:8, :] = jnp.zeros((8, 128), f32)
    tb[8 + ROWS_LAST :, :] = jnp.zeros((tb.shape[0] - 8 - ROWS_LAST, 128), f32)
    set_rows(tb, wt, vec_ref, (8, 9, 8 + FN - F2, 9 + FN - F2))
    set_ffn(tb, 8, dn_ref, up_ref)
    flatten(tb, 7, out_ref, 0, LAST_COUNT, D + 128 * LAST_Y - LAST_AT)


def pack_ahead(dn, up, vec):
    return pl.pallas_call(
        ahead_body,
        out_shape=o((LAST_COUNT, 128), f32),
        scratch_shapes=[pltpu.VMEM((ROWS_LAST + 24, 128), f32), pltpu.VMEM((128, 128), f32)],
        name="ahead",
        **params(2 * 10**9, 8 * 10**6),
    )(dn, up, vec)


def pack_body(
    me_ref, last_ref, dn1_ref, up1_ref, pr_ref, pw_ref, qkv_ref, o_ref, rel_ref, vec_ref, sums_ref,
    keep_ref, send_ref, tb, flat, stage, wt,
):
    tb[ROWS_HEAD:TAIL, :] = jnp.zeros((TAIL - ROWS_HEAD, 128), f32)
    tb[F2:, :] = jnp.zeros((tb.shape[0] - F2, 128), f32)
    set_rows(
        tb, wt, vec_ref, (CV, CV + 1, AT, AT + 1, F1, F1 + 1, CV + 259) + tuple(CV + 244 + k for k in range(KERNEL))
    )
    tb[CV + 260 : CV + 262, :] = sums_ref[0, 0:2, :]
    set_ffn(tb, F1, dn1_ref, up1_ref)
    for q in range(2):
        block = pad8(pw_ref[D * q : D * q + D, :]).T
        tb[pl.ds(CV + 2 + q, D, stride=2), :] = block[:D]
        tb[CV + 242 + q : CV + 243 + q, :] = block[D : D + 1]
    tb[CV + 262 : CV + 383, :] = clean(pr_ref[0 : D + 1, :])

    def gathered(ref, base):
        wt[...] = jnp.zeros_like(wt)
        for to, r, src, many in segments():
            start = base + to - WIN[r]
            wt[src : src + many, :] += ref[r, start : start + many, :]
        return wt[...]

    for w, at, bias_at in ((0, AT + 2, AT + 122), (1, AT + 123, None), (2, AT + 243, AT + 363)):
        block = gathered(qkv_ref, WROWS * w).T
        tb[at : at + D, :] = block[:D]
        if bias_at is not None:
            tb[bias_at : bias_at + 1, :] = block[D : D + 1]
    tb[AT + 364 : AT + 484, :] = clean(gathered(o_ref, 0)[:D])
    bias = sum(o_ref[r, MARKS[r] : MARKS[r] + 1, :] for r in range(GROUP))
    tb[AT + 484 : AT + 485, :] = clean(bias)

    tail_y = TAIL_AT // 128
    flat[LAST_Y + LAST_COUNT :, :] = jnp.zeros((flat.shape[0] - LAST_Y - LAST_COUNT, 128), f32)
    flat[REL_AT // 128 + 1 : tail_y, :] = jnp.zeros((tail_y - REL_AT // 128 - 1, 128), f32)
    flatten(tb, 0, flat, 0, REL_AT // 128 + 1, 0)
    flatten(tb, TAIL - 1, flat, tail_y, LAST_Y - tail_y + 1, 128 * tail_y - TAIL_AT + D)
    flat[LAST_Y : LAST_Y + 1, :] += last_ref[0:1, :]
    flat[LAST_Y + 1 : LAST_Y + LAST_COUNT, :] = last_ref[1:, :]
    here = lane_iota((1, 128))
    width = 2 * REL + 1
    for h in range(HEADS):
        at = REL_AT + width * h
        for y in range(at // 128, (at + width - 1) // 128 + 1):
            lo, hi = max(at - 128 * y, 0), min(at + width - 128 * y, 128)
            shift = (at - 128 * y) % 256
            turned = rel_ref[h : h + 1, :]
            if shift:
                turned = pltpu.roll(turned, shift, 1)
            flat[y : y + 1, :] += jnp.where((here >= lo) & (here < hi), turned[:, :128], 0.0)
    parts, rows = 2 * keep_ref.shape[0], keep_ref.shape[1]
    for d in range(parts):
        stage[d] = flat[rows * d : rows * (d + 1), :]
    for offset in range(0, parts, 2):
        keep_ref[place(offset, parts)] = stage[me_ref[0] ^ offset]
        send_ref[place(offset, parts)] = stage[me_ref[0] ^ (offset + 1)]


def pack(parts, rows, me, grads):
    half = o((parts // 2, rows, 128), f32)
    return pl.pallas_call(
        pack_body,
        in_specs=[SMEM] + [VMEM] * len(grads),
        out_shape=[half, half],
        scratch_shapes=[
            pltpu.VMEM((F2 + 24, 128), f32),
            pltpu.VMEM((parts * rows, 128), f32),
            pltpu.VMEM((parts, rows, 128), f32),
            pltpu.VMEM((128, 128), f32),
        ],
        name="pack",
        **params(10**9, 5 * 10**6),
    )(me, *grads)


def update_tables(total_len):
    rates = np.zeros(total_len, np.float32)
    decays = np.zeros(total_len, np.float32)
    vector, gain, ffn = (D, 0.1, 0.0), (D, 0.3, 0.0), lambda n, fan: (n, fan**-0.5, 0.01)
    block = [gain, vector, ffn(D * FF, D), (FF, 0.1, 0.0), ffn(FF * D, FF), vector]
    square = ffn(D * D, D)
    pieces = block + [gain, vector, square, vector, square, square, vector, ffn(D * D, 6.0 * D / MAXLEN), vector]
    pieces += [(HEADS * (2 * REL + 1), 0.5, 0.0)]
    pieces += [gain, vector, ffn(2 * D * D, D), (2 * D, 0.1, 0.0), ffn(KERNEL * D, KERNEL), vector, gain, vector]
    pieces += [square, vector] + block + [gain, vector]
    offset = 0
    for entries, rate, decay in pieces:
        rates[offset : offset + entries] = rate
        decays[offset : offset + entries] = decay
        offset += entries
    return rates, decays


def digits(devices):
    found, stride = [], 1
    while stride < devices:
        size = min(2 if stride == 1 else 4, devices // stride)
        found.append((stride, size))
        stride *= size
    return found


def place(offset, devices):
    at, weight = 0, devices
    for stride, size in digits(devices):
        weight //= size
        at = at + ((offset // stride) % size) * weight
    return at


def partner(values, offset, devices):
    return lax.ppermute(values, "dp", [(i, i ^ offset) for i in range(devices)])


def gather(values, devices, beside):
    held, made = values[None], []
    for k, (stride, size) in enumerate(reversed(digits(devices))):
        parts = [held] + [partner(held, stride * j, devices) for j in range(1, size)]
        if k < len(beside):
            parts, found = lax.optimization_barrier((parts, beside[k]))
            made.append(found)
        held = jnp.concatenate(parts, axis=0)
    return held, made + beside[len(made) :]


def scatter_sum(keep, send, devices, beside):
    total = keep + partner(send, 1, devices)
    for stride, size in digits(devices)[1:]:
        parts = total.reshape((size, total.shape[0] // size) + total.shape[1:])
        found = [partner(parts[j], stride * j, devices) for j in range(1, size)]
        if stride == 2:
            found, beside = lax.optimization_barrier((found, beside))
        total = parts[0]
        for part in found:
            total = total + part
    return total, beside


def local(frames, lengths, cotangent, master, moment_one, moment_two, average):
    shard_len = master.shape[0]
    devices = lax.axis_size("dp")
    rows = shard_len // 128
    me = lax.axis_index("dp").astype(jnp.int32).reshape(1)
    entered = enter(jnp.transpose(frames, (0, 2, 1)))
    cp = reorder(inward_body, jnp.transpose(cotangent, (0, 2, 1)), entered[3], "inward")
    gathered, (entered, cp) = gather(master.astype(bf16).reshape(rows, 128), devices, [entered, cp])
    xp, xf, rs_in, pm = entered
    early, late = prepare(me, gathered)
    up1, dn1, wqkv, wo, pw, cols, base = early
    upp1, dnp1, up2, upp2, dn2, dnp2, pwp, pr, prp, wqkvt, wob = late
    lf, xa, nrm, qkv, prob, att, aa, xc, cn, gat, sig, rgt, rs, dep, st = first(
        devices, lengths, xp, xf, (cols, up1, dn1, wqkv, wo, pw, base)
    )
    stats = lax.all_to_all(st, "dp", 0, 0)
    out, bgd, gc, sums, stc, gdn2, gup2, gpr, vec2 = second(
        lengths, stats, cp, aa, dep, (cols, up2, upp2, dn2, dnp2, pr, prp)
    )
    all_sums = lax.all_to_all(sums, "dp", 0, 0)
    last = pack_ahead(gdn2, gup2, vec2)
    out = reorder(outward_body, out, pm, "outward")
    (all_sums, last, out) = lax.optimization_barrier((all_sums, last, out))
    grad, gdn1, gup1, gpw, gqkv, go, rel, vec3 = third(
        lengths, all_sums, stc,
        (bgd, gc, dep, xf, lf, xa, nrm, qkv, prob, att, xc, cn, gat, sig, rgt, rs_in, rs),
        (cols, up1, upp1, dnp1, wqkvt, wob, pwp),
    )
    keep, send = pack(devices, rows, me, (last, gdn1, gup1, gpr, gpw, gqkv, go, rel, vec3, sums))
    gin = reorder(leave_body, grad, pm, "leave")
    reduced, gin = scatter_sum(keep, send, devices, gin)
    reduced = reduced.reshape(shard_len)
    rates_np, decays_np = update_tables(shard_len * devices)
    start_at = lax.axis_index("dp") * shard_len
    rates = lax.dynamic_slice_in_dim(jnp.asarray(rates_np), start_at, shard_len)
    decays = lax.dynamic_slice_in_dim(jnp.asarray(decays_np), start_at, shard_len)
    correction = 1.0 - 0.5**STEP
    new_one = 0.5 * moment_one + 0.5 * reduced
    new_two = 0.5 * moment_two + 0.5 * reduced * reduced
    direction = new_one / correction / (jnp.sqrt(new_two / correction) + EPS_ADAM)
    new_master = master - rates * (direction + decays * master)
    new_average = 0.75 * average + 0.25 * new_master
    return (
        jnp.transpose(out, (0, 2, 1)),
        jnp.transpose(gin, (0, 2, 1)),
        reduced,
        new_master,
        new_one,
        new_two,
        new_average,
    )


def solution(mesh):
    three = P("dp", None, None)
    one = P("dp")
    in_specs = (three, one, three, one, one, one, one)
    out_specs = (three, three, one, one, one, one, one)
    return jax.shard_map(local, mesh=mesh, in_specs=in_specs, out_specs=out_specs, check_vma=False)
```

```python
import math

import jax
import jax.numpy as jnp
import numpy as np
from jax import lax
from jax.experimental import pallas as pl
from jax.experimental.pallas import tpu as pltpu
from jax.sharding import PartitionSpec as P

D = 120
HEADS = 4
FF = 480
KERNEL = 15
GROUP = 3
REL = 127
STEP = 5
MAXLEN = 1536
LG = 512
HEAD = 90
HP = 96
GP = HEADS * HP
HALF = KERNEL // 2
WIN = (0, 112, 240)
WROWS = 144
MARKS = tuple(HP * r + HEAD - WIN[r] for r in range(GROUP))

EPS_NORM = 1e-05
EPS_ADAM = 1e-08
NEG_FILL = -1000000000.0
LOG2E = math.log2(math.e)
SCALE = HEAD ** (-0.5)

f32 = jnp.float32
bf16 = jnp.bfloat16
VMEM_BYTES = 58 * 2**20

REL_AT = 174240
TAIL_AT = 175260
TAIL = 1456
ROWS_HEAD = 1452
ROWS_TAIL = 1352
TABLE = 2824
F1 = 0
AT = 967
CV = TAIL
F2 = TAIL + 383
FN = TAIL + 1350
LIVE = 337500

C_F1, C_AT, C_CV, C_BN, C_F2, C_FN, C_DWB, C_DW = 0, 2, 4, 6, 8, 10, 12, 13


def dot(a, b):
    return lax.dot_general(a, b, (((1,), (0,)), ((), ())), preferred_element_type=f32)


def dot_nt(a, b):
    return lax.dot_general(a, b, (((1,), (1,)), ((), ())), preferred_element_type=f32)


def dot_tn(a, b):
    return lax.dot_general(a, b, (((0,), (0,)), ((), ())), preferred_element_type=f32)


def lane_iota(shape):
    return lax.broadcasted_iota(jnp.int32, shape, len(shape) - 1)


def row_iota(shape):
    return lax.broadcasted_iota(jnp.int32, shape, 0)


def segments():
    found = []
    for h in range(HEADS):
        for r in range(GROUP):
            lo, hi = max(HEAD * h, D * r), min(HEAD * h + HEAD, D * r + D)
            if lo < hi:
                found.append((HP * h + lo - HEAD * h, r, lo - D * r, hi - lo))
    return found


def pad8(values):
    return jnp.concatenate([values, jnp.zeros((8, values.shape[1]), f32)], axis=0)


def ext(values):
    width = values.shape[1]
    ones = jnp.where(row_iota((8, width)) == 0, 1.0, 0.0).astype(f32)
    return jnp.concatenate([values, ones], axis=0).astype(bf16)


def norm(values):
    mean = jnp.sum(values, axis=0, keepdims=True) * (1.0 / D)
    centre = values - mean
    var = jnp.sum(centre * centre, axis=0, keepdims=True) * (1.0 / D)
    rstd = lax.rsqrt(var + EPS_NORM)
    return centre * rstd, rstd


def norm_back(upstream, xhat, rstd, gain):
    scaled = upstream * gain
    mean_one = jnp.sum(scaled, axis=0, keepdims=True) * (1.0 / D)
    mean_two = jnp.sum(scaled * xhat, axis=0, keepdims=True) * (1.0 / D)
    return rstd * (scaled - mean_one - xhat * mean_two)


def fold(values):
    total = values[:, 0:128]
    for at in range(128, values.shape[1], 128):
        total = total + values[:, at : at + 128]
    return total


def permute_in(values, pm):
    low = pad8(values).astype(bf16)
    stack = jnp.concatenate([low[:, 384 * b : 384 * b + 384] for b in range(4)], axis=0)
    out = dot(stack, pm)
    tiles = [out[128 * b : 128 * b + D, 128 * r : 128 * r + 128] for r in range(3) for b in range(4)]
    return jnp.concatenate(tiles, axis=1)


def stack_out(values):
    low = pad8(values).astype(bf16)
    blocks = []
    for b in range(4):
        blocks.append(
            jnp.concatenate([low[:, 512 * r + 128 * b : 512 * r + 128 * b + 128] for r in range(3)], axis=1)
        )
    return jnp.concatenate(blocks, axis=0)


def unstack_out(out):
    return jnp.concatenate([out[128 * b : 128 * b + D, :] for b in range(4)], axis=1)


def permute_out(values, pm):
    return unstack_out(dot_nt(stack_out(values), pm))


def permute_out_wide(values, pm):
    high = values.astype(bf16).astype(f32)
    rest = values - high
    mid = rest.astype(bf16).astype(f32)
    return unstack_out(dot_nt(stack_out(high), pm) + dot_nt(stack_out(mid), pm))


def plane_mask(r, length):
    return jnp.where(lane_iota((1, LG)) * GROUP + r < length, 1.0, 0.0).astype(f32)


def span(r):
    return slice(LG * r, LG * r + LG)


def skewed(count, stages):
    held = [None] * count
    for step in range(count + len(stages) - 1):
        for k, stage in enumerate(stages):
            n = step - k
            if 0 <= n < count:
                held[n] = stage(n, held[n])


def window(ref, r, base=0):
    return ref[base + WIN[r] : base + WIN[r] + WROWS, :]


def join_windows(parts):
    a, b, c = parts
    return jnp.concatenate([a[:112], a[112:128] + b[:16], b[16:128], b[128:144] + c[:16], c[16:]], axis=0)


def shifted_planes(tiles):
    lanes = lane_iota((8, 128))
    zero = jnp.zeros((8, 128), f32)
    made = {}
    for m in range(-HALF, HALF + GROUP):
        r, s = m % GROUP, m // GROUP
        if s == 0:
            made[m] = tiles[r]
            continue
        turned = [pltpu.roll(tiles[r][:, 128 * k : 128 * k + 128], (-s) % 128, 1) for k in range(4)]
        if s > 0:
            pairs = zip(turned, turned[1:] + [zero])
            parts = [jnp.where(lanes < 128 - s, a, b) for a, b in pairs]
        else:
            pairs = zip([zero] + turned[:-1], turned)
            parts = [jnp.where(lanes < -s, a, b) for a, b in pairs]
        made[m] = jnp.concatenate(parts, axis=1)
    return made


def shifted(tiles, m):
    r, s = m % GROUP, m // GROUP
    if s == 0:
        return tiles[r]
    lanes = lane_iota((8, 128))
    zero = jnp.zeros((8, 128), f32)
    turned = [pltpu.roll(tiles[r][:, 128 * k : 128 * k + 128], (-s) % 128, 1) for k in range(4)]
    if s > 0:
        pairs = zip(turned, turned[1:] + [zero])
        parts = [jnp.where(lanes < 128 - s, a, b) for a, b in pairs]
    else:
        pairs = zip([zero] + turned[:-1], turned)
        parts = [jnp.where(lanes < -s, a, b) for a, b in pairs]
    return jnp.concatenate(parts, axis=1)


SMEM = pl.BlockSpec(memory_space=pltpu.SMEM)
VMEM = pl.BlockSpec(memory_space=pltpu.VMEM)
BIG = (D, MAXLEN)
LOW = (128, MAXLEN)


def whole(shape):
    zeros = (0,) * len(shape)
    return pl.BlockSpec(shape, lambda u: zeros)


def per_utt(shape):
    zeros = (0,) * len(shape)
    return pl.BlockSpec((1,) + shape, lambda u: (u,) + zeros)


def at_most(shape, utts):
    zeros = (0,) * len(shape)
    return pl.BlockSpec((1,) + shape, lambda u: (jnp.minimum(u, utts - 1),) + zeros)


def one_late(shape):
    zeros = (0,) * len(shape)
    return pl.BlockSpec((1,) + shape, lambda u: (jnp.maximum(u - 1, 0),) + zeros)


def o(shape, kind=bf16):
    return jax.ShapeDtypeStruct(shape, kind)


def params(flops=0, moved=0):
    cost = pl.CostEstimate(flops=flops, bytes_accessed=moved, transcendentals=0)
    return dict(compiler_params=pltpu.CompilerParams(vmem_limit_bytes=VMEM_BYTES), cost_estimate=cost)


def permutation():
    t = row_iota((384, 384))
    c = lane_iota((384, 384))
    return jnp.where(t == GROUP * (c % 128) + c // 128, 1.0, 0.0).astype(bf16)


def enter_body(x_ref, xp_ref, xf_ref, rs_ref, pm_ref):
    @pl.when(pl.program_id(0) == 0)
    def _():
        pm_ref[...] = permutation()

    x = permute_in(x_ref[0].astype(f32), pm_ref[...])
    xp_ref[0] = x.astype(bf16)
    xhat, rstd = norm(x)
    xf_ref[0] = xhat
    rs_ref[0] = jnp.broadcast_to(rstd, (8, MAXLEN))


def enter(x):
    utts = x.shape[0]
    return pl.pallas_call(
        enter_body,
        grid=(utts,),
        in_specs=[per_utt(BIG)],
        out_specs=[per_utt(BIG)] * 2 + [per_utt((8, MAXLEN)), whole((384, 384))],
        out_shape=[o((utts,) + BIG), o((utts,) + BIG, f32), o((utts, 8, MAXLEN), f32), o((384, 384))],
        name="enter",
        **params(2 * 10**9, 8 * 10**6),
    )(x)


def inward_body(cot_ref, pm_ref, cp_ref):
    cp_ref[0] = permute_in(cot_ref[0].astype(f32), pm_ref[...]).astype(bf16)


def outward_body(out_ref, pm_ref, done_ref):
    done_ref[0] = permute_out(out_ref[0].astype(f32), pm_ref[...]).astype(bf16)


def leave_body(grad_ref, pm_ref, gin_ref):
    gin_ref[0] = permute_out_wide(grad_ref[0], pm_ref[...])


def reorder(body, values, pm, name):
    utts = values.shape[0]
    return pl.pallas_call(
        body,
        grid=(utts,),
        in_specs=[per_utt(BIG), whole(pm.shape)],
        out_specs=per_utt(BIG),
        out_shape=o((utts,) + BIG, values.dtype),
        name=name,
        **params(2 * 10**9, 8 * 10**6),
    )(values, pm)


def unpack(me_ref, g_ref, flat, tb):
    parts = g_ref.shape[0]
    part_rows = flat.shape[0] // parts
    for d in range(parts):
        flat[part_rows * d : part_rows * (d + 1), :] = g_ref[place(me_ref[0] ^ d, parts)].astype(f32)[:part_rows]
    tb[ROWS_HEAD:TAIL, :] = jnp.zeros((TAIL - ROWS_HEAD, 128), f32)
    for start, count, base in ((0, ROWS_HEAD, 0), (TAIL_AT, ROWS_TAIL, TAIL)):
        for r in range(16):
            at = start + D * r
            first_row, col = at // 128, at % 128
            many = (count - r + 15) // 16
            here = flat[pl.ds(first_row, many, stride=15), :]
            then = flat[pl.ds(first_row + 1, many, stride=15), :]
            lanes = lane_iota((many, 128))
            got = jnp.where(lanes >= col, here, then)
            if col:
                got = pltpu.roll(got, 128 - col, 1)
            tb[pl.ds(base + r, many, stride=16), :] = jnp.where(lanes < D, got, 0.0)


def with_row(block, row):
    tail = jnp.where(row_iota((8, 128)) == 0, row, 0.0)
    return jnp.concatenate([block, tail], axis=0)


def up_rows(tb, base):
    parts_t = []
    for q in range(4):
        block = tb[pl.ds(base + 2 + q, D, stride=4), :]
        parts_t.append(with_row(block, tb[base + 482 + q : base + 483 + q, :]).T[:D, :])
    return jnp.concatenate(parts_t, axis=0)


def up_across(up_t):
    return jnp.concatenate([up_t, jnp.zeros((32, 128), f32)], axis=0).T[:, :FF].astype(bf16)


def down_across(tb, base):
    bias = jnp.where(row_iota((32, 128)) == 0, tb[base + 966 : base + 967, :], 0.0)
    down = jnp.concatenate([tb[base + 486 : base + 966, :], bias], axis=0)
    return (0.5 * down).T.astype(bf16)


def point_rows(tb):
    parts_t = []
    for q in range(2):
        block = tb[pl.ds(CV + 2 + q, D, stride=2), :]
        parts_t.append(with_row(block, tb[CV + 242 + q : CV + 243 + q, :]).T[:D, :])
    return jnp.concatenate(parts_t, axis=0)


def fill_windows(tb, wt, wins):
    none = jnp.zeros((1, 128), f32)
    wins[...] = jnp.zeros_like(wins)
    for w, at, bias_at in ((0, AT + 2, AT + 122), (1, AT + 123, None), (2, AT + 243, AT + 363)):
        bias = none if bias_at is None else tb[bias_at : bias_at + 1, :]
        wt[...] = with_row(tb[at : at + D, :], bias).T
        for to, r, src, many in segments():
            start = WROWS * w + to - WIN[r]
            wins[r, start : start + many, :] = wt[src : src + many, :]


def fill_output(tb, wins):
    wins[:, 0:256, :] = jnp.zeros((GROUP, 256, 128), f32)
    for to, r, src, many in segments():
        start = to - WIN[r]
        wins[r, start : start + many, :] = tb[AT + 364 + src : AT + 364 + src + many, :]


def early_body(me_ref, g_ref, up_ref, dn_ref, wqkv_ref, wo_ref, pw_ref, cols_ref, base_ref, flat, tb, wt, wins, rows):
    unpack(me_ref, g_ref, flat, tb)
    up_ref[...] = (0.5 * up_rows(tb, F1)).astype(bf16)
    dn_ref[...] = down_across(tb, F1)
    pw_ref[...] = (0.5 * point_rows(tb)).astype(bf16)
    fill_windows(tb, wt, wins)
    for r in range(GROUP):
        wqkv_ref[r] = wins[r, : 3 * WROWS].astype(bf16)
    fill_output(tb, wins)
    for r in range(GROUP):
        wins[r, MARKS[r] : MARKS[r] + 1, :] = tb[AT + 484 : AT + 485, :]
        wo_ref[r] = wins[r, 0:256, :].T[:, :WROWS].astype(bf16)

    rows[...] = jnp.zeros_like(rows)
    listed = []
    for base in (F1, AT, CV, CV + 260, F2, FN):
        listed += [base, base + 1]
    listed += [CV + 259] + [CV + 244 + k for k in range(KERNEL)]
    for to, src in enumerate(listed):
        rows[to : to + 1, :] = tb[src : src + 1, :]
    cols_ref[...] = rows[...].T

    rel_rows = []
    lanes = lane_iota((1, 128))
    for h in range(HEADS):
        at = REL_AT + (2 * REL + 1) * h
        first_row, col = at // 128, at % 128
        pieces = []
        for k in range(2):
            here = flat[first_row + k : first_row + k + 1, :]
            got = jnp.where(lanes >= col, here, flat[first_row + k + 1 : first_row + k + 2, :])
            pieces.append(pltpu.roll(got, (128 - col) % 128, 1) if col else got)
        rel_rows.append(jnp.concatenate(pieces, axis=1))
    rel = jnp.concatenate(rel_rows + [jnp.zeros((4, 256), f32)], axis=0)
    rel = jnp.where(lane_iota((8, 256)) < 2 * REL + 1, rel, 0.0)
    base_ref[...] = dot(rel.astype(bf16), distance_select()) * LOG2E


def late_body(
    me_ref, g_ref, upp1_ref, dnp1_ref, up2_ref, upp2_ref, dn2_ref, dnp2_ref, pwp_ref, pr_ref, prp_ref, wqkvt_ref, wob_ref,
    flat, tb, wt, wins,
):
    unpack(me_ref, g_ref, flat, tb)
    upp1_ref[...] = up_across(up_rows(tb, F1))
    dnp1_ref[...] = (0.25 * tb[F1 + 486 : F1 + 966, :]).astype(bf16)
    up_t = up_rows(tb, F2)
    up2_ref[...] = (0.5 * up_t).astype(bf16)
    upp2_ref[...] = up_across(up_t)
    dn2_ref[...] = down_across(tb, F2)
    dnp2_ref[...] = (0.25 * tb[F2 + 486 : F2 + 966, :]).astype(bf16)
    pwp_ref[...] = jnp.concatenate([point_rows(tb), jnp.zeros((16, 128), f32)], axis=0).T[:, :240].astype(bf16)
    block = with_row(tb[CV + 262 : CV + 382, :], tb[CV + 382 : CV + 383, :])
    prp_ref[...] = (0.5 * block).astype(bf16)
    pr_ref[...] = block.T.astype(bf16)
    fill_windows(tb, wt, wins)
    for r in range(GROUP):
        wqkvt_ref[r] = wins[r].T[:, : 3 * WROWS].astype(bf16)
    fill_output(tb, wins)
    for r in range(GROUP):
        wob_ref[r] = wins[r, 0:WROWS, :].astype(bf16)


def distance_select():
    l = lane_iota((256, 2 * LG))
    gap = jnp.where(l < LG, -l, 2 * LG - l)
    index = jnp.clip(gap, -REL, REL) + REL
    return jnp.where(row_iota((256, 2 * LG)) == index, 1.0, 0.0).astype(bf16)


def spread_table(line, tab, h):
    blocks = {}
    for gap in (-1, 0, 1):
        tiles = [line[:, 128 * (k % 8) : 128 * (k % 8) + 128] for k in (gap - 1, gap)]
        both = jnp.broadcast_to(jnp.concatenate(tiles, axis=1), (128, 256))
        blocks[gap] = pltpu.roll(both, 0, 1, stride=1, stride_axis=0)[:, 128:]
    blocks[2] = jnp.broadcast_to(line[:, 256:257], (128, 128))
    blocks[-2] = jnp.broadcast_to(line[:, 768:769], (128, 128))
    for j in range(4):
        for i in range(4):
            tab[h, 128 * j : 128 * j + 128, 128 * i : 128 * i + 128] = blocks[max(-2, min(2, i - j))]


def block_of(values, j, i):
    return values[128 * j : 128 * j + 128, 128 * i : 128 * i + 128]


def add_distances(values, near, far, h):
    for gap in (-1, 0, 1):
        parts = [block_of(values, j, j + gap) for j in range(4) if 0 <= j + gap < 4]
        total = parts[0]
        for part in parts[1:]:
            total = total + part
        near[h, :, 128 * (gap + 1) : 128 * (gap + 2)] += total
    for k, blocks in enumerate((((0, 2), (0, 3), (1, 3)), ((2, 0), (3, 0), (3, 1)))):
        total = sum(block_of(values, j, i) for j, i in blocks)
        rows = total[0:8]
        for at in range(8, 128, 8):
            rows = rows + total[at : at + 8]
        far[h, k] += rows


def diagonal_sum(near, far):
    wide_rows = jnp.concatenate([near, jnp.zeros((128, 128), f32)], axis=1)
    half = 64
    while half:
        wide_rows = wide_rows[:half] + pltpu.roll(wide_rows[half : 2 * half], LG - half, 1)
        half //= 2
    tiles = [wide_rows[:, 128 * k : 128 * k + 128] for k in range(4)]
    none = jnp.zeros((1, 128), f32)
    plus = jnp.sum(far[0], axis=0, keepdims=True)
    minus = jnp.sum(far[1], axis=0, keepdims=True)
    return jnp.concatenate([tiles[1], tiles[2], plus, none, none, minus, tiles[3], tiles[0]], axis=1)


def prepare(me, gathered, rows):
    total = gathered.shape[0] * rows
    room = [
        pltpu.VMEM((total, 128), f32),
        pltpu.VMEM((TABLE, 128), f32),
        pltpu.VMEM((128, 128), f32),
        pltpu.VMEM((GROUP, 512, 128), f32),
    ]
    early = pl.pallas_call(
        early_body,
        in_specs=[SMEM, VMEM],
        out_shape=[o((FF, 128)), o((128, 512)), o((GROUP, 3 * WROWS, 128)), o((GROUP, 128, WROWS)), o((240, 128))]
        + [o((128, 128), f32), o((8, 2 * LG), f32)],
        scratch_shapes=room + [pltpu.VMEM((128, 128), f32)],
        name="prepare",
        **params(10**9, 2 * 10**6),
    )(me, gathered)
    late = pl.pallas_call(
        late_body,
        in_specs=[SMEM, VMEM],
        out_shape=[o((128, FF)), o((FF, 128)), o((FF, 128)), o((128, FF)), o((128, 512)), o((FF, 128))]
        + [o((128, 240)), o((128, 128)), o((128, 128)), o((GROUP, 128, 3 * WROWS)), o((GROUP, WROWS, 128))],
        scratch_shapes=room,
        name="late",
        **params(3 * 10**9, 10 * 10**6),
    )(me, gathered)
    return early, late


def column(cols, k):
    return cols[:D, k : k + 1]


def valid_keys(length):
    return row_iota((LG, 1)) * GROUP < length


def set_tail(hid):
    hid[FF:, :] = jnp.where(row_iota((512 - FF, hid.shape[1])) == 0, 1.0, 0.0).astype(bf16)


def conv_columns(cols, cb):
    for k in range(KERNEL + 1):
        cb[k] = jnp.broadcast_to(cols[:D, C_DWB + k : C_DWB + k + 1], (D, 128))


def wide(tile, copies=4):
    return jnp.concatenate([tile] * copies, axis=1)


def first_body(
    len_ref, xp_ref, xf_ref, cols_ref, up_ref, dn_ref, wqkv_ref, wo_ref, pw_ref, base_ref,
    lf_ref, xa_ref, nrm_ref, qkv_ref, prob_ref, att_ref, aa_ref, xc_ref, cn_ref, gat_ref, sig_ref, rgt_ref,
    ra_ref, rc_ref, dep_ref, st_ref,
    hid, one, cb, tab, run,
):
    u = pl.program_id(0)
    length = len_ref[u]

    @pl.when(u == 0)
    def _():
        set_tail(hid)
        run[...] = jnp.zeros_like(run)
        conv_columns(cols_ref, cb)
        for h in range(HEADS):
            spread_table(base_ref[h : h + 1, :], tab, h)

    cols = cols_ref

    def ffn_up(r, held):
        low = ext(xf_ref[0, :, span(r)] * column(cols, C_F1) + column(cols, C_F1 + 1))
        lf_ref[0, :, span(r)] = low
        return dot(up_ref[...], low)

    def ffn_down(r, half):
        hid[:FF, span(r)] = (half + half * jnp.tanh(half)).astype(bf16)
        return dot(dn_ref[...], hid[:, span(r)])[:D]

    def ffn_norm(r, branch):
        after = xp_ref[0, :, span(r)].astype(f32) + branch
        one[:, span(r)] = after
        xhat, rstd = norm(after)
        xa_ref[0, :, span(r)] = xhat
        ra_ref[0, 0:1, span(r)] = rstd
        low = ext(xhat * column(cols, C_AT) + column(cols, C_AT + 1))
        nrm_ref[0, 128 * r : 128 * r + 128, :] = low
        return dot(wqkv_ref[r], low)

    made = [None] * GROUP

    def ffn_keep(r, found):
        made[r] = found

    skewed(GROUP, (ffn_up, ffn_down, ffn_norm, ffn_keep))
    for w in range(3):
        joined = join_windows([made[r][WROWS * w : WROWS * w + WROWS] for r in range(GROUP)])
        qkv_ref[0, GP * w : GP * w + GP, :] = joined.astype(bf16)
    keys = valid_keys(length)

    def rows(w, h):
        return slice(GP * w + HP * h, GP * w + HP * h + HP)

    def score(h, held):
        return dot_tn(qkv_ref[0, rows(1, h), :], qkv_ref[0, rows(0, h), :])

    def soften(h, raw):
        scores = raw * (SCALE * LOG2E) + tab[h]
        scores = jnp.where(keys, scores, NEG_FILL * LOG2E)
        peak = jnp.max(scores, axis=0, keepdims=True)
        power = jnp.exp2(scores - peak)
        total = jnp.sum(power, axis=0, keepdims=True)
        prob_ref[0, h] = (power * (1.0 / total)).astype(bf16)

    def mix(h, held):
        mixed = dot(qkv_ref[0, rows(2, h), :], prob_ref[0, h])
        if h < GROUP:
            mixed = jnp.where(row_iota((HP, LG)) == HEAD, 1.0, mixed)
        att_ref[0, rows(0, h), :] = mixed.astype(bf16)

    skewed(HEADS, (score, soften, mix))

    def project(r, held):
        return dot(wo_ref[r], window(att_ref.at[0], r))[:D]

    def gate_in(r, mixed):
        after = one[:, span(r)] + mixed
        aa_ref[0, :, span(r)] = after
        xhat, rstd = norm(after)
        xc_ref[0, :, span(r)] = xhat
        rc_ref[0, 0:1, span(r)] = rstd
        low = ext(xhat * column(cols, C_CV) + column(cols, C_CV + 1))
        cn_ref[0, :, span(r)] = low
        return dot(pw_ref[...], low)

    def gate_out(r, pre):
        mask = plane_mask(r, length)
        sig = (0.5 + 0.5 * jnp.tanh(pre[D:])) * mask
        gated = (pre[:D] + pre[:D]) * sig
        gat_ref[0, :, span(r)] = gated
        sig_ref[0, :, span(r)] = sig
        rgt_ref[0, :, span(r)] = gated * (1.0 - sig)

    skewed(GROUP, (project, gate_in, gate_out))

    def conv(f, carry):
        at = slice(8 * f, 8 * f + 8)
        tiles = [gat_ref[0, at, span(r)] for r in range(GROUP)]
        totals = [wide(cb[0, at, :])] * GROUP
        for m in range(-HALF, HALF + GROUP):
            here = shifted(tiles, m)
            for r in range(GROUP):
                k = m + HALF - r
                if 0 <= k < KERNEL:
                    totals[r] = totals[r] + wide(cb[1 + k, at, :]) * here
        for r in range(GROUP):
            dep_ref[0, at, span(r)] = totals[r]
        return carry

    for f in range(D // 8):
        conv(f, 0)

    count = length.astype(f32)
    mask = jnp.concatenate([plane_mask(r, length) for r in range(GROUP)], axis=1)
    dep = dep_ref[0]
    mean = jnp.sum(dep * mask, axis=1, keepdims=True) / count
    gap = (dep - mean) * mask
    spread = jnp.sum(gap * gap, axis=1, keepdims=True)
    old_mean, old_spread, old_count = run[0], run[1], run[2]
    new_count = old_count + count
    step = mean - old_mean
    new_mean = old_mean + step * (count / new_count)
    new_spread = old_spread + spread + step * step * (old_count * count / new_count)
    run[0] = new_mean
    run[1] = new_spread
    run[2] = new_count

    @pl.when(u == pl.num_programs(0) - 1)
    def _():
        lanes = lane_iota((D, 128))
        picked = jnp.where(lanes == 0, run[0], jnp.where(lanes == 1, run[1], jnp.where(lanes == 2, run[2], 0.0)))
        line = pad8(picked).T[0:8]
        for d in range(st_ref.shape[0]):
            st_ref[d] = line


def first(devices, lengths, xp, xf, weights):
    utts = xp.shape[0]
    per = [
        (LOW, bf16),
        (BIG, f32),
        ((GP, LG), bf16),
        ((3 * GP, LG), bf16),
        ((HEADS, LG, LG), bf16),
        ((GP, LG), bf16),
        (BIG, f32),
        (BIG, f32),
        (LOW, bf16),
        (BIG, f32),
        (BIG, f32),
        (BIG, f32),
        ((8, MAXLEN), f32),
        ((8, MAXLEN), f32),
        (BIG, f32),
    ]
    line = (devices, 8, 128)
    return pl.pallas_call(
        first_body,
        grid=(utts,),
        in_specs=[SMEM, per_utt(BIG), per_utt(BIG)] + [whole(w.shape) for w in weights],
        out_specs=[per_utt(s) for s, k in per] + [whole(line)],
        out_shape=[o((utts,) + s, k) for s, k in per] + [o(line, f32)],
        scratch_shapes=[
            pltpu.VMEM((512, MAXLEN), bf16),
            pltpu.VMEM(BIG, f32),
            pltpu.VMEM((KERNEL + 1, D, 128), f32),
            pltpu.VMEM((HEADS, LG, LG), f32),
            pltpu.VMEM((3, D, 128), f32),
        ],
        name="first",
        **params(10 * 10**9, 60 * 10**6),
    )(lengths, xp, xf, *weights)


def second_body(
    len_ref, stats_ref, cot_ref, aa_ref, dep_ref, cols_ref, up_ref, upp_ref, dn_ref, dnp_ref, pr_ref, prp_ref,
    out_ref, bgd_ref, gc_ref, sums_ref, stc_ref, gdn_ref, gup_ref, gpr_ref, vec_ref,
    hid, acc,
):
    u = pl.program_id(0)
    length = len_ref[u]
    cols = cols_ref

    @pl.when(u == 0)
    def _():
        set_tail(hid)
        parts = stats_ref.shape[0]
        count = jnp.zeros((1, 128), f32)
        total = jnp.zeros((1, 128), f32)
        for d in range(parts):
            many = stats_ref[d, 2:3, :]
            count = count + many
            total = total + many * stats_ref[d, 0:1, :]
        here = lane_iota((1, 128)) < D
        count = jnp.where(here, count, 1.0)
        mean = total / count
        spread = jnp.zeros((1, 128), f32)
        for d in range(parts):
            gap = stats_ref[d, 0:1, :] - mean
            spread = spread + stats_ref[d, 1:2, :] + stats_ref[d, 2:3, :] * gap * gap
        scale = lax.rsqrt(spread / count + EPS_NORM)
        at = row_iota((128, 128))
        table = jnp.where(at == 0, mean, jnp.where(at == 1, scale, jnp.where(at == 2, 1.0 / count, 0.0)))
        stc_ref[...] = table.T
        gdn_ref[...] = jnp.zeros_like(gdn_ref)
        gup_ref[...] = jnp.zeros_like(gup_ref)
        gpr_ref[...] = jnp.zeros_like(gpr_ref)
        vec_ref[...] = jnp.zeros_like(vec_ref)
        acc[...] = jnp.zeros_like(acc)

    half_gain = 0.5 * column(cols, C_BN)
    half_bias = 0.5 * column(cols, C_BN + 1)

    def enter(r, held):
        normal = (dep_ref[0, :, span(r)] - stc_ref[:D, 0:1]) * stc_ref[:D, 1:2]
        z = normal * half_gain + half_bias
        t = jnp.tanh(z)
        act = z + z * t
        act_low = ext(act)
        slope = (1.0 + t) * (1.0 + z * (1.0 - t))
        return act_low, normal, slope, dot(pr_ref[...], act_low)[:D]

    def ffn_up(r, held):
        act_low, normal, slope, moved = held
        after_conv = aa_ref[0, :, span(r)] + moved
        xhat, rstd = norm(after_conv)
        low = ext(xhat * column(cols, C_F2) + column(cols, C_F2 + 1))
        return act_low, normal, slope, after_conv, xhat, rstd, low, dot(up_ref[...], low)

    def ffn_down(r, held):
        act_low, normal, slope, after_conv, xhat, rstd, low, half = held
        t = jnp.tanh(half)
        hid[:FF, span(r)] = (half + half * t).astype(bf16)
        bend = (1.0 + t) * (1.0 + half * (1.0 - t))
        return act_low, normal, slope, after_conv, xhat, rstd, low, bend, dot(dn_ref[...], hid[:, span(r)])[:D]

    def finish(r, held):
        act_low, normal, slope, after_conv, xhat, rstd, low, bend, branch = held
        mask = plane_mask(r, length)
        xhat_f, rstd_f = norm(after_conv + branch)
        made = (xhat_f * column(cols, C_FN) + column(cols, C_FN + 1)) * mask
        out_ref[0, :, span(r)] = made.astype(bf16)
        up_grad = cot_ref[0, :, span(r)].astype(f32) * mask
        vec_ref[2] += fold(up_grad * xhat_f)
        vec_ref[3] += fold(up_grad)
        grad_two = norm_back(up_grad, xhat_f, rstd_f, column(cols, C_FN))
        branch = pad8(grad_two).astype(bf16)
        gdn_ref[...] += dot_nt(hid[:, span(r)], branch)
        return act_low, normal, slope, xhat, rstd, low, bend, grad_two, dot(dnp_ref[...], branch)

    def ffn_back(r, held):
        act_low, normal, slope, xhat, rstd, low, bend, grad_two, back = held
        pre_low = (bend * back).astype(bf16)
        gup_ref[...] += dot_nt(pre_low, low)
        return act_low, normal, slope, xhat, rstd, grad_two, dot(upp_ref[...], pre_low)[:D]

    def leave(r, held):
        act_low, normal, slope, xhat, rstd, grad_two, back = held
        vec_ref[0] += fold(back * xhat)
        vec_ref[1] += fold(back)
        grad_conv = grad_two + norm_back(back, xhat, rstd, column(cols, C_F2))
        gc_ref[0, :, span(r)] = grad_conv
        project = pad8(grad_conv).astype(bf16)
        gpr_ref[...] += dot_nt(act_low, project)
        return normal, slope, dot(prp_ref[...], project)[:D]

    def last(r, held):
        normal, slope, back = held
        batch = slope * back
        bgd_ref[0, :, span(r)] = batch
        acc[0] += fold(batch * normal)
        acc[1] += fold(batch)

    skewed(GROUP, (enter, ffn_up, ffn_down, finish, ffn_back, leave, last))

    @pl.when(u == pl.num_programs(0) - 1)
    def _():
        lanes = lane_iota((D, 128))
        gain = jnp.sum(acc[0], axis=1, keepdims=True)
        shift = jnp.sum(acc[1], axis=1, keepdims=True)
        line = pad8(jnp.where(lanes == 0, gain, jnp.where(lanes == 1, shift, 0.0))).T[0:8]
        for d in range(sums_ref.shape[0]):
            sums_ref[d] = line


def second(lengths, stats, cot, aa, dep, weights):
    utts = cot.shape[0]
    big = (D, MAXLEN)
    outs = [
        (per_utt(big), (utts,) + big, bf16),
        (per_utt(big), (utts,) + big, f32),
        (per_utt(big), (utts,) + big, f32),
    ]
    for s in (stats.shape, (128, 128), (512, 128), (FF, 128), (128, 128), (4, D, 128)):
        outs.append((whole(s), s, f32))
    return pl.pallas_call(
        second_body,
        grid=(utts,),
        in_specs=[SMEM, whole(stats.shape)] + [per_utt(big)] * 3 + [whole(w.shape) for w in weights],
        out_specs=[o[0] for o in outs],
        out_shape=[jax.ShapeDtypeStruct(o[1], o[2]) for o in outs],
        scratch_shapes=[
            pltpu.VMEM((512, MAXLEN), bf16),
            pltpu.VMEM((2, D, 128), f32),
        ],
        name="second",
        **params(15000000000, 30000000),
    )(lengths, stats, cot, aa, dep, *weights)


def third_body(
    len_ref, sums_ref, stc_ref, bgd_ref, dep_ref, gat_ref, ri_ref, ra_ref, rc_ref,
    gc_far, xc_far, cn_far, sig_far, rgt_far, att_far, qkv_far, prob_far, nrm_far, lf_far, xa_far, xf_far,
    cols_ref, up_ref, upp_ref, dnp_ref, wqkv_t_ref, wob_ref, pwp_ref,
    grad_ref, gdn_ref, gup_ref, gpw_ref, gqkv_ref, go_ref, rel_ref, vec_ref,
    gc_ref, xc_ref, cn_ref, sig_ref, rgt_ref, att_ref, qkv_ref, prob_ref, nrm_ref, lf_ref, xa_ref, xf_ref, sems,
    hid, dgx, dgs, olg, agr, back_s, gg, near_s, far_s, cb, tot,
):
    far = (gc_far, xc_far, cn_far, sig_far, rgt_far, att_far, qkv_far, prob_far, nrm_far, lf_far, xa_far, xf_far)
    near = (gc_ref, xc_ref, cn_ref, sig_ref, rgt_ref, att_ref, qkv_ref, prob_ref, nrm_ref, lf_ref, xa_ref, xf_ref)
    u = pl.program_id(0)
    utts = pl.num_programs(0) - 1
    slot = 1 - u % 2

    def copies(step):
        at = step % 2
        return [pltpu.make_async_copy(far[i].at[step], near[i].at[at], sems.at[i, at]) for i in range(len(far))]

    cols = cols_ref

    @pl.when(u == 0)
    def _():
        set_tail(hid)
        conv_columns(cols_ref, cb)
        parts = sums_ref.shape[0]
        total = sums_ref[0]
        for d in range(1, parts):
            total = total + sums_ref[d]
        tot[...] = jnp.concatenate([total, jnp.zeros((120, 128), f32)], axis=0).T
        for ref in (gdn_ref, gup_ref, gpw_ref, gqkv_ref, go_ref, vec_ref, near_s, far_s):
            ref[...] = jnp.zeros_like(ref)

    @pl.when(u < utts)
    def _():
        for copy in copies(u):
            copy.start()

    @pl.when(u > 0)
    def _():
        for copy in copies(u - 1):
            copy.wait()

    def front():
        scale = stc_ref[:D, 1:2]
        lead = column(cols, C_BN) * scale
        share = lead * stc_ref[:D, 2:3]
        shift_part = share * tot[:D, 1:2]
        gain_part = share * tot[:D, 0:1] * scale
        for r in range(GROUP):
            normal = dep_ref[0, :, span(r)] - stc_ref[:D, 0:1]
            mask = plane_mask(r, len_ref[u])
            dgx[:, span(r)] = bgd_ref[0, :, span(r)] * lead - mask * (shift_part + normal * gain_part)

        def conv(f, carry):
            at = slice(8 * f, 8 * f + 8)
            tiles = [dgx[at, span(r)] for r in range(GROUP)]
            gated = [gat_ref[0, at, span(r)] for r in range(GROUP)]
            totals = [None] * GROUP
            taps = [None] * KERNEL
            for m in range(-HALF, HALF + GROUP):
                here = shifted(tiles, m)
                for r in range(GROUP):
                    k = r + HALF - m
                    if 0 <= k < KERNEL:
                        term = wide(cb[1 + k, at, :]) * here
                        totals[r] = term if totals[r] is None else totals[r] + term
                        part = fold(gated[r] * here)
                        taps[k] = part if taps[k] is None else taps[k] + part
            vec_ref[6, at, :] += fold(tiles[0] + tiles[1] + tiles[2])
            for k in range(KERNEL):
                vec_ref[7 + k, at, :] += taps[k]
            for r in range(GROUP):
                gg[at, span(r)] = totals[r]
            return carry

        for f in range(D // 8):
            conv(f, 0)

    def back():
        def gate(r, held):
            grad = gg[:, span(r)]
            left = grad * sig_ref[slot, :, span(r)]
            right = grad * rgt_ref[slot, :, span(r)]
            pre_low = jnp.concatenate([left, right], axis=0).astype(bf16)
            gpw_ref[...] += dot_nt(pre_low, cn_ref[slot, :, span(r)])
            return dot(pwp_ref[...], pre_low)[:D]

        def residual(r, back):
            xhat = xc_ref[slot, :, span(r)]
            vec_ref[0] += fold(back * xhat)
            vec_ref[1] += fold(back)
            grad = gc_ref[slot, :, span(r)] + norm_back(back, xhat, rc_ref[0, 0:1, span(r)], column(cols, C_CV))
            dgs[:, span(r)] = grad
            low = pad8(grad).astype(bf16)
            olg[128 * r : 128 * r + 128, :] = low
            return dot(wob_ref[r], low)

        made = [None] * GROUP

        def keep(r, found):
            go_ref[r] += dot_nt(window(att_ref.at[slot], r), olg[128 * r : 128 * r + 128, :])
            made[r] = found

        skewed(GROUP, (gate, residual, keep))
        agr[...] = join_windows(made).astype(bf16)

        def rows(w, h):
            return slice(GP * w + HP * h, GP * w + HP * h + HP)

        def enter(h, held):
            grad = agr[rows(0, h), :]
            back_s[rows(2, h), :] = dot_nt(grad, prob_ref[slot, h]).astype(bf16)
            return dot_tn(qkv_ref[slot, rows(2, h), :], grad)

        def soften(h, prob_grad):
            probs = prob_ref[slot, h].astype(f32)
            inner = jnp.sum(probs * prob_grad, axis=0, keepdims=True)
            score = probs * (prob_grad - inner)
            add_distances(score, near_s, far_s, h)
            return score.astype(bf16)

        def turn(h, low):
            back_s[rows(0, h), :] = (dot(qkv_ref[slot, rows(1, h), :], low) * SCALE).astype(bf16)
            back_s[rows(1, h), :] = (dot_nt(qkv_ref[slot, rows(0, h), :], low) * SCALE).astype(bf16)

        skewed(HEADS, (enter, soften, turn))

        def project(r, held):
            stack = jnp.concatenate([window(back_s, r, GP * w) for w in range(3)], axis=0)
            gqkv_ref[r] += dot_nt(stack, nrm_ref[slot, 128 * r : 128 * r + 128, :])
            return dot(wqkv_t_ref[r], stack)[:D], dot(up_ref[...], lf_ref[slot, :, span(r)])

        def ffn_in(r, held):
            back, half = held
            xhat = xa_ref[slot, :, span(r)]
            vec_ref[2] += fold(back * xhat)
            vec_ref[3] += fold(back)
            grad = dgs[:, span(r)] + norm_back(back, xhat, ra_ref[0, 0:1, span(r)], column(cols, C_AT))
            low = pad8(grad).astype(bf16)
            return grad, low, half, dot(dnp_ref[...], low)

        def ffn_mid(r, held):
            grad, branch, half, back = held
            t = jnp.tanh(half)
            hid[:FF, span(r)] = (half + half * t).astype(bf16)
            pre_low = ((1.0 + t) * (1.0 + half * (1.0 - t)) * back).astype(bf16)
            gdn_ref[...] += dot_nt(hid[:, span(r)], branch)
            gup_ref[...] += dot_nt(pre_low, lf_ref[slot, :, span(r)])
            return grad, dot(upp_ref[...], pre_low)[:D]

        def ffn_out(r, held):
            grad, back = held
            xhat = xf_ref[slot, :, span(r)]
            vec_ref[4] += fold(back * xhat)
            vec_ref[5] += fold(back)
            grad_ref[0, :, span(r)] = grad + norm_back(back, xhat, ri_ref[0, 0:1, span(r)], column(cols, C_F1))

        skewed(GROUP, (project, ffn_in, ffn_mid, ffn_out))

    @pl.when(u == 0)
    def _():
        front()

    @pl.when((u > 0) & (u < utts))
    def _():
        back()
        front()

    @pl.when(u == utts)
    def _():
        back()
        found = []
        for h in range(HEADS):
            found.append(diagonal_sum(near_s[h], far_s[h]))
        stacked = jnp.concatenate(found + [jnp.zeros((4, 2 * LG), f32)], axis=0)
        high = stacked.astype(bf16)
        rest = stacked - high.astype(f32)
        mid = rest.astype(bf16)
        rest = rest - mid.astype(f32)
        select = distance_select()
        rel_ref[...] = dot_nt(high, select) + dot_nt(mid, select) + dot_nt(rest.astype(bf16), select)


def third(lengths, sums, stc, soon, later, weights):
    utts = soon[0].shape[0]
    big = (D, MAXLEN)
    outs = [(one_late(big), (utts,) + big)]
    for s in ((512, 128), (FF, 128), (240, 128), (GROUP, 3 * WROWS, 128), (GROUP, WROWS, 128), (8, 256), (22, D, 128)):
        outs.append((whole(s), s))
    return pl.pallas_call(
        third_body,
        grid=(utts + 1,),
        in_specs=[SMEM, whole(sums.shape), whole(stc.shape)]
        + [at_most(s.shape[1:], utts) for s in soon[:3]]
        + [one_late(s.shape[1:]) for s in soon[3:]]
        + [pl.BlockSpec(memory_space=pl.ANY)] * len(later)
        + [whole(w.shape) for w in weights],
        out_specs=[o[0] for o in outs],
        out_shape=[jax.ShapeDtypeStruct(o[1], f32) for o in outs],
        scratch_shapes=[pltpu.VMEM((2,) + s.shape[1:], s.dtype) for s in later]
        + [
            pltpu.SemaphoreType.DMA((len(later), 2)),
            pltpu.VMEM((512, MAXLEN), bf16),
            pltpu.VMEM(big, f32),
            pltpu.VMEM(big, f32),
            pltpu.VMEM((GP, LG), bf16),
            pltpu.VMEM((GP, LG), bf16),
            pltpu.VMEM((3 * GP, LG), bf16),
            pltpu.VMEM(big, f32),
            pltpu.VMEM((HEADS, 128, 384), f32),
            pltpu.VMEM((HEADS, 2, 8, 128), f32),
            pltpu.VMEM((KERNEL + 1, D, 128), f32),
            pltpu.VMEM((128, 128), f32),
        ],
        name="third",
        **params(20000000000, 80000000),
    )(lengths, sums, stc, *soon, *later, *weights)


def clean(block):
    return jnp.where(lane_iota(block.shape) < D, block, 0.0)


def set_rows(tb, wt, ref, at):
    lanes = lane_iota((D, 128))
    table = jnp.zeros((D, 128), f32)
    for k in range(len(at)):
        table = jnp.where(lanes == k, jnp.sum(ref[k], axis=1, keepdims=True), table)
    wt[...] = pad8(table).T
    for k, to in enumerate(at):
        tb[to : to + 1, :] = wt[k : k + 1, :]


def set_ffn(tb, base, dn_ref, up_ref):
    tb[base + 486 : base + 967, :] = 0.5 * clean(dn_ref[0 : FF + 1, :])
    for q in range(4):
        block = pad8(up_ref[D * q : D * q + D, :]).T
        tb[pl.ds(base + 2 + q, D, stride=4), :] = block[:D]
        tb[base + 482 + q : base + 483 + q, :] = block[D : D + 1]


def flatten(tb, base, flat, at_row, y_count, offset):
    for k in range(15):
        at = 128 * k + offset
        first_row, col = at // D, at % D
        many = (y_count - k + 14) // 15
        here = lane_iota((many, 128))
        got = tb[pl.ds(base + first_row, many, stride=16), :]
        if col:
            got = pltpu.roll(got, 128 - col, 1)
        then = pltpu.roll(tb[pl.ds(base + first_row + 1, many, stride=16), :], D - col, 1)
        got = jnp.where(here < D - col, got, then)
        if 2 * D - col < 128:
            then = pltpu.roll(tb[pl.ds(base + first_row + 2, many, stride=16), :], 2 * D - col, 1)
            got = jnp.where(here < 2 * D - col, got, then)
        flat[pl.ds(at_row + k, many, stride=15), :] = got


SPLIT = F2 - TAIL
ROWS_LAST = ROWS_TAIL - SPLIT
LAST_AT = TAIL_AT + D * SPLIT
LAST_Y = LAST_AT // 128
LAST_COUNT = (LIVE - 1) // 128 - LAST_Y + 1


def ahead_body(dn_ref, up_ref, vec_ref, out_ref, tb, wt):
    tb[0:8, :] = jnp.zeros((8, 128), f32)
    tb[8 + ROWS_LAST :, :] = jnp.zeros((tb.shape[0] - 8 - ROWS_LAST, 128), f32)
    set_rows(tb, wt, vec_ref, (8, 9, 8 + FN - F2, 9 + FN - F2))
    set_ffn(tb, 8, dn_ref, up_ref)
    flatten(tb, 7, out_ref, 0, LAST_COUNT, D + 128 * LAST_Y - LAST_AT)


def pack_ahead(dn, up, vec):
    return pl.pallas_call(
        ahead_body,
        out_shape=o((LAST_COUNT, 128), f32),
        scratch_shapes=[pltpu.VMEM((ROWS_LAST + 24, 128), f32), pltpu.VMEM((128, 128), f32)],
        name="ahead",
        **params(2 * 10**9, 8 * 10**6),
    )(dn, up, vec)


def pack_body(
    me_ref, last_ref, dn1_ref, up1_ref, pr_ref, pw_ref, qkv_ref, o_ref, rel_ref, vec_ref, sums_ref,
    keep_ref, send_ref, tb, flat, stage, wt,
):
    tb[ROWS_HEAD:TAIL, :] = jnp.zeros((TAIL - ROWS_HEAD, 128), f32)
    tb[F2:, :] = jnp.zeros((tb.shape[0] - F2, 128), f32)
    set_rows(
        tb, wt, vec_ref, (CV, CV + 1, AT, AT + 1, F1, F1 + 1, CV + 259) + tuple(CV + 244 + k for k in range(KERNEL))
    )
    tb[CV + 260 : CV + 262, :] = sums_ref[0, 0:2, :]
    set_ffn(tb, F1, dn1_ref, up1_ref)
    for q in range(2):
        block = pad8(pw_ref[D * q : D * q + D, :]).T
        tb[pl.ds(CV + 2 + q, D, stride=2), :] = block[:D]
        tb[CV + 242 + q : CV + 243 + q, :] = block[D : D + 1]
    tb[CV + 262 : CV + 383, :] = clean(pr_ref[0 : D + 1, :])

    def gathered(ref, base):
        wt[...] = jnp.zeros_like(wt)
        for to, r, src, many in segments():
            start = base + to - WIN[r]
            wt[src : src + many, :] += ref[r, start : start + many, :]
        return wt[...]

    for w, at, bias_at in ((0, AT + 2, AT + 122), (1, AT + 123, None), (2, AT + 243, AT + 363)):
        block = gathered(qkv_ref, WROWS * w).T
        tb[at : at + D, :] = block[:D]
        if bias_at is not None:
            tb[bias_at : bias_at + 1, :] = block[D : D + 1]
    tb[AT + 364 : AT + 484, :] = clean(gathered(o_ref, 0)[:D])
    bias = sum(o_ref[r, MARKS[r] : MARKS[r] + 1, :] for r in range(GROUP))
    tb[AT + 484 : AT + 485, :] = clean(bias)

    tail_y = TAIL_AT // 128
    flat[LAST_Y + LAST_COUNT :, :] = jnp.zeros((flat.shape[0] - LAST_Y - LAST_COUNT, 128), f32)
    flat[REL_AT // 128 + 1 : tail_y, :] = jnp.zeros((tail_y - REL_AT // 128 - 1, 128), f32)
    flatten(tb, 0, flat, 0, REL_AT // 128 + 1, 0)
    flatten(tb, TAIL - 1, flat, tail_y, LAST_Y - tail_y + 1, 128 * tail_y - TAIL_AT + D)
    flat[LAST_Y : LAST_Y + 1, :] += last_ref[0:1, :]
    flat[LAST_Y + 1 : LAST_Y + LAST_COUNT, :] = last_ref[1:, :]
    here = lane_iota((1, 128))
    width = 2 * REL + 1
    for h in range(HEADS):
        at = REL_AT + width * h
        for y in range(at // 128, (at + width - 1) // 128 + 1):
            lo, hi = max(at - 128 * y, 0), min(at + width - 128 * y, 128)
            shift = (at - 128 * y) % 256
            turned = rel_ref[h : h + 1, :]
            if shift:
                turned = pltpu.roll(turned, shift, 1)
            flat[y : y + 1, :] += jnp.where((here >= lo) & (here < hi), turned[:, :128], 0.0)
    parts, padded = 2 * keep_ref.shape[0], keep_ref.shape[1]
    rows = flat.shape[0] // parts
    for d in range(parts):
        stage[d, 0:rows, :] = flat[rows * d : rows * (d + 1), :]
        if rows < padded:
            stage[d, rows:padded, :] = jnp.zeros((padded - rows, 128), f32)
    for offset in range(0, parts, 2):
        keep_ref[place(offset, parts)] = stage[me_ref[0] ^ offset]
        send_ref[place(offset, parts)] = stage[me_ref[0] ^ (offset + 1)]


def pack(parts, rows, me, grads):
    half = o((parts // 2, whole_tiles(rows), 128), f32)
    return pl.pallas_call(
        pack_body,
        in_specs=[SMEM] + [VMEM] * len(grads),
        out_shape=[half, half],
        scratch_shapes=[
            pltpu.VMEM((F2 + 24, 128), f32),
            pltpu.VMEM((parts * rows, 128), f32),
            pltpu.VMEM((parts, whole_tiles(rows), 128), f32),
            pltpu.VMEM((128, 128), f32),
        ],
        name="pack",
        **params(10**9, 5 * 10**6),
    )(me, *grads)


def update_tables(total_len):
    rates = np.zeros(total_len, np.float32)
    decays = np.zeros(total_len, np.float32)
    vector, gain, ffn = (D, 0.1, 0.0), (D, 0.3, 0.0), lambda n, fan: (n, fan**-0.5, 0.01)
    block = [gain, vector, ffn(D * FF, D), (FF, 0.1, 0.0), ffn(FF * D, FF), vector]
    square = ffn(D * D, D)
    pieces = block + [gain, vector, square, vector, square, square, vector, ffn(D * D, 6.0 * D / MAXLEN), vector]
    pieces += [(HEADS * (2 * REL + 1), 0.5, 0.0)]
    pieces += [gain, vector, ffn(2 * D * D, D), (2 * D, 0.1, 0.0), ffn(KERNEL * D, KERNEL), vector, gain, vector]
    pieces += [square, vector] + block + [gain, vector]
    offset = 0
    for entries, rate, decay in pieces:
        rates[offset : offset + entries] = rate
        decays[offset : offset + entries] = decay
        offset += entries
    return rates, decays


def whole_tiles(rows):
    return -(-rows // 8) * 8


def digits(devices):
    found, stride = [], 1
    while stride < devices:
        size = min(2 if stride == 1 else 4, devices // stride)
        found.append((stride, size))
        stride *= size
    return found


def place(offset, devices):
    at, weight = 0, devices
    for stride, size in digits(devices):
        weight //= size
        at = at + ((offset // stride) % size) * weight
    return at


def partner(values, offset, devices):
    return lax.ppermute(values, "dp", [(i, i ^ offset) for i in range(devices)])


def gather(values, devices, beside):
    held, made = values[None], []
    for k, (stride, size) in enumerate(reversed(digits(devices))):
        parts = [held] + [partner(held, stride * j, devices) for j in range(1, size)]
        if k < len(beside):
            parts, found = lax.optimization_barrier((parts, beside[k]))
            made.append(found)
        held = jnp.concatenate(parts, axis=0)
    return held, made + beside[len(made) :]


def scatter_sum(keep, send, devices, beside):
    total = keep + partner(send, 1, devices)
    for stride, size in digits(devices)[1:]:
        parts = total.reshape((size, total.shape[0] // size) + total.shape[1:])
        found = [partner(parts[j], stride * j, devices) for j in range(1, size)]
        if stride == 2:
            found, beside = lax.optimization_barrier((found, beside))
        total = parts[0]
        for part in found:
            total = total + part
    return total, beside


def local(frames, lengths, cotangent, master, moment_one, moment_two, average):
    shard_len = master.shape[0]
    devices = lax.axis_size("dp")
    rows = shard_len // 128
    me = lax.axis_index("dp").astype(jnp.int32).reshape(1)
    entered = enter(jnp.transpose(frames, (0, 2, 1)))
    mine = jnp.pad(master.astype(bf16).reshape(rows, 128), ((0, whole_tiles(rows) - rows), (0, 0)))
    cp = reorder(inward_body, jnp.transpose(cotangent, (0, 2, 1)), entered[3], "inward")
    gathered, (entered, cp) = gather(mine, devices, [entered, cp])
    xp, xf, rs_in, pm = entered
    early, late = prepare(me, gathered, rows)
    up1, dn1, wqkv, wo, pw, cols, base = early
    upp1, dnp1, up2, upp2, dn2, dnp2, pwp, pr, prp, wqkvt, wob = late
    lf, xa, nrm, qkv, prob, att, aa, xc, cn, gat, sig, rgt, ra, rc, dep, st = first(
        devices, lengths, xp, xf, (cols, up1, dn1, wqkv, wo, pw, base)
    )
    stats = lax.all_to_all(st, "dp", 0, 0)
    out, bgd, gc, sums, stc, gdn2, gup2, gpr, vec2 = second(
        lengths, stats, cp, aa, dep, (cols, up2, upp2, dn2, dnp2, pr, prp)
    )
    all_sums = lax.all_to_all(sums, "dp", 0, 0)
    last = pack_ahead(gdn2, gup2, vec2)
    out = reorder(outward_body, out, pm, "outward")
    (all_sums, last, out) = lax.optimization_barrier((all_sums, last, out))
    grad, gdn1, gup1, gpw, gqkv, go, rel, vec3 = third(
        lengths, all_sums, stc,
        (bgd, dep, gat, rs_in, ra, rc),
        (gc, xc, cn, sig, rgt, att, qkv, prob, nrm, lf, xa, xf),
        (cols, up1, upp1, dnp1, wqkvt, wob, pwp),
    )
    keep, send = pack(devices, rows, me, (last, gdn1, gup1, gpr, gpw, gqkv, go, rel, vec3, sums))
    gin = reorder(leave_body, grad, pm, "leave")
    reduced, gin = scatter_sum(keep, send, devices, gin)
    reduced = reduced.reshape(-1)[:shard_len]
    rates_np, decays_np = update_tables(shard_len * devices)
    start_at = lax.axis_index("dp") * shard_len
    rates = lax.dynamic_slice_in_dim(jnp.asarray(rates_np), start_at, shard_len)
    decays = lax.dynamic_slice_in_dim(jnp.asarray(decays_np), start_at, shard_len)
    correction = 1.0 - 0.5**STEP
    new_one = 0.5 * moment_one + 0.5 * reduced
    new_two = 0.5 * moment_two + 0.5 * reduced * reduced
    direction = new_one / correction / (jnp.sqrt(new_two / correction) + EPS_ADAM)
    new_master = master - rates * (direction + decays * master)
    new_average = 0.75 * average + 0.25 * new_master
    return (
        jnp.transpose(out, (0, 2, 1)),
        jnp.transpose(gin, (0, 2, 1)),
        reduced,
        new_master,
        new_one,
        new_two,
        new_average,
    )


def solution(mesh):
    three = P("dp", None, None)
    one = P("dp")
    in_specs = (three, one, three, one, one, one, one)
    out_specs = (three, three, one, one, one, one, one)
    return jax.shard_map(local, mesh=mesh, in_specs=in_specs, out_specs=out_specs, check_vma=False)
```

```python
import math

import jax
import jax.numpy as jnp
import numpy as np
from jax import lax
from jax.experimental import pallas as pl
from jax.experimental.pallas import tpu as pltpu
from jax.sharding import PartitionSpec as P

D = 120
HEADS = 4
FF = 480
KERNEL = 15
GROUP = 3
REL = 127
STEP = 5
MAXLEN = 1536
LG = 512
HEAD = 90
HP = 96
GP = HEADS * HP
HALF = KERNEL // 2
WIN = (0, 112, 240)
WROWS = 144
MARKS = tuple(HP * r + HEAD - WIN[r] for r in range(GROUP))

EPS_NORM = 1e-05
EPS_ADAM = 1e-08
NEG_FILL = -1000000000.0
LOG2E = math.log2(math.e)
SCALE = HEAD ** (-0.5)

f32 = jnp.float32
bf16 = jnp.bfloat16
VMEM_BYTES = 58 * 2**20

REL_AT = 174240
TAIL_AT = 175260
TAIL = 1456
ROWS_HEAD = 1452
ROWS_TAIL = 1352
TABLE = 2824
F1 = 0
AT = 967
CV = TAIL
F2 = TAIL + 383
FN = TAIL + 1350
LIVE = 337500

C_F1, C_AT, C_CV, C_BN, C_F2, C_FN, C_DWB, C_DW = 0, 2, 4, 6, 8, 10, 12, 13


def dot(a, b):
    return lax.dot_general(a, b, (((1,), (0,)), ((), ())), preferred_element_type=f32)


def dot_nt(a, b):
    return lax.dot_general(a, b, (((1,), (1,)), ((), ())), preferred_element_type=f32)


def dot_tn(a, b):
    return lax.dot_general(a, b, (((0,), (0,)), ((), ())), preferred_element_type=f32)


def lane_iota(shape):
    return lax.broadcasted_iota(jnp.int32, shape, len(shape) - 1)


def row_iota(shape):
    return lax.broadcasted_iota(jnp.int32, shape, 0)


def segments():
    found = []
    for h in range(HEADS):
        for r in range(GROUP):
            lo, hi = max(HEAD * h, D * r), min(HEAD * h + HEAD, D * r + D)
            if lo < hi:
                found.append((HP * h + lo - HEAD * h, r, lo - D * r, hi - lo))
    return found


def pad8(values):
    return jnp.concatenate([values, jnp.zeros((8, values.shape[1]), f32)], axis=0)


def ext(values):
    width = values.shape[1]
    ones = jnp.where(row_iota((8, width)) == 0, 1.0, 0.0).astype(f32)
    return jnp.concatenate([values, ones], axis=0).astype(bf16)


def norm(values):
    mean = jnp.sum(values, axis=0, keepdims=True) * (1.0 / D)
    centre = values - mean
    var = jnp.sum(centre * centre, axis=0, keepdims=True) * (1.0 / D)
    rstd = lax.rsqrt(var + EPS_NORM)
    return centre * rstd, rstd


def norm_back(upstream, xhat, rstd, gain):
    scaled = upstream * gain
    mean_one = jnp.sum(scaled, axis=0, keepdims=True) * (1.0 / D)
    mean_two = jnp.sum(scaled * xhat, axis=0, keepdims=True) * (1.0 / D)
    return rstd * (scaled - mean_one - xhat * mean_two)


def fold(values):
    total = values[:, 0:128]
    for at in range(128, values.shape[1], 128):
        total = total + values[:, at : at + 128]
    return total


def permute_in(values, pm):
    low = pad8(values).astype(bf16)
    stack = jnp.concatenate([low[:, 384 * b : 384 * b + 384] for b in range(4)], axis=0)
    out = dot(stack, pm)
    tiles = [out[128 * b : 128 * b + D, 128 * r : 128 * r + 128] for r in range(3) for b in range(4)]
    return jnp.concatenate(tiles, axis=1)


def stack_out(values):
    low = pad8(values).astype(bf16)
    blocks = []
    for b in range(4):
        blocks.append(
            jnp.concatenate([low[:, 512 * r + 128 * b : 512 * r + 128 * b + 128] for r in range(3)], axis=1)
        )
    return jnp.concatenate(blocks, axis=0)


def unstack_out(out):
    return jnp.concatenate([out[128 * b : 128 * b + D, :] for b in range(4)], axis=1)


def permute_out(values, pm):
    return unstack_out(dot_nt(stack_out(values), pm))


def permute_out_wide(values, pm):
    high = values.astype(bf16).astype(f32)
    rest = values - high
    mid = rest.astype(bf16).astype(f32)
    return unstack_out(dot_nt(stack_out(high), pm) + dot_nt(stack_out(mid), pm))


def plane_mask(r, length):
    return jnp.where(lane_iota((1, LG)) * GROUP + r < length, 1.0, 0.0).astype(f32)


def span(r):
    return slice(LG * r, LG * r + LG)


def skewed(count, stages):
    held = [None] * count
    for step in range(count + len(stages) - 1):
        for k, stage in enumerate(stages):
            n = step - k
            if 0 <= n < count:
                held[n] = stage(n, held[n])


def window(ref, r, base=0):
    return ref[base + WIN[r] : base + WIN[r] + WROWS, :]


def join_windows(parts):
    a, b, c = parts
    return jnp.concatenate([a[:112], a[112:128] + b[:16], b[16:128], b[128:144] + c[:16], c[16:]], axis=0)


def shifted_planes(tiles):
    lanes = lane_iota((8, 128))
    zero = jnp.zeros((8, 128), f32)
    made = {}
    for m in range(-HALF, HALF + GROUP):
        r, s = m % GROUP, m // GROUP
        if s == 0:
            made[m] = tiles[r]
            continue
        turned = [pltpu.roll(tiles[r][:, 128 * k : 128 * k + 128], (-s) % 128, 1) for k in range(4)]
        if s > 0:
            pairs = zip(turned, turned[1:] + [zero])
            parts = [jnp.where(lanes < 128 - s, a, b) for a, b in pairs]
        else:
            pairs = zip([zero] + turned[:-1], turned)
            parts = [jnp.where(lanes < -s, a, b) for a, b in pairs]
        made[m] = jnp.concatenate(parts, axis=1)
    return made


def shifted(tiles, m):
    r, s = m % GROUP, m // GROUP
    if s == 0:
        return tiles[r]
    lanes = lane_iota((8, 128))
    zero = jnp.zeros((8, 128), f32)
    turned = [pltpu.roll(tiles[r][:, 128 * k : 128 * k + 128], (-s) % 128, 1) for k in range(4)]
    if s > 0:
        pairs = zip(turned, turned[1:] + [zero])
        parts = [jnp.where(lanes < 128 - s, a, b) for a, b in pairs]
    else:
        pairs = zip([zero] + turned[:-1], turned)
        parts = [jnp.where(lanes < -s, a, b) for a, b in pairs]
    return jnp.concatenate(parts, axis=1)


SMEM = pl.BlockSpec(memory_space=pltpu.SMEM)
VMEM = pl.BlockSpec(memory_space=pltpu.VMEM)
BIG = (D, MAXLEN)
LOW = (128, MAXLEN)


def whole(shape):
    zeros = (0,) * len(shape)
    return pl.BlockSpec(shape, lambda u: zeros)


def per_utt(shape):
    zeros = (0,) * len(shape)
    return pl.BlockSpec((1,) + shape, lambda u: (u,) + zeros)


def at_most(shape, utts):
    zeros = (0,) * len(shape)
    return pl.BlockSpec((1,) + shape, lambda u: (jnp.minimum(u, utts - 1),) + zeros)


def one_late(shape):
    zeros = (0,) * len(shape)
    return pl.BlockSpec((1,) + shape, lambda u: (jnp.maximum(u - 1, 0),) + zeros)


def o(shape, kind=bf16):
    return jax.ShapeDtypeStruct(shape, kind)


def params(flops=0, moved=0):
    cost = pl.CostEstimate(flops=flops, bytes_accessed=moved, transcendentals=0)
    return dict(compiler_params=pltpu.CompilerParams(vmem_limit_bytes=VMEM_BYTES), cost_estimate=cost)


def permutation():
    t = row_iota((384, 384))
    c = lane_iota((384, 384))
    return jnp.where(t == GROUP * (c % 128) + c // 128, 1.0, 0.0).astype(bf16)


ANY = pl.BlockSpec(memory_space=pl.ANY)


def streamed(work, far_in, near_in, far_out, near_out, sems, first_utt):
    count = near_in.shape[0]

    def coming(u):
        return pltpu.make_async_copy(far_in.at[u + first_utt], near_in.at[u], sems.at[0, u])

    def going(u):
        pairs = enumerate(zip(near_out, far_out))
        return [pltpu.make_async_copy(near.at[u], far.at[u + first_utt], sems.at[k + 1, u]) for k, (near, far) in pairs]

    for u in range(count):
        coming(u).start()

    def step(u, carry):
        coming(u).wait()
        work(u)
        for copy in going(u):
            copy.start()
        return carry

    lax.fori_loop(0, count, step, 0)
    for u in range(count):
        for copy in going(u):
            copy.wait()


def enter_body(x_far, xp_far, xf_far, rs_far, pm_ref, x_near, xp_near, xf_near, rs_near, sems):
    pm_ref[...] = permutation()

    def work(u):
        x = permute_in(x_near[u].astype(f32), pm_ref[...])
        xp_near[u] = x.astype(bf16)
        xhat, rstd = norm(x)
        xf_near[u] = xhat
        rs_near[u] = jnp.broadcast_to(rstd, (8, MAXLEN))

    streamed(work, x_far, x_near, (xp_far, xf_far, rs_far), (xp_near, xf_near, rs_near), sems, 0)


def enter(x):
    utts = x.shape[0]
    made = [o((utts,) + BIG), o((utts,) + BIG, f32), o((utts, 8, MAXLEN), f32)]
    return pl.pallas_call(
        enter_body,
        in_specs=[ANY],
        out_specs=[ANY] * 3 + [VMEM],
        out_shape=made + [o((384, 384))],
        scratch_shapes=[pltpu.VMEM(m.shape, m.dtype) for m in [x] + made] + [pltpu.SemaphoreType.DMA((4, utts))],
        name="enter",
        **params(2 * 10**9, 8 * 10**6),
    )(x)


def inward(values, pm):
    return permute_in(values.astype(f32), pm).astype(bf16)


def outward(values, pm):
    return permute_out(values.astype(f32), pm).astype(bf16)


def reorder(turn, values, pm, name, first_utt=0, count=None, begun=None):
    count = values.shape[0] if count is None else count
    more = [] if begun is None else [begun]

    def body(far_in, pm_ref, *refs):
        far_out, near_in, near_out, sems = refs[len(more) :]

        def work(u):
            near_out[u] = turn(near_in[u], pm_ref[...])

        streamed(work, far_in, near_in, (far_out,), (near_out,), sems, first_utt)

    room = pltpu.VMEM((count,) + BIG, values.dtype)
    return pl.pallas_call(
        body,
        in_specs=[ANY, VMEM] + [ANY] * len(more),
        out_specs=ANY,
        out_shape=o(values.shape, values.dtype),
        scratch_shapes=[room, room, pltpu.SemaphoreType.DMA((2, count))],
        input_output_aliases={2: 0} if more else {},
        name=name,
        **params(2 * 10**9, 8 * 10**6),
    )(values, pm, *more)


def unpack(me_ref, g_ref, flat, tb):
    parts = g_ref.shape[0]
    part_rows = flat.shape[0] // parts
    for d in range(parts):
        flat[part_rows * d : part_rows * (d + 1), :] = g_ref[place(me_ref[0] ^ d, parts)].astype(f32)[:part_rows]
    tb[ROWS_HEAD:TAIL, :] = jnp.zeros((TAIL - ROWS_HEAD, 128), f32)
    for start, count, base in ((0, ROWS_HEAD, 0), (TAIL_AT, ROWS_TAIL, TAIL)):
        for r in range(16):
            at = start + D * r
            first_row, col = at // 128, at % 128
            many = (count - r + 15) // 16
            here = flat[pl.ds(first_row, many, stride=15), :]
            then = flat[pl.ds(first_row + 1, many, stride=15), :]
            lanes = lane_iota((many, 128))
            got = jnp.where(lanes >= col, here, then)
            if col:
                got = pltpu.roll(got, 128 - col, 1)
            tb[pl.ds(base + r, many, stride=16), :] = jnp.where(lanes < D, got, 0.0)


def with_row(block, row):
    tail = jnp.where(row_iota((8, 128)) == 0, row, 0.0)
    return jnp.concatenate([block, tail], axis=0)


def up_rows(tb, base):
    parts_t = []
    for q in range(4):
        block = tb[pl.ds(base + 2 + q, D, stride=4), :]
        parts_t.append(with_row(block, tb[base + 482 + q : base + 483 + q, :]).T[:D, :])
    return jnp.concatenate(parts_t, axis=0)


def up_across(up_t):
    return jnp.concatenate([up_t, jnp.zeros((32, 128), f32)], axis=0).T[:, :FF].astype(bf16)


def down_across(tb, base):
    bias = jnp.where(row_iota((32, 128)) == 0, tb[base + 966 : base + 967, :], 0.0)
    down = jnp.concatenate([tb[base + 486 : base + 966, :], bias], axis=0)
    return (0.5 * down).T.astype(bf16)


def point_rows(tb):
    parts_t = []
    for q in range(2):
        block = tb[pl.ds(CV + 2 + q, D, stride=2), :]
        parts_t.append(with_row(block, tb[CV + 242 + q : CV + 243 + q, :]).T[:D, :])
    return jnp.concatenate(parts_t, axis=0)


def fill_windows(tb, wt, wins):
    none = jnp.zeros((1, 128), f32)
    wins[...] = jnp.zeros_like(wins)
    for w, at, bias_at in ((0, AT + 2, AT + 122), (1, AT + 123, None), (2, AT + 243, AT + 363)):
        bias = none if bias_at is None else tb[bias_at : bias_at + 1, :]
        wt[...] = with_row(tb[at : at + D, :], bias).T
        for to, r, src, many in segments():
            start = WROWS * w + to - WIN[r]
            wins[r, start : start + many, :] = wt[src : src + many, :]


def fill_output(tb, wins):
    wins[:, 0:256, :] = jnp.zeros((GROUP, 256, 128), f32)
    for to, r, src, many in segments():
        start = to - WIN[r]
        wins[r, start : start + many, :] = tb[AT + 364 + src : AT + 364 + src + many, :]


def early_body(me_ref, g_ref, up_ref, dn_ref, wqkv_ref, wo_ref, pw_ref, cols_ref, base_ref, flat, tb, wt, wins, rows):
    unpack(me_ref, g_ref, flat, tb)
    up_ref[...] = (0.5 * up_rows(tb, F1)).astype(bf16)
    dn_ref[...] = down_across(tb, F1)
    pw_ref[...] = (0.5 * point_rows(tb)).astype(bf16)
    fill_windows(tb, wt, wins)
    for r in range(GROUP):
        wqkv_ref[r] = wins[r, : 3 * WROWS].astype(bf16)
    fill_output(tb, wins)
    for r in range(GROUP):
        wins[r, MARKS[r] : MARKS[r] + 1, :] = tb[AT + 484 : AT + 485, :]
        wo_ref[r] = wins[r, 0:256, :].T[:, :WROWS].astype(bf16)

    rows[...] = jnp.zeros_like(rows)
    listed = []
    for base in (F1, AT, CV, CV + 260, F2, FN):
        listed += [base, base + 1]
    listed += [CV + 259] + [CV + 244 + k for k in range(KERNEL)]
    for to, src in enumerate(listed):
        rows[to : to + 1, :] = tb[src : src + 1, :]
    cols_ref[...] = rows[...].T

    rel_rows = []
    lanes = lane_iota((1, 128))
    for h in range(HEADS):
        at = REL_AT + (2 * REL + 1) * h
        first_row, col = at // 128, at % 128
        pieces = []
        for k in range(2):
            here = flat[first_row + k : first_row + k + 1, :]
            got = jnp.where(lanes >= col, here, flat[first_row + k + 1 : first_row + k + 2, :])
            pieces.append(pltpu.roll(got, (128 - col) % 128, 1) if col else got)
        rel_rows.append(jnp.concatenate(pieces, axis=1))
    rel = jnp.concatenate(rel_rows + [jnp.zeros((4, 256), f32)], axis=0)
    rel = jnp.where(lane_iota((8, 256)) < 2 * REL + 1, rel, 0.0)
    base_ref[...] = dot(rel.astype(bf16), distance_select()) * LOG2E


def late_body(
    me_ref, g_ref, upp1_ref, dnp1_ref, up2_ref, upp2_ref, dn2_ref, dnp2_ref, pwp_ref, pr_ref, prp_ref, wqkvt_ref, wob_ref,
    flat, tb, wt, wins,
):
    unpack(me_ref, g_ref, flat, tb)
    upp1_ref[...] = up_across(up_rows(tb, F1))
    dnp1_ref[...] = (0.25 * tb[F1 + 486 : F1 + 966, :]).astype(bf16)
    up_t = up_rows(tb, F2)
    up2_ref[...] = (0.5 * up_t).astype(bf16)
    upp2_ref[...] = up_across(up_t)
    dn2_ref[...] = down_across(tb, F2)
    dnp2_ref[...] = (0.25 * tb[F2 + 486 : F2 + 966, :]).astype(bf16)
    pwp_ref[...] = jnp.concatenate([point_rows(tb), jnp.zeros((16, 128), f32)], axis=0).T[:, :240].astype(bf16)
    block = with_row(tb[CV + 262 : CV + 382, :], tb[CV + 382 : CV + 383, :])
    prp_ref[...] = (0.5 * block).astype(bf16)
    pr_ref[...] = block.T.astype(bf16)
    fill_windows(tb, wt, wins)
    for r in range(GROUP):
        wqkvt_ref[r] = wins[r].T[:, : 3 * WROWS].astype(bf16)
    fill_output(tb, wins)
    for r in range(GROUP):
        wob_ref[r] = wins[r, 0:WROWS, :].astype(bf16)


def distance_select():
    l = lane_iota((256, 2 * LG))
    gap = jnp.where(l < LG, -l, 2 * LG - l)
    index = jnp.clip(gap, -REL, REL) + REL
    return jnp.where(row_iota((256, 2 * LG)) == index, 1.0, 0.0).astype(bf16)


def spread_table(line, tab, h):
    blocks = {}
    for gap in (-1, 0, 1):
        tiles = [line[:, 128 * (k % 8) : 128 * (k % 8) + 128] for k in (gap - 1, gap)]
        both = jnp.broadcast_to(jnp.concatenate(tiles, axis=1), (128, 256))
        blocks[gap] = pltpu.roll(both, 0, 1, stride=1, stride_axis=0)[:, 128:]
    blocks[2] = jnp.broadcast_to(line[:, 256:257], (128, 128))
    blocks[-2] = jnp.broadcast_to(line[:, 768:769], (128, 128))
    for j in range(4):
        for i in range(4):
            tab[h, 128 * j : 128 * j + 128, 128 * i : 128 * i + 128] = blocks[max(-2, min(2, i - j))]


def block_of(values, j, i):
    return values[128 * j : 128 * j + 128, 128 * i : 128 * i + 128]


def add_distances(values, near, far, h):
    for gap in (-1, 0, 1):
        parts = [block_of(values, j, j + gap) for j in range(4) if 0 <= j + gap < 4]
        total = parts[0]
        for part in parts[1:]:
            total = total + part
        near[h, :, 128 * (gap + 1) : 128 * (gap + 2)] += total
    for k, blocks in enumerate((((0, 2), (0, 3), (1, 3)), ((2, 0), (3, 0), (3, 1)))):
        total = sum(block_of(values, j, i) for j, i in blocks)
        rows = total[0:8]
        for at in range(8, 128, 8):
            rows = rows + total[at : at + 8]
        far[h, k] += rows


def diagonal_sum(near, far):
    wide_rows = jnp.concatenate([near, jnp.zeros((128, 128), f32)], axis=1)
    half = 64
    while half:
        wide_rows = wide_rows[:half] + pltpu.roll(wide_rows[half : 2 * half], LG - half, 1)
        half //= 2
    tiles = [wide_rows[:, 128 * k : 128 * k + 128] for k in range(4)]
    none = jnp.zeros((1, 128), f32)
    plus = jnp.sum(far[0], axis=0, keepdims=True)
    minus = jnp.sum(far[1], axis=0, keepdims=True)
    return jnp.concatenate([tiles[1], tiles[2], plus, none, none, minus, tiles[3], tiles[0]], axis=1)


def prepare(me, gathered, rows):
    total = gathered.shape[0] * rows
    room = [
        pltpu.VMEM((total, 128), f32),
        pltpu.VMEM((TABLE, 128), f32),
        pltpu.VMEM((128, 128), f32),
        pltpu.VMEM((GROUP, 512, 128), f32),
    ]
    early = pl.pallas_call(
        early_body,
        in_specs=[SMEM, VMEM],
        out_shape=[o((FF, 128)), o((128, 512)), o((GROUP, 3 * WROWS, 128)), o((GROUP, 128, WROWS)), o((240, 128))]
        + [o((128, 128), f32), o((8, 2 * LG), f32)],
        scratch_shapes=room + [pltpu.VMEM((128, 128), f32)],
        name="prepare",
        **params(10**9, 2 * 10**6),
    )(me, gathered)
    late = pl.pallas_call(
        late_body,
        in_specs=[SMEM, VMEM],
        out_shape=[o((128, FF)), o((FF, 128)), o((FF, 128)), o((128, FF)), o((128, 512)), o((FF, 128))]
        + [o((128, 240)), o((128, 128)), o((128, 128)), o((GROUP, 128, 3 * WROWS)), o((GROUP, WROWS, 128))],
        scratch_shapes=room,
        name="late",
        **params(3 * 10**9, 10 * 10**6),
    )(me, gathered)
    return early, late


def column(cols, k):
    return cols[:D, k : k + 1]


def valid_keys(length):
    return row_iota((LG, 1)) * GROUP < length


def set_tail(hid):
    hid[FF:, :] = jnp.where(row_iota((512 - FF, hid.shape[1])) == 0, 1.0, 0.0).astype(bf16)


def conv_columns(cols, cb):
    for k in range(KERNEL + 1):
        cb[k] = jnp.broadcast_to(cols[:D, C_DWB + k : C_DWB + k + 1], (D, 128))


def wide(tile, copies=4):
    return jnp.concatenate([tile] * copies, axis=1)


def first_body(
    len_ref, xp_ref, xf_ref, cols_ref, up_ref, dn_ref, wqkv_ref, wo_ref, pw_ref, base_ref,
    lf_ref, xa_ref, nrm_ref, qkv_ref, prob_ref, att_ref, aa_ref, xc_ref, cn_ref, gat_ref, sig_ref, rgt_ref,
    ra_ref, rc_ref, dep_ref, st_ref,
    hid, one, cb, tab, run,
):
    u = pl.program_id(0)
    length = len_ref[u]

    @pl.when(u == 0)
    def _():
        set_tail(hid)
        run[...] = jnp.zeros_like(run)
        conv_columns(cols_ref, cb)
        for h in range(HEADS):
            spread_table(base_ref[h : h + 1, :], tab, h)

    cols = cols_ref

    def ffn_up(r, held):
        low = ext(xf_ref[0, :, span(r)] * column(cols, C_F1) + column(cols, C_F1 + 1))
        lf_ref[0, :, span(r)] = low
        return dot(up_ref[...], low)

    def ffn_down(r, half):
        hid[:FF, span(r)] = (half + half * jnp.tanh(half)).astype(bf16)
        return dot(dn_ref[...], hid[:, span(r)])[:D]

    def ffn_norm(r, branch):
        after = xp_ref[0, :, span(r)].astype(f32) + branch
        one[:, span(r)] = after
        xhat, rstd = norm(after)
        xa_ref[0, :, span(r)] = xhat
        ra_ref[0, 0:1, span(r)] = rstd
        low = ext(xhat * column(cols, C_AT) + column(cols, C_AT + 1))
        nrm_ref[0, 128 * r : 128 * r + 128, :] = low
        return dot(wqkv_ref[r], low)

    made = [None] * GROUP

    def ffn_keep(r, found):
        made[r] = found

    skewed(GROUP, (ffn_up, ffn_down, ffn_norm, ffn_keep))
    for w in range(3):
        joined = join_windows([made[r][WROWS * w : WROWS * w + WROWS] for r in range(GROUP)])
        qkv_ref[0, GP * w : GP * w + GP, :] = joined.astype(bf16)
    keys = valid_keys(length)

    def rows(w, h):
        return slice(GP * w + HP * h, GP * w + HP * h + HP)

    def score(h, held):
        return dot_tn(qkv_ref[0, rows(1, h), :], qkv_ref[0, rows(0, h), :])

    def soften(h, raw):
        scores = raw * (SCALE * LOG2E) + tab[h]
        scores = jnp.where(keys, scores, NEG_FILL * LOG2E)
        peak = jnp.max(scores, axis=0, keepdims=True)
        power = jnp.exp2(scores - peak)
        total = jnp.sum(power, axis=0, keepdims=True)
        prob_ref[0, h] = (power * (1.0 / total)).astype(bf16)

    def mix(h, held):
        mixed = dot(qkv_ref[0, rows(2, h), :], prob_ref[0, h])
        if h < GROUP:
            mixed = jnp.where(row_iota((HP, LG)) == HEAD, 1.0, mixed)
        att_ref[0, rows(0, h), :] = mixed.astype(bf16)

    skewed(HEADS, (score, soften, mix))

    def project(r, held):
        return dot(wo_ref[r], window(att_ref.at[0], r))[:D]

    def gate_in(r, mixed):
        after = one[:, span(r)] + mixed
        aa_ref[0, :, span(r)] = after
        xhat, rstd = norm(after)
        xc_ref[0, :, span(r)] = xhat
        rc_ref[0, 0:1, span(r)] = rstd
        low = ext(xhat * column(cols, C_CV) + column(cols, C_CV + 1))
        cn_ref[0, :, span(r)] = low
        return dot(pw_ref[...], low)

    def gate_out(r, pre):
        mask = plane_mask(r, length)
        sig = (0.5 + 0.5 * jnp.tanh(pre[D:])) * mask
        gated = (pre[:D] + pre[:D]) * sig
        gat_ref[0, :, span(r)] = gated
        sig_ref[0, :, span(r)] = sig
        rgt_ref[0, :, span(r)] = gated * (1.0 - sig)

    skewed(GROUP, (project, gate_in, gate_out))

    def conv(f, carry):
        at = slice(8 * f, 8 * f + 8)
        tiles = [gat_ref[0, at, span(r)] for r in range(GROUP)]
        totals = [wide(cb[0, at, :])] * GROUP
        for m in range(-HALF, HALF + GROUP):
            here = shifted(tiles, m)
            for r in range(GROUP):
                k = m + HALF - r
                if 0 <= k < KERNEL:
                    totals[r] = totals[r] + wide(cb[1 + k, at, :]) * here
        for r in range(GROUP):
            dep_ref[0, at, span(r)] = totals[r]
        return carry

    for f in range(D // 8):
        conv(f, 0)

    count = length.astype(f32)
    mask = jnp.concatenate([plane_mask(r, length) for r in range(GROUP)], axis=1)
    dep = dep_ref[0]
    mean = jnp.sum(dep * mask, axis=1, keepdims=True) / count
    gap = (dep - mean) * mask
    spread = jnp.sum(gap * gap, axis=1, keepdims=True)
    old_mean, old_spread, old_count = run[0], run[1], run[2]
    new_count = old_count + count
    step = mean - old_mean
    new_mean = old_mean + step * (count / new_count)
    new_spread = old_spread + spread + step * step * (old_count * count / new_count)
    run[0] = new_mean
    run[1] = new_spread
    run[2] = new_count

    @pl.when(u == pl.num_programs(0) - 1)
    def _():
        lanes = lane_iota((D, 128))
        picked = jnp.where(lanes == 0, run[0], jnp.where(lanes == 1, run[1], jnp.where(lanes == 2, run[2], 0.0)))
        line = pad8(picked).T[0:8]
        for d in range(st_ref.shape[0]):
            st_ref[d] = line


def first(devices, lengths, xp, xf, weights):
    utts = xp.shape[0]
    per = [
        (LOW, bf16),
        (BIG, f32),
        ((GP, LG), bf16),
        ((3 * GP, LG), bf16),
        ((HEADS, LG, LG), bf16),
        ((GP, LG), bf16),
        (BIG, f32),
        (BIG, f32),
        (LOW, bf16),
        (BIG, f32),
        (BIG, f32),
        (BIG, f32),
        ((8, MAXLEN), f32),
        ((8, MAXLEN), f32),
        (BIG, f32),
    ]
    line = (devices, 8, 128)
    return pl.pallas_call(
        first_body,
        grid=(utts,),
        in_specs=[SMEM, per_utt(BIG), per_utt(BIG)] + [whole(w.shape) for w in weights],
        out_specs=[per_utt(s) for s, k in per] + [whole(line)],
        out_shape=[o((utts,) + s, k) for s, k in per] + [o(line, f32)],
        scratch_shapes=[
            pltpu.VMEM((512, MAXLEN), bf16),
            pltpu.VMEM(BIG, f32),
            pltpu.VMEM((KERNEL + 1, D, 128), f32),
            pltpu.VMEM((HEADS, LG, LG), f32),
            pltpu.VMEM((3, D, 128), f32),
        ],
        name="first",
        **params(10 * 10**9, 60 * 10**6),
    )(lengths, xp, xf, *weights)


def second_body(
    len_ref, stats_ref, cot_ref, aa_ref, dep_ref, cols_ref, up_ref, upp_ref, dn_ref, dnp_ref, pr_ref, prp_ref,
    out_ref, bgd_ref, gc_ref, sums_ref, stc_ref, gdn_ref, gup_ref, gpr_ref, vec_ref,
    hid, acc,
):
    u = pl.program_id(0)
    length = len_ref[u]
    cols = cols_ref

    @pl.when(u == 0)
    def _():
        set_tail(hid)
        parts = stats_ref.shape[0]
        count = jnp.zeros((1, 128), f32)
        total = jnp.zeros((1, 128), f32)
        for d in range(parts):
            many = stats_ref[d, 2:3, :]
            count = count + many
            total = total + many * stats_ref[d, 0:1, :]
        here = lane_iota((1, 128)) < D
        count = jnp.where(here, count, 1.0)
        mean = total / count
        spread = jnp.zeros((1, 128), f32)
        for d in range(parts):
            gap = stats_ref[d, 0:1, :] - mean
            spread = spread + stats_ref[d, 1:2, :] + stats_ref[d, 2:3, :] * gap * gap
        scale = lax.rsqrt(spread / count + EPS_NORM)
        at = row_iota((128, 128))
        table = jnp.where(at == 0, mean, jnp.where(at == 1, scale, jnp.where(at == 2, 1.0 / count, 0.0)))
        stc_ref[...] = table.T
        gdn_ref[...] = jnp.zeros_like(gdn_ref)
        gup_ref[...] = jnp.zeros_like(gup_ref)
        gpr_ref[...] = jnp.zeros_like(gpr_ref)
        vec_ref[...] = jnp.zeros_like(vec_ref)
        acc[...] = jnp.zeros_like(acc)

    half_gain = 0.5 * column(cols, C_BN)
    half_bias = 0.5 * column(cols, C_BN + 1)

    def enter(r, held):
        normal = (dep_ref[0, :, span(r)] - stc_ref[:D, 0:1]) * stc_ref[:D, 1:2]
        z = normal * half_gain + half_bias
        t = jnp.tanh(z)
        act = z + z * t
        act_low = ext(act)
        slope = (1.0 + t) * (1.0 + z * (1.0 - t))
        return act_low, normal, slope, dot(pr_ref[...], act_low)[:D]

    def ffn_up(r, held):
        act_low, normal, slope, moved = held
        after_conv = aa_ref[0, :, span(r)] + moved
        xhat, rstd = norm(after_conv)
        low = ext(xhat * column(cols, C_F2) + column(cols, C_F2 + 1))
        return act_low, normal, slope, after_conv, xhat, rstd, low, dot(up_ref[...], low)

    def ffn_down(r, held):
        act_low, normal, slope, after_conv, xhat, rstd, low, half = held
        t = jnp.tanh(half)
        hid[:FF, span(r)] = (half + half * t).astype(bf16)
        bend = (1.0 + t) * (1.0 + half * (1.0 - t))
        return act_low, normal, slope, after_conv, xhat, rstd, low, bend, dot(dn_ref[...], hid[:, span(r)])[:D]

    def finish(r, held):
        act_low, normal, slope, after_conv, xhat, rstd, low, bend, branch = held
        mask = plane_mask(r, length)
        xhat_f, rstd_f = norm(after_conv + branch)
        made = (xhat_f * column(cols, C_FN) + column(cols, C_FN + 1)) * mask
        out_ref[0, :, span(r)] = made.astype(bf16)
        up_grad = cot_ref[0, :, span(r)].astype(f32) * mask
        vec_ref[2] += fold(up_grad * xhat_f)
        vec_ref[3] += fold(up_grad)
        grad_two = norm_back(up_grad, xhat_f, rstd_f, column(cols, C_FN))
        branch = pad8(grad_two).astype(bf16)
        gdn_ref[...] += dot_nt(hid[:, span(r)], branch)
        return act_low, normal, slope, xhat, rstd, low, bend, grad_two, dot(dnp_ref[...], branch)

    def ffn_back(r, held):
        act_low, normal, slope, xhat, rstd, low, bend, grad_two, back = held
        pre_low = (bend * back).astype(bf16)
        gup_ref[...] += dot_nt(pre_low, low)
        return act_low, normal, slope, xhat, rstd, grad_two, dot(upp_ref[...], pre_low)[:D]

    def leave(r, held):
        act_low, normal, slope, xhat, rstd, grad_two, back = held
        vec_ref[0] += fold(back * xhat)
        vec_ref[1] += fold(back)
        grad_conv = grad_two + norm_back(back, xhat, rstd, column(cols, C_F2))
        gc_ref[0, :, span(r)] = grad_conv
        project = pad8(grad_conv).astype(bf16)
        gpr_ref[...] += dot_nt(act_low, project)
        return normal, slope, dot(prp_ref[...], project)[:D]

    def last(r, held):
        normal, slope, back = held
        batch = slope * back
        bgd_ref[0, :, span(r)] = batch
        acc[0] += fold(batch * normal)
        acc[1] += fold(batch)

    skewed(GROUP, (enter, ffn_up, ffn_down, finish, ffn_back, leave, last))

    @pl.when(u == pl.num_programs(0) - 1)
    def _():
        lanes = lane_iota((D, 128))
        gain = jnp.sum(acc[0], axis=1, keepdims=True)
        shift = jnp.sum(acc[1], axis=1, keepdims=True)
        line = pad8(jnp.where(lanes == 0, gain, jnp.where(lanes == 1, shift, 0.0))).T[0:8]
        for d in range(sums_ref.shape[0]):
            sums_ref[d] = line


def second(lengths, stats, cot, aa, dep, weights):
    utts = cot.shape[0]
    big = (D, MAXLEN)
    outs = [
        (per_utt(big), (utts,) + big, bf16),
        (per_utt(big), (utts,) + big, f32),
        (per_utt(big), (utts,) + big, f32),
    ]
    for s in (stats.shape, (128, 128), (512, 128), (FF, 128), (128, 128), (4, D, 128)):
        outs.append((whole(s), s, f32))
    return pl.pallas_call(
        second_body,
        grid=(utts,),
        in_specs=[SMEM, whole(stats.shape)] + [per_utt(big)] * 3 + [whole(w.shape) for w in weights],
        out_specs=[o[0] for o in outs],
        out_shape=[jax.ShapeDtypeStruct(o[1], o[2]) for o in outs],
        scratch_shapes=[
            pltpu.VMEM((512, MAXLEN), bf16),
            pltpu.VMEM((2, D, 128), f32),
        ],
        name="second",
        **params(15000000000, 30000000),
    )(lengths, stats, cot, aa, dep, *weights)


def third_body(
    len_ref, sums_ref, stc_ref, bgd_ref, dep_ref, gat_ref, ri_ref, ra_ref, rc_ref,
    gc_far, xc_far, cn_far, sig_far, rgt_far, att_far, qkv_far, prob_far, nrm_far, lf_far, xa_far, xf_far,
    cols_ref, up_ref, upp_ref, dnp_ref, wqkv_t_ref, wob_ref, pwp_ref,
    grad_ref, gdn_ref, gup_ref, gpw_ref, gqkv_ref, go_ref, rel_ref, vec_ref,
    gc_ref, xc_ref, cn_ref, sig_ref, rgt_ref, att_ref, qkv_ref, prob_ref, nrm_ref, lf_ref, xa_ref, xf_ref, sems,
    hid, dgx, dgs, olg, agr, back_s, gg, near_s, far_s, cb, tot,
):
    far = (gc_far, xc_far, cn_far, sig_far, rgt_far, att_far, qkv_far, prob_far, nrm_far, lf_far, xa_far, xf_far)
    near = (gc_ref, xc_ref, cn_ref, sig_ref, rgt_ref, att_ref, qkv_ref, prob_ref, nrm_ref, lf_ref, xa_ref, xf_ref)
    u = pl.program_id(0)
    utts = pl.num_programs(0) - 1
    slot = 1 - u % 2

    def copies(step):
        at = step % 2
        return [pltpu.make_async_copy(far[i].at[step], near[i].at[at], sems.at[i, at]) for i in range(len(far))]

    cols = cols_ref

    @pl.when(u == 0)
    def _():
        set_tail(hid)
        conv_columns(cols_ref, cb)
        parts = sums_ref.shape[0]
        total = sums_ref[0]
        for d in range(1, parts):
            total = total + sums_ref[d]
        tot[...] = jnp.concatenate([total, jnp.zeros((120, 128), f32)], axis=0).T
        for ref in (gdn_ref, gup_ref, gpw_ref, gqkv_ref, go_ref, vec_ref, near_s, far_s):
            ref[...] = jnp.zeros_like(ref)

    @pl.when(u < utts)
    def _():
        for copy in copies(u):
            copy.start()

    @pl.when(u > 0)
    def _():
        for copy in copies(u - 1):
            copy.wait()

    def front():
        scale = stc_ref[:D, 1:2]
        lead = column(cols, C_BN) * scale
        share = lead * stc_ref[:D, 2:3]
        shift_part = share * tot[:D, 1:2]
        gain_part = share * tot[:D, 0:1] * scale
        for r in range(GROUP):
            normal = dep_ref[0, :, span(r)] - stc_ref[:D, 0:1]
            mask = plane_mask(r, len_ref[u])
            dgx[:, span(r)] = bgd_ref[0, :, span(r)] * lead - mask * (shift_part + normal * gain_part)

        def conv(f, carry):
            at = slice(8 * f, 8 * f + 8)
            tiles = [dgx[at, span(r)] for r in range(GROUP)]
            gated = [gat_ref[0, at, span(r)] for r in range(GROUP)]
            totals = [None] * GROUP
            taps = [None] * KERNEL
            for m in range(-HALF, HALF + GROUP):
                here = shifted(tiles, m)
                for r in range(GROUP):
                    k = r + HALF - m
                    if 0 <= k < KERNEL:
                        term = wide(cb[1 + k, at, :]) * here
                        totals[r] = term if totals[r] is None else totals[r] + term
                        part = fold(gated[r] * here)
                        taps[k] = part if taps[k] is None else taps[k] + part
            vec_ref[6, at, :] += fold(tiles[0] + tiles[1] + tiles[2])
            for k in range(KERNEL):
                vec_ref[7 + k, at, :] += taps[k]
            for r in range(GROUP):
                gg[at, span(r)] = totals[r]
            return carry

        for f in range(D // 8):
            conv(f, 0)

    def back():
        def gate(r, held):
            grad = gg[:, span(r)]
            left = grad * sig_ref[slot, :, span(r)]
            right = grad * rgt_ref[slot, :, span(r)]
            pre_low = jnp.concatenate([left, right], axis=0).astype(bf16)
            gpw_ref[...] += dot_nt(pre_low, cn_ref[slot, :, span(r)])
            return dot(pwp_ref[...], pre_low)[:D]

        def residual(r, back):
            xhat = xc_ref[slot, :, span(r)]
            vec_ref[0] += fold(back * xhat)
            vec_ref[1] += fold(back)
            grad = gc_ref[slot, :, span(r)] + norm_back(back, xhat, rc_ref[0, 0:1, span(r)], column(cols, C_CV))
            dgs[:, span(r)] = grad
            low = pad8(grad).astype(bf16)
            olg[128 * r : 128 * r + 128, :] = low
            return dot(wob_ref[r], low)

        made = [None] * GROUP

        def keep(r, found):
            go_ref[r] += dot_nt(window(att_ref.at[slot], r), olg[128 * r : 128 * r + 128, :])
            made[r] = found

        skewed(GROUP, (gate, residual, keep))
        agr[...] = join_windows(made).astype(bf16)

        def rows(w, h):
            return slice(GP * w + HP * h, GP * w + HP * h + HP)

        def enter(h, held):
            grad = agr[rows(0, h), :]
            back_s[rows(2, h), :] = dot_nt(grad, prob_ref[slot, h]).astype(bf16)
            return dot_tn(qkv_ref[slot, rows(2, h), :], grad)

        def soften(h, prob_grad):
            probs = prob_ref[slot, h].astype(f32)
            inner = jnp.sum(probs * prob_grad, axis=0, keepdims=True)
            score = probs * (prob_grad - inner)
            add_distances(score, near_s, far_s, h)
            return score.astype(bf16)

        def turn(h, low):
            back_s[rows(0, h), :] = (dot(qkv_ref[slot, rows(1, h), :], low) * SCALE).astype(bf16)
            back_s[rows(1, h), :] = (dot_nt(qkv_ref[slot, rows(0, h), :], low) * SCALE).astype(bf16)

        skewed(HEADS, (enter, soften, turn))

        def project(r, held):
            stack = jnp.concatenate([window(back_s, r, GP * w) for w in range(3)], axis=0)
            gqkv_ref[r] += dot_nt(stack, nrm_ref[slot, 128 * r : 128 * r + 128, :])
            return dot(wqkv_t_ref[r], stack)[:D], dot(up_ref[...], lf_ref[slot, :, span(r)])

        def ffn_in(r, held):
            back, half = held
            xhat = xa_ref[slot, :, span(r)]
            vec_ref[2] += fold(back * xhat)
            vec_ref[3] += fold(back)
            grad = dgs[:, span(r)] + norm_back(back, xhat, ra_ref[0, 0:1, span(r)], column(cols, C_AT))
            low = pad8(grad).astype(bf16)
            return grad, low, half, dot(dnp_ref[...], low)

        def ffn_mid(r, held):
            grad, branch, half, back = held
            t = jnp.tanh(half)
            hid[:FF, span(r)] = (half + half * t).astype(bf16)
            pre_low = ((1.0 + t) * (1.0 + half * (1.0 - t)) * back).astype(bf16)
            gdn_ref[...] += dot_nt(hid[:, span(r)], branch)
            gup_ref[...] += dot_nt(pre_low, lf_ref[slot, :, span(r)])
            return grad, dot(upp_ref[...], pre_low)[:D]

        def ffn_out(r, held):
            grad, back = held
            xhat = xf_ref[slot, :, span(r)]
            vec_ref[4] += fold(back * xhat)
            vec_ref[5] += fold(back)
            grad_ref[0, :, span(r)] = grad + norm_back(back, xhat, ri_ref[0, 0:1, span(r)], column(cols, C_F1))

        skewed(GROUP, (project, ffn_in, ffn_mid, ffn_out))

    @pl.when(u == 0)
    def _():
        front()

    @pl.when((u > 0) & (u < utts))
    def _():
        back()
        front()

    @pl.when(u == utts)
    def _():
        back()
        found = []
        for h in range(HEADS):
            found.append(diagonal_sum(near_s[h], far_s[h]))
        stacked = jnp.concatenate(found + [jnp.zeros((4, 2 * LG), f32)], axis=0)
        high = stacked.astype(bf16)
        rest = stacked - high.astype(f32)
        mid = rest.astype(bf16)
        rest = rest - mid.astype(f32)
        select = distance_select()
        rel_ref[...] = dot_nt(high, select) + dot_nt(mid, select) + dot_nt(rest.astype(bf16), select)


def third(lengths, sums, stc, soon, later, weights):
    utts = soon[0].shape[0]
    big = (D, MAXLEN)
    outs = [(one_late(big), (utts,) + big)]
    for s in ((512, 128), (FF, 128), (240, 128), (GROUP, 3 * WROWS, 128), (GROUP, WROWS, 128), (8, 256), (22, D, 128)):
        outs.append((whole(s), s))
    return pl.pallas_call(
        third_body,
        grid=(utts + 1,),
        in_specs=[SMEM, whole(sums.shape), whole(stc.shape)]
        + [at_most(s.shape[1:], utts) for s in soon[:3]]
        + [one_late(s.shape[1:]) for s in soon[3:]]
        + [pl.BlockSpec(memory_space=pl.ANY)] * len(later)
        + [whole(w.shape) for w in weights],
        out_specs=[o[0] for o in outs],
        out_shape=[jax.ShapeDtypeStruct(o[1], f32) for o in outs],
        scratch_shapes=[pltpu.VMEM((2,) + s.shape[1:], s.dtype) for s in later]
        + [
            pltpu.SemaphoreType.DMA((len(later), 2)),
            pltpu.VMEM((512, MAXLEN), bf16),
            pltpu.VMEM(big, f32),
            pltpu.VMEM(big, f32),
            pltpu.VMEM((GP, LG), bf16),
            pltpu.VMEM((GP, LG), bf16),
            pltpu.VMEM((3 * GP, LG), bf16),
            pltpu.VMEM(big, f32),
            pltpu.VMEM((HEADS, 128, 384), f32),
            pltpu.VMEM((HEADS, 2, 8, 128), f32),
            pltpu.VMEM((KERNEL + 1, D, 128), f32),
            pltpu.VMEM((128, 128), f32),
        ],
        name="third",
        **params(20000000000, 80000000),
    )(lengths, sums, stc, *soon, *later, *weights)


def clean(block):
    return jnp.where(lane_iota(block.shape) < D, block, 0.0)


def set_rows(tb, wt, ref, at):
    lanes = lane_iota((D, 128))
    table = jnp.zeros((D, 128), f32)
    for k in range(len(at)):
        table = jnp.where(lanes == k, jnp.sum(ref[k], axis=1, keepdims=True), table)
    wt[...] = pad8(table).T
    for k, to in enumerate(at):
        tb[to : to + 1, :] = wt[k : k + 1, :]


def set_ffn(tb, base, dn_ref, up_ref):
    tb[base + 486 : base + 967, :] = 0.5 * clean(dn_ref[0 : FF + 1, :])
    for q in range(4):
        block = pad8(up_ref[D * q : D * q + D, :]).T
        tb[pl.ds(base + 2 + q, D, stride=4), :] = block[:D]
        tb[base + 482 + q : base + 483 + q, :] = block[D : D + 1]


def flatten(tb, base, flat, at_row, y_count, offset):
    for k in range(15):
        at = 128 * k + offset
        first_row, col = at // D, at % D
        many = (y_count - k + 14) // 15
        here = lane_iota((many, 128))
        got = tb[pl.ds(base + first_row, many, stride=16), :]
        if col:
            got = pltpu.roll(got, 128 - col, 1)
        then = pltpu.roll(tb[pl.ds(base + first_row + 1, many, stride=16), :], D - col, 1)
        got = jnp.where(here < D - col, got, then)
        if 2 * D - col < 128:
            then = pltpu.roll(tb[pl.ds(base + first_row + 2, many, stride=16), :], 2 * D - col, 1)
            got = jnp.where(here < 2 * D - col, got, then)
        flat[pl.ds(at_row + k, many, stride=15), :] = got


SPLIT = F2 - TAIL
ROWS_LAST = ROWS_TAIL - SPLIT
LAST_AT = TAIL_AT + D * SPLIT
LAST_Y = LAST_AT // 128
LAST_COUNT = (LIVE - 1) // 128 - LAST_Y + 1


def ahead_body(dn_ref, up_ref, vec_ref, out_ref, tb, wt):
    tb[0:8, :] = jnp.zeros((8, 128), f32)
    tb[8 + ROWS_LAST :, :] = jnp.zeros((tb.shape[0] - 8 - ROWS_LAST, 128), f32)
    set_rows(tb, wt, vec_ref, (8, 9, 8 + FN - F2, 9 + FN - F2))
    set_ffn(tb, 8, dn_ref, up_ref)
    flatten(tb, 7, out_ref, 0, LAST_COUNT, D + 128 * LAST_Y - LAST_AT)


def pack_ahead(dn, up, vec):
    return pl.pallas_call(
        ahead_body,
        out_shape=o((LAST_COUNT, 128), f32),
        scratch_shapes=[pltpu.VMEM((ROWS_LAST + 24, 128), f32), pltpu.VMEM((128, 128), f32)],
        name="ahead",
        **params(2 * 10**9, 8 * 10**6),
    )(dn, up, vec)


def pack_body(
    me_ref, last_ref, dn1_ref, up1_ref, pr_ref, pw_ref, qkv_ref, o_ref, rel_ref, vec_ref, sums_ref,
    keep_ref, send_ref, tb, flat, stage, wt,
):
    tb[ROWS_HEAD:TAIL, :] = jnp.zeros((TAIL - ROWS_HEAD, 128), f32)
    tb[F2:, :] = jnp.zeros((tb.shape[0] - F2, 128), f32)
    set_rows(
        tb, wt, vec_ref, (CV, CV + 1, AT, AT + 1, F1, F1 + 1, CV + 259) + tuple(CV + 244 + k for k in range(KERNEL))
    )
    tb[CV + 260 : CV + 262, :] = sums_ref[0, 0:2, :]
    set_ffn(tb, F1, dn1_ref, up1_ref)
    for q in range(2):
        block = pad8(pw_ref[D * q : D * q + D, :]).T
        tb[pl.ds(CV + 2 + q, D, stride=2), :] = block[:D]
        tb[CV + 242 + q : CV + 243 + q, :] = block[D : D + 1]
    tb[CV + 262 : CV + 383, :] = clean(pr_ref[0 : D + 1, :])

    def gathered(ref, base):
        wt[...] = jnp.zeros_like(wt)
        for to, r, src, many in segments():
            start = base + to - WIN[r]
            wt[src : src + many, :] += ref[r, start : start + many, :]
        return wt[...]

    for w, at, bias_at in ((0, AT + 2, AT + 122), (1, AT + 123, None), (2, AT + 243, AT + 363)):
        block = gathered(qkv_ref, WROWS * w).T
        tb[at : at + D, :] = block[:D]
        if bias_at is not None:
            tb[bias_at : bias_at + 1, :] = block[D : D + 1]
    tb[AT + 364 : AT + 484, :] = clean(gathered(o_ref, 0)[:D])
    bias = sum(o_ref[r, MARKS[r] : MARKS[r] + 1, :] for r in range(GROUP))
    tb[AT + 484 : AT + 485, :] = clean(bias)

    tail_y = TAIL_AT // 128
    flat[LAST_Y + LAST_COUNT :, :] = jnp.zeros((flat.shape[0] - LAST_Y - LAST_COUNT, 128), f32)
    flat[REL_AT // 128 + 1 : tail_y, :] = jnp.zeros((tail_y - REL_AT // 128 - 1, 128), f32)
    flatten(tb, 0, flat, 0, REL_AT // 128 + 1, 0)
    flatten(tb, TAIL - 1, flat, tail_y, LAST_Y - tail_y + 1, 128 * tail_y - TAIL_AT + D)
    flat[LAST_Y : LAST_Y + 1, :] += last_ref[0:1, :]
    flat[LAST_Y + 1 : LAST_Y + LAST_COUNT, :] = last_ref[1:, :]
    here = lane_iota((1, 128))
    width = 2 * REL + 1
    for h in range(HEADS):
        at = REL_AT + width * h
        for y in range(at // 128, (at + width - 1) // 128 + 1):
            lo, hi = max(at - 128 * y, 0), min(at + width - 128 * y, 128)
            shift = (at - 128 * y) % 256
            turned = rel_ref[h : h + 1, :]
            if shift:
                turned = pltpu.roll(turned, shift, 1)
            flat[y : y + 1, :] += jnp.where((here >= lo) & (here < hi), turned[:, :128], 0.0)
    parts, padded = 2 * keep_ref.shape[0], keep_ref.shape[1]
    rows = flat.shape[0] // parts
    for d in range(parts):
        stage[d, 0:rows, :] = flat[rows * d : rows * (d + 1), :]
        if rows < padded:
            stage[d, rows:padded, :] = jnp.zeros((padded - rows, 128), f32)
    for offset in range(0, parts, 2):
        keep_ref[place(offset, parts)] = stage[me_ref[0] ^ offset]
        send_ref[place(offset, parts)] = stage[me_ref[0] ^ (offset + 1)]


def pack(parts, rows, me, grads):
    half = o((parts // 2, whole_tiles(rows), 128), f32)
    return pl.pallas_call(
        pack_body,
        in_specs=[SMEM] + [VMEM] * len(grads),
        out_shape=[half, half],
        scratch_shapes=[
            pltpu.VMEM((F2 + 24, 128), f32),
            pltpu.VMEM((parts * rows, 128), f32),
            pltpu.VMEM((parts, whole_tiles(rows), 128), f32),
            pltpu.VMEM((128, 128), f32),
        ],
        name="pack",
        **params(10**9, 5 * 10**6),
    )(me, *grads)


def update_tables(total_len):
    rates = np.zeros(total_len, np.float32)
    decays = np.zeros(total_len, np.float32)
    vector, gain, ffn = (D, 0.1, 0.0), (D, 0.3, 0.0), lambda n, fan: (n, fan**-0.5, 0.01)
    block = [gain, vector, ffn(D * FF, D), (FF, 0.1, 0.0), ffn(FF * D, FF), vector]
    square = ffn(D * D, D)
    pieces = block + [gain, vector, square, vector, square, square, vector, ffn(D * D, 6.0 * D / MAXLEN), vector]
    pieces += [(HEADS * (2 * REL + 1), 0.5, 0.0)]
    pieces += [gain, vector, ffn(2 * D * D, D), (2 * D, 0.1, 0.0), ffn(KERNEL * D, KERNEL), vector, gain, vector]
    pieces += [square, vector] + block + [gain, vector]
    offset = 0
    for entries, rate, decay in pieces:
        rates[offset : offset + entries] = rate
        decays[offset : offset + entries] = decay
        offset += entries
    return rates, decays


def whole_tiles(rows):
    return -(-rows // 8) * 8


def digits(devices):
    found, stride = [], 1
    while stride < devices:
        size = min(2 if stride == 1 else 4, devices // stride)
        found.append((stride, size))
        stride *= size
    return found


def place(offset, devices):
    at, weight = 0, devices
    for stride, size in digits(devices):
        weight //= size
        at = at + ((offset // stride) % size) * weight
    return at


def partner(values, offset, devices):
    return lax.ppermute(values, "dp", [(i, i ^ offset) for i in range(devices)])


def gather(values, devices, beside):
    held, made = values[None], []
    for k, (stride, size) in enumerate(reversed(digits(devices))):
        parts = [held] + [partner(held, stride * j, devices) for j in range(1, size)]
        if k < len(beside):
            parts, found = lax.optimization_barrier((parts, beside[k]))
            made.append(found)
        held = jnp.concatenate(parts, axis=0)
    return held, made + beside[len(made) :]


def scatter_sum(keep, send, devices, beside):
    total = keep + partner(send, 1, devices)
    made = None
    for k, (stride, size) in enumerate(digits(devices)[1:]):
        parts = total.reshape((size, total.shape[0] // size) + total.shape[1:])
        kind = bf16 if stride == 2 else f32
        found = [partner(parts[j].astype(kind), stride * j, devices) for j in range(1, size)]
        if k < len(beside):
            found, made = lax.optimization_barrier((found, beside[k](made)))
        total = parts[0]
        for part in found:
            total = total + part.astype(f32)
    for work in beside[max(0, len(digits(devices)) - 1) :]:
        made = work(made)
    return total, made


def local(frames, lengths, cotangent, master, moment_one, moment_two, average):
    shard_len = master.shape[0]
    devices = lax.axis_size("dp")
    rows = shard_len // 128
    me = lax.axis_index("dp").astype(jnp.int32).reshape(1)
    entered = enter(jnp.transpose(frames, (0, 2, 1)))
    mine = jnp.pad(master.astype(bf16).reshape(rows, 128), ((0, whole_tiles(rows) - rows), (0, 0)))
    cp = reorder(inward, jnp.transpose(cotangent, (0, 2, 1)), entered[3], "inward")
    gathered, (entered, cp) = gather(mine, devices, [entered, cp])
    xp, xf, rs_in, pm = entered
    early, late = prepare(me, gathered, rows)
    up1, dn1, wqkv, wo, pw, cols, base = early
    upp1, dnp1, up2, upp2, dn2, dnp2, pwp, pr, prp, wqkvt, wob = late
    lf, xa, nrm, qkv, prob, att, aa, xc, cn, gat, sig, rgt, ra, rc, dep, st = first(
        devices, lengths, xp, xf, (cols, up1, dn1, wqkv, wo, pw, base)
    )
    stats = lax.all_to_all(st, "dp", 0, 0)
    out, bgd, gc, sums, stc, gdn2, gup2, gpr, vec2 = second(
        lengths, stats, cp, aa, dep, (cols, up2, upp2, dn2, dnp2, pr, prp)
    )
    all_sums = lax.all_to_all(sums, "dp", 0, 0)
    last = pack_ahead(gdn2, gup2, vec2)
    out = reorder(outward, out, pm, "outward")
    (all_sums, last, out) = lax.optimization_barrier((all_sums, last, out))
    grad, gdn1, gup1, gpw, gqkv, go, rel, vec3 = third(
        lengths, all_sums, stc,
        (bgd, dep, gat, rs_in, ra, rc),
        (gc, xc, cn, sig, rgt, att, qkv, prob, nrm, lf, xa, xf),
        (cols, up1, upp1, dnp1, wqkvt, wob, pwp),
    )
    keep, send = pack(devices, rows, me, (last, gdn1, gup1, gpr, gpw, gqkv, go, rel, vec3, sums))
    utts = grad.shape[0]
    begin = (utts + 1) // 2
    reduced, gin = scatter_sum(
        keep,
        send,
        devices,
        [
            lambda made: reorder(permute_out_wide, grad, pm, "leave", 0, begin),
            lambda made: reorder(permute_out_wide, grad, pm, "leave", begin, utts - begin, made),
        ],
    )
    reduced = reduced.reshape(-1)[:shard_len]
    rates_np, decays_np = update_tables(shard_len * devices)
    start_at = lax.axis_index("dp") * shard_len
    rates = lax.dynamic_slice_in_dim(jnp.asarray(rates_np), start_at, shard_len)
    decays = lax.dynamic_slice_in_dim(jnp.asarray(decays_np), start_at, shard_len)
    correction = 1.0 - 0.5**STEP
    new_one = 0.5 * moment_one + 0.5 * reduced
    new_two = 0.5 * moment_two + 0.5 * reduced * reduced
    direction = new_one / correction / (jnp.sqrt(new_two / correction) + EPS_ADAM)
    new_master = master - rates * (direction + decays * master)
    new_average = 0.75 * average + 0.25 * new_master
    return (
        jnp.transpose(out, (0, 2, 1)),
        jnp.transpose(gin, (0, 2, 1)),
        reduced,
        new_master,
        new_one,
        new_two,
        new_average,
    )


def solution(mesh):
    three = P("dp", None, None)
    one = P("dp")
    in_specs = (three, one, three, one, one, one, one)
    out_specs = (three, three, one, one, one, one, one)
    return jax.shard_map(local, mesh=mesh, in_specs=in_specs, out_specs=out_specs, check_vma=False)
```

```python
import math

import jax
import jax.numpy as jnp
import numpy as np
from jax import lax
from jax.experimental import pallas as pl
from jax.experimental.pallas import tpu as pltpu
from jax.sharding import PartitionSpec as P

D = 120
HEADS = 4
FF = 480
KERNEL = 15
GROUP = 3
REL = 127
STEP = 5
MAXLEN = 1536
LG = 512
HEAD = 90
HP = 96
GP = HEADS * HP
HALF = KERNEL // 2
WIN = (0, 112, 240)
WROWS = 144
MARKS = tuple(HP * r + HEAD - WIN[r] for r in range(GROUP))

EPS_NORM = 1e-05
EPS_ADAM = 1e-08
NEG_FILL = -1000000000.0
LOG2E = math.log2(math.e)
SCALE = HEAD ** (-0.5)

f32 = jnp.float32
bf16 = jnp.bfloat16
VMEM_BYTES = 58 * 2**20

REL_AT = 174240
TAIL_AT = 175260
TAIL = 1456
ROWS_HEAD = 1452
ROWS_TAIL = 1352
TABLE = 2824
F1 = 0
AT = 967
CV = TAIL
F2 = TAIL + 383
FN = TAIL + 1350
LIVE = 337500

C_F1, C_AT, C_CV, C_BN, C_F2, C_FN, C_DWB, C_DW = 0, 2, 4, 6, 8, 10, 12, 13


def dot(a, b):
    return lax.dot_general(a, b, (((1,), (0,)), ((), ())), preferred_element_type=f32)


def dot_nt(a, b):
    return lax.dot_general(a, b, (((1,), (1,)), ((), ())), preferred_element_type=f32)


def dot_tn(a, b):
    return lax.dot_general(a, b, (((0,), (0,)), ((), ())), preferred_element_type=f32)


def lane_iota(shape):
    return lax.broadcasted_iota(jnp.int32, shape, len(shape) - 1)


def row_iota(shape):
    return lax.broadcasted_iota(jnp.int32, shape, 0)


def segments():
    found = []
    for h in range(HEADS):
        for r in range(GROUP):
            lo, hi = max(HEAD * h, D * r), min(HEAD * h + HEAD, D * r + D)
            if lo < hi:
                found.append((HP * h + lo - HEAD * h, r, lo - D * r, hi - lo))
    return found


def pad8(values):
    return jnp.concatenate([values, jnp.zeros((8, values.shape[1]), f32)], axis=0)


def ext(values):
    width = values.shape[1]
    ones = jnp.where(row_iota((8, width)) == 0, 1.0, 0.0).astype(f32)
    return jnp.concatenate([values, ones], axis=0).astype(bf16)


def norm(values):
    mean = jnp.sum(values, axis=0, keepdims=True) * (1.0 / D)
    centre = values - mean
    var = jnp.sum(centre * centre, axis=0, keepdims=True) * (1.0 / D)
    rstd = lax.rsqrt(var + EPS_NORM)
    return centre * rstd, rstd


def norm_back(upstream, xhat, rstd, gain):
    scaled = upstream * gain
    mean_one = jnp.sum(scaled, axis=0, keepdims=True) * (1.0 / D)
    mean_two = jnp.sum(scaled * xhat, axis=0, keepdims=True) * (1.0 / D)
    return rstd * (scaled - mean_one - xhat * mean_two)


def fold(values):
    total = values[:, 0:128]
    for at in range(128, values.shape[1], 128):
        total = total + values[:, at : at + 128]
    return total


def permute_in(values, pm):
    low = pad8(values).astype(bf16)
    stack = jnp.concatenate([low[:, 384 * b : 384 * b + 384] for b in range(4)], axis=0)
    out = dot(stack, pm)
    tiles = [out[128 * b : 128 * b + D, 128 * r : 128 * r + 128] for r in range(3) for b in range(4)]
    return jnp.concatenate(tiles, axis=1)


def stack_out(values):
    low = pad8(values).astype(bf16)
    blocks = []
    for b in range(4):
        blocks.append(
            jnp.concatenate([low[:, 512 * r + 128 * b : 512 * r + 128 * b + 128] for r in range(3)], axis=1)
        )
    return jnp.concatenate(blocks, axis=0)


def unstack_out(out):
    return jnp.concatenate([out[128 * b : 128 * b + D, :] for b in range(4)], axis=1)


def permute_out(values, pm):
    return unstack_out(dot_nt(stack_out(values), pm))


def permute_out_wide(values, pm):
    high = values.astype(bf16).astype(f32)
    rest = values - high
    mid = rest.astype(bf16).astype(f32)
    return unstack_out(dot_nt(stack_out(high), pm) + dot_nt(stack_out(mid), pm))


def plane_mask(r, length):
    return jnp.where(lane_iota((1, LG)) * GROUP + r < length, 1.0, 0.0).astype(f32)


def span(r):
    return slice(LG * r, LG * r + LG)


def skewed(count, stages):
    held = [None] * count
    for step in range(count + len(stages) - 1):
        for k, stage in enumerate(stages):
            n = step - k
            if 0 <= n < count:
                held[n] = stage(n, held[n])


def window(ref, r, base=0):
    return ref[base + WIN[r] : base + WIN[r] + WROWS, :]


def join_windows(parts):
    a, b, c = parts
    return jnp.concatenate([a[:112], a[112:128] + b[:16], b[16:128], b[128:144] + c[:16], c[16:]], axis=0)


def shifted_planes(tiles):
    lanes = lane_iota((8, 128))
    zero = jnp.zeros((8, 128), f32)
    made = {}
    for m in range(-HALF, HALF + GROUP):
        r, s = m % GROUP, m // GROUP
        if s == 0:
            made[m] = tiles[r]
            continue
        turned = [pltpu.roll(tiles[r][:, 128 * k : 128 * k + 128], (-s) % 128, 1) for k in range(4)]
        if s > 0:
            pairs = zip(turned, turned[1:] + [zero])
            parts = [jnp.where(lanes < 128 - s, a, b) for a, b in pairs]
        else:
            pairs = zip([zero] + turned[:-1], turned)
            parts = [jnp.where(lanes < -s, a, b) for a, b in pairs]
        made[m] = jnp.concatenate(parts, axis=1)
    return made


def shifted(tiles, m):
    r, s = m % GROUP, m // GROUP
    if s == 0:
        return tiles[r]
    lanes = lane_iota((8, 128))
    zero = jnp.zeros((8, 128), f32)
    turned = [pltpu.roll(tiles[r][:, 128 * k : 128 * k + 128], (-s) % 128, 1) for k in range(4)]
    if s > 0:
        pairs = zip(turned, turned[1:] + [zero])
        parts = [jnp.where(lanes < 128 - s, a, b) for a, b in pairs]
    else:
        pairs = zip([zero] + turned[:-1], turned)
        parts = [jnp.where(lanes < -s, a, b) for a, b in pairs]
    return jnp.concatenate(parts, axis=1)


SMEM = pl.BlockSpec(memory_space=pltpu.SMEM)
VMEM = pl.BlockSpec(memory_space=pltpu.VMEM)
BIG = (D, MAXLEN)
LOW = (128, MAXLEN)


def whole(shape):
    zeros = (0,) * len(shape)
    return pl.BlockSpec(shape, lambda u: zeros)


def per_utt(shape):
    zeros = (0,) * len(shape)
    return pl.BlockSpec((1,) + shape, lambda u: (u,) + zeros)


def at_most(shape, utts):
    zeros = (0,) * len(shape)
    return pl.BlockSpec((1,) + shape, lambda u: (jnp.minimum(u, utts - 1),) + zeros)


def one_late(shape):
    zeros = (0,) * len(shape)
    return pl.BlockSpec((1,) + shape, lambda u: (jnp.maximum(u - 1, 0),) + zeros)


def o(shape, kind=bf16):
    return jax.ShapeDtypeStruct(shape, kind)


def params(flops=0, moved=0):
    cost = pl.CostEstimate(flops=flops, bytes_accessed=moved, transcendentals=0)
    return dict(compiler_params=pltpu.CompilerParams(vmem_limit_bytes=VMEM_BYTES), cost_estimate=cost)


def permutation():
    t = row_iota((384, 384))
    c = lane_iota((384, 384))
    return jnp.where(t == GROUP * (c % 128) + c // 128, 1.0, 0.0).astype(bf16)


ANY = pl.BlockSpec(memory_space=pl.ANY)


def streamed(work, far_in, near_in, far_out, near_out, sems, first_utt):
    count = near_in.shape[0]

    def coming(u):
        return pltpu.make_async_copy(far_in.at[u + first_utt], near_in.at[u], sems.at[0, u])

    def going(u):
        pairs = enumerate(zip(near_out, far_out))
        return [pltpu.make_async_copy(near.at[u], far.at[u + first_utt], sems.at[k + 1, u]) for k, (near, far) in pairs]

    for u in range(count):
        coming(u).start()

    def step(u, carry):
        coming(u).wait()
        work(u)
        for copy in going(u):
            copy.start()
        return carry

    lax.fori_loop(0, count, step, 0)
    for u in range(count):
        for copy in going(u):
            copy.wait()


def enter_body(x_far, xp_far, xf_far, rs_far, pm_ref, x_near, xp_near, xf_near, rs_near, sems):
    pm_ref[...] = permutation()

    def work(u):
        x = permute_in(x_near[u].astype(f32), pm_ref[...])
        xp_near[u] = x.astype(bf16)
        xhat, rstd = norm(x)
        xf_near[u] = xhat
        rs_near[u] = jnp.broadcast_to(rstd, (8, MAXLEN))

    streamed(work, x_far, x_near, (xp_far, xf_far, rs_far), (xp_near, xf_near, rs_near), sems, 0)


def enter(x):
    utts = x.shape[0]
    made = [o((utts,) + BIG), o((utts,) + BIG, f32), o((utts, 8, MAXLEN), f32)]
    return pl.pallas_call(
        enter_body,
        in_specs=[ANY],
        out_specs=[ANY] * 3 + [VMEM],
        out_shape=made + [o((384, 384))],
        scratch_shapes=[pltpu.VMEM(m.shape, m.dtype) for m in [x] + made] + [pltpu.SemaphoreType.DMA((4, utts))],
        name="enter",
        **params(2 * 10**9, 8 * 10**6),
    )(x)


def inward(values, pm):
    return permute_in(values.astype(f32), pm).astype(bf16)


def outward(values, pm):
    return permute_out(values.astype(f32), pm).astype(bf16)


def reorder(turn, values, pm, name, first_utt=0, count=None, begun=None):
    count = values.shape[0] if count is None else count
    more = [] if begun is None else [begun]

    def body(far_in, pm_ref, *refs):
        far_out, near_in, near_out, sems = refs[len(more) :]

        def work(u):
            near_out[u] = turn(near_in[u], pm_ref[...])

        streamed(work, far_in, near_in, (far_out,), (near_out,), sems, first_utt)

    room = pltpu.VMEM((count,) + BIG, values.dtype)
    return pl.pallas_call(
        body,
        in_specs=[ANY, VMEM] + [ANY] * len(more),
        out_specs=ANY,
        out_shape=o(values.shape, values.dtype),
        scratch_shapes=[room, room, pltpu.SemaphoreType.DMA((2, count))],
        input_output_aliases={2: 0} if more else {},
        name=name,
        **params(2 * 10**9, 8 * 10**6),
    )(values, pm, *more)


def unpack(me_ref, g_ref, flat, tb):
    parts = g_ref.shape[0]
    part_rows = flat.shape[0] // parts
    for d in range(parts):
        flat[part_rows * d : part_rows * (d + 1), :] = g_ref[place(me_ref[0] ^ d, parts)].astype(f32)[:part_rows]
    tb[ROWS_HEAD:TAIL, :] = jnp.zeros((TAIL - ROWS_HEAD, 128), f32)
    for start, count, base in ((0, ROWS_HEAD, 0), (TAIL_AT, ROWS_TAIL, TAIL)):
        for r in range(16):
            at = start + D * r
            first_row, col = at // 128, at % 128
            many = (count - r + 15) // 16
            here = flat[pl.ds(first_row, many, stride=15), :]
            then = flat[pl.ds(first_row + 1, many, stride=15), :]
            lanes = lane_iota((many, 128))
            got = jnp.where(lanes >= col, here, then)
            if col:
                got = pltpu.roll(got, 128 - col, 1)
            tb[pl.ds(base + r, many, stride=16), :] = jnp.where(lanes < D, got, 0.0)


def with_row(block, row):
    tail = jnp.where(row_iota((8, 128)) == 0, row, 0.0)
    return jnp.concatenate([block, tail], axis=0)


def up_rows(tb, base):
    parts_t = []
    for q in range(4):
        block = tb[pl.ds(base + 2 + q, D, stride=4), :]
        parts_t.append(with_row(block, tb[base + 482 + q : base + 483 + q, :]).T[:D, :])
    return jnp.concatenate(parts_t, axis=0)


def up_across(up_t):
    return jnp.concatenate([up_t, jnp.zeros((32, 128), f32)], axis=0).T[:, :FF].astype(bf16)


def down_across(tb, base):
    bias = jnp.where(row_iota((32, 128)) == 0, tb[base + 966 : base + 967, :], 0.0)
    down = jnp.concatenate([tb[base + 486 : base + 966, :], bias], axis=0)
    return (0.5 * down).T.astype(bf16)


def point_rows(tb):
    parts_t = []
    for q in range(2):
        block = tb[pl.ds(CV + 2 + q, D, stride=2), :]
        parts_t.append(with_row(block, tb[CV + 242 + q : CV + 243 + q, :]).T[:D, :])
    return jnp.concatenate(parts_t, axis=0)


def fill_windows(tb, wt, wins):
    none = jnp.zeros((1, 128), f32)
    wins[...] = jnp.zeros_like(wins)
    for w, at, bias_at in ((0, AT + 2, AT + 122), (1, AT + 123, None), (2, AT + 243, AT + 363)):
        bias = none if bias_at is None else tb[bias_at : bias_at + 1, :]
        wt[...] = with_row(tb[at : at + D, :], bias).T
        for to, r, src, many in segments():
            start = WROWS * w + to - WIN[r]
            wins[r, start : start + many, :] = wt[src : src + many, :]


def fill_output(tb, wins):
    wins[:, 0:256, :] = jnp.zeros((GROUP, 256, 128), f32)
    for to, r, src, many in segments():
        start = to - WIN[r]
        wins[r, start : start + many, :] = tb[AT + 364 + src : AT + 364 + src + many, :]


def early_body(me_ref, g_ref, up_ref, dn_ref, wqkv_ref, wo_ref, pw_ref, cols_ref, base_ref, flat, tb, wt, wins, rows):
    unpack(me_ref, g_ref, flat, tb)
    up_ref[...] = (0.5 * up_rows(tb, F1)).astype(bf16)
    dn_ref[...] = down_across(tb, F1)
    pw_ref[...] = (0.5 * point_rows(tb)).astype(bf16)
    fill_windows(tb, wt, wins)
    for r in range(GROUP):
        wqkv_ref[r] = wins[r, : 3 * WROWS].astype(bf16)
    fill_output(tb, wins)
    for r in range(GROUP):
        wins[r, MARKS[r] : MARKS[r] + 1, :] = tb[AT + 484 : AT + 485, :]
        wo_ref[r] = wins[r, 0:256, :].T[:, :WROWS].astype(bf16)

    rows[...] = jnp.zeros_like(rows)
    listed = []
    for base in (F1, AT, CV, CV + 260, F2, FN):
        listed += [base, base + 1]
    listed += [CV + 259] + [CV + 244 + k for k in range(KERNEL)]
    for to, src in enumerate(listed):
        rows[to : to + 1, :] = tb[src : src + 1, :]
    cols_ref[...] = rows[...].T

    rel_rows = []
    lanes = lane_iota((1, 128))
    for h in range(HEADS):
        at = REL_AT + (2 * REL + 1) * h
        first_row, col = at // 128, at % 128
        pieces = []
        for k in range(2):
            here = flat[first_row + k : first_row + k + 1, :]
            got = jnp.where(lanes >= col, here, flat[first_row + k + 1 : first_row + k + 2, :])
            pieces.append(pltpu.roll(got, (128 - col) % 128, 1) if col else got)
        rel_rows.append(jnp.concatenate(pieces, axis=1))
    rel = jnp.concatenate(rel_rows + [jnp.zeros((4, 256), f32)], axis=0)
    rel = jnp.where(lane_iota((8, 256)) < 2 * REL + 1, rel, 0.0)
    base_ref[...] = dot(rel.astype(bf16), distance_select()) * LOG2E


def late_body(
    me_ref, g_ref, upp1_ref, dnp1_ref, up2_ref, upp2_ref, dn2_ref, dnp2_ref, pwp_ref, pr_ref, prp_ref, wqkvt_ref, wob_ref,
    flat, tb, wt, wins,
):
    unpack(me_ref, g_ref, flat, tb)
    upp1_ref[...] = up_across(up_rows(tb, F1))
    dnp1_ref[...] = (0.25 * tb[F1 + 486 : F1 + 966, :]).astype(bf16)
    up_t = up_rows(tb, F2)
    up2_ref[...] = (0.5 * up_t).astype(bf16)
    upp2_ref[...] = up_across(up_t)
    dn2_ref[...] = down_across(tb, F2)
    dnp2_ref[...] = (0.25 * tb[F2 + 486 : F2 + 966, :]).astype(bf16)
    pwp_ref[...] = jnp.concatenate([point_rows(tb), jnp.zeros((16, 128), f32)], axis=0).T[:, :240].astype(bf16)
    block = with_row(tb[CV + 262 : CV + 382, :], tb[CV + 382 : CV + 383, :])
    prp_ref[...] = (0.5 * block).astype(bf16)
    pr_ref[...] = block.T.astype(bf16)
    fill_windows(tb, wt, wins)
    for r in range(GROUP):
        wqkvt_ref[r] = wins[r].T[:, : 3 * WROWS].astype(bf16)
    fill_output(tb, wins)
    for r in range(GROUP):
        wob_ref[r] = wins[r, 0:WROWS, :].astype(bf16)


def distance_select():
    l = lane_iota((256, 2 * LG))
    gap = jnp.where(l < LG, -l, 2 * LG - l)
    index = jnp.clip(gap, -REL, REL) + REL
    return jnp.where(row_iota((256, 2 * LG)) == index, 1.0, 0.0).astype(bf16)


def spread_table(line, tab, h):
    blocks = {}
    for gap in (-1, 0, 1):
        tiles = [line[:, 128 * (k % 8) : 128 * (k % 8) + 128] for k in (gap - 1, gap)]
        both = jnp.broadcast_to(jnp.concatenate(tiles, axis=1), (128, 256))
        blocks[gap] = pltpu.roll(both, 0, 1, stride=1, stride_axis=0)[:, 128:]
    blocks[2] = jnp.broadcast_to(line[:, 256:257], (128, 128))
    blocks[-2] = jnp.broadcast_to(line[:, 768:769], (128, 128))
    for j in range(4):
        for i in range(4):
            tab[h, 128 * j : 128 * j + 128, 128 * i : 128 * i + 128] = blocks[max(-2, min(2, i - j))]


def block_of(values, j, i):
    return values[128 * j : 128 * j + 128, 128 * i : 128 * i + 128]


def add_distances(values, near, far, h):
    for gap in (-1, 0, 1):
        parts = [block_of(values, j, j + gap) for j in range(4) if 0 <= j + gap < 4]
        total = parts[0]
        for part in parts[1:]:
            total = total + part
        near[h, :, 128 * (gap + 1) : 128 * (gap + 2)] += total
    for k, blocks in enumerate((((0, 2), (0, 3), (1, 3)), ((2, 0), (3, 0), (3, 1)))):
        total = sum(block_of(values, j, i) for j, i in blocks)
        rows = total[0:8]
        for at in range(8, 128, 8):
            rows = rows + total[at : at + 8]
        far[h, k] += rows


def diagonal_sum(near, far):
    wide_rows = jnp.concatenate([near, jnp.zeros((128, 128), f32)], axis=1)
    half = 64
    while half:
        wide_rows = wide_rows[:half] + pltpu.roll(wide_rows[half : 2 * half], LG - half, 1)
        half //= 2
    tiles = [wide_rows[:, 128 * k : 128 * k + 128] for k in range(4)]
    none = jnp.zeros((1, 128), f32)
    plus = jnp.sum(far[0], axis=0, keepdims=True)
    minus = jnp.sum(far[1], axis=0, keepdims=True)
    return jnp.concatenate([tiles[1], tiles[2], plus, none, none, minus, tiles[3], tiles[0]], axis=1)


def prepare(me, gathered, rows):
    total = gathered.shape[0] * rows
    room = [
        pltpu.VMEM((total, 128), f32),
        pltpu.VMEM((TABLE, 128), f32),
        pltpu.VMEM((128, 128), f32),
        pltpu.VMEM((GROUP, 512, 128), f32),
    ]
    early = pl.pallas_call(
        early_body,
        in_specs=[SMEM, VMEM],
        out_shape=[o((FF, 128)), o((128, 512)), o((GROUP, 3 * WROWS, 128)), o((GROUP, 128, WROWS)), o((240, 128))]
        + [o((128, 128), f32), o((8, 2 * LG), f32)],
        scratch_shapes=room + [pltpu.VMEM((128, 128), f32)],
        name="prepare",
        **params(10**9, 2 * 10**6),
    )(me, gathered)
    late = pl.pallas_call(
        late_body,
        in_specs=[SMEM, VMEM],
        out_shape=[o((128, FF)), o((FF, 128)), o((FF, 128)), o((128, FF)), o((128, 512)), o((FF, 128))]
        + [o((128, 240)), o((128, 128)), o((128, 128)), o((GROUP, 128, 3 * WROWS)), o((GROUP, WROWS, 128))],
        scratch_shapes=room,
        name="late",
        **params(3 * 10**9, 10 * 10**6),
    )(me, gathered)
    return early, late


def column(cols, k):
    return cols[:D, k : k + 1]


def valid_keys(length):
    return row_iota((LG, 1)) * GROUP < length


def lane_sums(vec):
    lanes = lane_iota((D, 128))
    table = jnp.zeros((D, 128), f32)
    for k in range(vec.shape[0]):
        table = jnp.where(lanes == k, jnp.sum(vec[k], axis=1, keepdims=True), table)
    return pad8(table).T


def set_tail(hid):
    hid[FF:, :] = jnp.where(row_iota((512 - FF, hid.shape[1])) == 0, 1.0, 0.0).astype(bf16)


def conv_columns(cols, cb):
    for k in range(KERNEL + 1):
        cb[k] = jnp.broadcast_to(cols[:D, C_DWB + k : C_DWB + k + 1], (D, 128))


def wide(tile, copies=4):
    return jnp.concatenate([tile] * copies, axis=1)


def first_body(
    len_ref, xp_ref, xf_ref, cols_ref, up_ref, dn_ref, wqkv_ref, wo_ref, pw_ref, base_ref,
    lf_ref, xa_ref, nrm_ref, qkv_ref, prob_ref, att_ref, aa_ref, xc_ref, cn_ref, gat_ref, sig_ref, rgt_ref,
    ra_ref, rc_ref, dep_ref, st_ref,
    hid, one, cb, tab, run,
):
    u = pl.program_id(0)
    length = len_ref[u]

    @pl.when(u == 0)
    def _():
        set_tail(hid)
        run[...] = jnp.zeros_like(run)
        conv_columns(cols_ref, cb)
        for h in range(HEADS):
            spread_table(base_ref[h : h + 1, :], tab, h)

    cols = cols_ref

    def ffn_up(r, held):
        low = ext(xf_ref[0, :, span(r)] * column(cols, C_F1) + column(cols, C_F1 + 1))
        lf_ref[0, :, span(r)] = low
        return dot(up_ref[...], low)

    def ffn_down(r, half):
        hid[:FF, span(r)] = (half + half * jnp.tanh(half)).astype(bf16)
        return dot(dn_ref[...], hid[:, span(r)])[:D]

    def ffn_norm(r, branch):
        after = xp_ref[0, :, span(r)].astype(f32) + branch
        one[:, span(r)] = after
        xhat, rstd = norm(after)
        xa_ref[0, :, span(r)] = xhat
        ra_ref[0, 0:1, span(r)] = rstd
        low = ext(xhat * column(cols, C_AT) + column(cols, C_AT + 1))
        nrm_ref[0, 128 * r : 128 * r + 128, :] = low
        return dot(wqkv_ref[r], low)

    made = [None] * GROUP

    def ffn_keep(r, found):
        made[r] = found

    skewed(GROUP, (ffn_up, ffn_down, ffn_norm, ffn_keep))
    for w in range(3):
        joined = join_windows([made[r][WROWS * w : WROWS * w + WROWS] for r in range(GROUP)])
        qkv_ref[0, GP * w : GP * w + GP, :] = joined.astype(bf16)
    keys = valid_keys(length)

    def rows(w, h):
        return slice(GP * w + HP * h, GP * w + HP * h + HP)

    def score(h, held):
        return dot_tn(qkv_ref[0, rows(1, h), :], qkv_ref[0, rows(0, h), :])

    def soften(h, raw):
        scores = raw * (SCALE * LOG2E) + tab[h]
        scores = jnp.where(keys, scores, NEG_FILL * LOG2E)
        peak = jnp.max(scores, axis=0, keepdims=True)
        power = jnp.exp2(scores - peak)
        total = jnp.sum(power, axis=0, keepdims=True)
        prob_ref[0, h] = (power * (1.0 / total)).astype(bf16)

    def mix(h, held):
        mixed = dot(qkv_ref[0, rows(2, h), :], prob_ref[0, h])
        if h < GROUP:
            mixed = jnp.where(row_iota((HP, LG)) == HEAD, 1.0, mixed)
        att_ref[0, rows(0, h), :] = mixed.astype(bf16)

    skewed(HEADS, (score, soften, mix))

    def project(r, held):
        return dot(wo_ref[r], window(att_ref.at[0], r))[:D]

    def gate_in(r, mixed):
        after = one[:, span(r)] + mixed
        aa_ref[0, :, span(r)] = after
        xhat, rstd = norm(after)
        xc_ref[0, :, span(r)] = xhat
        rc_ref[0, 0:1, span(r)] = rstd
        low = ext(xhat * column(cols, C_CV) + column(cols, C_CV + 1))
        cn_ref[0, :, span(r)] = low
        return dot(pw_ref[...], low)

    def gate_out(r, pre):
        mask = plane_mask(r, length)
        sig = (0.5 + 0.5 * jnp.tanh(pre[D:])) * mask
        gated = (pre[:D] + pre[:D]) * sig
        gat_ref[0, :, span(r)] = gated
        sig_ref[0, :, span(r)] = sig
        rgt_ref[0, :, span(r)] = gated * (1.0 - sig)

    skewed(GROUP, (project, gate_in, gate_out))

    def conv(f, carry):
        at = slice(8 * f, 8 * f + 8)
        tiles = [gat_ref[0, at, span(r)] for r in range(GROUP)]
        totals = [wide(cb[0, at, :])] * GROUP
        for m in range(-HALF, HALF + GROUP):
            here = shifted(tiles, m)
            for r in range(GROUP):
                k = m + HALF - r
                if 0 <= k < KERNEL:
                    totals[r] = totals[r] + wide(cb[1 + k, at, :]) * here
        for r in range(GROUP):
            dep_ref[0, at, span(r)] = totals[r]
        return carry

    for f in range(D // 8):
        conv(f, 0)

    count = length.astype(f32)
    mask = jnp.concatenate([plane_mask(r, length) for r in range(GROUP)], axis=1)
    dep = dep_ref[0]
    mean = jnp.sum(dep * mask, axis=1, keepdims=True) / count
    gap = (dep - mean) * mask
    spread = jnp.sum(gap * gap, axis=1, keepdims=True)
    old_mean, old_spread, old_count = run[0], run[1], run[2]
    new_count = old_count + count
    step = mean - old_mean
    new_mean = old_mean + step * (count / new_count)
    new_spread = old_spread + spread + step * step * (old_count * count / new_count)
    run[0] = new_mean
    run[1] = new_spread
    run[2] = new_count

    @pl.when(u == pl.num_programs(0) - 1)
    def _():
        lanes = lane_iota((D, 128))
        picked = jnp.where(lanes == 0, run[0], jnp.where(lanes == 1, run[1], jnp.where(lanes == 2, run[2], 0.0)))
        line = pad8(picked).T[0:8]
        for d in range(st_ref.shape[0]):
            st_ref[d] = line


def first(devices, lengths, xp, xf, weights):
    utts = xp.shape[0]
    per = [
        (LOW, bf16),
        (BIG, f32),
        ((GP, LG), bf16),
        ((3 * GP, LG), bf16),
        ((HEADS, LG, LG), bf16),
        ((GP, LG), bf16),
        (BIG, f32),
        (BIG, f32),
        (LOW, bf16),
        (BIG, f32),
        (BIG, f32),
        (BIG, f32),
        ((8, MAXLEN), f32),
        ((8, MAXLEN), f32),
        (BIG, f32),
    ]
    line = (devices, 8, 128)
    return pl.pallas_call(
        first_body,
        grid=(utts,),
        in_specs=[SMEM, per_utt(BIG), per_utt(BIG)] + [whole(w.shape) for w in weights],
        out_specs=[per_utt(s) for s, k in per] + [whole(line)],
        out_shape=[o((utts,) + s, k) for s, k in per] + [o(line, f32)],
        scratch_shapes=[
            pltpu.VMEM((512, MAXLEN), bf16),
            pltpu.VMEM(BIG, f32),
            pltpu.VMEM((KERNEL + 1, D, 128), f32),
            pltpu.VMEM((HEADS, LG, LG), f32),
            pltpu.VMEM((3, D, 128), f32),
        ],
        name="first",
        **params(10 * 10**9, 60 * 10**6),
    )(lengths, xp, xf, *weights)


def second_body(
    len_ref, stats_ref, cot_ref, aa_ref, dep_ref, cols_ref, up_ref, upp_ref, dn_ref, dnp_ref, pr_ref, prp_ref,
    out_ref, bgd_ref, gc_ref, sums_ref, stc_ref, gdn_ref, gup_ref, gpr_ref, vec_ref,
    hid, acc,
):
    u = pl.program_id(0)
    length = len_ref[u]
    cols = cols_ref

    @pl.when(u == 0)
    def _():
        set_tail(hid)
        parts = stats_ref.shape[0]
        count = jnp.zeros((1, 128), f32)
        total = jnp.zeros((1, 128), f32)
        for d in range(parts):
            many = stats_ref[d, 2:3, :]
            count = count + many
            total = total + many * stats_ref[d, 0:1, :]
        here = lane_iota((1, 128)) < D
        count = jnp.where(here, count, 1.0)
        mean = total / count
        spread = jnp.zeros((1, 128), f32)
        for d in range(parts):
            gap = stats_ref[d, 0:1, :] - mean
            spread = spread + stats_ref[d, 1:2, :] + stats_ref[d, 2:3, :] * gap * gap
        scale = lax.rsqrt(spread / count + EPS_NORM)
        at = row_iota((128, 128))
        table = jnp.where(at == 0, mean, jnp.where(at == 1, scale, jnp.where(at == 2, 1.0 / count, 0.0)))
        stc_ref[...] = table.T
        gdn_ref[...] = jnp.zeros_like(gdn_ref)
        gup_ref[...] = jnp.zeros_like(gup_ref)
        gpr_ref[...] = jnp.zeros_like(gpr_ref)
        vec_ref[...] = jnp.zeros_like(vec_ref)
        acc[...] = jnp.zeros_like(acc)

    half_gain = 0.5 * column(cols, C_BN)
    half_bias = 0.5 * column(cols, C_BN + 1)

    def enter(r, held):
        normal = (dep_ref[0, :, span(r)] - stc_ref[:D, 0:1]) * stc_ref[:D, 1:2]
        z = normal * half_gain + half_bias
        t = jnp.tanh(z)
        act = z + z * t
        act_low = ext(act)
        slope = (1.0 + t) * (1.0 + z * (1.0 - t))
        return act_low, normal, slope, dot(pr_ref[...], act_low)[:D]

    def ffn_up(r, held):
        act_low, normal, slope, moved = held
        after_conv = aa_ref[0, :, span(r)] + moved
        xhat, rstd = norm(after_conv)
        low = ext(xhat * column(cols, C_F2) + column(cols, C_F2 + 1))
        return act_low, normal, slope, after_conv, xhat, rstd, low, dot(up_ref[...], low)

    def ffn_down(r, held):
        act_low, normal, slope, after_conv, xhat, rstd, low, half = held
        t = jnp.tanh(half)
        hid[:FF, span(r)] = (half + half * t).astype(bf16)
        bend = (1.0 + t) * (1.0 + half * (1.0 - t))
        return act_low, normal, slope, after_conv, xhat, rstd, low, bend, dot(dn_ref[...], hid[:, span(r)])[:D]

    def finish(r, held):
        act_low, normal, slope, after_conv, xhat, rstd, low, bend, branch = held
        mask = plane_mask(r, length)
        xhat_f, rstd_f = norm(after_conv + branch)
        made = (xhat_f * column(cols, C_FN) + column(cols, C_FN + 1)) * mask
        out_ref[0, :, span(r)] = made.astype(bf16)
        up_grad = cot_ref[0, :, span(r)].astype(f32) * mask
        vec_ref[2] += fold(up_grad * xhat_f)
        vec_ref[3] += fold(up_grad)
        grad_two = norm_back(up_grad, xhat_f, rstd_f, column(cols, C_FN))
        branch = pad8(grad_two).astype(bf16)
        gdn_ref[...] += dot_nt(hid[:, span(r)], branch)
        return act_low, normal, slope, xhat, rstd, low, bend, grad_two, dot(dnp_ref[...], branch)

    def ffn_back(r, held):
        act_low, normal, slope, xhat, rstd, low, bend, grad_two, back = held
        pre_low = (bend * back).astype(bf16)
        gup_ref[...] += dot_nt(pre_low, low)
        return act_low, normal, slope, xhat, rstd, grad_two, dot(upp_ref[...], pre_low)[:D]

    def leave(r, held):
        act_low, normal, slope, xhat, rstd, grad_two, back = held
        vec_ref[0] += fold(back * xhat)
        vec_ref[1] += fold(back)
        grad_conv = grad_two + norm_back(back, xhat, rstd, column(cols, C_F2))
        gc_ref[0, :, span(r)] = grad_conv
        project = pad8(grad_conv).astype(bf16)
        gpr_ref[...] += dot_nt(act_low, project)
        return normal, slope, dot(prp_ref[...], project)[:D]

    def last(r, held):
        normal, slope, back = held
        batch = slope * back
        bgd_ref[0, :, span(r)] = batch
        acc[0] += fold(batch * normal)
        acc[1] += fold(batch)

    skewed(GROUP, (enter, ffn_up, ffn_down, finish, ffn_back, leave, last))

    @pl.when(u == pl.num_programs(0) - 1)
    def _():
        lanes = lane_iota((D, 128))
        gain = jnp.sum(acc[0], axis=1, keepdims=True)
        shift = jnp.sum(acc[1], axis=1, keepdims=True)
        line = pad8(jnp.where(lanes == 0, gain, jnp.where(lanes == 1, shift, 0.0))).T[0:8]
        for d in range(sums_ref.shape[0]):
            sums_ref[d] = line


def second(lengths, stats, cot, aa, dep, weights):
    utts = cot.shape[0]
    big = (D, MAXLEN)
    outs = [
        (per_utt(big), (utts,) + big, bf16),
        (per_utt(big), (utts,) + big, f32),
        (per_utt(big), (utts,) + big, f32),
    ]
    for s in (stats.shape, (128, 128), (512, 128), (FF, 128), (128, 128), (4, D, 128)):
        outs.append((whole(s), s, f32))
    return pl.pallas_call(
        second_body,
        grid=(utts,),
        in_specs=[SMEM, whole(stats.shape)] + [per_utt(big)] * 3 + [whole(w.shape) for w in weights],
        out_specs=[o[0] for o in outs],
        out_shape=[jax.ShapeDtypeStruct(o[1], o[2]) for o in outs],
        scratch_shapes=[
            pltpu.VMEM((512, MAXLEN), bf16),
            pltpu.VMEM((2, D, 128), f32),
        ],
        name="second",
        **params(15000000000, 30000000),
    )(lengths, stats, cot, aa, dep, *weights)


def third_body(
    len_ref, sums_ref, stc_ref, bgd_ref, dep_ref, gat_ref, ri_ref, ra_ref, rc_ref,
    gc_far, xc_far, cn_far, sig_far, rgt_far, att_far, qkv_far, prob_far, nrm_far, lf_far, xa_far, xf_far,
    cols_ref, up_ref, upp_ref, dnp_ref, wqkv_t_ref, wob_ref, pwp_ref,
    grad_ref, gdn_ref, gup_ref, gpw_ref, gqkv_ref, go_ref, rel_ref, rows_ref,
    gc_ref, xc_ref, cn_ref, sig_ref, rgt_ref, att_ref, qkv_ref, prob_ref, nrm_ref, lf_ref, xa_ref, xf_ref, sems,
    hid, dgx, dgs, olg, agr, back_s, gg, near_s, far_s, vec_ref, cb, tot,
):
    far = (gc_far, xc_far, cn_far, sig_far, rgt_far, att_far, qkv_far, prob_far, nrm_far, lf_far, xa_far, xf_far)
    near = (gc_ref, xc_ref, cn_ref, sig_ref, rgt_ref, att_ref, qkv_ref, prob_ref, nrm_ref, lf_ref, xa_ref, xf_ref)
    u = pl.program_id(0)
    utts = pl.num_programs(0) - 1
    slot = 1 - u % 2

    def copies(step):
        at = step % 2
        return [pltpu.make_async_copy(far[i].at[step], near[i].at[at], sems.at[i, at]) for i in range(len(far))]

    cols = cols_ref

    @pl.when(u == 0)
    def _():
        set_tail(hid)
        conv_columns(cols_ref, cb)
        parts = sums_ref.shape[0]
        total = sums_ref[0]
        for d in range(1, parts):
            total = total + sums_ref[d]
        tot[...] = jnp.concatenate([total, jnp.zeros((120, 128), f32)], axis=0).T
        for ref in (gdn_ref, gup_ref, gpw_ref, gqkv_ref, go_ref, vec_ref, near_s, far_s):
            ref[...] = jnp.zeros_like(ref)

    @pl.when(u < utts)
    def _():
        for copy in copies(u):
            copy.start()

    @pl.when(u > 0)
    def _():
        for copy in copies(u - 1):
            copy.wait()

    def front():
        scale = stc_ref[:D, 1:2]
        lead = column(cols, C_BN) * scale
        share = lead * stc_ref[:D, 2:3]
        shift_part = share * tot[:D, 1:2]
        gain_part = share * tot[:D, 0:1] * scale
        for r in range(GROUP):
            normal = dep_ref[0, :, span(r)] - stc_ref[:D, 0:1]
            mask = plane_mask(r, len_ref[u])
            dgx[:, span(r)] = bgd_ref[0, :, span(r)] * lead - mask * (shift_part + normal * gain_part)

        def conv(f, carry):
            at = slice(8 * f, 8 * f + 8)
            tiles = [dgx[at, span(r)] for r in range(GROUP)]
            gated = [gat_ref[0, at, span(r)] for r in range(GROUP)]
            totals = [None] * GROUP
            taps = [None] * KERNEL
            for m in range(-HALF, HALF + GROUP):
                here = shifted(tiles, m)
                for r in range(GROUP):
                    k = r + HALF - m
                    if 0 <= k < KERNEL:
                        term = wide(cb[1 + k, at, :]) * here
                        totals[r] = term if totals[r] is None else totals[r] + term
                        part = fold(gated[r] * here)
                        taps[k] = part if taps[k] is None else taps[k] + part
            vec_ref[6, at, :] += fold(tiles[0] + tiles[1] + tiles[2])
            for k in range(KERNEL):
                vec_ref[7 + k, at, :] += taps[k]
            for r in range(GROUP):
                gg[at, span(r)] = totals[r]
            return carry

        for f in range(D // 8):
            conv(f, 0)

    def back():
        def gate(r, held):
            grad = gg[:, span(r)]
            left = grad * sig_ref[slot, :, span(r)]
            right = grad * rgt_ref[slot, :, span(r)]
            pre_low = jnp.concatenate([left, right], axis=0).astype(bf16)
            gpw_ref[...] += dot_nt(pre_low, cn_ref[slot, :, span(r)])
            return dot(pwp_ref[...], pre_low)[:D]

        def residual(r, back):
            xhat = xc_ref[slot, :, span(r)]
            vec_ref[0] += fold(back * xhat)
            vec_ref[1] += fold(back)
            grad = gc_ref[slot, :, span(r)] + norm_back(back, xhat, rc_ref[0, 0:1, span(r)], column(cols, C_CV))
            dgs[:, span(r)] = grad
            low = pad8(grad).astype(bf16)
            olg[128 * r : 128 * r + 128, :] = low
            return dot(wob_ref[r], low)

        made = [None] * GROUP

        def keep(r, found):
            go_ref[r] += dot_nt(window(att_ref.at[slot], r), olg[128 * r : 128 * r + 128, :])
            made[r] = found

        skewed(GROUP, (gate, residual, keep))
        agr[...] = join_windows(made).astype(bf16)

        def rows(w, h):
            return slice(GP * w + HP * h, GP * w + HP * h + HP)

        def enter(h, held):
            grad = agr[rows(0, h), :]
            back_s[rows(2, h), :] = dot_nt(grad, prob_ref[slot, h]).astype(bf16)
            return dot_tn(qkv_ref[slot, rows(2, h), :], grad)

        def soften(h, prob_grad):
            probs = prob_ref[slot, h].astype(f32)
            inner = jnp.sum(probs * prob_grad, axis=0, keepdims=True)
            score = probs * (prob_grad - inner)
            add_distances(score, near_s, far_s, h)
            return score.astype(bf16)

        def turn(h, low):
            back_s[rows(0, h), :] = (dot(qkv_ref[slot, rows(1, h), :], low) * SCALE).astype(bf16)
            back_s[rows(1, h), :] = (dot_nt(qkv_ref[slot, rows(0, h), :], low) * SCALE).astype(bf16)

        skewed(HEADS, (enter, soften, turn))

        def project(r, held):
            stack = jnp.concatenate([window(back_s, r, GP * w) for w in range(3)], axis=0)
            gqkv_ref[r] += dot_nt(stack, nrm_ref[slot, 128 * r : 128 * r + 128, :])
            return dot(wqkv_t_ref[r], stack)[:D], dot(up_ref[...], lf_ref[slot, :, span(r)])

        def ffn_in(r, held):
            back, half = held
            xhat = xa_ref[slot, :, span(r)]
            vec_ref[2] += fold(back * xhat)
            vec_ref[3] += fold(back)
            grad = dgs[:, span(r)] + norm_back(back, xhat, ra_ref[0, 0:1, span(r)], column(cols, C_AT))
            low = pad8(grad).astype(bf16)
            return grad, low, half, dot(dnp_ref[...], low)

        def ffn_mid(r, held):
            grad, branch, half, back = held
            t = jnp.tanh(half)
            hid[:FF, span(r)] = (half + half * t).astype(bf16)
            pre_low = ((1.0 + t) * (1.0 + half * (1.0 - t)) * back).astype(bf16)
            gdn_ref[...] += dot_nt(hid[:, span(r)], branch)
            gup_ref[...] += dot_nt(pre_low, lf_ref[slot, :, span(r)])
            return grad, dot(upp_ref[...], pre_low)[:D]

        def ffn_out(r, held):
            grad, back = held
            xhat = xf_ref[slot, :, span(r)]
            vec_ref[4] += fold(back * xhat)
            vec_ref[5] += fold(back)
            grad_ref[0, :, span(r)] = grad + norm_back(back, xhat, ri_ref[0, 0:1, span(r)], column(cols, C_F1))

        skewed(GROUP, (project, ffn_in, ffn_mid, ffn_out))

    @pl.when(u == 0)
    def _():
        front()

    @pl.when((u > 0) & (u < utts))
    def _():
        back()
        front()

    @pl.when(u == utts)
    def _():
        back()
        rows_ref[...] = lane_sums(vec_ref)
        found = []
        for h in range(HEADS):
            found.append(diagonal_sum(near_s[h], far_s[h]))
        stacked = jnp.concatenate(found + [jnp.zeros((4, 2 * LG), f32)], axis=0)
        high = stacked.astype(bf16)
        rest = stacked - high.astype(f32)
        mid = rest.astype(bf16)
        rest = rest - mid.astype(f32)
        select = distance_select()
        rel_ref[...] = dot_nt(high, select) + dot_nt(mid, select) + dot_nt(rest.astype(bf16), select)


def third(lengths, sums, stc, soon, later, weights):
    utts = soon[0].shape[0]
    big = (D, MAXLEN)
    outs = [(one_late(big), (utts,) + big)]
    for s in ((512, 128), (FF, 128), (240, 128), (GROUP, 3 * WROWS, 128), (GROUP, WROWS, 128), (8, 256), (128, 128)):
        outs.append((whole(s), s))
    return pl.pallas_call(
        third_body,
        grid=(utts + 1,),
        in_specs=[SMEM, whole(sums.shape), whole(stc.shape)]
        + [at_most(s.shape[1:], utts) for s in soon[:3]]
        + [one_late(s.shape[1:]) for s in soon[3:]]
        + [pl.BlockSpec(memory_space=pl.ANY)] * len(later)
        + [whole(w.shape) for w in weights],
        out_specs=[o[0] for o in outs],
        out_shape=[jax.ShapeDtypeStruct(o[1], f32) for o in outs],
        scratch_shapes=[pltpu.VMEM((2,) + s.shape[1:], s.dtype) for s in later]
        + [
            pltpu.SemaphoreType.DMA((len(later), 2)),
            pltpu.VMEM((512, MAXLEN), bf16),
            pltpu.VMEM(big, f32),
            pltpu.VMEM(big, f32),
            pltpu.VMEM((GP, LG), bf16),
            pltpu.VMEM((GP, LG), bf16),
            pltpu.VMEM((3 * GP, LG), bf16),
            pltpu.VMEM(big, f32),
            pltpu.VMEM((HEADS, 128, 384), f32),
            pltpu.VMEM((HEADS, 2, 8, 128), f32),
            pltpu.VMEM((22, D, 128), f32),
            pltpu.VMEM((KERNEL + 1, D, 128), f32),
            pltpu.VMEM((128, 128), f32),
        ],
        name="third",
        **params(20000000000, 80000000),
    )(lengths, sums, stc, *soon, *later, *weights)


def clean(block):
    return jnp.where(lane_iota(block.shape) < D, block, 0.0)


def set_rows(tb, ref, at):
    for k, to in enumerate(at):
        tb[to : to + 1, :] = ref[k : k + 1, :]


def set_ffn(tb, base, dn_ref, up_ref):
    tb[base + 486 : base + 967, :] = 0.5 * clean(dn_ref[0 : FF + 1, :])
    for q in range(4):
        block = pad8(up_ref[D * q : D * q + D, :]).T
        tb[pl.ds(base + 2 + q, D, stride=4), :] = block[:D]
        tb[base + 482 + q : base + 483 + q, :] = block[D : D + 1]


def flatten(tb, base, flat, at_row, y_count, offset):
    for k in range(15):
        at = 128 * k + offset
        first_row, col = at // D, at % D
        many = (y_count - k + 14) // 15
        here = lane_iota((many, 128))
        got = tb[pl.ds(base + first_row, many, stride=16), :]
        if col:
            got = pltpu.roll(got, 128 - col, 1)
        then = pltpu.roll(tb[pl.ds(base + first_row + 1, many, stride=16), :], D - col, 1)
        got = jnp.where(here < D - col, got, then)
        if 2 * D - col < 128:
            then = pltpu.roll(tb[pl.ds(base + first_row + 2, many, stride=16), :], 2 * D - col, 1)
            got = jnp.where(here < 2 * D - col, got, then)
        flat[pl.ds(at_row + k, many, stride=15), :] = got


SPLIT = F2 - TAIL
ROWS_LAST = ROWS_TAIL - SPLIT
LAST_AT = TAIL_AT + D * SPLIT
LAST_Y = LAST_AT // 128
LAST_COUNT = (LIVE - 1) // 128 - LAST_Y + 1


def ahead_body(dn_ref, up_ref, vec_ref, out_ref, tb, wt):
    tb[0:8, :] = jnp.zeros((8, 128), f32)
    tb[8 + ROWS_LAST :, :] = jnp.zeros((tb.shape[0] - 8 - ROWS_LAST, 128), f32)
    wt[...] = lane_sums(vec_ref)
    set_rows(tb, wt, (8, 9, 8 + FN - F2, 9 + FN - F2))
    set_ffn(tb, 8, dn_ref, up_ref)
    flatten(tb, 7, out_ref, 0, LAST_COUNT, D + 128 * LAST_Y - LAST_AT)


def pack_ahead(dn, up, vec):
    return pl.pallas_call(
        ahead_body,
        out_shape=o((LAST_COUNT, 128), f32),
        scratch_shapes=[pltpu.VMEM((ROWS_LAST + 24, 128), f32), pltpu.VMEM((128, 128), f32)],
        name="ahead",
        **params(2 * 10**9, 8 * 10**6),
    )(dn, up, vec)


def pack_body(
    me_ref, last_ref, dn1_ref, up1_ref, pr_ref, pw_ref, qkv_ref, o_ref, rel_ref, vec_ref, sums_ref,
    keep_ref, send_ref, tb, flat, stage, wt,
):
    tb[ROWS_HEAD:TAIL, :] = jnp.zeros((TAIL - ROWS_HEAD, 128), f32)
    tb[F2:, :] = jnp.zeros((tb.shape[0] - F2, 128), f32)
    set_rows(tb, vec_ref, (CV, CV + 1, AT, AT + 1, F1, F1 + 1, CV + 259) + tuple(CV + 244 + k for k in range(KERNEL)))
    tb[CV + 260 : CV + 262, :] = sums_ref[0, 0:2, :]
    set_ffn(tb, F1, dn1_ref, up1_ref)
    for q in range(2):
        block = pad8(pw_ref[D * q : D * q + D, :]).T
        tb[pl.ds(CV + 2 + q, D, stride=2), :] = block[:D]
        tb[CV + 242 + q : CV + 243 + q, :] = block[D : D + 1]
    tb[CV + 262 : CV + 383, :] = clean(pr_ref[0 : D + 1, :])

    def gathered(ref, base):
        wt[...] = jnp.zeros_like(wt)
        for to, r, src, many in segments():
            start = base + to - WIN[r]
            wt[src : src + many, :] += ref[r, start : start + many, :]
        return wt[...]

    for w, at, bias_at in ((0, AT + 2, AT + 122), (1, AT + 123, None), (2, AT + 243, AT + 363)):
        block = gathered(qkv_ref, WROWS * w).T
        tb[at : at + D, :] = block[:D]
        if bias_at is not None:
            tb[bias_at : bias_at + 1, :] = block[D : D + 1]
    tb[AT + 364 : AT + 484, :] = clean(gathered(o_ref, 0)[:D])
    bias = sum(o_ref[r, MARKS[r] : MARKS[r] + 1, :] for r in range(GROUP))
    tb[AT + 484 : AT + 485, :] = clean(bias)

    tail_y = TAIL_AT // 128
    flat[LAST_Y + LAST_COUNT :, :] = jnp.zeros((flat.shape[0] - LAST_Y - LAST_COUNT, 128), f32)
    flat[REL_AT // 128 + 1 : tail_y, :] = jnp.zeros((tail_y - REL_AT // 128 - 1, 128), f32)
    flatten(tb, 0, flat, 0, REL_AT // 128 + 1, 0)
    flatten(tb, TAIL - 1, flat, tail_y, LAST_Y - tail_y + 1, 128 * tail_y - TAIL_AT + D)
    flat[LAST_Y : LAST_Y + 1, :] += last_ref[0:1, :]
    flat[LAST_Y + 1 : LAST_Y + LAST_COUNT, :] = last_ref[1:, :]
    here = lane_iota((1, 128))
    width = 2 * REL + 1
    for h in range(HEADS):
        at = REL_AT + width * h
        for y in range(at // 128, (at + width - 1) // 128 + 1):
            lo, hi = max(at - 128 * y, 0), min(at + width - 128 * y, 128)
            shift = (at - 128 * y) % 256
            turned = rel_ref[h : h + 1, :]
            if shift:
                turned = pltpu.roll(turned, shift, 1)
            flat[y : y + 1, :] += jnp.where((here >= lo) & (here < hi), turned[:, :128], 0.0)
    parts, padded = 2 * keep_ref.shape[0], keep_ref.shape[1]
    rows = flat.shape[0] // parts
    for d in range(parts):
        stage[d, 0:rows, :] = flat[rows * d : rows * (d + 1), :]
        if rows < padded:
            stage[d, rows:padded, :] = jnp.zeros((padded - rows, 128), f32)
    for offset in range(0, parts, 2):
        keep_ref[place(offset, parts)] = stage[me_ref[0] ^ offset]
        send_ref[place(offset, parts)] = stage[me_ref[0] ^ (offset + 1)]


def pack(parts, rows, me, grads):
    half = o((parts // 2, whole_tiles(rows), 128), f32)
    return pl.pallas_call(
        pack_body,
        in_specs=[SMEM] + [VMEM] * len(grads),
        out_shape=[half, half],
        scratch_shapes=[
            pltpu.VMEM((F2 + 24, 128), f32),
            pltpu.VMEM((parts * rows, 128), f32),
            pltpu.VMEM((parts, whole_tiles(rows), 128), f32),
            pltpu.VMEM((128, 128), f32),
        ],
        name="pack",
        **params(10**9, 5 * 10**6),
    )(me, *grads)


def update_tables(total_len):
    rates = np.zeros(total_len, np.float32)
    decays = np.zeros(total_len, np.float32)
    vector, gain, ffn = (D, 0.1, 0.0), (D, 0.3, 0.0), lambda n, fan: (n, fan**-0.5, 0.01)
    block = [gain, vector, ffn(D * FF, D), (FF, 0.1, 0.0), ffn(FF * D, FF), vector]
    square = ffn(D * D, D)
    pieces = block + [gain, vector, square, vector, square, square, vector, ffn(D * D, 6.0 * D / MAXLEN), vector]
    pieces += [(HEADS * (2 * REL + 1), 0.5, 0.0)]
    pieces += [gain, vector, ffn(2 * D * D, D), (2 * D, 0.1, 0.0), ffn(KERNEL * D, KERNEL), vector, gain, vector]
    pieces += [square, vector] + block + [gain, vector]
    offset = 0
    for entries, rate, decay in pieces:
        rates[offset : offset + entries] = rate
        decays[offset : offset + entries] = decay
        offset += entries
    return rates, decays


def whole_tiles(rows):
    return -(-rows // 8) * 8


def digits(devices):
    found, stride = [], 1
    while stride < devices:
        size = min(2 if stride == 1 else 4, devices // stride)
        found.append((stride, size))
        stride *= size
    return found


def place(offset, devices):
    at, weight = 0, devices
    for stride, size in digits(devices):
        weight //= size
        at = at + ((offset // stride) % size) * weight
    return at


def partner(values, offset, devices):
    return lax.ppermute(values, "dp", [(i, i ^ offset) for i in range(devices)])


def gather(values, devices, beside):
    held, made = values[None], []
    for k, (stride, size) in enumerate(reversed(digits(devices))):
        parts = [held] + [partner(held, stride * j, devices) for j in range(1, size)]
        if k < len(beside):
            parts, found = lax.optimization_barrier((parts, beside[k]))
            made.append(found)
        held = jnp.concatenate(parts, axis=0)
    return held, made + beside[len(made) :]


def scatter_sum(keep, send, devices, beside):
    total = keep + partner(send, 1, devices)
    made = None
    for k, (stride, size) in enumerate(digits(devices)[1:]):
        parts = total.reshape((size, total.shape[0] // size) + total.shape[1:])
        kind = bf16 if stride == 2 else f32
        found = [partner(parts[j].astype(kind), stride * j, devices) for j in range(1, size)]
        if k < len(beside):
            found, made = lax.optimization_barrier((found, beside[k](made)))
        total = parts[0]
        for part in found:
            total = total + part.astype(f32)
    for work in beside[max(0, len(digits(devices)) - 1) :]:
        made = work(made)
    return total, made


def local(frames, lengths, cotangent, master, moment_one, moment_two, average):
    shard_len = master.shape[0]
    devices = lax.axis_size("dp")
    rows = shard_len // 128
    me = lax.axis_index("dp").astype(jnp.int32).reshape(1)
    entered = enter(jnp.transpose(frames, (0, 2, 1)))
    mine = jnp.pad(master.astype(bf16).reshape(rows, 128), ((0, whole_tiles(rows) - rows), (0, 0)))
    cp = reorder(inward, jnp.transpose(cotangent, (0, 2, 1)), entered[3], "inward")
    gathered, (entered, cp) = gather(mine, devices, [entered, cp])
    xp, xf, rs_in, pm = entered
    early, late = prepare(me, gathered, rows)
    up1, dn1, wqkv, wo, pw, cols, base = early
    upp1, dnp1, up2, upp2, dn2, dnp2, pwp, pr, prp, wqkvt, wob = late
    lf, xa, nrm, qkv, prob, att, aa, xc, cn, gat, sig, rgt, ra, rc, dep, st = first(
        devices, lengths, xp, xf, (cols, up1, dn1, wqkv, wo, pw, base)
    )
    stats = lax.all_to_all(st, "dp", 0, 0)
    out, bgd, gc, sums, stc, gdn2, gup2, gpr, vec2 = second(
        lengths, stats, cp, aa, dep, (cols, up2, upp2, dn2, dnp2, pr, prp)
    )
    all_sums = lax.all_to_all(sums, "dp", 0, 0)
    last = pack_ahead(gdn2, gup2, vec2)
    out = reorder(outward, out, pm, "outward")
    (all_sums, last, out) = lax.optimization_barrier((all_sums, last, out))
    grad, gdn1, gup1, gpw, gqkv, go, rel, vec3 = third(
        lengths, all_sums, stc,
        (bgd, dep, gat, rs_in, ra, rc),
        (gc, xc, cn, sig, rgt, att, qkv, prob, nrm, lf, xa, xf),
        (cols, up1, upp1, dnp1, wqkvt, wob, pwp),
    )
    keep, send = pack(devices, rows, me, (last, gdn1, gup1, gpr, gpw, gqkv, go, rel, vec3, sums))
    utts = grad.shape[0]
    begin = (utts + 1) // 2
    reduced, gin = scatter_sum(
        keep,
        send,
        devices,
        [
            lambda made: reorder(permute_out_wide, grad, pm, "leave", 0, begin),
            lambda made: reorder(permute_out_wide, grad, pm, "leave", begin, utts - begin, made),
        ],
    )
    reduced = reduced.reshape(-1)[:shard_len]
    rates_np, decays_np = update_tables(shard_len * devices)
    start_at = lax.axis_index("dp") * shard_len
    rates = lax.dynamic_slice_in_dim(jnp.asarray(rates_np), start_at, shard_len)
    decays = lax.dynamic_slice_in_dim(jnp.asarray(decays_np), start_at, shard_len)
    correction = 1.0 - 0.5**STEP
    new_one = 0.5 * moment_one + 0.5 * reduced
    new_two = 0.5 * moment_two + 0.5 * reduced * reduced
    direction = new_one / correction / (jnp.sqrt(new_two / correction) + EPS_ADAM)
    new_master = master - rates * (direction + decays * master)
    new_average = 0.75 * average + 0.25 * new_master
    return (
        jnp.transpose(out, (0, 2, 1)),
        jnp.transpose(gin, (0, 2, 1)),
        reduced,
        new_master,
        new_one,
        new_two,
        new_average,
    )


def solution(mesh):
    three = P("dp", None, None)
    one = P("dp")
    in_specs = (three, one, three, one, one, one, one)
    out_specs = (three, three, one, one, one, one, one)
    return jax.shard_map(local, mesh=mesh, in_specs=in_specs, out_specs=out_specs, check_vma=False)
```

```python
import math

import jax
import jax.numpy as jnp
import numpy as np
from jax import lax
from jax.experimental import pallas as pl
from jax.experimental.pallas import tpu as pltpu
from jax.sharding import PartitionSpec as P

D = 120
HEADS = 4
FF = 480
KERNEL = 15
GROUP = 3
REL = 127
STEP = 5
MAXLEN = 1536
LG = 512
HEAD = 90
HP = 96
GP = HEADS * HP
HALF = KERNEL // 2
SURE = 128
WIN = (0, 112, 240)
WROWS = 144
MARKS = tuple(HP * r + HEAD - WIN[r] for r in range(GROUP))

EPS_NORM = 1e-05
EPS_ADAM = 1e-08
NEG_FILL = -1000000000.0
LOG2E = math.log2(math.e)
SCALE = HEAD ** (-0.5)

f32 = jnp.float32
bf16 = jnp.bfloat16
VMEM_BYTES = 58 * 2**20

REL_AT = 174240
TAIL_AT = 175260
TAIL = 1456
ROWS_HEAD = 1452
ROWS_TAIL = 1352
TABLE = 2824
F1 = 0
AT = 967
CV = TAIL
F2 = TAIL + 383
FN = TAIL + 1350
LIVE = 337500

C_F1, C_AT, C_CV, C_BN, C_F2, C_FN, C_DWB, C_DW = 0, 2, 4, 6, 8, 10, 12, 13


def dot(a, b):
    return lax.dot_general(a, b, (((1,), (0,)), ((), ())), preferred_element_type=f32)


def dot_nt(a, b):
    return lax.dot_general(a, b, (((1,), (1,)), ((), ())), preferred_element_type=f32)


def dot_tn(a, b):
    return lax.dot_general(a, b, (((0,), (0,)), ((), ())), preferred_element_type=f32)


def lane_iota(shape):
    return lax.broadcasted_iota(jnp.int32, shape, len(shape) - 1)


def row_iota(shape):
    return lax.broadcasted_iota(jnp.int32, shape, 0)


def segments():
    found = []
    for h in range(HEADS):
        for r in range(GROUP):
            lo, hi = max(HEAD * h, D * r), min(HEAD * h + HEAD, D * r + D)
            if lo < hi:
                found.append((HP * h + lo - HEAD * h, r, lo - D * r, hi - lo))
    return found


def pad8(values):
    return jnp.concatenate([values, jnp.zeros((8, values.shape[1]), f32)], axis=0)


def ext(values):
    width = values.shape[1]
    ones = jnp.where(row_iota((8, width)) == 0, 1.0, 0.0).astype(f32)
    return jnp.concatenate([values, ones], axis=0).astype(bf16)


def norm(values):
    mean = jnp.sum(values, axis=0, keepdims=True) * (1.0 / D)
    centre = values - mean
    var = jnp.sum(centre * centre, axis=0, keepdims=True) * (1.0 / D)
    rstd = lax.rsqrt(var + EPS_NORM)
    return centre * rstd, rstd


def norm_back(upstream, xhat, rstd, gain):
    scaled = upstream * gain
    mean_one = jnp.sum(scaled, axis=0, keepdims=True) * (1.0 / D)
    mean_two = jnp.sum(scaled * xhat, axis=0, keepdims=True) * (1.0 / D)
    return rstd * (scaled - mean_one - xhat * mean_two)


def fold(values):
    total = values[:, 0:128]
    for at in range(128, values.shape[1], 128):
        total = total + values[:, at : at + 128]
    return total


def permute_in(values, pm):
    low = pad8(values).astype(bf16)
    stack = jnp.concatenate([low[:, 384 * b : 384 * b + 384] for b in range(4)], axis=0)
    out = dot(stack, pm)
    tiles = [out[128 * b : 128 * b + D, 128 * r : 128 * r + 128] for r in range(3) for b in range(4)]
    return jnp.concatenate(tiles, axis=1)


def stack_out(values):
    low = pad8(values).astype(bf16)
    blocks = []
    for b in range(4):
        blocks.append(
            jnp.concatenate([low[:, 512 * r + 128 * b : 512 * r + 128 * b + 128] for r in range(3)], axis=1)
        )
    return jnp.concatenate(blocks, axis=0)


def unstack_out(out):
    return jnp.concatenate([out[128 * b : 128 * b + D, :] for b in range(4)], axis=1)


def permute_out(values, pm):
    return unstack_out(dot_nt(stack_out(values), pm))


def permute_out_wide(values, pm):
    high = values.astype(bf16).astype(f32)
    rest = values - high
    mid = rest.astype(bf16).astype(f32)
    return unstack_out(dot_nt(stack_out(high), pm) + dot_nt(stack_out(mid), pm))


def plane_mask(r, length):
    return jnp.where(lane_iota((1, LG)) * GROUP + r < length, 1.0, 0.0).astype(f32)


def span(r):
    return slice(LG * r, LG * r + LG)


def skewed(count, stages):
    held = [None] * count
    for step in range(count + len(stages) - 1):
        for k, stage in enumerate(stages):
            n = step - k
            if 0 <= n < count:
                held[n] = stage(n, held[n])


def window(ref, r, base=0):
    return ref[base + WIN[r] : base + WIN[r] + WROWS, :]


def join_windows(parts):
    a, b, c = parts
    return jnp.concatenate([a[:112], a[112:128] + b[:16], b[16:128], b[128:144] + c[:16], c[16:]], axis=0)


def shifted_planes(tiles):
    lanes = lane_iota((8, 128))
    zero = jnp.zeros((8, 128), f32)
    made = {}
    for m in range(-HALF, HALF + GROUP):
        r, s = m % GROUP, m // GROUP
        if s == 0:
            made[m] = tiles[r]
            continue
        turned = [pltpu.roll(tiles[r][:, 128 * k : 128 * k + 128], (-s) % 128, 1) for k in range(4)]
        if s > 0:
            pairs = zip(turned, turned[1:] + [zero])
            parts = [jnp.where(lanes < 128 - s, a, b) for a, b in pairs]
        else:
            pairs = zip([zero] + turned[:-1], turned)
            parts = [jnp.where(lanes < -s, a, b) for a, b in pairs]
        made[m] = jnp.concatenate(parts, axis=1)
    return made


def shifted(tiles, m):
    r, s = m % GROUP, m // GROUP
    if s == 0:
        return tiles[r]
    lanes = lane_iota((8, 128))
    zero = jnp.zeros((8, 128), f32)
    turned = [pltpu.roll(tiles[r][:, 128 * k : 128 * k + 128], (-s) % 128, 1) for k in range(4)]
    if s > 0:
        pairs = zip(turned, turned[1:] + [zero])
        parts = [jnp.where(lanes < 128 - s, a, b) for a, b in pairs]
    else:
        pairs = zip([zero] + turned[:-1], turned)
        parts = [jnp.where(lanes < -s, a, b) for a, b in pairs]
    return jnp.concatenate(parts, axis=1)


SMEM = pl.BlockSpec(memory_space=pltpu.SMEM)
VMEM = pl.BlockSpec(memory_space=pltpu.VMEM)
BIG = (D, MAXLEN)
LOW = (128, MAXLEN)


def whole(shape):
    zeros = (0,) * len(shape)
    return pl.BlockSpec(shape, lambda u: zeros)


def per_utt(shape):
    zeros = (0,) * len(shape)
    return pl.BlockSpec((1,) + shape, lambda u: (u,) + zeros)


def at_most(shape, utts):
    zeros = (0,) * len(shape)
    return pl.BlockSpec((1,) + shape, lambda u: (jnp.minimum(u, utts - 1),) + zeros)


def one_late(shape):
    zeros = (0,) * len(shape)
    return pl.BlockSpec((1,) + shape, lambda u: (jnp.maximum(u - 1, 0),) + zeros)


def o(shape, kind=bf16):
    return jax.ShapeDtypeStruct(shape, kind)


def params(flops=0, moved=0):
    cost = pl.CostEstimate(flops=flops, bytes_accessed=moved, transcendentals=0)
    return dict(compiler_params=pltpu.CompilerParams(vmem_limit_bytes=VMEM_BYTES), cost_estimate=cost)


def permutation():
    t = row_iota((384, 384))
    c = lane_iota((384, 384))
    return jnp.where(t == GROUP * (c % 128) + c // 128, 1.0, 0.0).astype(bf16)


ANY = pl.BlockSpec(memory_space=pl.ANY)


def streamed(work, far_in, near_in, far_out, near_out, sems, first_utt):
    count = near_in.shape[0]

    def coming(u):
        return pltpu.make_async_copy(far_in.at[u + first_utt], near_in.at[u], sems.at[0, u])

    def going(u):
        pairs = enumerate(zip(near_out, far_out))
        return [pltpu.make_async_copy(near.at[u], far.at[u + first_utt], sems.at[k + 1, u]) for k, (near, far) in pairs]

    for u in range(count):
        coming(u).start()

    def step(u, carry):
        coming(u).wait()
        work(u)
        for copy in going(u):
            copy.start()
        return carry

    lax.fori_loop(0, count, step, 0)
    for u in range(count):
        for copy in going(u):
            copy.wait()


def enter_body(x_far, xp_far, xf_far, rs_far, pm_ref, x_near, xp_near, xf_near, rs_near, sems):
    pm_ref[...] = permutation()

    def work(u):
        x = permute_in(x_near[u].astype(f32), pm_ref[...])
        xp_near[u] = x.astype(bf16)
        xhat, rstd = norm(x)
        xf_near[u] = xhat
        rs_near[u] = jnp.broadcast_to(rstd, (8, MAXLEN))

    streamed(work, x_far, x_near, (xp_far, xf_far, rs_far), (xp_near, xf_near, rs_near), sems, 0)


def enter(x):
    utts = x.shape[0]
    made = [o((utts,) + BIG), o((utts,) + BIG, f32), o((utts, 8, MAXLEN), f32)]
    return pl.pallas_call(
        enter_body,
        in_specs=[ANY],
        out_specs=[ANY] * 3 + [VMEM],
        out_shape=made + [o((384, 384))],
        scratch_shapes=[pltpu.VMEM(m.shape, m.dtype) for m in [x] + made] + [pltpu.SemaphoreType.DMA((4, utts))],
        name="enter",
        **params(2 * 10**9, 8 * 10**6),
    )(x)


def inward(values, pm):
    return permute_in(values.astype(f32), pm).astype(bf16)


def outward(values, pm):
    return permute_out(values.astype(f32), pm).astype(bf16)


def reorder(turn, values, pm, name, first_utt=0, count=None, begun=None):
    count = values.shape[0] if count is None else count
    more = [] if begun is None else [begun]

    def body(far_in, pm_ref, *refs):
        far_out, near_in, near_out, sems = refs[len(more) :]

        def work(u):
            near_out[u] = turn(near_in[u], pm_ref[...])

        streamed(work, far_in, near_in, (far_out,), (near_out,), sems, first_utt)

    room = pltpu.VMEM((count,) + BIG, values.dtype)
    return pl.pallas_call(
        body,
        in_specs=[ANY, VMEM] + [ANY] * len(more),
        out_specs=ANY,
        out_shape=o(values.shape, values.dtype),
        scratch_shapes=[room, room, pltpu.SemaphoreType.DMA((2, count))],
        input_output_aliases={2: 0} if more else {},
        name=name,
        **params(2 * 10**9, 8 * 10**6),
    )(values, pm, *more)


def unpack(me_ref, g_ref, flat, tb, regions):
    parts = g_ref.shape[0]
    part_rows = flat.shape[0] // parts
    for d in range(parts):
        flat[part_rows * d : part_rows * (d + 1), :] = g_ref[place(me_ref[0] ^ d, parts)].astype(f32)[:part_rows]
    for base, count in regions:
        start = D * base if base < TAIL else TAIL_AT + D * (base - TAIL)
        for r in range(min(16, count)):
            at = start + D * r
            first_row, col = at // 128, at % 128
            many = (count - r + 15) // 16
            here = flat[pl.ds(first_row, many, stride=15), :]
            then = flat[pl.ds(first_row + 1, many, stride=15), :]
            lanes = lane_iota((many, 128))
            got = jnp.where(lanes >= col, here, then)
            if col:
                got = pltpu.roll(got, 128 - col, 1)
            tb[pl.ds(base + r, many, stride=16), :] = jnp.where(lanes < D, got, 0.0)


def with_row(block, row):
    tail = jnp.where(row_iota((8, 128)) == 0, row, 0.0)
    return jnp.concatenate([block, tail], axis=0)


def up_rows(tb, base):
    parts_t = []
    for q in range(4):
        block = tb[pl.ds(base + 2 + q, D, stride=4), :]
        parts_t.append(with_row(block, tb[base + 482 + q : base + 483 + q, :]).T[:D, :])
    return jnp.concatenate(parts_t, axis=0)


def up_across(up_t):
    return jnp.concatenate([up_t, jnp.zeros((32, 128), f32)], axis=0).T[:, :FF].astype(bf16)


def down_across(tb, base):
    bias = jnp.where(row_iota((32, 128)) == 0, tb[base + 966 : base + 967, :], 0.0)
    down = jnp.concatenate([tb[base + 486 : base + 966, :], bias], axis=0)
    return (0.5 * down).T.astype(bf16)


def point_rows(tb):
    parts_t = []
    for q in range(2):
        block = tb[pl.ds(CV + 2 + q, D, stride=2), :]
        parts_t.append(with_row(block, tb[CV + 242 + q : CV + 243 + q, :]).T[:D, :])
    return jnp.concatenate(parts_t, axis=0)


def fill_windows(tb, wt, wins):
    none = jnp.zeros((1, 128), f32)
    wins[...] = jnp.zeros_like(wins)
    for w, at, bias_at in ((0, AT + 2, AT + 122), (1, AT + 123, None), (2, AT + 243, AT + 363)):
        bias = none if bias_at is None else tb[bias_at : bias_at + 1, :]
        wt[...] = with_row(tb[at : at + D, :], bias).T
        for to, r, src, many in segments():
            start = WROWS * w + to - WIN[r]
            wins[r, start : start + many, :] = wt[src : src + many, :]


def fill_output(tb, wins):
    wins[:, 0:256, :] = jnp.zeros((GROUP, 256, 128), f32)
    for to, r, src, many in segments():
        start = to - WIN[r]
        wins[r, start : start + many, :] = tb[AT + 364 + src : AT + 364 + src + many, :]


def early_body(me_ref, g_ref, up_ref, dn_ref, wqkv_ref, wo_ref, pw_ref, cols_ref, base_ref, flat, tb, wt, wins, rows):
    unpack(me_ref, g_ref, flat, tb, ((0, ROWS_HEAD), (CV, F2 + 2 - CV), (FN, 2)))
    up_ref[...] = (0.5 * up_rows(tb, F1)).astype(bf16)
    dn_ref[...] = down_across(tb, F1)
    pw_ref[...] = (0.5 * point_rows(tb)).astype(bf16)
    fill_windows(tb, wt, wins)
    for r in range(GROUP):
        wqkv_ref[r] = wins[r, : 3 * WROWS].astype(bf16)
    fill_output(tb, wins)
    for r in range(GROUP):
        wins[r, MARKS[r] : MARKS[r] + 1, :] = tb[AT + 484 : AT + 485, :]
        wo_ref[r] = wins[r, 0:256, :].T[:, :WROWS].astype(bf16)

    rows[...] = jnp.zeros_like(rows)
    listed = []
    for base in (F1, AT, CV, CV + 260, F2, FN):
        listed += [base, base + 1]
    listed += [CV + 259] + [CV + 244 + k for k in range(KERNEL)]
    for to, src in enumerate(listed):
        rows[to : to + 1, :] = tb[src : src + 1, :]
    cols_ref[...] = rows[...].T

    rel_rows = []
    lanes = lane_iota((1, 128))
    for h in range(HEADS):
        at = REL_AT + (2 * REL + 1) * h
        first_row, col = at // 128, at % 128
        pieces = []
        for k in range(2):
            here = flat[first_row + k : first_row + k + 1, :]
            got = jnp.where(lanes >= col, here, flat[first_row + k + 1 : first_row + k + 2, :])
            pieces.append(pltpu.roll(got, (128 - col) % 128, 1) if col else got)
        rel_rows.append(jnp.concatenate(pieces, axis=1))
    rel = jnp.concatenate(rel_rows + [jnp.zeros((4, 256), f32)], axis=0)
    rel = jnp.where(lane_iota((8, 256)) < 2 * REL + 1, rel, 0.0)
    base_ref[...] = dot(rel.astype(bf16), distance_select()) * LOG2E


def late_body(
    me_ref, g_ref, upp1_ref, dnp1_ref, up2_ref, upp2_ref, dn2_ref, dnp2_ref, pwp_ref, pr_ref, prp_ref, wqkvt_ref, wob_ref,
    flat, tb, wt, wins,
):
    unpack(me_ref, g_ref, flat, tb, ((0, ROWS_HEAD), (TAIL, ROWS_TAIL)))
    upp1_ref[...] = up_across(up_rows(tb, F1))
    dnp1_ref[...] = (0.25 * tb[F1 + 486 : F1 + 966, :]).astype(bf16)
    up_t = up_rows(tb, F2)
    up2_ref[...] = (0.5 * up_t).astype(bf16)
    upp2_ref[...] = up_across(up_t)
    dn2_ref[...] = down_across(tb, F2)
    dnp2_ref[...] = (0.25 * tb[F2 + 486 : F2 + 966, :]).astype(bf16)
    pwp_ref[...] = jnp.concatenate([point_rows(tb), jnp.zeros((16, 128), f32)], axis=0).T[:, :240].astype(bf16)
    block = with_row(tb[CV + 262 : CV + 382, :], tb[CV + 382 : CV + 383, :])
    prp_ref[...] = (0.5 * block).astype(bf16)
    pr_ref[...] = block.T.astype(bf16)
    fill_windows(tb, wt, wins)
    for r in range(GROUP):
        wqkvt_ref[r] = wins[r].T[:, : 3 * WROWS].astype(bf16)
    fill_output(tb, wins)
    for r in range(GROUP):
        wob_ref[r] = wins[r, 0:WROWS, :].astype(bf16)


def distance_select():
    l = lane_iota((256, 2 * LG))
    gap = jnp.where(l < LG, -l, 2 * LG - l)
    index = jnp.clip(gap, -REL, REL) + REL
    return jnp.where(row_iota((256, 2 * LG)) == index, 1.0, 0.0).astype(bf16)


def spread_table(line, tab, h):
    blocks = {}
    for gap in (-1, 0, 1):
        tiles = [line[:, 128 * (k % 8) : 128 * (k % 8) + 128] for k in (gap - 1, gap)]
        both = jnp.broadcast_to(jnp.concatenate(tiles, axis=1), (128, 256))
        blocks[gap] = pltpu.roll(both, 0, 1, stride=1, stride_axis=0)[:, 128:]
    blocks[2] = jnp.broadcast_to(line[:, 256:257], (128, 128))
    blocks[-2] = jnp.broadcast_to(line[:, 768:769], (128, 128))
    for j in range(4):
        for i in range(4):
            tab[h, 128 * j : 128 * j + 128, 128 * i : 128 * i + 128] = blocks[max(-2, min(2, i - j))]


def block_of(values, j, i):
    return values[128 * j : 128 * j + 128, 128 * i : 128 * i + 128]


def add_distances(values, near, far, h):
    for gap in (-1, 0, 1):
        parts = [block_of(values, j, j + gap) for j in range(4) if 0 <= j + gap < 4]
        total = parts[0]
        for part in parts[1:]:
            total = total + part
        near[h, :, 128 * (gap + 1) : 128 * (gap + 2)] += total
    for k, blocks in enumerate((((0, 2), (0, 3), (1, 3)), ((2, 0), (3, 0), (3, 1)))):
        total = sum(block_of(values, j, i) for j, i in blocks)
        rows = total[0:8]
        for at in range(8, 128, 8):
            rows = rows + total[at : at + 8]
        far[h, k] += rows


def diagonal_sum(near, far):
    wide_rows = jnp.concatenate([near, jnp.zeros((128, 128), f32)], axis=1)
    half = 64
    while half:
        wide_rows = wide_rows[:half] + pltpu.roll(wide_rows[half : 2 * half], LG - half, 1)
        half //= 2
    tiles = [wide_rows[:, 128 * k : 128 * k + 128] for k in range(4)]
    none = jnp.zeros((1, 128), f32)
    plus = jnp.sum(far[0], axis=0, keepdims=True)
    minus = jnp.sum(far[1], axis=0, keepdims=True)
    return jnp.concatenate([tiles[1], tiles[2], plus, none, none, minus, tiles[3], tiles[0]], axis=1)


def prepare(me, gathered, rows):
    total = gathered.shape[0] * rows
    room = [
        pltpu.VMEM((total, 128), f32),
        pltpu.VMEM((TABLE, 128), f32),
        pltpu.VMEM((128, 128), f32),
        pltpu.VMEM((GROUP, 512, 128), f32),
    ]
    early = pl.pallas_call(
        early_body,
        in_specs=[SMEM, VMEM],
        out_shape=[o((FF, 128)), o((128, 512)), o((GROUP, 3 * WROWS, 128)), o((GROUP, 128, WROWS)), o((240, 128))]
        + [o((128, 128), f32), o((8, 2 * LG), f32)],
        scratch_shapes=room + [pltpu.VMEM((128, 128), f32)],
        name="prepare",
        **params(10**9, 2 * 10**6),
    )(me, gathered)
    late = pl.pallas_call(
        late_body,
        in_specs=[SMEM, VMEM],
        out_shape=[o((128, FF)), o((FF, 128)), o((FF, 128)), o((128, FF)), o((128, 512)), o((FF, 128))]
        + [o((128, 240)), o((128, 128)), o((128, 128)), o((GROUP, 128, 3 * WROWS)), o((GROUP, WROWS, 128))],
        scratch_shapes=room,
        name="late",
        **params(3 * 10**9, 10 * 10**6),
    )(me, gathered)
    return early, late


def column(cols, k):
    return cols[:D, k : k + 1]


def valid_keys(length):
    return row_iota((LG, 1)) * GROUP < length


def lane_sums(vec):
    lanes = lane_iota((D, 128))
    table = jnp.zeros((D, 128), f32)
    for k in range(vec.shape[0]):
        table = jnp.where(lanes == k, jnp.sum(vec[k], axis=1, keepdims=True), table)
    return pad8(table).T


def set_tail(hid):
    hid[FF:, :] = jnp.where(row_iota((512 - FF, hid.shape[1])) == 0, 1.0, 0.0).astype(bf16)


def conv_columns(cols, cb):
    for k in range(KERNEL + 1):
        cb[k] = jnp.broadcast_to(cols[:D, C_DWB + k : C_DWB + k + 1], (D, 128))


def wide(tile, copies=4):
    return jnp.concatenate([tile] * copies, axis=1)


def first_body(
    len_ref, xp_ref, xf_ref, cols_ref, up_ref, dn_ref, wqkv_ref, wo_ref, pw_ref, base_ref,
    lf_ref, xa_ref, nrm_ref, qkv_ref, prob_ref, att_ref, aa_ref, xc_ref, cn_ref, gat_ref, sig_ref, rgt_ref,
    ra_ref, rc_ref, dep_ref, st_ref,
    hid, one, cb, tab, run,
):
    u = pl.program_id(0)
    length = len_ref[u]

    @pl.when(u == 0)
    def _():
        set_tail(hid)
        run[...] = jnp.zeros_like(run)
        conv_columns(cols_ref, cb)
        for h in range(HEADS):
            spread_table(base_ref[h : h + 1, :], tab, h)

    cols = cols_ref

    def ffn_up(r, held):
        low = ext(xf_ref[0, :, span(r)] * column(cols, C_F1) + column(cols, C_F1 + 1))
        lf_ref[0, :, span(r)] = low
        return dot(up_ref[...], low)

    def ffn_down(r, half):
        hid[:FF, span(r)] = (half + half * jnp.tanh(half)).astype(bf16)
        return dot(dn_ref[...], hid[:, span(r)])[:D]

    def ffn_norm(r, branch):
        after = xp_ref[0, :, span(r)].astype(f32) + branch
        one[:, span(r)] = after
        xhat, rstd = norm(after)
        xa_ref[0, :, span(r)] = xhat
        ra_ref[0, 0:1, span(r)] = rstd
        low = ext(xhat * column(cols, C_AT) + column(cols, C_AT + 1))
        nrm_ref[0, 128 * r : 128 * r + 128, :] = low
        return dot(wqkv_ref[r], low)

    made = [None] * GROUP

    def ffn_keep(r, found):
        made[r] = found

    skewed(GROUP, (ffn_up, ffn_down, ffn_norm, ffn_keep))
    for w in range(3):
        joined = join_windows([made[r][WROWS * w : WROWS * w + WROWS] for r in range(GROUP)])
        if w == 0:
            joined = joined * (SCALE * LOG2E)
        qkv_ref[0, GP * w : GP * w + GP, :] = joined.astype(bf16)
    keys = valid_keys(length)

    def rows(w, h):
        return slice(GP * w + HP * h, GP * w + HP * h + HP)

    def score(h, held):
        return dot_tn(qkv_ref[0, rows(1, h), :], qkv_ref[0, rows(0, h), :])

    def soften(h, raw):
        scores = raw + tab[h]
        later = jnp.where(keys[SURE:], scores[SURE:], NEG_FILL * LOG2E)
        scores = jnp.concatenate([scores[:SURE], later], axis=0)
        peak = jnp.max(scores, axis=0, keepdims=True)
        power = jnp.exp2(scores - peak)
        total = jnp.sum(power, axis=0, keepdims=True)
        prob_ref[0, h] = (power * (1.0 / total)).astype(bf16)

    def mix(h, held):
        mixed = dot(qkv_ref[0, rows(2, h), :], prob_ref[0, h])
        if h < GROUP:
            mixed = jnp.where(row_iota((HP, LG)) == HEAD, 1.0, mixed)
        att_ref[0, rows(0, h), :] = mixed.astype(bf16)

    skewed(HEADS, (score, soften, mix))

    def project(r, held):
        return dot(wo_ref[r], window(att_ref.at[0], r))[:D]

    def gate_in(r, mixed):
        after = one[:, span(r)] + mixed
        aa_ref[0, :, span(r)] = after
        xhat, rstd = norm(after)
        xc_ref[0, :, span(r)] = xhat
        rc_ref[0, 0:1, span(r)] = rstd
        low = ext(xhat * column(cols, C_CV) + column(cols, C_CV + 1))
        cn_ref[0, :, span(r)] = low
        return dot(pw_ref[...], low)

    def gate_out(r, pre):
        mask = plane_mask(r, length)
        sig = (0.5 + 0.5 * jnp.tanh(pre[D:])) * mask
        gated = (pre[:D] + pre[:D]) * sig
        gat_ref[0, :, span(r)] = gated
        sig_ref[0, :, span(r)] = sig
        rgt_ref[0, :, span(r)] = gated * (1.0 - sig)

    skewed(GROUP, (project, gate_in, gate_out))

    def conv(f, carry):
        at = slice(8 * f, 8 * f + 8)
        tiles = [gat_ref[0, at, span(r)] for r in range(GROUP)]
        totals = [wide(cb[0, at, :])] * GROUP
        for m in range(-HALF, HALF + GROUP):
            here = shifted(tiles, m)
            for r in range(GROUP):
                k = m + HALF - r
                if 0 <= k < KERNEL:
                    totals[r] = totals[r] + wide(cb[1 + k, at, :]) * here
        for r in range(GROUP):
            dep_ref[0, at, span(r)] = totals[r]
        return carry

    for f in range(D // 8):
        conv(f, 0)

    count = length.astype(f32)
    mask = jnp.concatenate([plane_mask(r, length) for r in range(GROUP)], axis=1)
    dep = dep_ref[0]
    mean = jnp.sum(dep * mask, axis=1, keepdims=True) / count
    gap = (dep - mean) * mask
    spread = jnp.sum(gap * gap, axis=1, keepdims=True)
    old_mean, old_spread, old_count = run[0], run[1], run[2]
    new_count = old_count + count
    step = mean - old_mean
    new_mean = old_mean + step * (count / new_count)
    new_spread = old_spread + spread + step * step * (old_count * count / new_count)
    run[0] = new_mean
    run[1] = new_spread
    run[2] = new_count

    @pl.when(u == pl.num_programs(0) - 1)
    def _():
        lanes = lane_iota((D, 128))
        picked = jnp.where(lanes == 0, run[0], jnp.where(lanes == 1, run[1], jnp.where(lanes == 2, run[2], 0.0)))
        line = pad8(picked).T[0:8]
        for d in range(st_ref.shape[0]):
            st_ref[d] = line


def first(devices, lengths, xp, xf, weights):
    utts = xp.shape[0]
    per = [
        (LOW, bf16),
        (BIG, f32),
        ((GP, LG), bf16),
        ((3 * GP, LG), bf16),
        ((HEADS, LG, LG), bf16),
        ((GP, LG), bf16),
        (BIG, f32),
        (BIG, f32),
        (LOW, bf16),
        (BIG, f32),
        (BIG, f32),
        (BIG, f32),
        ((8, MAXLEN), f32),
        ((8, MAXLEN), f32),
        (BIG, f32),
    ]
    line = (devices, 8, 128)
    return pl.pallas_call(
        first_body,
        grid=(utts,),
        in_specs=[SMEM, per_utt(BIG), per_utt(BIG)] + [whole(w.shape) for w in weights],
        out_specs=[per_utt(s) for s, k in per] + [whole(line)],
        out_shape=[o((utts,) + s, k) for s, k in per] + [o(line, f32)],
        scratch_shapes=[
            pltpu.VMEM((512, MAXLEN), bf16),
            pltpu.VMEM(BIG, f32),
            pltpu.VMEM((KERNEL + 1, D, 128), f32),
            pltpu.VMEM((HEADS, LG, LG), f32),
            pltpu.VMEM((3, D, 128), f32),
        ],
        name="first",
        **params(10 * 10**9, 60 * 10**6),
    )(lengths, xp, xf, *weights)


def second_body(
    len_ref, stats_ref, cot_ref, aa_ref, dep_ref, cols_ref, up_ref, upp_ref, dn_ref, dnp_ref, pr_ref, prp_ref,
    out_ref, bgd_ref, gc_ref, sums_ref, stc_ref, gdn_ref, gup_ref, gpr_ref, vec_ref,
    hid, acc,
):
    u = pl.program_id(0)
    length = len_ref[u]
    cols = cols_ref

    @pl.when(u == 0)
    def _():
        set_tail(hid)
        parts = stats_ref.shape[0]
        count = jnp.zeros((1, 128), f32)
        total = jnp.zeros((1, 128), f32)
        for d in range(parts):
            many = stats_ref[d, 2:3, :]
            count = count + many
            total = total + many * stats_ref[d, 0:1, :]
        here = lane_iota((1, 128)) < D
        count = jnp.where(here, count, 1.0)
        mean = total / count
        spread = jnp.zeros((1, 128), f32)
        for d in range(parts):
            gap = stats_ref[d, 0:1, :] - mean
            spread = spread + stats_ref[d, 1:2, :] + stats_ref[d, 2:3, :] * gap * gap
        scale = lax.rsqrt(spread / count + EPS_NORM)
        at = row_iota((128, 128))
        table = jnp.where(at == 0, mean, jnp.where(at == 1, scale, jnp.where(at == 2, 1.0 / count, 0.0)))
        stc_ref[...] = table.T
        gdn_ref[...] = jnp.zeros_like(gdn_ref)
        gup_ref[...] = jnp.zeros_like(gup_ref)
        gpr_ref[...] = jnp.zeros_like(gpr_ref)
        vec_ref[...] = jnp.zeros_like(vec_ref)
        acc[...] = jnp.zeros_like(acc)

    half_gain = 0.5 * column(cols, C_BN)
    half_bias = 0.5 * column(cols, C_BN + 1)

    def enter(r, held):
        normal = (dep_ref[0, :, span(r)] - stc_ref[:D, 0:1]) * stc_ref[:D, 1:2]
        z = normal * half_gain + half_bias
        t = jnp.tanh(z)
        act = z + z * t
        act_low = ext(act)
        slope = (1.0 + t) * (1.0 + z * (1.0 - t))
        return act_low, normal, slope, dot(pr_ref[...], act_low)[:D]

    def ffn_up(r, held):
        act_low, normal, slope, moved = held
        after_conv = aa_ref[0, :, span(r)] + moved
        xhat, rstd = norm(after_conv)
        low = ext(xhat * column(cols, C_F2) + column(cols, C_F2 + 1))
        return act_low, normal, slope, after_conv, xhat, rstd, low, dot(up_ref[...], low)

    def ffn_down(r, held):
        act_low, normal, slope, after_conv, xhat, rstd, low, half = held
        t = jnp.tanh(half)
        hid[:FF, span(r)] = (half + half * t).astype(bf16)
        bend = (1.0 + t) * (1.0 + half * (1.0 - t))
        return act_low, normal, slope, after_conv, xhat, rstd, low, bend, dot(dn_ref[...], hid[:, span(r)])[:D]

    def finish(r, held):
        act_low, normal, slope, after_conv, xhat, rstd, low, bend, branch = held
        mask = plane_mask(r, length)
        xhat_f, rstd_f = norm(after_conv + branch)
        made = (xhat_f * column(cols, C_FN) + column(cols, C_FN + 1)) * mask
        out_ref[0, :, span(r)] = made.astype(bf16)
        up_grad = cot_ref[0, :, span(r)].astype(f32) * mask
        vec_ref[2] += fold(up_grad * xhat_f)
        vec_ref[3] += fold(up_grad)
        grad_two = norm_back(up_grad, xhat_f, rstd_f, column(cols, C_FN))
        branch = pad8(grad_two).astype(bf16)
        gdn_ref[...] += dot_nt(hid[:, span(r)], branch)
        return act_low, normal, slope, xhat, rstd, low, bend, grad_two, dot(dnp_ref[...], branch)

    def ffn_back(r, held):
        act_low, normal, slope, xhat, rstd, low, bend, grad_two, back = held
        pre_low = (bend * back).astype(bf16)
        gup_ref[...] += dot_nt(pre_low, low)
        return act_low, normal, slope, xhat, rstd, grad_two, dot(upp_ref[...], pre_low)[:D]

    def leave(r, held):
        act_low, normal, slope, xhat, rstd, grad_two, back = held
        vec_ref[0] += fold(back * xhat)
        vec_ref[1] += fold(back)
        grad_conv = grad_two + norm_back(back, xhat, rstd, column(cols, C_F2))
        gc_ref[0, :, span(r)] = grad_conv
        project = pad8(grad_conv).astype(bf16)
        gpr_ref[...] += dot_nt(act_low, project)
        return normal, slope, dot(prp_ref[...], project)[:D]

    def last(r, held):
        normal, slope, back = held
        batch = slope * back
        bgd_ref[0, :, span(r)] = batch
        acc[0] += fold(batch * normal)
        acc[1] += fold(batch)

    skewed(GROUP, (enter, ffn_up, ffn_down, finish, ffn_back, leave, last))

    @pl.when(u == pl.num_programs(0) - 1)
    def _():
        lanes = lane_iota((D, 128))
        gain = jnp.sum(acc[0], axis=1, keepdims=True)
        shift = jnp.sum(acc[1], axis=1, keepdims=True)
        line = pad8(jnp.where(lanes == 0, gain, jnp.where(lanes == 1, shift, 0.0))).T[0:8]
        for d in range(sums_ref.shape[0]):
            sums_ref[d] = line


def second(lengths, stats, cot, aa, dep, weights):
    utts = cot.shape[0]
    big = (D, MAXLEN)
    outs = [
        (per_utt(big), (utts,) + big, bf16),
        (per_utt(big), (utts,) + big, f32),
        (per_utt(big), (utts,) + big, f32),
    ]
    for s in (stats.shape, (128, 128), (512, 128), (FF, 128), (128, 128), (4, D, 128)):
        outs.append((whole(s), s, f32))
    return pl.pallas_call(
        second_body,
        grid=(utts,),
        in_specs=[SMEM, whole(stats.shape)] + [per_utt(big)] * 3 + [whole(w.shape) for w in weights],
        out_specs=[o[0] for o in outs],
        out_shape=[jax.ShapeDtypeStruct(o[1], o[2]) for o in outs],
        scratch_shapes=[
            pltpu.VMEM((512, MAXLEN), bf16),
            pltpu.VMEM((2, D, 128), f32),
        ],
        name="second",
        **params(15000000000, 30000000),
    )(lengths, stats, cot, aa, dep, *weights)


def third_body(
    len_ref, sums_ref, stc_ref, bgd_ref, dep_ref, gat_ref, ri_ref, ra_ref, rc_ref,
    gc_far, xc_far, cn_far, sig_far, rgt_far, att_far, qkv_far, prob_far, nrm_far, lf_far, xa_far, xf_far,
    cols_ref, up_ref, upp_ref, dnp_ref, wqkv_t_ref, wob_ref, pwp_ref,
    grad_ref, gdn_ref, gup_ref, gpw_ref, gqkv_ref, go_ref, rel_ref, rows_ref,
    gc_ref, xc_ref, cn_ref, sig_ref, rgt_ref, att_ref, qkv_ref, prob_ref, nrm_ref, lf_ref, xa_ref, xf_ref, sems,
    hid, dgx, dgs, olg, agr, back_s, gg, near_s, far_s, vec_ref, cb, tot,
):
    far = (gc_far, xc_far, cn_far, sig_far, rgt_far, att_far, qkv_far, prob_far, nrm_far, lf_far, xa_far, xf_far)
    near = (gc_ref, xc_ref, cn_ref, sig_ref, rgt_ref, att_ref, qkv_ref, prob_ref, nrm_ref, lf_ref, xa_ref, xf_ref)
    u = pl.program_id(0)
    utts = pl.num_programs(0) - 1
    slot = 1 - u % 2

    def copies(step):
        at = step % 2
        return [pltpu.make_async_copy(far[i].at[step], near[i].at[at], sems.at[i, at]) for i in range(len(far))]

    cols = cols_ref

    @pl.when(u == 0)
    def _():
        set_tail(hid)
        conv_columns(cols_ref, cb)
        parts = sums_ref.shape[0]
        total = sums_ref[0]
        for d in range(1, parts):
            total = total + sums_ref[d]
        tot[...] = jnp.concatenate([total, jnp.zeros((120, 128), f32)], axis=0).T
        for ref in (gdn_ref, gup_ref, gpw_ref, gqkv_ref, go_ref, vec_ref, near_s, far_s):
            ref[...] = jnp.zeros_like(ref)

    @pl.when(u < utts)
    def _():
        for copy in copies(u):
            copy.start()

    @pl.when(u > 0)
    def _():
        for copy in copies(u - 1):
            copy.wait()

    def front():
        scale = stc_ref[:D, 1:2]
        lead = column(cols, C_BN) * scale
        share = lead * stc_ref[:D, 2:3]
        shift_part = share * tot[:D, 1:2]
        gain_part = share * tot[:D, 0:1] * scale
        for r in range(GROUP):
            normal = dep_ref[0, :, span(r)] - stc_ref[:D, 0:1]
            mask = plane_mask(r, len_ref[u])
            dgx[:, span(r)] = bgd_ref[0, :, span(r)] * lead - mask * (shift_part + normal * gain_part)

        def conv(f, carry):
            at = slice(8 * f, 8 * f + 8)
            tiles = [dgx[at, span(r)] for r in range(GROUP)]
            gated = [gat_ref[0, at, span(r)] for r in range(GROUP)]
            totals = [None] * GROUP
            taps = [None] * KERNEL
            for m in range(-HALF, HALF + GROUP):
                here = shifted(tiles, m)
                for r in range(GROUP):
                    k = r + HALF - m
                    if 0 <= k < KERNEL:
                        term = wide(cb[1 + k, at, :]) * here
                        totals[r] = term if totals[r] is None else totals[r] + term
                        part = fold(gated[r] * here)
                        taps[k] = part if taps[k] is None else taps[k] + part
            vec_ref[6, at, :] += fold(tiles[0] + tiles[1] + tiles[2])
            for k in range(KERNEL):
                vec_ref[7 + k, at, :] += taps[k]
            for r in range(GROUP):
                gg[at, span(r)] = totals[r]
            return carry

        for f in range(D // 8):
            conv(f, 0)

    def back():
        def gate(r, held):
            grad = gg[:, span(r)]
            left = grad * sig_ref[slot, :, span(r)]
            right = grad * rgt_ref[slot, :, span(r)]
            pre_low = jnp.concatenate([left, right], axis=0).astype(bf16)
            gpw_ref[...] += dot_nt(pre_low, cn_ref[slot, :, span(r)])
            return dot(pwp_ref[...], pre_low)[:D]

        def residual(r, back):
            xhat = xc_ref[slot, :, span(r)]
            vec_ref[0] += fold(back * xhat)
            vec_ref[1] += fold(back)
            grad = gc_ref[slot, :, span(r)] + norm_back(back, xhat, rc_ref[0, 0:1, span(r)], column(cols, C_CV))
            dgs[:, span(r)] = grad
            low = pad8(grad).astype(bf16)
            olg[128 * r : 128 * r + 128, :] = low
            return dot(wob_ref[r], low)

        made = [None] * GROUP

        def keep(r, found):
            go_ref[r] += dot_nt(window(att_ref.at[slot], r), olg[128 * r : 128 * r + 128, :])
            made[r] = found

        skewed(GROUP, (gate, residual, keep))
        agr[...] = join_windows(made).astype(bf16)

        def rows(w, h):
            return slice(GP * w + HP * h, GP * w + HP * h + HP)

        def enter(h, held):
            grad = agr[rows(0, h), :]
            back_s[rows(2, h), :] = dot_nt(grad, prob_ref[slot, h]).astype(bf16)
            return dot_tn(qkv_ref[slot, rows(2, h), :], grad)

        def soften(h, prob_grad):
            probs = prob_ref[slot, h].astype(f32)
            inner = jnp.sum(probs * prob_grad, axis=0, keepdims=True)
            score = probs * (prob_grad - inner)
            add_distances(score, near_s, far_s, h)
            return score.astype(bf16)

        def turn(h, low):
            back_s[rows(0, h), :] = (dot(qkv_ref[slot, rows(1, h), :], low) * SCALE).astype(bf16)
            back_s[rows(1, h), :] = (dot_nt(qkv_ref[slot, rows(0, h), :], low) * (1.0 / LOG2E)).astype(bf16)

        skewed(HEADS, (enter, soften, turn))

        def project(r, held):
            stack = jnp.concatenate([window(back_s, r, GP * w) for w in range(3)], axis=0)
            gqkv_ref[r] += dot_nt(stack, nrm_ref[slot, 128 * r : 128 * r + 128, :])
            return dot(wqkv_t_ref[r], stack)[:D], dot(up_ref[...], lf_ref[slot, :, span(r)])

        def ffn_in(r, held):
            back, half = held
            xhat = xa_ref[slot, :, span(r)]
            vec_ref[2] += fold(back * xhat)
            vec_ref[3] += fold(back)
            grad = dgs[:, span(r)] + norm_back(back, xhat, ra_ref[0, 0:1, span(r)], column(cols, C_AT))
            low = pad8(grad).astype(bf16)
            return grad, low, half, dot(dnp_ref[...], low)

        def ffn_mid(r, held):
            grad, branch, half, back = held
            t = jnp.tanh(half)
            hid[:FF, span(r)] = (half + half * t).astype(bf16)
            pre_low = ((1.0 + t) * (1.0 + half * (1.0 - t)) * back).astype(bf16)
            gdn_ref[...] += dot_nt(hid[:, span(r)], branch)
            gup_ref[...] += dot_nt(pre_low, lf_ref[slot, :, span(r)])
            return grad, dot(upp_ref[...], pre_low)[:D]

        def ffn_out(r, held):
            grad, back = held
            xhat = xf_ref[slot, :, span(r)]
            vec_ref[4] += fold(back * xhat)
            vec_ref[5] += fold(back)
            grad_ref[0, :, span(r)] = grad + norm_back(back, xhat, ri_ref[0, 0:1, span(r)], column(cols, C_F1))

        skewed(GROUP, (project, ffn_in, ffn_mid, ffn_out))

    @pl.when(u == 0)
    def _():
        front()

    @pl.when((u > 0) & (u < utts))
    def _():
        back()
        front()

    @pl.when(u == utts)
    def _():
        back()
        rows_ref[...] = lane_sums(vec_ref)
        found = []
        for h in range(HEADS):
            found.append(diagonal_sum(near_s[h], far_s[h]))
        stacked = jnp.concatenate(found + [jnp.zeros((4, 2 * LG), f32)], axis=0)
        high = stacked.astype(bf16)
        rest = stacked - high.astype(f32)
        mid = rest.astype(bf16)
        rest = rest - mid.astype(f32)
        select = distance_select()
        rel_ref[...] = dot_nt(high, select) + dot_nt(mid, select) + dot_nt(rest.astype(bf16), select)


def third(lengths, sums, stc, soon, later, weights):
    utts = soon[0].shape[0]
    big = (D, MAXLEN)
    outs = [(one_late(big), (utts,) + big)]
    for s in ((512, 128), (FF, 128), (240, 128), (GROUP, 3 * WROWS, 128), (GROUP, WROWS, 128), (8, 256), (128, 128)):
        outs.append((whole(s), s))
    return pl.pallas_call(
        third_body,
        grid=(utts + 1,),
        in_specs=[SMEM, whole(sums.shape), whole(stc.shape)]
        + [at_most(s.shape[1:], utts) for s in soon[:3]]
        + [one_late(s.shape[1:]) for s in soon[3:]]
        + [pl.BlockSpec(memory_space=pl.ANY)] * len(later)
        + [whole(w.shape) for w in weights],
        out_specs=[o[0] for o in outs],
        out_shape=[jax.ShapeDtypeStruct(o[1], f32) for o in outs],
        scratch_shapes=[pltpu.VMEM((2,) + s.shape[1:], s.dtype) for s in later]
        + [
            pltpu.SemaphoreType.DMA((len(later), 2)),
            pltpu.VMEM((512, MAXLEN), bf16),
            pltpu.VMEM(big, f32),
            pltpu.VMEM(big, f32),
            pltpu.VMEM((GP, LG), bf16),
            pltpu.VMEM((GP, LG), bf16),
            pltpu.VMEM((3 * GP, LG), bf16),
            pltpu.VMEM(big, f32),
            pltpu.VMEM((HEADS, 128, 384), f32),
            pltpu.VMEM((HEADS, 2, 8, 128), f32),
            pltpu.VMEM((22, D, 128), f32),
            pltpu.VMEM((KERNEL + 1, D, 128), f32),
            pltpu.VMEM((128, 128), f32),
        ],
        name="third",
        **params(20000000000, 80000000),
    )(lengths, sums, stc, *soon, *later, *weights)


def clean(block):
    return jnp.where(lane_iota(block.shape) < D, block, 0.0)


def set_rows(tb, ref, at):
    for k, to in enumerate(at):
        tb[to : to + 1, :] = ref[k : k + 1, :]


def set_ffn(tb, base, dn_ref, up_ref):
    tb[base + 486 : base + 967, :] = 0.5 * clean(dn_ref[0 : FF + 1, :])
    for q in range(4):
        block = pad8(up_ref[D * q : D * q + D, :]).T
        tb[pl.ds(base + 2 + q, D, stride=4), :] = block[:D]
        tb[base + 482 + q : base + 483 + q, :] = block[D : D + 1]


def flatten(tb, base, flat, at_row, y_count, offset):
    for k in range(15):
        at = 128 * k + offset
        first_row, col = at // D, at % D
        many = (y_count - k + 14) // 15
        here = lane_iota((many, 128))
        got = tb[pl.ds(base + first_row, many, stride=16), :]
        if col:
            got = pltpu.roll(got, 128 - col, 1)
        then = pltpu.roll(tb[pl.ds(base + first_row + 1, many, stride=16), :], D - col, 1)
        got = jnp.where(here < D - col, got, then)
        if 2 * D - col < 128:
            then = pltpu.roll(tb[pl.ds(base + first_row + 2, many, stride=16), :], 2 * D - col, 1)
            got = jnp.where(here < 2 * D - col, got, then)
        flat[pl.ds(at_row + k, many, stride=15), :] = got


SPLIT = F2 - TAIL
ROWS_LAST = ROWS_TAIL - SPLIT
LAST_AT = TAIL_AT + D * SPLIT
LAST_Y = LAST_AT // 128
LAST_COUNT = (LIVE - 1) // 128 - LAST_Y + 1


def ahead_body(dn_ref, up_ref, vec_ref, out_ref, tb, wt):
    tb[0:8, :] = jnp.zeros((8, 128), f32)
    tb[8 + ROWS_LAST :, :] = jnp.zeros((tb.shape[0] - 8 - ROWS_LAST, 128), f32)
    wt[...] = lane_sums(vec_ref)
    set_rows(tb, wt, (8, 9, 8 + FN - F2, 9 + FN - F2))
    set_ffn(tb, 8, dn_ref, up_ref)
    flatten(tb, 7, out_ref, 0, LAST_COUNT, D + 128 * LAST_Y - LAST_AT)


def pack_ahead(dn, up, vec):
    return pl.pallas_call(
        ahead_body,
        out_shape=o((LAST_COUNT, 128), f32),
        scratch_shapes=[pltpu.VMEM((ROWS_LAST + 24, 128), f32), pltpu.VMEM((128, 128), f32)],
        name="ahead",
        **params(2 * 10**9, 8 * 10**6),
    )(dn, up, vec)


def pack_body(
    me_ref, last_ref, dn1_ref, up1_ref, pr_ref, pw_ref, qkv_ref, o_ref, rel_ref, vec_ref, sums_ref,
    keep_ref, send_ref, tb, flat, stage, wt,
):
    tb[ROWS_HEAD:TAIL, :] = jnp.zeros((TAIL - ROWS_HEAD, 128), f32)
    tb[F2:, :] = jnp.zeros((tb.shape[0] - F2, 128), f32)
    set_rows(tb, vec_ref, (CV, CV + 1, AT, AT + 1, F1, F1 + 1, CV + 259) + tuple(CV + 244 + k for k in range(KERNEL)))
    tb[CV + 260 : CV + 262, :] = sums_ref[0, 0:2, :]
    set_ffn(tb, F1, dn1_ref, up1_ref)
    for q in range(2):
        block = pad8(pw_ref[D * q : D * q + D, :]).T
        tb[pl.ds(CV + 2 + q, D, stride=2), :] = block[:D]
        tb[CV + 242 + q : CV + 243 + q, :] = block[D : D + 1]
    tb[CV + 262 : CV + 383, :] = clean(pr_ref[0 : D + 1, :])

    def gathered(ref, base):
        wt[...] = jnp.zeros_like(wt)
        for to, r, src, many in segments():
            start = base + to - WIN[r]
            wt[src : src + many, :] += ref[r, start : start + many, :]
        return wt[...]

    for w, at, bias_at in ((0, AT + 2, AT + 122), (1, AT + 123, None), (2, AT + 243, AT + 363)):
        block = gathered(qkv_ref, WROWS * w).T
        tb[at : at + D, :] = block[:D]
        if bias_at is not None:
            tb[bias_at : bias_at + 1, :] = block[D : D + 1]
    tb[AT + 364 : AT + 484, :] = clean(gathered(o_ref, 0)[:D])
    bias = sum(o_ref[r, MARKS[r] : MARKS[r] + 1, :] for r in range(GROUP))
    tb[AT + 484 : AT + 485, :] = clean(bias)

    tail_y = TAIL_AT // 128
    flat[LAST_Y + LAST_COUNT :, :] = jnp.zeros((flat.shape[0] - LAST_Y - LAST_COUNT, 128), f32)
    flat[REL_AT // 128 + 1 : tail_y, :] = jnp.zeros((tail_y - REL_AT // 128 - 1, 128), f32)
    flatten(tb, 0, flat, 0, REL_AT // 128 + 1, 0)
    flatten(tb, TAIL - 1, flat, tail_y, LAST_Y - tail_y + 1, 128 * tail_y - TAIL_AT + D)
    flat[LAST_Y : LAST_Y + 1, :] += last_ref[0:1, :]
    flat[LAST_Y + 1 : LAST_Y + LAST_COUNT, :] = last_ref[1:, :]
    here = lane_iota((1, 128))
    width = 2 * REL + 1
    for h in range(HEADS):
        at = REL_AT + width * h
        for y in range(at // 128, (at + width - 1) // 128 + 1):
            lo, hi = max(at - 128 * y, 0), min(at + width - 128 * y, 128)
            shift = (at - 128 * y) % 256
            turned = rel_ref[h : h + 1, :]
            if shift:
                turned = pltpu.roll(turned, shift, 1)
            flat[y : y + 1, :] += jnp.where((here >= lo) & (here < hi), turned[:, :128], 0.0)
    parts, padded = 2 * keep_ref.shape[0], keep_ref.shape[1]
    rows = flat.shape[0] // parts
    for d in range(parts):
        stage[d, 0:rows, :] = flat[rows * d : rows * (d + 1), :]
        if rows < padded:
            stage[d, rows:padded, :] = jnp.zeros((padded - rows, 128), f32)
    for offset in range(0, parts, 2):
        keep_ref[place(offset, parts)] = stage[me_ref[0] ^ offset]
        send_ref[place(offset, parts)] = stage[me_ref[0] ^ (offset + 1)]


def pack(parts, rows, me, grads):
    half = o((parts // 2, whole_tiles(rows), 128), f32)
    return pl.pallas_call(
        pack_body,
        in_specs=[SMEM] + [VMEM] * len(grads),
        out_shape=[half, half],
        scratch_shapes=[
            pltpu.VMEM((F2 + 24, 128), f32),
            pltpu.VMEM((parts * rows, 128), f32),
            pltpu.VMEM((parts, whole_tiles(rows), 128), f32),
            pltpu.VMEM((128, 128), f32),
        ],
        name="pack",
        **params(10**9, 5 * 10**6),
    )(me, *grads)


def update_tables(total_len):
    rates = np.zeros(total_len, np.float32)
    decays = np.zeros(total_len, np.float32)
    vector, gain, ffn = (D, 0.1, 0.0), (D, 0.3, 0.0), lambda n, fan: (n, fan**-0.5, 0.01)
    block = [gain, vector, ffn(D * FF, D), (FF, 0.1, 0.0), ffn(FF * D, FF), vector]
    square = ffn(D * D, D)
    pieces = block + [gain, vector, square, vector, square, square, vector, ffn(D * D, 6.0 * D / MAXLEN), vector]
    pieces += [(HEADS * (2 * REL + 1), 0.5, 0.0)]
    pieces += [gain, vector, ffn(2 * D * D, D), (2 * D, 0.1, 0.0), ffn(KERNEL * D, KERNEL), vector, gain, vector]
    pieces += [square, vector] + block + [gain, vector]
    offset = 0
    for entries, rate, decay in pieces:
        rates[offset : offset + entries] = rate
        decays[offset : offset + entries] = decay
        offset += entries
    return rates, decays


def whole_tiles(rows):
    return -(-rows // 8) * 8


def digits(devices):
    found, stride = [], 1
    while stride < devices:
        size = min(2 if stride == 1 else 4, devices // stride)
        found.append((stride, size))
        stride *= size
    return found


def place(offset, devices):
    at, weight = 0, devices
    for stride, size in digits(devices):
        weight //= size
        at = at + ((offset // stride) % size) * weight
    return at


def partner(values, offset, devices):
    return lax.ppermute(values, "dp", [(i, i ^ offset) for i in range(devices)])


def gather(values, devices, beside):
    held, made = values[None], []
    for k, (stride, size) in enumerate(reversed(digits(devices))):
        parts = [held] + [partner(held, stride * j, devices) for j in range(1, size)]
        if k < len(beside):
            parts, found = lax.optimization_barrier((parts, beside[k]))
            made.append(found)
        held = jnp.concatenate(parts, axis=0)
    return held, made + beside[len(made) :]


def scatter_sum(keep, send, devices, beside):
    total = keep + partner(send, 1, devices)
    made = None
    for k, (stride, size) in enumerate(digits(devices)[1:]):
        parts = total.reshape((size, total.shape[0] // size) + total.shape[1:])
        kind = bf16 if stride == 2 else f32
        found = [partner(parts[j].astype(kind), stride * j, devices) for j in range(1, size)]
        if k < len(beside):
            found, made = lax.optimization_barrier((found, beside[k](made)))
        total = parts[0]
        for part in found:
            total = total + part.astype(f32)
    for work in beside[max(0, len(digits(devices)) - 1) :]:
        made = work(made)
    return total, made


def local(frames, lengths, cotangent, master, moment_one, moment_two, average):
    shard_len = master.shape[0]
    devices = lax.axis_size("dp")
    rows = shard_len // 128
    me = lax.axis_index("dp").astype(jnp.int32).reshape(1)
    entered = enter(jnp.transpose(frames, (0, 2, 1)))
    mine = jnp.pad(master.astype(bf16).reshape(rows, 128), ((0, whole_tiles(rows) - rows), (0, 0)))
    cp = reorder(inward, jnp.transpose(cotangent, (0, 2, 1)), entered[3], "inward")
    gathered, (entered, cp) = gather(mine, devices, [entered, cp])
    xp, xf, rs_in, pm = entered
    early, late = prepare(me, gathered, rows)
    up1, dn1, wqkv, wo, pw, cols, base = early
    upp1, dnp1, up2, upp2, dn2, dnp2, pwp, pr, prp, wqkvt, wob = late
    lf, xa, nrm, qkv, prob, att, aa, xc, cn, gat, sig, rgt, ra, rc, dep, st = first(
        devices, lengths, xp, xf, (cols, up1, dn1, wqkv, wo, pw, base)
    )
    stats = lax.all_to_all(st, "dp", 0, 0)
    out, bgd, gc, sums, stc, gdn2, gup2, gpr, vec2 = second(
        lengths, stats, cp, aa, dep, (cols, up2, upp2, dn2, dnp2, pr, prp)
    )
    all_sums = lax.all_to_all(sums, "dp", 0, 0)
    last = pack_ahead(gdn2, gup2, vec2)
    out = reorder(outward, out, pm, "outward")
    (all_sums, last, out) = lax.optimization_barrier((all_sums, last, out))
    grad, gdn1, gup1, gpw, gqkv, go, rel, vec3 = third(
        lengths, all_sums, stc,
        (bgd, dep, gat, rs_in, ra, rc),
        (gc, xc, cn, sig, rgt, att, qkv, prob, nrm, lf, xa, xf),
        (cols, up1, upp1, dnp1, wqkvt, wob, pwp),
    )
    keep, send = pack(devices, rows, me, (last, gdn1, gup1, gpr, gpw, gqkv, go, rel, vec3, sums))
    utts = grad.shape[0]
    begin = (utts + 1) // 2
    reduced, gin = scatter_sum(
        keep,
        send,
        devices,
        [
            lambda made: reorder(permute_out_wide, grad, pm, "leave", 0, begin),
            lambda made: reorder(permute_out_wide, grad, pm, "leave", begin, utts - begin, made),
        ],
    )
    reduced = reduced.reshape(-1)[:shard_len]
    rates_np, decays_np = update_tables(shard_len * devices)
    start_at = lax.axis_index("dp") * shard_len
    rates = lax.dynamic_slice_in_dim(jnp.asarray(rates_np), start_at, shard_len)
    decays = lax.dynamic_slice_in_dim(jnp.asarray(decays_np), start_at, shard_len)
    correction = 1.0 - 0.5**STEP
    new_one = 0.5 * moment_one + 0.5 * reduced
    new_two = 0.5 * moment_two + 0.5 * reduced * reduced
    direction = new_one / correction / (jnp.sqrt(new_two / correction) + EPS_ADAM)
    new_master = master - rates * (direction + decays * master)
    new_average = 0.75 * average + 0.25 * new_master
    return (
        jnp.transpose(out, (0, 2, 1)),
        jnp.transpose(gin, (0, 2, 1)),
        reduced,
        new_master,
        new_one,
        new_two,
        new_average,
    )


def solution(mesh):
    three = P("dp", None, None)
    one = P("dp")
    in_specs = (three, one, three, one, one, one, one)
    out_specs = (three, three, one, one, one, one, one)
    return jax.shard_map(local, mesh=mesh, in_specs=in_specs, out_specs=out_specs, check_vma=False)
```

```python
import math

import jax
import jax.numpy as jnp
import numpy as np
from jax import lax
from jax.experimental import pallas as pl
from jax.experimental.pallas import tpu as pltpu
from jax.sharding import PartitionSpec as P

D = 120
HEADS = 4
FF = 480
KERNEL = 15
GROUP = 3
REL = 127
STEP = 5
MAXLEN = 1536
LG = 512
HEAD = 90
HP = 96
GP = HEADS * HP
HALF = KERNEL // 2
SURE = 128
WIN = (0, 112, 240)
WROWS = 144
MARKS = tuple(HP * r + HEAD - WIN[r] for r in range(GROUP))

EPS_NORM = 1e-05
EPS_ADAM = 1e-08
NEG_FILL = -1000000000.0
LOG2E = math.log2(math.e)
SCALE = HEAD ** (-0.5)

f32 = jnp.float32
bf16 = jnp.bfloat16
VMEM_BYTES = 58 * 2**20

REL_AT = 174240
TAIL_AT = 175260
TAIL = 1456
ROWS_HEAD = 1452
ROWS_TAIL = 1352
TABLE = 2824
F1 = 0
AT = 967
CV = TAIL
F2 = TAIL + 383
FN = TAIL + 1350
LIVE = 337500

C_F1, C_AT, C_CV, C_BN, C_F2, C_FN, C_DWB, C_DW = 0, 2, 4, 6, 8, 10, 12, 13


def dot(a, b):
    return lax.dot_general(a, b, (((1,), (0,)), ((), ())), preferred_element_type=f32)


def dot_nt(a, b):
    return lax.dot_general(a, b, (((1,), (1,)), ((), ())), preferred_element_type=f32)


def dot_tn(a, b):
    return lax.dot_general(a, b, (((0,), (0,)), ((), ())), preferred_element_type=f32)


def lane_iota(shape):
    return lax.broadcasted_iota(jnp.int32, shape, len(shape) - 1)


def row_iota(shape):
    return lax.broadcasted_iota(jnp.int32, shape, 0)


def segments():
    found = []
    for h in range(HEADS):
        for r in range(GROUP):
            lo, hi = max(HEAD * h, D * r), min(HEAD * h + HEAD, D * r + D)
            if lo < hi:
                found.append((HP * h + lo - HEAD * h, r, lo - D * r, hi - lo))
    return found


def pad8(values):
    return jnp.concatenate([values, jnp.zeros((8, values.shape[1]), f32)], axis=0)


def ext(values):
    width = values.shape[1]
    ones = jnp.where(row_iota((8, width)) == 0, 1.0, 0.0).astype(f32)
    return jnp.concatenate([values, ones], axis=0).astype(bf16)


def norm(values):
    mean = jnp.sum(values, axis=0, keepdims=True) * (1.0 / D)
    centre = values - mean
    var = jnp.sum(centre * centre, axis=0, keepdims=True) * (1.0 / D)
    rstd = lax.rsqrt(var + EPS_NORM)
    return centre * rstd, rstd


def norm_back(upstream, xhat, rstd, gain):
    scaled = upstream * gain
    mean_one = jnp.sum(scaled, axis=0, keepdims=True) * (1.0 / D)
    mean_two = jnp.sum(scaled * xhat, axis=0, keepdims=True) * (1.0 / D)
    return rstd * (scaled - mean_one - xhat * mean_two)


def fold(values):
    total = values[:, 0:128]
    for at in range(128, values.shape[1], 128):
        total = total + values[:, at : at + 128]
    return total


def permute_in(values, pm):
    low = pad8(values).astype(bf16)
    stack = jnp.concatenate([low[:, 384 * b : 384 * b + 384] for b in range(4)], axis=0)
    out = dot(stack, pm)
    tiles = [out[128 * b : 128 * b + D, 128 * r : 128 * r + 128] for r in range(3) for b in range(4)]
    return jnp.concatenate(tiles, axis=1)


def stack_out(values):
    low = pad8(values).astype(bf16)
    blocks = []
    for b in range(4):
        blocks.append(
            jnp.concatenate([low[:, 512 * r + 128 * b : 512 * r + 128 * b + 128] for r in range(3)], axis=1)
        )
    return jnp.concatenate(blocks, axis=0)


def unstack_out(out):
    return jnp.concatenate([out[128 * b : 128 * b + D, :] for b in range(4)], axis=1)


def permute_out(values, pm):
    return unstack_out(dot_nt(stack_out(values), pm))


def permute_out_wide(values, pm):
    high = values.astype(bf16).astype(f32)
    rest = values - high
    mid = rest.astype(bf16).astype(f32)
    return unstack_out(dot_nt(stack_out(high), pm) + dot_nt(stack_out(mid), pm))


def plane_mask(r, length):
    return jnp.where(lane_iota((1, LG)) * GROUP + r < length, 1.0, 0.0).astype(f32)


def span(r):
    return slice(LG * r, LG * r + LG)


def skewed(count, stages):
    held = [None] * count
    for step in range(count + len(stages) - 1):
        for k, stage in enumerate(stages):
            n = step - k
            if 0 <= n < count:
                held[n] = stage(n, held[n])


def window(ref, r, base=0):
    return ref[base + WIN[r] : base + WIN[r] + WROWS, :]


def join_windows(parts):
    a, b, c = parts
    return jnp.concatenate([a[:112], a[112:128] + b[:16], b[16:128], b[128:144] + c[:16], c[16:]], axis=0)


def shifted_planes(tiles):
    lanes = lane_iota((8, 128))
    zero = jnp.zeros((8, 128), f32)
    made = {}
    for m in range(-HALF, HALF + GROUP):
        r, s = m % GROUP, m // GROUP
        if s == 0:
            made[m] = tiles[r]
            continue
        turned = [pltpu.roll(tiles[r][:, 128 * k : 128 * k + 128], (-s) % 128, 1) for k in range(4)]
        if s > 0:
            pairs = zip(turned, turned[1:] + [zero])
            parts = [jnp.where(lanes < 128 - s, a, b) for a, b in pairs]
        else:
            pairs = zip([zero] + turned[:-1], turned)
            parts = [jnp.where(lanes < -s, a, b) for a, b in pairs]
        made[m] = jnp.concatenate(parts, axis=1)
    return made


def shifted(tiles, m):
    r, s = m % GROUP, m // GROUP
    if s == 0:
        return tiles[r]
    lanes = lane_iota((8, 128))
    zero = jnp.zeros((8, 128), f32)
    turned = [pltpu.roll(tiles[r][:, 128 * k : 128 * k + 128], (-s) % 128, 1) for k in range(4)]
    if s > 0:
        pairs = zip(turned, turned[1:] + [zero])
        parts = [jnp.where(lanes < 128 - s, a, b) for a, b in pairs]
    else:
        pairs = zip([zero] + turned[:-1], turned)
        parts = [jnp.where(lanes < -s, a, b) for a, b in pairs]
    return jnp.concatenate(parts, axis=1)


SMEM = pl.BlockSpec(memory_space=pltpu.SMEM)
VMEM = pl.BlockSpec(memory_space=pltpu.VMEM)
BIG = (D, MAXLEN)
LOW = (128, MAXLEN)


def whole(shape):
    zeros = (0,) * len(shape)
    return pl.BlockSpec(shape, lambda u: zeros)


def per_utt(shape):
    zeros = (0,) * len(shape)
    return pl.BlockSpec((1,) + shape, lambda u: (u,) + zeros)


def at_most(shape, utts):
    zeros = (0,) * len(shape)
    return pl.BlockSpec((1,) + shape, lambda u: (jnp.minimum(u, utts - 1),) + zeros)


def one_late(shape):
    zeros = (0,) * len(shape)
    return pl.BlockSpec((1,) + shape, lambda u: (jnp.maximum(u - 1, 0),) + zeros)


def o(shape, kind=bf16):
    return jax.ShapeDtypeStruct(shape, kind)


def params(flops=0, moved=0):
    cost = pl.CostEstimate(flops=flops, bytes_accessed=moved, transcendentals=0)
    return dict(compiler_params=pltpu.CompilerParams(vmem_limit_bytes=VMEM_BYTES), cost_estimate=cost)


def permutation():
    t = row_iota((384, 384))
    c = lane_iota((384, 384))
    return jnp.where(t == GROUP * (c % 128) + c // 128, 1.0, 0.0).astype(bf16)


ANY = pl.BlockSpec(memory_space=pl.ANY)


def streamed(work, far_in, near_in, far_out, near_out, sems, first_utt):
    count = near_in.shape[0]

    def coming(u):
        return pltpu.make_async_copy(far_in.at[u + first_utt], near_in.at[u], sems.at[0, u])

    def going(u):
        pairs = enumerate(zip(near_out, far_out))
        return [pltpu.make_async_copy(near.at[u], far.at[u + first_utt], sems.at[k + 1, u]) for k, (near, far) in pairs]

    for u in range(count):
        coming(u).start()

    def step(u, carry):
        coming(u).wait()
        work(u)
        for copy in going(u):
            copy.start()
        return carry

    lax.fori_loop(0, count, step, 0)
    for u in range(count):
        for copy in going(u):
            copy.wait()


def enter_body(x_far, xp_far, xf_far, rs_far, pm_ref, x_near, xp_near, xf_near, rs_near, sems):
    pm_ref[...] = permutation()

    def work(u):
        x = permute_in(x_near[u].astype(f32), pm_ref[...])
        xp_near[u] = x.astype(bf16)
        xhat, rstd = norm(x)
        xf_near[u] = xhat
        rs_near[u] = jnp.broadcast_to(rstd, (8, MAXLEN))

    streamed(work, x_far, x_near, (xp_far, xf_far, rs_far), (xp_near, xf_near, rs_near), sems, 0)


def enter(x):
    utts = x.shape[0]
    made = [o((utts,) + BIG), o((utts,) + BIG, f32), o((utts, 8, MAXLEN), f32)]
    return pl.pallas_call(
        enter_body,
        in_specs=[ANY],
        out_specs=[ANY] * 3 + [VMEM],
        out_shape=made + [o((384, 384))],
        scratch_shapes=[pltpu.VMEM(m.shape, m.dtype) for m in [x] + made] + [pltpu.SemaphoreType.DMA((4, utts))],
        name="enter",
        **params(2 * 10**9, 8 * 10**6),
    )(x)


def inward(values, pm):
    return permute_in(values.astype(f32), pm).astype(bf16)


def outward(values, pm):
    return permute_out(values.astype(f32), pm).astype(bf16)


def reorder(turn, values, pm, name, first_utt=0, count=None, begun=None):
    count = values.shape[0] if count is None else count
    more = [] if begun is None else [begun]

    def body(far_in, pm_ref, *refs):
        far_out, near_in, near_out, sems = refs[len(more) :]

        def work(u):
            near_out[u] = turn(near_in[u], pm_ref[...])

        streamed(work, far_in, near_in, (far_out,), (near_out,), sems, first_utt)

    room = pltpu.VMEM((count,) + BIG, values.dtype)
    return pl.pallas_call(
        body,
        in_specs=[ANY, VMEM] + [ANY] * len(more),
        out_specs=ANY,
        out_shape=o(values.shape, values.dtype),
        scratch_shapes=[room, room, pltpu.SemaphoreType.DMA((2, count))],
        input_output_aliases={2: 0} if more else {},
        name=name,
        **params(2 * 10**9, 8 * 10**6),
    )(values, pm, *more)


def unpack(me_ref, g_ref, flat, tb, regions):
    parts = g_ref.shape[0]
    part_rows = flat.shape[0] // parts
    for d in range(parts):
        flat[part_rows * d : part_rows * (d + 1), :] = g_ref[place(me_ref[0] ^ d, parts)].astype(f32)[:part_rows]
    for base, count in regions:
        start = D * base if base < TAIL else TAIL_AT + D * (base - TAIL)
        for r in range(min(16, count)):
            at = start + D * r
            first_row, col = at // 128, at % 128
            many = (count - r + 15) // 16
            here = flat[pl.ds(first_row, many, stride=15), :]
            then = flat[pl.ds(first_row + 1, many, stride=15), :]
            lanes = lane_iota((many, 128))
            got = jnp.where(lanes >= col, here, then)
            if col:
                got = pltpu.roll(got, 128 - col, 1)
            tb[pl.ds(base + r, many, stride=16), :] = jnp.where(lanes < D, got, 0.0)


def with_row(block, row):
    tail = jnp.where(row_iota((8, 128)) == 0, row, 0.0)
    return jnp.concatenate([block, tail], axis=0)


def up_rows(tb, base):
    parts_t = []
    for q in range(4):
        block = tb[pl.ds(base + 2 + q, D, stride=4), :]
        parts_t.append(with_row(block, tb[base + 482 + q : base + 483 + q, :]).T[:D, :])
    return jnp.concatenate(parts_t, axis=0)


def up_across(up_t):
    return jnp.concatenate([up_t, jnp.zeros((32, 128), f32)], axis=0).T[:, :FF].astype(bf16)


def down_across(tb, base):
    bias = jnp.where(row_iota((32, 128)) == 0, tb[base + 966 : base + 967, :], 0.0)
    down = jnp.concatenate([tb[base + 486 : base + 966, :], bias], axis=0)
    return (0.5 * down).T.astype(bf16)


def point_rows(tb):
    parts_t = []
    for q in range(2):
        block = tb[pl.ds(CV + 2 + q, D, stride=2), :]
        parts_t.append(with_row(block, tb[CV + 242 + q : CV + 243 + q, :]).T[:D, :])
    return jnp.concatenate(parts_t, axis=0)


def fill_windows(tb, wt, wins):
    none = jnp.zeros((1, 128), f32)
    wins[...] = jnp.zeros_like(wins)
    for w, at, bias_at in ((0, AT + 2, AT + 122), (1, AT + 123, None), (2, AT + 243, AT + 363)):
        bias = none if bias_at is None else tb[bias_at : bias_at + 1, :]
        wt[...] = with_row(tb[at : at + D, :], bias).T
        for to, r, src, many in segments():
            start = WROWS * w + to - WIN[r]
            wins[r, start : start + many, :] = wt[src : src + many, :]


def fill_output(tb, wins):
    wins[:, 0:256, :] = jnp.zeros((GROUP, 256, 128), f32)
    for to, r, src, many in segments():
        start = to - WIN[r]
        wins[r, start : start + many, :] = tb[AT + 364 + src : AT + 364 + src + many, :]


def early_body(me_ref, g_ref, up_ref, dn_ref, wqkv_ref, wo_ref, pw_ref, cols_ref, base_ref, flat, tb, wt, wins, rows):
    unpack(me_ref, g_ref, flat, tb, ((0, ROWS_HEAD), (CV, F2 + 2 - CV), (FN, 2)))
    up_ref[...] = (0.5 * up_rows(tb, F1)).astype(bf16)
    dn_ref[...] = down_across(tb, F1)
    pw_ref[...] = (0.5 * point_rows(tb)).astype(bf16)
    fill_windows(tb, wt, wins)
    for r in range(GROUP):
        wqkv_ref[r] = wins[r, : 3 * WROWS].astype(bf16)
    fill_output(tb, wins)
    for r in range(GROUP):
        wins[r, MARKS[r] : MARKS[r] + 1, :] = tb[AT + 484 : AT + 485, :]
        wo_ref[r] = wins[r, 0:256, :].T[:, :WROWS].astype(bf16)

    rows[...] = jnp.zeros_like(rows)
    listed = []
    for base in (F1, AT, CV, CV + 260, F2, FN):
        listed += [base, base + 1]
    listed += [CV + 259] + [CV + 244 + k for k in range(KERNEL)]
    for to, src in enumerate(listed):
        rows[to : to + 1, :] = tb[src : src + 1, :]
    cols_ref[...] = rows[...].T

    rel_rows = []
    lanes = lane_iota((1, 128))
    for h in range(HEADS):
        at = REL_AT + (2 * REL + 1) * h
        first_row, col = at // 128, at % 128
        pieces = []
        for k in range(2):
            here = flat[first_row + k : first_row + k + 1, :]
            got = jnp.where(lanes >= col, here, flat[first_row + k + 1 : first_row + k + 2, :])
            pieces.append(pltpu.roll(got, (128 - col) % 128, 1) if col else got)
        rel_rows.append(jnp.concatenate(pieces, axis=1))
    rel = jnp.concatenate(rel_rows + [jnp.zeros((4, 256), f32)], axis=0)
    rel = jnp.where(lane_iota((8, 256)) < 2 * REL + 1, rel, 0.0)
    base_ref[...] = dot(rel.astype(bf16), distance_select()) * LOG2E


def late_body(
    me_ref, g_ref, upp1_ref, dnp1_ref, up2_ref, upp2_ref, dn2_ref, dnp2_ref, pwp_ref, pr_ref, prp_ref, wqkvt_ref, wob_ref,
    flat, tb, wt, wins,
):
    unpack(me_ref, g_ref, flat, tb, ((0, ROWS_HEAD), (TAIL, ROWS_TAIL)))
    upp1_ref[...] = up_across(up_rows(tb, F1))
    dnp1_ref[...] = (0.25 * tb[F1 + 486 : F1 + 966, :]).astype(bf16)
    up_t = up_rows(tb, F2)
    up2_ref[...] = (0.5 * up_t).astype(bf16)
    upp2_ref[...] = up_across(up_t)
    dn2_ref[...] = down_across(tb, F2)
    dnp2_ref[...] = (0.25 * tb[F2 + 486 : F2 + 966, :]).astype(bf16)
    pwp_ref[...] = jnp.concatenate([point_rows(tb), jnp.zeros((16, 128), f32)], axis=0).T[:, :240].astype(bf16)
    block = with_row(tb[CV + 262 : CV + 382, :], tb[CV + 382 : CV + 383, :])
    prp_ref[...] = (0.5 * block).astype(bf16)
    pr_ref[...] = block.T.astype(bf16)
    fill_windows(tb, wt, wins)
    for r in range(GROUP):
        wqkvt_ref[r] = wins[r].T[:, : 3 * WROWS].astype(bf16)
    fill_output(tb, wins)
    for r in range(GROUP):
        wob_ref[r] = wins[r, 0:WROWS, :].astype(bf16)


def distance_select():
    l = lane_iota((256, 2 * LG))
    gap = jnp.where(l < LG, -l, 2 * LG - l)
    index = jnp.clip(gap, -REL, REL) + REL
    return jnp.where(row_iota((256, 2 * LG)) == index, 1.0, 0.0).astype(bf16)


def spread_table(line, tab, h):
    blocks = {}
    for gap in (-1, 0, 1):
        tiles = [line[:, 128 * (k % 8) : 128 * (k % 8) + 128] for k in (gap - 1, gap)]
        both = jnp.broadcast_to(jnp.concatenate(tiles, axis=1), (128, 256))
        blocks[gap] = pltpu.roll(both, 0, 1, stride=1, stride_axis=0)[:, 128:]
    blocks[2] = jnp.broadcast_to(line[:, 256:257], (128, 128))
    blocks[-2] = jnp.broadcast_to(line[:, 768:769], (128, 128))
    for j in range(4):
        for i in range(4):
            tab[h, 128 * j : 128 * j + 128, 128 * i : 128 * i + 128] = blocks[max(-2, min(2, i - j))]


def block_of(values, j, i):
    return values[128 * j : 128 * j + 128, 128 * i : 128 * i + 128]


def add_distances(values, near, far, h):
    for gap in (-1, 0, 1):
        parts = [block_of(values, j, j + gap) for j in range(4) if 0 <= j + gap < 4]
        total = parts[0]
        for part in parts[1:]:
            total = total + part
        near[h, :, 128 * (gap + 1) : 128 * (gap + 2)] += total
    for k, blocks in enumerate((((0, 2), (0, 3), (1, 3)), ((2, 0), (3, 0), (3, 1)))):
        total = sum(block_of(values, j, i) for j, i in blocks)
        rows = total[0:8]
        for at in range(8, 128, 8):
            rows = rows + total[at : at + 8]
        far[h, k] += rows


def diagonal_sum(near, far):
    wide_rows = jnp.concatenate([near, jnp.zeros((128, 128), f32)], axis=1)
    half = 64
    while half:
        wide_rows = wide_rows[:half] + pltpu.roll(wide_rows[half : 2 * half], LG - half, 1)
        half //= 2
    tiles = [wide_rows[:, 128 * k : 128 * k + 128] for k in range(4)]
    none = jnp.zeros((1, 128), f32)
    plus = jnp.sum(far[0], axis=0, keepdims=True)
    minus = jnp.sum(far[1], axis=0, keepdims=True)
    return jnp.concatenate([tiles[1], tiles[2], plus, none, none, minus, tiles[3], tiles[0]], axis=1)


def prepare(me, gathered, rows):
    total = gathered.shape[0] * rows
    room = [
        pltpu.VMEM((total, 128), f32),
        pltpu.VMEM((TABLE, 128), f32),
        pltpu.VMEM((128, 128), f32),
        pltpu.VMEM((GROUP, 512, 128), f32),
    ]
    early = pl.pallas_call(
        early_body,
        in_specs=[SMEM, VMEM],
        out_shape=[o((FF, 128)), o((128, 512)), o((GROUP, 3 * WROWS, 128)), o((GROUP, 128, WROWS)), o((240, 128))]
        + [o((128, 128), f32), o((8, 2 * LG), f32)],
        scratch_shapes=room + [pltpu.VMEM((128, 128), f32)],
        name="prepare",
        **params(10**9, 2 * 10**6),
    )(me, gathered)
    late = pl.pallas_call(
        late_body,
        in_specs=[SMEM, VMEM],
        out_shape=[o((128, FF)), o((FF, 128)), o((FF, 128)), o((128, FF)), o((128, 512)), o((FF, 128))]
        + [o((128, 240)), o((128, 128)), o((128, 128)), o((GROUP, 128, 3 * WROWS)), o((GROUP, WROWS, 128))],
        scratch_shapes=room,
        name="late",
        **params(3 * 10**9, 10 * 10**6),
    )(me, gathered)
    return early, late


def column(cols, k):
    return cols[:D, k : k + 1]


def valid_keys(length):
    return row_iota((LG, 1)) * GROUP < length


def lane_sums(vec):
    lanes = lane_iota((D, 128))
    table = jnp.zeros((D, 128), f32)
    for k in range(vec.shape[0]):
        table = jnp.where(lanes == k, jnp.sum(vec[k], axis=1, keepdims=True), table)
    return pad8(table).T


def set_tail(hid):
    hid[FF:, :] = jnp.where(row_iota((512 - FF, hid.shape[1])) == 0, 1.0, 0.0).astype(bf16)


def conv_columns(cols, cb):
    for k in range(KERNEL + 1):
        cb[k] = jnp.broadcast_to(cols[:D, C_DWB + k : C_DWB + k + 1], (D, 128))


def wide(tile, copies=4):
    return jnp.concatenate([tile] * copies, axis=1)


def first_body(
    len_ref, xp_ref, xf_ref, cols_ref, up_ref, dn_ref, wqkv_ref, wo_ref, pw_ref, base_ref,
    lf_ref, xa_ref, nrm_ref, qkv_ref, prob_ref, att_ref, aa_ref, xc_ref, cn_ref, gat_ref, sig_ref,
    ra_ref, rc_ref, dep_ref, st_ref,
    hid, one, cb, tab, run,
):
    u = pl.program_id(0)
    length = len_ref[u]

    @pl.when(u == 0)
    def _():
        set_tail(hid)
        run[...] = jnp.zeros_like(run)
        conv_columns(cols_ref, cb)
        for h in range(HEADS):
            spread_table(base_ref[h : h + 1, :], tab, h)

    cols = cols_ref

    def ffn_up(r, held):
        low = ext(xf_ref[0, :, span(r)] * column(cols, C_F1) + column(cols, C_F1 + 1))
        lf_ref[0, :, span(r)] = low
        return dot(up_ref[...], low)

    def ffn_down(r, half):
        hid[:FF, span(r)] = (half + half * jnp.tanh(half)).astype(bf16)
        return dot(dn_ref[...], hid[:, span(r)])[:D]

    def ffn_norm(r, branch):
        after = xp_ref[0, :, span(r)].astype(f32) + branch
        one[:, span(r)] = after
        xhat, rstd = norm(after)
        xa_ref[0, :, span(r)] = xhat
        ra_ref[0, 0:1, span(r)] = rstd
        low = ext(xhat * column(cols, C_AT) + column(cols, C_AT + 1))
        nrm_ref[0, 128 * r : 128 * r + 128, :] = low
        return dot(wqkv_ref[r], low)

    made = [None] * GROUP

    def ffn_keep(r, found):
        made[r] = found

    skewed(GROUP, (ffn_up, ffn_down, ffn_norm, ffn_keep))
    for w in range(3):
        joined = join_windows([made[r][WROWS * w : WROWS * w + WROWS] for r in range(GROUP)])
        if w == 0:
            joined = joined * (SCALE * LOG2E)
        qkv_ref[0, GP * w : GP * w + GP, :] = joined.astype(bf16)
    keys = valid_keys(length)

    def rows(w, h):
        return slice(GP * w + HP * h, GP * w + HP * h + HP)

    def score(h, held):
        return dot_tn(qkv_ref[0, rows(1, h), :], qkv_ref[0, rows(0, h), :])

    def soften(h, raw):
        scores = raw + tab[h]
        later = jnp.where(keys[SURE:], scores[SURE:], NEG_FILL * LOG2E)
        scores = jnp.concatenate([scores[:SURE], later], axis=0)
        peak = jnp.max(scores, axis=0, keepdims=True)
        power = jnp.exp2(scores - peak)
        total = jnp.sum(power, axis=0, keepdims=True)
        prob_ref[0, h] = (power * (1.0 / total)).astype(bf16)

    def mix(h, held):
        mixed = dot(qkv_ref[0, rows(2, h), :], prob_ref[0, h])
        if h < GROUP:
            mixed = jnp.where(row_iota((HP, LG)) == HEAD, 1.0, mixed)
        att_ref[0, rows(0, h), :] = mixed.astype(bf16)

    skewed(HEADS, (score, soften, mix))

    def project(r, held):
        return dot(wo_ref[r], window(att_ref.at[0], r))[:D]

    def gate_in(r, mixed):
        after = one[:, span(r)] + mixed
        aa_ref[0, :, span(r)] = after
        xhat, rstd = norm(after)
        xc_ref[0, :, span(r)] = xhat
        rc_ref[0, 0:1, span(r)] = rstd
        low = ext(xhat * column(cols, C_CV) + column(cols, C_CV + 1))
        cn_ref[0, :, span(r)] = low
        return dot(pw_ref[...], low)

    def gate_out(r, pre):
        mask = plane_mask(r, length)
        sig = (0.5 + 0.5 * jnp.tanh(pre[D:])) * mask
        gated = (pre[:D] + pre[:D]) * sig
        gat_ref[0, :, span(r)] = gated
        sig_ref[0, :, span(r)] = sig

    skewed(GROUP, (project, gate_in, gate_out))

    def conv(f, carry):
        at = slice(8 * f, 8 * f + 8)
        tiles = [gat_ref[0, at, span(r)] for r in range(GROUP)]
        totals = [wide(cb[0, at, :])] * GROUP
        for m in range(-HALF, HALF + GROUP):
            here = shifted(tiles, m)
            for r in range(GROUP):
                k = m + HALF - r
                if 0 <= k < KERNEL:
                    totals[r] = totals[r] + wide(cb[1 + k, at, :]) * here
        for r in range(GROUP):
            dep_ref[0, at, span(r)] = totals[r]
        return carry

    for f in range(D // 8):
        conv(f, 0)

    count = length.astype(f32)
    mask = jnp.concatenate([plane_mask(r, length) for r in range(GROUP)], axis=1)
    dep = dep_ref[0]
    mean = jnp.sum(dep * mask, axis=1, keepdims=True) / count
    gap = (dep - mean) * mask
    spread = jnp.sum(gap * gap, axis=1, keepdims=True)
    old_mean, old_spread, old_count = run[0], run[1], run[2]
    new_count = old_count + count
    step = mean - old_mean
    new_mean = old_mean + step * (count / new_count)
    new_spread = old_spread + spread + step * step * (old_count * count / new_count)
    run[0] = new_mean
    run[1] = new_spread
    run[2] = new_count

    @pl.when(u == pl.num_programs(0) - 1)
    def _():
        lanes = lane_iota((D, 128))
        picked = jnp.where(lanes == 0, run[0], jnp.where(lanes == 1, run[1], jnp.where(lanes == 2, run[2], 0.0)))
        line = pad8(picked).T[0:8]
        for d in range(st_ref.shape[0]):
            st_ref[d] = line


def first(devices, lengths, xp, xf, weights):
    utts = xp.shape[0]
    per = [
        (LOW, bf16),
        (BIG, f32),
        ((GP, LG), bf16),
        ((3 * GP, LG), bf16),
        ((HEADS, LG, LG), bf16),
        ((GP, LG), bf16),
        (BIG, f32),
        (BIG, f32),
        (LOW, bf16),
        (BIG, f32),
        (BIG, f32),
        ((8, MAXLEN), f32),
        ((8, MAXLEN), f32),
        (BIG, f32),
    ]
    line = (devices, 8, 128)
    return pl.pallas_call(
        first_body,
        grid=(utts,),
        in_specs=[SMEM, per_utt(BIG), per_utt(BIG)] + [whole(w.shape) for w in weights],
        out_specs=[per_utt(s) for s, k in per] + [whole(line)],
        out_shape=[o((utts,) + s, k) for s, k in per] + [o(line, f32)],
        scratch_shapes=[
            pltpu.VMEM((512, MAXLEN), bf16),
            pltpu.VMEM(BIG, f32),
            pltpu.VMEM((KERNEL + 1, D, 128), f32),
            pltpu.VMEM((HEADS, LG, LG), f32),
            pltpu.VMEM((3, D, 128), f32),
        ],
        name="first",
        **params(10 * 10**9, 60 * 10**6),
    )(lengths, xp, xf, *weights)


def second_body(
    len_ref, stats_ref, cot_ref, aa_ref, dep_ref, cols_ref, up_ref, upp_ref, dn_ref, dnp_ref, pr_ref, prp_ref,
    out_ref, bgd_ref, gc_ref, sums_ref, stc_ref, gdn_ref, gup_ref, gpr_ref, vec_ref,
    hid, acc,
):
    u = pl.program_id(0)
    length = len_ref[u]
    cols = cols_ref

    @pl.when(u == 0)
    def _():
        set_tail(hid)
        parts = stats_ref.shape[0]
        count = jnp.zeros((1, 128), f32)
        total = jnp.zeros((1, 128), f32)
        for d in range(parts):
            many = stats_ref[d, 2:3, :]
            count = count + many
            total = total + many * stats_ref[d, 0:1, :]
        here = lane_iota((1, 128)) < D
        count = jnp.where(here, count, 1.0)
        mean = total / count
        spread = jnp.zeros((1, 128), f32)
        for d in range(parts):
            gap = stats_ref[d, 0:1, :] - mean
            spread = spread + stats_ref[d, 1:2, :] + stats_ref[d, 2:3, :] * gap * gap
        scale = lax.rsqrt(spread / count + EPS_NORM)
        at = row_iota((128, 128))
        table = jnp.where(at == 0, mean, jnp.where(at == 1, scale, jnp.where(at == 2, 1.0 / count, 0.0)))
        stc_ref[...] = table.T
        gdn_ref[...] = jnp.zeros_like(gdn_ref)
        gup_ref[...] = jnp.zeros_like(gup_ref)
        gpr_ref[...] = jnp.zeros_like(gpr_ref)
        vec_ref[...] = jnp.zeros_like(vec_ref)
        acc[...] = jnp.zeros_like(acc)

    half_gain = 0.5 * column(cols, C_BN)
    half_bias = 0.5 * column(cols, C_BN + 1)

    def enter(r, held):
        normal = (dep_ref[0, :, span(r)] - stc_ref[:D, 0:1]) * stc_ref[:D, 1:2]
        z = normal * half_gain + half_bias
        t = jnp.tanh(z)
        act = z + z * t
        act_low = ext(act)
        slope = (1.0 + t) * (1.0 + z * (1.0 - t))
        return act_low, normal, slope, dot(pr_ref[...], act_low)[:D]

    def ffn_up(r, held):
        act_low, normal, slope, moved = held
        after_conv = aa_ref[0, :, span(r)] + moved
        xhat, rstd = norm(after_conv)
        low = ext(xhat * column(cols, C_F2) + column(cols, C_F2 + 1))
        return act_low, normal, slope, after_conv, xhat, rstd, low, dot(up_ref[...], low)

    def ffn_down(r, held):
        act_low, normal, slope, after_conv, xhat, rstd, low, half = held
        t = jnp.tanh(half)
        hid[:FF, span(r)] = (half + half * t).astype(bf16)
        bend = (1.0 + t) * (1.0 + half * (1.0 - t))
        return act_low, normal, slope, after_conv, xhat, rstd, low, bend, dot(dn_ref[...], hid[:, span(r)])[:D]

    def finish(r, held):
        act_low, normal, slope, after_conv, xhat, rstd, low, bend, branch = held
        mask = plane_mask(r, length)
        xhat_f, rstd_f = norm(after_conv + branch)
        made = (xhat_f * column(cols, C_FN) + column(cols, C_FN + 1)) * mask
        out_ref[0, :, span(r)] = made.astype(bf16)
        up_grad = cot_ref[0, :, span(r)].astype(f32) * mask
        vec_ref[2] += fold(up_grad * xhat_f)
        vec_ref[3] += fold(up_grad)
        grad_two = norm_back(up_grad, xhat_f, rstd_f, column(cols, C_FN))
        branch = pad8(grad_two).astype(bf16)
        gdn_ref[...] += dot_nt(hid[:, span(r)], branch)
        return act_low, normal, slope, xhat, rstd, low, bend, grad_two, dot(dnp_ref[...], branch)

    def ffn_back(r, held):
        act_low, normal, slope, xhat, rstd, low, bend, grad_two, back = held
        pre_low = (bend * back).astype(bf16)
        gup_ref[...] += dot_nt(pre_low, low)
        return act_low, normal, slope, xhat, rstd, grad_two, dot(upp_ref[...], pre_low)[:D]

    def leave(r, held):
        act_low, normal, slope, xhat, rstd, grad_two, back = held
        vec_ref[0] += fold(back * xhat)
        vec_ref[1] += fold(back)
        grad_conv = grad_two + norm_back(back, xhat, rstd, column(cols, C_F2))
        gc_ref[0, :, span(r)] = grad_conv
        project = pad8(grad_conv).astype(bf16)
        gpr_ref[...] += dot_nt(act_low, project)
        return normal, slope, dot(prp_ref[...], project)[:D]

    def last(r, held):
        normal, slope, back = held
        batch = slope * back
        bgd_ref[0, :, span(r)] = batch
        acc[0] += fold(batch * normal)
        acc[1] += fold(batch)

    skewed(GROUP, (enter, ffn_up, ffn_down, finish, ffn_back, leave, last))

    @pl.when(u == pl.num_programs(0) - 1)
    def _():
        lanes = lane_iota((D, 128))
        gain = jnp.sum(acc[0], axis=1, keepdims=True)
        shift = jnp.sum(acc[1], axis=1, keepdims=True)
        line = pad8(jnp.where(lanes == 0, gain, jnp.where(lanes == 1, shift, 0.0))).T[0:8]
        for d in range(sums_ref.shape[0]):
            sums_ref[d] = line


def second(lengths, stats, cot, aa, dep, weights):
    utts = cot.shape[0]
    big = (D, MAXLEN)
    outs = [
        (per_utt(big), (utts,) + big, bf16),
        (per_utt(big), (utts,) + big, f32),
        (per_utt(big), (utts,) + big, f32),
    ]
    for s in (stats.shape, (128, 128), (512, 128), (FF, 128), (128, 128), (4, D, 128)):
        outs.append((whole(s), s, f32))
    return pl.pallas_call(
        second_body,
        grid=(utts,),
        in_specs=[SMEM, whole(stats.shape)] + [per_utt(big)] * 3 + [whole(w.shape) for w in weights],
        out_specs=[o[0] for o in outs],
        out_shape=[jax.ShapeDtypeStruct(o[1], o[2]) for o in outs],
        scratch_shapes=[
            pltpu.VMEM((512, MAXLEN), bf16),
            pltpu.VMEM((2, D, 128), f32),
        ],
        name="second",
        **params(15000000000, 30000000),
    )(lengths, stats, cot, aa, dep, *weights)


def third_body(
    len_ref, sums_ref, stc_ref, bgd_ref, dep_ref, gat_ref, ri_ref, ra_ref, rc_ref,
    gc_far, xc_far, cn_far, sig_far, gated_far, att_far, qkv_far, prob_far, nrm_far, lf_far, xa_far, xf_far,
    cols_ref, up_ref, upp_ref, dnp_ref, wqkv_t_ref, wob_ref, pwp_ref,
    grad_ref, gdn_ref, gup_ref, gpw_ref, gqkv_ref, go_ref, rel_ref, rows_ref,
    gc_ref, xc_ref, cn_ref, sig_ref, gated_ref, att_ref, qkv_ref, prob_ref, nrm_ref, lf_ref, xa_ref, xf_ref, sems,
    hid, dgx, dgs, olg, agr, back_s, gg, near_s, far_s, vec_ref, cb, tot,
):
    far = (gc_far, xc_far, cn_far, sig_far, gated_far, att_far, qkv_far, prob_far, nrm_far, lf_far, xa_far, xf_far)
    near = (gc_ref, xc_ref, cn_ref, sig_ref, gated_ref, att_ref, qkv_ref, prob_ref, nrm_ref, lf_ref, xa_ref, xf_ref)
    u = pl.program_id(0)
    utts = pl.num_programs(0) - 1
    slot = 1 - u % 2

    def copies(step):
        at = step % 2
        return [pltpu.make_async_copy(far[i].at[step], near[i].at[at], sems.at[i, at]) for i in range(len(far))]

    cols = cols_ref

    @pl.when(u == 0)
    def _():
        set_tail(hid)
        conv_columns(cols_ref, cb)
        parts = sums_ref.shape[0]
        total = sums_ref[0]
        for d in range(1, parts):
            total = total + sums_ref[d]
        tot[...] = jnp.concatenate([total, jnp.zeros((120, 128), f32)], axis=0).T
        for ref in (gdn_ref, gup_ref, gpw_ref, gqkv_ref, go_ref, vec_ref, near_s, far_s):
            ref[...] = jnp.zeros_like(ref)

    @pl.when(u < utts)
    def _():
        for copy in copies(u):
            copy.start()

    @pl.when(u > 0)
    def _():
        for copy in copies(u - 1):
            copy.wait()

    def front():
        scale = stc_ref[:D, 1:2]
        lead = column(cols, C_BN) * scale
        share = lead * stc_ref[:D, 2:3]
        shift_part = share * tot[:D, 1:2]
        gain_part = share * tot[:D, 0:1] * scale
        for r in range(GROUP):
            normal = dep_ref[0, :, span(r)] - stc_ref[:D, 0:1]
            mask = plane_mask(r, len_ref[u])
            dgx[:, span(r)] = bgd_ref[0, :, span(r)] * lead - mask * (shift_part + normal * gain_part)

        def conv(f, carry):
            at = slice(8 * f, 8 * f + 8)
            tiles = [dgx[at, span(r)] for r in range(GROUP)]
            gated = [gat_ref[0, at, span(r)] for r in range(GROUP)]
            totals = [None] * GROUP
            taps = [None] * KERNEL
            for m in range(-HALF, HALF + GROUP):
                here = shifted(tiles, m)
                for r in range(GROUP):
                    k = r + HALF - m
                    if 0 <= k < KERNEL:
                        term = wide(cb[1 + k, at, :]) * here
                        totals[r] = term if totals[r] is None else totals[r] + term
                        part = fold(gated[r] * here)
                        taps[k] = part if taps[k] is None else taps[k] + part
            vec_ref[6, at, :] += fold(tiles[0] + tiles[1] + tiles[2])
            for k in range(KERNEL):
                vec_ref[7 + k, at, :] += taps[k]
            for r in range(GROUP):
                gg[at, span(r)] = totals[r]
            return carry

        for f in range(D // 8):
            conv(f, 0)

    def back():
        def gate(r, held):
            grad = gg[:, span(r)]
            sig = sig_ref[slot, :, span(r)]
            left = grad * sig
            right = grad * gated_ref[slot, :, span(r)] * (1.0 - sig)
            pre_low = jnp.concatenate([left, right], axis=0).astype(bf16)
            gpw_ref[...] += dot_nt(pre_low, cn_ref[slot, :, span(r)])
            return dot(pwp_ref[...], pre_low)[:D]

        def residual(r, back):
            xhat = xc_ref[slot, :, span(r)]
            vec_ref[0] += fold(back * xhat)
            vec_ref[1] += fold(back)
            grad = gc_ref[slot, :, span(r)] + norm_back(back, xhat, rc_ref[0, 0:1, span(r)], column(cols, C_CV))
            dgs[:, span(r)] = grad
            low = pad8(grad).astype(bf16)
            olg[128 * r : 128 * r + 128, :] = low
            return dot(wob_ref[r], low)

        made = [None] * GROUP

        def keep(r, found):
            go_ref[r] += dot_nt(window(att_ref.at[slot], r), olg[128 * r : 128 * r + 128, :])
            made[r] = found

        skewed(GROUP, (gate, residual, keep))
        agr[...] = join_windows(made).astype(bf16)

        def rows(w, h):
            return slice(GP * w + HP * h, GP * w + HP * h + HP)

        def enter(h, held):
            grad = agr[rows(0, h), :]
            back_s[rows(2, h), :] = dot_nt(grad, prob_ref[slot, h]).astype(bf16)
            return dot_tn(qkv_ref[slot, rows(2, h), :], grad)

        def soften(h, prob_grad):
            probs = prob_ref[slot, h].astype(f32)
            inner = jnp.sum(probs * prob_grad, axis=0, keepdims=True)
            score = probs * (prob_grad - inner)
            add_distances(score, near_s, far_s, h)
            return score.astype(bf16)

        def turn(h, low):
            back_s[rows(0, h), :] = (dot(qkv_ref[slot, rows(1, h), :], low) * SCALE).astype(bf16)
            back_s[rows(1, h), :] = (dot_nt(qkv_ref[slot, rows(0, h), :], low) * (1.0 / LOG2E)).astype(bf16)

        skewed(HEADS, (enter, soften, turn))

        def project(r, held):
            stack = jnp.concatenate([window(back_s, r, GP * w) for w in range(3)], axis=0)
            gqkv_ref[r] += dot_nt(stack, nrm_ref[slot, 128 * r : 128 * r + 128, :])
            return dot(wqkv_t_ref[r], stack)[:D], dot(up_ref[...], lf_ref[slot, :, span(r)])

        def ffn_in(r, held):
            back, half = held
            xhat = xa_ref[slot, :, span(r)]
            vec_ref[2] += fold(back * xhat)
            vec_ref[3] += fold(back)
            grad = dgs[:, span(r)] + norm_back(back, xhat, ra_ref[0, 0:1, span(r)], column(cols, C_AT))
            low = pad8(grad).astype(bf16)
            return grad, low, half, dot(dnp_ref[...], low)

        def ffn_mid(r, held):
            grad, branch, half, back = held
            t = jnp.tanh(half)
            hid[:FF, span(r)] = (half + half * t).astype(bf16)
            pre_low = ((1.0 + t) * (1.0 + half * (1.0 - t)) * back).astype(bf16)
            gdn_ref[...] += dot_nt(hid[:, span(r)], branch)
            gup_ref[...] += dot_nt(pre_low, lf_ref[slot, :, span(r)])
            return grad, dot(upp_ref[...], pre_low)[:D]

        def ffn_out(r, held):
            grad, back = held
            xhat = xf_ref[slot, :, span(r)]
            vec_ref[4] += fold(back * xhat)
            vec_ref[5] += fold(back)
            grad_ref[0, :, span(r)] = grad + norm_back(back, xhat, ri_ref[0, 0:1, span(r)], column(cols, C_F1))

        skewed(GROUP, (project, ffn_in, ffn_mid, ffn_out))

    @pl.when(u == 0)
    def _():
        front()

    @pl.when((u > 0) & (u < utts))
    def _():
        back()
        front()

    @pl.when(u == utts)
    def _():
        back()
        rows_ref[...] = lane_sums(vec_ref)
        found = []
        for h in range(HEADS):
            found.append(diagonal_sum(near_s[h], far_s[h]))
        stacked = jnp.concatenate(found + [jnp.zeros((4, 2 * LG), f32)], axis=0)
        high = stacked.astype(bf16)
        rest = stacked - high.astype(f32)
        mid = rest.astype(bf16)
        rest = rest - mid.astype(f32)
        select = distance_select()
        rel_ref[...] = dot_nt(high, select) + dot_nt(mid, select) + dot_nt(rest.astype(bf16), select)


def third(lengths, sums, stc, soon, later, weights):
    utts = soon[0].shape[0]
    big = (D, MAXLEN)
    outs = [(one_late(big), (utts,) + big)]
    for s in ((512, 128), (FF, 128), (240, 128), (GROUP, 3 * WROWS, 128), (GROUP, WROWS, 128), (8, 256), (128, 128)):
        outs.append((whole(s), s))
    return pl.pallas_call(
        third_body,
        grid=(utts + 1,),
        in_specs=[SMEM, whole(sums.shape), whole(stc.shape)]
        + [at_most(s.shape[1:], utts) for s in soon[:3]]
        + [one_late(s.shape[1:]) for s in soon[3:]]
        + [pl.BlockSpec(memory_space=pl.ANY)] * len(later)
        + [whole(w.shape) for w in weights],
        out_specs=[o[0] for o in outs],
        out_shape=[jax.ShapeDtypeStruct(o[1], f32) for o in outs],
        scratch_shapes=[pltpu.VMEM((2,) + s.shape[1:], s.dtype) for s in later]
        + [
            pltpu.SemaphoreType.DMA((len(later), 2)),
            pltpu.VMEM((512, MAXLEN), bf16),
            pltpu.VMEM(big, f32),
            pltpu.VMEM(big, f32),
            pltpu.VMEM((GP, LG), bf16),
            pltpu.VMEM((GP, LG), bf16),
            pltpu.VMEM((3 * GP, LG), bf16),
            pltpu.VMEM(big, f32),
            pltpu.VMEM((HEADS, 128, 384), f32),
            pltpu.VMEM((HEADS, 2, 8, 128), f32),
            pltpu.VMEM((22, D, 128), f32),
            pltpu.VMEM((KERNEL + 1, D, 128), f32),
            pltpu.VMEM((128, 128), f32),
        ],
        name="third",
        **params(20000000000, 80000000),
    )(lengths, sums, stc, *soon, *later, *weights)


def clean(block):
    return jnp.where(lane_iota(block.shape) < D, block, 0.0)


def set_rows(tb, ref, at):
    for k, to in enumerate(at):
        tb[to : to + 1, :] = ref[k : k + 1, :]


def set_ffn(tb, base, dn_ref, up_ref):
    tb[base + 486 : base + 967, :] = 0.5 * clean(dn_ref[0 : FF + 1, :])
    for q in range(4):
        block = pad8(up_ref[D * q : D * q + D, :]).T
        tb[pl.ds(base + 2 + q, D, stride=4), :] = block[:D]
        tb[base + 482 + q : base + 483 + q, :] = block[D : D + 1]


def flatten(tb, base, flat, at_row, y_count, offset):
    for k in range(15):
        at = 128 * k + offset
        first_row, col = at // D, at % D
        many = (y_count - k + 14) // 15
        here = lane_iota((many, 128))
        got = tb[pl.ds(base + first_row, many, stride=16), :]
        if col:
            got = pltpu.roll(got, 128 - col, 1)
        then = pltpu.roll(tb[pl.ds(base + first_row + 1, many, stride=16), :], D - col, 1)
        got = jnp.where(here < D - col, got, then)
        if 2 * D - col < 128:
            then = pltpu.roll(tb[pl.ds(base + first_row + 2, many, stride=16), :], 2 * D - col, 1)
            got = jnp.where(here < 2 * D - col, got, then)
        flat[pl.ds(at_row + k, many, stride=15), :] = got


SPLIT = F2 - TAIL
ROWS_LAST = ROWS_TAIL - SPLIT
LAST_AT = TAIL_AT + D * SPLIT
LAST_Y = LAST_AT // 128
LAST_COUNT = (LIVE - 1) // 128 - LAST_Y + 1


def ahead_body(dn_ref, up_ref, vec_ref, out_ref, tb, wt):
    tb[0:8, :] = jnp.zeros((8, 128), f32)
    tb[8 + ROWS_LAST :, :] = jnp.zeros((tb.shape[0] - 8 - ROWS_LAST, 128), f32)
    wt[...] = lane_sums(vec_ref)
    set_rows(tb, wt, (8, 9, 8 + FN - F2, 9 + FN - F2))
    set_ffn(tb, 8, dn_ref, up_ref)
    flatten(tb, 7, out_ref, 0, LAST_COUNT, D + 128 * LAST_Y - LAST_AT)


def pack_ahead(dn, up, vec):
    return pl.pallas_call(
        ahead_body,
        out_shape=o((LAST_COUNT, 128), f32),
        scratch_shapes=[pltpu.VMEM((ROWS_LAST + 24, 128), f32), pltpu.VMEM((128, 128), f32)],
        name="ahead",
        **params(2 * 10**9, 8 * 10**6),
    )(dn, up, vec)


def pack_body(
    me_ref, last_ref, dn1_ref, up1_ref, pr_ref, pw_ref, qkv_ref, o_ref, rel_ref, vec_ref, sums_ref,
    keep_ref, send_ref, tb, flat, stage, wt,
):
    tb[ROWS_HEAD:TAIL, :] = jnp.zeros((TAIL - ROWS_HEAD, 128), f32)
    tb[F2:, :] = jnp.zeros((tb.shape[0] - F2, 128), f32)
    set_rows(tb, vec_ref, (CV, CV + 1, AT, AT + 1, F1, F1 + 1, CV + 259) + tuple(CV + 244 + k for k in range(KERNEL)))
    tb[CV + 260 : CV + 262, :] = sums_ref[0, 0:2, :]
    set_ffn(tb, F1, dn1_ref, up1_ref)
    for q in range(2):
        block = pad8(pw_ref[D * q : D * q + D, :]).T
        tb[pl.ds(CV + 2 + q, D, stride=2), :] = block[:D]
        tb[CV + 242 + q : CV + 243 + q, :] = block[D : D + 1]
    tb[CV + 262 : CV + 383, :] = clean(pr_ref[0 : D + 1, :])

    def gathered(ref, base):
        wt[...] = jnp.zeros_like(wt)
        for to, r, src, many in segments():
            start = base + to - WIN[r]
            wt[src : src + many, :] += ref[r, start : start + many, :]
        return wt[...]

    for w, at, bias_at in ((0, AT + 2, AT + 122), (1, AT + 123, None), (2, AT + 243, AT + 363)):
        block = gathered(qkv_ref, WROWS * w).T
        tb[at : at + D, :] = block[:D]
        if bias_at is not None:
            tb[bias_at : bias_at + 1, :] = block[D : D + 1]
    tb[AT + 364 : AT + 484, :] = clean(gathered(o_ref, 0)[:D])
    bias = sum(o_ref[r, MARKS[r] : MARKS[r] + 1, :] for r in range(GROUP))
    tb[AT + 484 : AT + 485, :] = clean(bias)

    tail_y = TAIL_AT // 128
    flat[LAST_Y + LAST_COUNT :, :] = jnp.zeros((flat.shape[0] - LAST_Y - LAST_COUNT, 128), f32)
    flat[REL_AT // 128 + 1 : tail_y, :] = jnp.zeros((tail_y - REL_AT // 128 - 1, 128), f32)
    flatten(tb, 0, flat, 0, REL_AT // 128 + 1, 0)
    flatten(tb, TAIL - 1, flat, tail_y, LAST_Y - tail_y + 1, 128 * tail_y - TAIL_AT + D)
    flat[LAST_Y : LAST_Y + 1, :] += last_ref[0:1, :]
    flat[LAST_Y + 1 : LAST_Y + LAST_COUNT, :] = last_ref[1:, :]
    here = lane_iota((1, 128))
    width = 2 * REL + 1
    for h in range(HEADS):
        at = REL_AT + width * h
        for y in range(at // 128, (at + width - 1) // 128 + 1):
            lo, hi = max(at - 128 * y, 0), min(at + width - 128 * y, 128)
            shift = (at - 128 * y) % 256
            turned = rel_ref[h : h + 1, :]
            if shift:
                turned = pltpu.roll(turned, shift, 1)
            flat[y : y + 1, :] += jnp.where((here >= lo) & (here < hi), turned[:, :128], 0.0)
    parts, padded = 2 * keep_ref.shape[0], keep_ref.shape[1]
    rows = flat.shape[0] // parts
    for d in range(parts):
        stage[d, 0:rows, :] = flat[rows * d : rows * (d + 1), :]
        if rows < padded:
            stage[d, rows:padded, :] = jnp.zeros((padded - rows, 128), f32)
    for offset in range(0, parts, 2):
        keep_ref[place(offset, parts)] = stage[me_ref[0] ^ offset]
        send_ref[place(offset, parts)] = stage[me_ref[0] ^ (offset + 1)]


def pack(parts, rows, me, grads):
    half = o((parts // 2, whole_tiles(rows), 128), f32)
    return pl.pallas_call(
        pack_body,
        in_specs=[SMEM] + [VMEM] * len(grads),
        out_shape=[half, half],
        scratch_shapes=[
            pltpu.VMEM((F2 + 24, 128), f32),
            pltpu.VMEM((parts * rows, 128), f32),
            pltpu.VMEM((parts, whole_tiles(rows), 128), f32),
            pltpu.VMEM((128, 128), f32),
        ],
        name="pack",
        **params(10**9, 5 * 10**6),
    )(me, *grads)


def update_tables(total_len):
    rates = np.zeros(total_len, np.float32)
    decays = np.zeros(total_len, np.float32)
    vector, gain, ffn = (D, 0.1, 0.0), (D, 0.3, 0.0), lambda n, fan: (n, fan**-0.5, 0.01)
    block = [gain, vector, ffn(D * FF, D), (FF, 0.1, 0.0), ffn(FF * D, FF), vector]
    square = ffn(D * D, D)
    pieces = block + [gain, vector, square, vector, square, square, vector, ffn(D * D, 6.0 * D / MAXLEN), vector]
    pieces += [(HEADS * (2 * REL + 1), 0.5, 0.0)]
    pieces += [gain, vector, ffn(2 * D * D, D), (2 * D, 0.1, 0.0), ffn(KERNEL * D, KERNEL), vector, gain, vector]
    pieces += [square, vector] + block + [gain, vector]
    offset = 0
    for entries, rate, decay in pieces:
        rates[offset : offset + entries] = rate
        decays[offset : offset + entries] = decay
        offset += entries
    return rates, decays


def whole_tiles(rows):
    return -(-rows // 8) * 8


def digits(devices):
    found, stride = [], 1
    while stride < devices:
        size = min(2 if stride == 1 else 4, devices // stride)
        found.append((stride, size))
        stride *= size
    return found


def place(offset, devices):
    at, weight = 0, devices
    for stride, size in digits(devices):
        weight //= size
        at = at + ((offset // stride) % size) * weight
    return at


def partner(values, offset, devices):
    return lax.ppermute(values, "dp", [(i, i ^ offset) for i in range(devices)])


def gather(values, devices, beside):
    held, made = values[None], []
    for k, (stride, size) in enumerate(reversed(digits(devices))):
        parts = [held] + [partner(held, stride * j, devices) for j in range(1, size)]
        if k < len(beside):
            parts, found = lax.optimization_barrier((parts, beside[k]))
            made.append(found)
        held = jnp.concatenate(parts, axis=0)
    return held, made + beside[len(made) :]


def scatter_sum(keep, send, devices, beside):
    total = keep + partner(send, 1, devices)
    made = None
    for k, (stride, size) in enumerate(digits(devices)[1:]):
        parts = total.reshape((size, total.shape[0] // size) + total.shape[1:])
        kind = bf16 if stride == 2 else f32
        found = [partner(parts[j].astype(kind), stride * j, devices) for j in range(1, size)]
        if k < len(beside):
            found, made = lax.optimization_barrier((found, beside[k](made)))
        total = parts[0]
        for part in found:
            total = total + part.astype(f32)
    for work in beside[max(0, len(digits(devices)) - 1) :]:
        made = work(made)
    return total, made


def local(frames, lengths, cotangent, master, moment_one, moment_two, average):
    shard_len = master.shape[0]
    devices = lax.axis_size("dp")
    rows = shard_len // 128
    me = lax.axis_index("dp").astype(jnp.int32).reshape(1)
    entered = enter(jnp.transpose(frames, (0, 2, 1)))
    mine = jnp.pad(master.astype(bf16).reshape(rows, 128), ((0, whole_tiles(rows) - rows), (0, 0)))
    cp = reorder(inward, jnp.transpose(cotangent, (0, 2, 1)), entered[3], "inward")
    gathered, (entered, cp) = gather(mine, devices, [entered, cp])
    xp, xf, rs_in, pm = entered
    early, late = prepare(me, gathered, rows)
    up1, dn1, wqkv, wo, pw, cols, base = early
    upp1, dnp1, up2, upp2, dn2, dnp2, pwp, pr, prp, wqkvt, wob = late
    lf, xa, nrm, qkv, prob, att, aa, xc, cn, gat, sig, ra, rc, dep, st = first(
        devices, lengths, xp, xf, (cols, up1, dn1, wqkv, wo, pw, base)
    )
    stats = lax.all_to_all(st, "dp", 0, 0)
    out, bgd, gc, sums, stc, gdn2, gup2, gpr, vec2 = second(
        lengths, stats, cp, aa, dep, (cols, up2, upp2, dn2, dnp2, pr, prp)
    )
    all_sums = lax.all_to_all(sums, "dp", 0, 0)
    last = pack_ahead(gdn2, gup2, vec2)
    out = reorder(outward, out, pm, "outward")
    (all_sums, last, out) = lax.optimization_barrier((all_sums, last, out))
    grad, gdn1, gup1, gpw, gqkv, go, rel, vec3 = third(
        lengths, all_sums, stc,
        (bgd, dep, gat, rs_in, ra, rc),
        (gc, xc, cn, sig, gat, att, qkv, prob, nrm, lf, xa, xf),
        (cols, up1, upp1, dnp1, wqkvt, wob, pwp),
    )
    keep, send = pack(devices, rows, me, (last, gdn1, gup1, gpr, gpw, gqkv, go, rel, vec3, sums))
    utts = grad.shape[0]
    begin = (utts + 1) // 2
    reduced, gin = scatter_sum(
        keep,
        send,
        devices,
        [
            lambda made: reorder(permute_out_wide, grad, pm, "leave", 0, begin),
            lambda made: reorder(permute_out_wide, grad, pm, "leave", begin, utts - begin, made),
        ],
    )
    reduced = reduced.reshape(-1)[:shard_len]
    rates_np, decays_np = update_tables(shard_len * devices)
    start_at = lax.axis_index("dp") * shard_len
    rates = lax.dynamic_slice_in_dim(jnp.asarray(rates_np), start_at, shard_len)
    decays = lax.dynamic_slice_in_dim(jnp.asarray(decays_np), start_at, shard_len)
    correction = 1.0 - 0.5**STEP
    new_one = 0.5 * moment_one + 0.5 * reduced
    new_two = 0.5 * moment_two + 0.5 * reduced * reduced
    direction = new_one / correction / (jnp.sqrt(new_two / correction) + EPS_ADAM)
    new_master = master - rates * (direction + decays * master)
    new_average = 0.75 * average + 0.25 * new_master
    return (
        jnp.transpose(out, (0, 2, 1)),
        jnp.transpose(gin, (0, 2, 1)),
        reduced,
        new_master,
        new_one,
        new_two,
        new_average,
    )


def solution(mesh):
    three = P("dp", None, None)
    one = P("dp")
    in_specs = (three, one, three, one, one, one, one)
    out_specs = (three, three, one, one, one, one, one)
    return jax.shard_map(local, mesh=mesh, in_specs=in_specs, out_specs=out_specs, check_vma=False)
```
